32 devices in a mesh: row: 4 (over y, x), col: 8 (over z, core).
Axes of the slice: x: 2, y: 2, z: 4, core: 2. Of those that a mesh axis runs over, the one named last changes fastest.
Arguments:
- homolog_tensor: float32 [256, 256, 256], P('row', 'col'), may hold values from -6 to 6
- couplings: float32 [256, 256, 128], P('row', 'col'), may hold values from -6 to 6
- attention_probe_matrix: bfloat16 [256, 256], replicated, may hold values from -4 to 4
- attention_extra_matrices: bfloat16 [256, 768], replicated, may hold values from -0.375 to 0.375
- attention_final_matrix: bfloat16 [256, 256], replicated, may hold values from -0.375 to 0.375
- tensor_entry_matrices: bfloat16 [256, 64], replicated, may hold values from -0.375 to 0.375
- tensor_final_matrix: bfloat16 [1024, 128], replicated, may hold values from -3 to 3
- incoming_entry_matrices: bfloat16 [128, 512], replicated, may hold values from -0.5 to 0.5
- incoming_switch_matrix: bfloat16 [128, 128], replicated, may hold values from -0.5 to 0.5
- incoming_final_matrix: bfloat16 [128, 128], replicated, may hold values from -0.5 to 0.5
Outputs:
- refreshed_homologs: float32 [256, 256, 256], P('row', 'col')
- pair_output: float32 [256, 256, 128], P('row', 'col')
The draws below stay inside these ranges and needn't reach their ends.
All inputs are finite; a program needn't handle non-finite values.
Results may differ from the reference program's by a relative error of at most 0.017.
The reference program's roundings to bfloat16 on the way count: a program that leaves them out, or rounds other values in their place, can miss the bound.
Values may be sent and summed in bfloat16 or wider, within the bound.
No kernel may reach another device: no remote copies, remote signals or barrier semaphores. Data moves between devices by JAX's collectives and lax.ppermute only.
A program may use at most 128 MiB of HBM per device.

```python
import jax
import jax.numpy as jnp
from jax import lax

FEATURE_DEPTH = 256
C_Z = 128
TENSOR_FEATURES = 32
C_TRI = 128
ATTENTION_UNITS = 8
UNIT_WIDTH = 32
AMINO_LENGTH = 256
HOMOLOG_NUMBER = 256


def draw_attention_probe_matrix(key, part):
    key = jax.random.fold_in(key, 7)
    attended_contents = jnp.clip(jax.random.normal(key, (FEATURE_DEPTH, ATTENTION_UNITS * UNIT_WIDTH), jnp.float32) * FEATURE_DEPTH ** (-0.5), -4.0, 4.0)
    return attended_contents.astype(jnp.bfloat16)


def level_of(own_key, extent, pieces, smallest, top_value):
    def one(position, parts):
        heights = jax.random.uniform(jax.random.fold_in(jax.random.fold_in(own_key, 6), position), (parts,), jnp.float32, smallest / len(pieces), top_value / len(pieces))
        return jnp.repeat(jnp.exp(heights), extent[position] // parts).reshape((-1,) + (1,) * (len(extent) - position - 1))

    loudness = one(*pieces[0])
    for cut in pieces[1:]:
        loudness = loudness * one(*cut)
    return loudness


def bell_draw(stream_key, extent, scale, bound, split=(), dtype=jnp.bfloat16):
    values = jax.random.normal(stream_key, extent, jnp.float32) * scale
    if len(split) > 0:
        values = level_of(stream_key, extent, split, -0.22, 0.18) * values
    return jnp.clip(values, min=-bound, max=bound).astype(dtype)


def setup_inputs(seed: int = 0) -> dict:
    seeds = jax.random.split(jax.random.key(seed), 11)
    homolog_tensor = bell_draw(seeds[0], (HOMOLOG_NUMBER, AMINO_LENGTH, FEATURE_DEPTH), 1.0, 6.0, ((0, 4), (1, 8)), jnp.float32)
    couplings = bell_draw(seeds[1], (AMINO_LENGTH, AMINO_LENGTH, C_Z), 1.0, 6.0, ((0, 4), (1, 8)), jnp.float32)
    attention_probe_matrix = draw_attention_probe_matrix(jax.random.fold_in(seeds[10], 71), 0)
    attention_extra_matrices = bell_draw(seeds[3], (FEATURE_DEPTH, 3 * ATTENTION_UNITS * UNIT_WIDTH), FEATURE_DEPTH ** -0.5, 0.375)
    attention_final_matrix = bell_draw(seeds[4], (ATTENTION_UNITS * UNIT_WIDTH, FEATURE_DEPTH), (ATTENTION_UNITS * UNIT_WIDTH) ** -0.5, 0.375)
    tensor_entry_matrices = bell_draw(seeds[5], (FEATURE_DEPTH, 2 * TENSOR_FEATURES), FEATURE_DEPTH ** -0.5, 0.375)
    tensor_final_matrix = bell_draw(seeds[6], (TENSOR_FEATURES * TENSOR_FEATURES, C_Z), (max(1, TENSOR_FEATURES * TENSOR_FEATURES // HOMOLOG_NUMBER)) ** -0.5, 3.0)
    incoming_entry_matrices = bell_draw(seeds[7], (C_Z, 4 * C_TRI), C_Z ** -0.5, 0.5)
    incoming_switch_matrix = bell_draw(seeds[8], (C_Z, C_Z), C_Z ** -0.5, 0.5)
    incoming_final_matrix = bell_draw(seeds[9], (C_TRI, C_Z), C_TRI ** -0.5, 0.5)
    return dict(homolog_tensor=homolog_tensor, couplings=couplings, attention_probe_matrix=attention_probe_matrix, attention_extra_matrices=attention_extra_matrices, attention_final_matrix=attention_final_matrix, tensor_entry_matrices=tensor_entry_matrices, tensor_final_matrix=tensor_final_matrix, incoming_entry_matrices=incoming_entry_matrices, incoming_switch_matrix=incoming_switch_matrix, incoming_final_matrix=incoming_final_matrix)


def standardise_features(attended_contents):
    centre = lax.optimization_barrier(jnp.mean(attended_contents, axis=-1, keepdims=True))
    centred = attended_contents - centre
    spread = lax.optimization_barrier(jnp.mean(centred * centred, axis=-1, keepdims=True))
    return centred * lax.rsqrt(spread + 1e-05)

def attend_column(column, attention_probe_matrix, attention_extra_matrices):
    homolog_amount = column.shape[0]
    inner_width = ATTENTION_UNITS * UNIT_WIDTH
    queries = (jnp.dot(column, attention_probe_matrix, preferred_element_type=jnp.float32) * UNIT_WIDTH ** (-0.5)).astype(jnp.bfloat16)
    projected_rows = jnp.dot(column, attention_extra_matrices, preferred_element_type=jnp.float32)
    key_rows = projected_rows[:, :inner_width].astype(jnp.bfloat16)
    value_rows = projected_rows[:, inner_width:2 * inner_width].astype(jnp.bfloat16)
    gate_cols = jax.nn.sigmoid(projected_rows[:, 2 * inner_width:])
    queries = queries.reshape(homolog_amount, ATTENTION_UNITS, UNIT_WIDTH).astype(jnp.float32)
    key_rows = key_rows.reshape(homolog_amount, ATTENTION_UNITS, UNIT_WIDTH).astype(jnp.float32)
    value_rows = value_rows.reshape(homolog_amount, ATTENTION_UNITS, UNIT_WIDTH).astype(jnp.float32)
    scores = jnp.einsum('shd,thd->hst', queries, key_rows)
    weights = jax.nn.softmax(scores, axis=-1).astype(jnp.bfloat16)
    attended = jnp.einsum('hst,thd->shd', weights.astype(jnp.float32), value_rows).reshape(homolog_amount, inner_width)
    return (attended * gate_cols).astype(jnp.bfloat16)

def reference(homolog_tensor, couplings, attention_probe_matrix, attention_extra_matrices, attention_final_matrix, tensor_entry_matrices, tensor_final_matrix, incoming_entry_matrices, incoming_switch_matrix, incoming_final_matrix):
    homolog_amount = homolog_tensor.shape[0]
    amino_number = homolog_tensor.shape[1]
    standardised = standardise_features(homolog_tensor).astype(jnp.bfloat16)
    gated = lax.map(lambda column: attend_column(column, attention_probe_matrix, attention_extra_matrices), jnp.transpose(standardised, (1, 0, 2)))
    gated = jnp.transpose(gated, (1, 0, 2))
    residual_change = jnp.dot(gated.reshape(-1, ATTENTION_UNITS * UNIT_WIDTH), attention_final_matrix, preferred_element_type=jnp.float32)
    refreshed_homologs = homolog_tensor + residual_change.reshape(homolog_tensor.shape)
    standardised_result = standardise_features(refreshed_homologs).astype(jnp.bfloat16).reshape(-1, FEATURE_DEPTH)
    projected_rows = jnp.dot(standardised_result, tensor_entry_matrices, preferred_element_type=jnp.float32).astype(jnp.bfloat16)
    projected_rows = projected_rows.reshape(homolog_amount, amino_number, 2 * TENSOR_FEATURES)
    left_alignment = projected_rows[:, :, :TENSOR_FEATURES].reshape(homolog_amount, amino_number * TENSOR_FEATURES)
    right_alignment = projected_rows[:, :, TENSOR_FEATURES:].reshape(homolog_amount, amino_number * TENSOR_FEATURES)
    residue_block = min(64, amino_number)
    left_residue_blocks = jnp.transpose(left_alignment.reshape(homolog_amount, amino_number // residue_block, residue_block * TENSOR_FEATURES), (1, 0, 2))

    def outer_block(left_residue_block):
        outer_product_sum = jnp.dot(left_residue_block.T, right_alignment, preferred_element_type=jnp.float32)
        outer_product_sum = outer_product_sum.reshape(residue_block, TENSOR_FEATURES, amino_number, TENSOR_FEATURES)
        outer_product_sum = jnp.transpose(outer_product_sum, (0, 2, 1, 3)).reshape(residue_block * amino_number, TENSOR_FEATURES * TENSOR_FEATURES)
        outer_mean = (outer_product_sum / homolog_amount).astype(jnp.bfloat16)
        return jnp.dot(outer_mean, tensor_final_matrix, preferred_element_type=jnp.float32).reshape(residue_block, amino_number, C_Z)
    opm_update = lax.map(outer_block, left_residue_blocks).reshape(amino_number, amino_number, C_Z)
    pair_mid = couplings + opm_update
    pair_normed = standardise_features(pair_mid).astype(jnp.bfloat16).reshape(-1, C_Z)
    projected_rows = jnp.dot(pair_normed, incoming_entry_matrices, preferred_element_type=jnp.float32)
    left_pair = (jax.nn.sigmoid(projected_rows[:, C_TRI:2 * C_TRI]) * projected_rows[:, :C_TRI]).astype(jnp.bfloat16)
    right_pair = (jax.nn.sigmoid(projected_rows[:, 3 * C_TRI:]) * projected_rows[:, 2 * C_TRI:3 * C_TRI]).astype(jnp.bfloat16)
    gate_pair = jax.nn.sigmoid(jnp.dot(pair_normed, incoming_switch_matrix, preferred_element_type=jnp.float32))
    left_pair = left_pair.reshape(amino_number, amino_number, C_TRI).astype(jnp.float32)
    right_pair = right_pair.reshape(amino_number, amino_number, C_TRI).astype(jnp.float32)
    product = jnp.einsum('kic,kjc->ijc', left_pair, right_pair)
    product_normed = standardise_features(product).astype(jnp.bfloat16).reshape(-1, C_TRI)
    tri_update = jnp.dot(product_normed, incoming_final_matrix, preferred_element_type=jnp.float32)
    pair_output = pair_mid + (gate_pair * tri_update).reshape(couplings.shape)
    return (refreshed_homologs, pair_output)
```

```python
import functools

import jax
import jax.numpy as jnp
from jax import lax
from jax.experimental import pallas as pl
from jax.experimental.pallas import tpu as pltpu
from jax.sharding import PartitionSpec as P

FEATURE_DEPTH = 256
C_Z = 128
TENSOR_FEATURES = 32
C_TRI = 128
ATTENTION_UNITS = 8
UNIT_WIDTH = 32
EPS = 1e-05
HALF = C_TRI // 2
GROUP = 4
F32 = jnp.float32
BF16 = jnp.bfloat16
NT = (((1,), (1,)), ((), ()))
VMEM_LIMIT = 56 * 1024 * 1024


def matmul(left, right):
    return jnp.dot(left, right, preferred_element_type=F32)


def matmul_nt(left, right):
    return lax.dot_general(left, right, NT, preferred_element_type=F32)


def sigmoid(values):
    return 1.0 / (1.0 + jnp.exp(-values))


def params(*semantics):
    return pltpu.CompilerParams(
        dimension_semantics=semantics or None, vmem_limit_bytes=VMEM_LIMIT
    )


def standardise_kernel(first_ref, second_ref, high_ref, low_ref):
    seqs, residues, lanes = first_ref.shape
    first_rows = first_ref.reshape(seqs * residues, lanes)
    second_rows = second_ref.reshape(seqs * residues, lanes)
    lane = lax.broadcasted_iota(jnp.int32, (seqs, 128), 1)
    spreads = jnp.zeros((seqs, 128), F32)
    for n in range(residues):
        rows = pl.ds(n, seqs, stride=residues)
        column = jnp.concatenate([first_rows[rows, :], second_rows[rows, :]], axis=1)
        centred = column - jnp.mean(column, axis=1, keepdims=True)
        variance = jnp.mean(centred * centred, axis=1, keepdims=True) + EPS
        scale = lax.rsqrt(variance)
        normed = centred * scale
        high = normed.astype(BF16)
        high_ref[n] = high
        low_ref[n, :seqs, :] = (normed - high.astype(F32)).astype(BF16)
        spreads = jnp.where(lane == n, variance * scale, spreads)
    spreads = spreads.T
    row = lax.broadcasted_iota(jnp.int32, (16, seqs), 0)
    for n in range(residues):
        spread = jnp.broadcast_to(spreads[n : n + 1, :], (16, seqs))
        coarse = spread.astype(BF16).astype(F32)
        kept = jnp.where(row == 0, coarse, jnp.where(row == 1, spread - coarse, 0.0))
        kept = jnp.concatenate([kept, jnp.zeros((16, 2 * lanes - seqs), F32)], axis=1)
        low_ref[n, seqs:, :] = kept.astype(BF16)


def standardise(block):
    seqs, residues, depth = block.shape
    half = depth // 2
    return pl.pallas_call(
        standardise_kernel,
        grid=(residues // 8,),
        in_specs=[
            pl.BlockSpec((seqs, 8, half), lambda g: (0, g, 0)),
            pl.BlockSpec((seqs, 8, half), lambda g: (0, g, 1)),
        ],
        out_specs=[
            pl.BlockSpec((8, seqs, depth), lambda g: (g, 0, 0)),
            pl.BlockSpec((8, seqs + 16, depth), lambda g: (g, 0, 0)),
        ],
        out_shape=[
            jax.ShapeDtypeStruct((residues, seqs, depth), BF16),
            jax.ShapeDtypeStruct((residues, seqs + 16, depth), BF16),
        ],
        compiler_params=params("arbitrary"),
        name="standardise",
    )(block, block)


def attention_kernel(normed_ref, key_ref, others_ref, gated_ref, turned_ref):
    blocks, _, seqs, depth = normed_ref.shape
    total = blocks * seqs
    inner = ATTENTION_UNITS * UNIT_WIDTH
    column = normed_ref[...].reshape(total, depth)
    key_rows = matmul(column, key_ref[...]).astype(BF16)
    projected = matmul_nt(others_ref[...], column)
    queries = (projected[:inner] * UNIT_WIDTH ** (-0.5)).astype(BF16)
    value_rows = projected[inner : 2 * inner].astype(BF16)
    gates = sigmoid(projected[2 * inner :])
    ones = jnp.ones((16, total), BF16)
    parts = []
    for h in range(ATTENTION_UNITS):
        low, high = h * UNIT_WIDTH, (h + 1) * UNIT_WIDTH
        pieces = [queries[low:high]]
        if low > 0:
            pieces.insert(0, jnp.zeros((low, total), BF16))
        if high < inner:
            pieces.append(jnp.zeros((inner - high, total), BF16))
        scores = matmul(key_rows, jnp.concatenate(pieces, axis=0))
        weights = jnp.exp(scores - jnp.max(scores, axis=0, keepdims=True)).astype(BF16)
        attended = matmul(jnp.concatenate([value_rows[low:high], ones], axis=0), weights)
        parts.append(
            attended[:UNIT_WIDTH] * (gates[low:high] / attended[UNIT_WIDTH : UNIT_WIDTH + 1])
        )
    gated = jnp.concatenate(parts, axis=0)
    turned_ref[0] = gated.astype(BF16)
    gated_ref[...] = gated.T.astype(BF16).reshape(gated_ref.shape)


def attention(normed, key_matrix, other_matrices):
    blocks, residues, seqs, depth = normed.shape
    total = blocks * seqs
    inner = ATTENTION_UNITS * UNIT_WIDTH
    return pl.pallas_call(
        attention_kernel,
        grid=(residues,),
        in_specs=[
            pl.BlockSpec((blocks, 1, seqs, depth), lambda n: (0, n, 0, 0)),
            pl.BlockSpec((depth, inner), lambda n: (0, 0)),
            pl.BlockSpec((3 * inner, depth), lambda n: (0, 0)),
        ],
        out_specs=[
            pl.BlockSpec((blocks, 1, seqs, inner), lambda n: (0, n, 0, 0)),
            pl.BlockSpec((1, inner, total), lambda n: (n, 0, 0)),
        ],
        out_shape=[
            jax.ShapeDtypeStruct((blocks, residues, seqs, inner), BF16),
            jax.ShapeDtypeStruct((residues, inner, total), BF16),
        ],
        compiler_params=params("arbitrary"),
        name="attention",
    )(normed, key_matrix, other_matrices)


def alignment_kernel(high_ref, low_ref, turned_ref, final_ref, entry_ref, left_ref, right_ref):
    blocks, _, seqs, depth = high_ref.shape
    total = blocks * seqs
    low = low_ref[:, 0, :seqs, :].reshape(total, depth)
    column = high_ref[...].reshape(total, depth).astype(F32) + low.astype(F32)
    spreads = []
    for block in range(blocks):
        kept = low_ref[block, 0, seqs:, :seqs].astype(F32)
        spreads.append(jnp.sum(kept, axis=0, keepdims=True))
    spread = jnp.concatenate(spreads, axis=1)
    updated = column.T * spread + matmul(final_ref[...], turned_ref[0])
    centred = updated - jnp.mean(updated, axis=0, keepdims=True)
    variance = jnp.mean(centred * centred, axis=0, keepdims=True)
    normed = (centred * lax.rsqrt(variance + EPS)).astype(BF16)
    projected = matmul(entry_ref[...], normed).astype(BF16)
    left_ref[0] = projected[:TENSOR_FEATURES]
    right_ref[0] = projected[TENSOR_FEATURES:]


def alignment(high, low, turned, final_matrix, entry_matrices):
    blocks, residues, seqs, depth = high.shape
    total = blocks * seqs
    side = jax.ShapeDtypeStruct((residues, TENSOR_FEATURES, total), BF16)
    side_spec = pl.BlockSpec((1, TENSOR_FEATURES, total), lambda n: (n, 0, 0))
    return pl.pallas_call(
        alignment_kernel,
        grid=(residues,),
        in_specs=[
            pl.BlockSpec((blocks, 1, seqs, depth), lambda n: (0, n, 0, 0)),
            pl.BlockSpec((blocks, 1, seqs + 16, depth), lambda n: (0, n, 0, 0)),
            pl.BlockSpec((1, depth, total), lambda n: (n, 0, 0)),
            pl.BlockSpec(final_matrix.shape, lambda n: (0, 0)),
            pl.BlockSpec(entry_matrices.shape, lambda n: (0, 0)),
        ],
        out_specs=[side_spec, side_spec],
        out_shape=[side, side],
        compiler_params=params("arbitrary"),
        name="alignment",
    )(high, low, turned, final_matrix, entry_matrices)


def pair_kernel(
    left_ref,
    right_ref,
    spread_ref,
    couplings_ref,
    entry_ref,
    switch_ref,
    mid_ref,
    gate_ref,
    left_pair_ref,
    right_pair_ref,
    outer_ref,
    sum_ref,
    left_rows_ref,
    right_rows_ref,
):
    features = TENSOR_FEATURES
    total = left_ref.shape[1]
    rows = left_ref.shape[0] // features
    columns = right_ref.shape[0] // features
    groups = columns // GROUP
    pairs = features // 2
    step = 512

    def outer_step(m, carry):
        piece = left_ref[pl.ds(pl.multiple_of(m * step, step), step), :]
        for g in range(0, groups, 2):
            wide = right_ref[g * 128 : (g + 2) * 128, :]
            outer = matmul_nt(piece, wide) * (1.0 / total)
            target = pl.ds(pl.multiple_of(m * step, step), step)
            outer_ref[g, target, :] = outer[:, :128]
            outer_ref[g + 1, target, :] = outer[:, 128:]
        return carry

    lax.fori_loop(0, left_ref.shape[0] // step, outer_step, 0)

    def channel_step(p, carry):
        pieces = []
        for g in range(groups):
            first = outer_ref[g, pl.ds(2 * p, rows, stride=features), :]
            second = outer_ref[g, pl.ds(2 * p + 1, rows, stride=features), :]
            pieces.append(jnp.concatenate([first, second], axis=1).astype(BF16))
        update = matmul(jnp.concatenate(pieces, axis=0), spread_ref[p])

        @pl.when(p == 0)
        def _():
            sum_ref[...] = update

        @pl.when(p > 0)
        def _():
            sum_ref[...] += update

        return carry

    lax.fori_loop(0, pairs, channel_step, 0)

    for b in range(columns):
        g, place = b // GROUP, b % GROUP
        mid = sum_ref[g * rows : (g + 1) * rows, place * C_Z : (place + 1) * C_Z]
        mid = mid + couplings_ref[pl.ds(b, rows, stride=columns), :]
        mid_ref[b] = mid
        centred = mid - jnp.mean(mid, axis=1, keepdims=True)
        variance = jnp.mean(centred * centred, axis=1, keepdims=True)
        normed = (centred * lax.rsqrt(variance + EPS)).astype(BF16)
        gate_ref[b] = sigmoid(matmul(normed, switch_ref[...]))
        blank = jnp.zeros_like(normed)
        twice = jnp.concatenate(
            [
                jnp.concatenate([normed, blank], axis=1),
                jnp.concatenate([blank, normed], axis=1),
            ],
            axis=0,
        )
        sides = matmul_nt(entry_ref[...], twice)
        target = slice(b * HALF, (b + 1) * HALF)
        left_rows_ref[target, :] = sigmoid(sides[HALF : 2 * HALF]) * sides[:HALF]
        right_rows_ref[target, :] = sigmoid(sides[3 * HALF :]) * sides[2 * HALF : 3 * HALF]

    def turn_step(c, carry):
        chosen = pl.ds(c, columns, stride=HALF)
        left_pair_ref[c] = left_rows_ref[chosen, :].astype(BF16)
        right_pair_ref[c] = right_rows_ref[chosen, :].astype(BF16)
        return carry

    lax.fori_loop(0, HALF, turn_step, 0)


def pair_update(left, right, spread, couplings, entry_matrices, switch_matrix):
    rows, columns, depth = couplings.shape
    side = jax.ShapeDtypeStruct((HALF, columns, 2 * rows), BF16)
    whole = jax.ShapeDtypeStruct((columns, rows, depth), F32)
    vmem = pl.BlockSpec(memory_space=pltpu.VMEM)
    return pl.pallas_call(
        pair_kernel,
        in_specs=[vmem] * 6,
        out_specs=[vmem] * 4,
        out_shape=[whole, whole, side, side],
        scratch_shapes=[
            pltpu.VMEM((columns // GROUP, rows * TENSOR_FEATURES, 128), F32),
            pltpu.VMEM((columns // GROUP * rows, GROUP * depth), F32),
            pltpu.VMEM((columns * HALF, 2 * rows), F32),
            pltpu.VMEM((columns * HALF, 2 * rows), F32),
        ],
        compiler_params=params(),
        name="pair_update",
    )(left, right, spread, couplings.reshape(rows * columns, depth), entry_matrices, switch_matrix)


def triangle_kernel(left_ref, right_ref, mid_ref, gate_ref, final_ref, out_ref, product_ref):
    halves, blocks, channels, part, lanes = left_ref.shape
    rows = halves * part
    columns = right_ref.shape[2]
    step = pl.program_id(0)
    lane = lax.broadcasted_iota(jnp.int32, (rows, blocks * lanes), 1)
    front = lax.rem(lane, lanes) < lanes // 2
    for c in range(channels):
        left = jnp.concatenate(
            [
                jnp.concatenate([left_ref[h, k, c] for k in range(blocks)], axis=1)
                for h in range(halves)
            ],
            axis=0,
        )
        right = jnp.concatenate([right_ref[k, c] for k in range(blocks)], axis=1)
        blank = jnp.zeros_like(left)
        masked = jnp.concatenate(
            [jnp.where(front, left, blank), jnp.where(front, blank, left)], axis=0
        )
        first = pl.multiple_of((step * channels + c) * columns, columns)
        product_ref[pl.ds(first, columns), :] = matmul_nt(right, masked)

    @pl.when(step == pl.num_programs(0) - 1)
    def _():
        for j in range(columns):
            product = product_ref[pl.ds(j, HALF, stride=columns), :]
            mean = jnp.sum(product, axis=0, keepdims=True)
            mean = (mean + pltpu.roll(mean, rows, 1)) * (1.0 / C_TRI)
            centred = product - mean
            variance = jnp.sum(centred * centred, axis=0, keepdims=True)
            variance = (variance + pltpu.roll(variance, rows, 1)) * (1.0 / C_TRI)
            normed = (centred * lax.rsqrt(variance + EPS)).T.astype(BF16)
            update = matmul(normed[:rows], final_ref[:HALF, :])
            update = update + matmul(normed[rows:], final_ref[HALF:, :])
            out_ref[pl.ds(j, rows, stride=columns), :] = mid_ref[j] + gate_ref[j] * update


def triangle(left, right, mid, gate, final_matrix):
    halves, blocks, _, part, lanes = left.shape
    columns, rows, depth = mid.shape
    channels = 8
    whole = pl.BlockSpec((columns, rows, depth), lambda c: (0, 0, 0))
    out = pl.pallas_call(
        triangle_kernel,
        grid=(HALF // channels,),
        in_specs=[
            pl.BlockSpec((halves, blocks, channels, part, lanes), lambda c: (0, 0, c, 0, 0)),
            pl.BlockSpec((blocks, channels, columns, lanes), lambda c: (0, c, 0, 0)),
            whole,
            whole,
            pl.BlockSpec(final_matrix.shape, lambda c: (0, 0)),
        ],
        out_specs=pl.BlockSpec((rows * columns, depth), lambda c: (0, 0)),
        out_shape=jax.ShapeDtypeStruct((rows * columns, depth), F32),
        scratch_shapes=[pltpu.VMEM((HALF * columns, 2 * rows), F32)],
        compiler_params=params("arbitrary"),
        name="triangle",
    )(left, right, mid, gate, final_matrix)
    return out.reshape(rows, columns, depth)


def swap_cores(block):
    count = lax.axis_size("col")
    return lax.ppermute(block, "col", [(c, c ^ 1) for c in range(count)])


def in_core_order(own, other):
    first = lax.rem(lax.axis_index("col"), 2) == 0
    return jnp.where(first, jnp.stack([own, other]), jnp.stack([other, own]))


def gather_turned_direct(block):
    rows, columns = lax.axis_size("row"), lax.axis_size("col")
    me = lax.axis_index("col") // 2
    arrived = []
    for shift in range(rows):
        moves = []
        for r in range(rows):
            for q in range(rows):
                for core in range(columns // rows):
                    source = r * columns + 2 * q + core
                    moves.append((source, q * columns + 2 * ((r + shift) % rows) + core))
        arrived.append(lax.ppermute(block, ("row", "col"), moves))
    arrived = jnp.stack(arrived)
    order = lax.rem(me - jnp.arange(rows) + rows, rows)
    own = jnp.take(arrived, order, axis=0)
    return in_core_order(own, swap_cores(own))


def gather_turned(block):
    columns = lax.axis_size("col")
    same_core = [list(range(core, columns, 2)) for core in range(2)]
    gathered = lax.all_gather(block, "col", axis_index_groups=same_core)
    own = lax.all_to_all(gathered, "row", split_axis=0, concat_axis=0)
    return in_core_order(own, swap_cores(own))


def spread_weights(matrix):
    weights = matrix.reshape(TENSOR_FEATURES // 2, 2, 1, TENSOR_FEATURES, 1, C_Z)
    same = jnp.eye(GROUP, dtype=matrix.dtype).reshape(1, 1, GROUP, 1, GROUP, 1)
    return (weights * same).reshape(TENSOR_FEATURES // 2, 2 * 128, GROUP * C_Z)


def paired_entries(matrices):
    turned = matrices.reshape(C_Z, 4, 2, HALF)
    return jnp.transpose(turned, (1, 3, 2, 0)).reshape(4 * HALF, 2 * C_Z)


def body(
    homolog_tensor,
    couplings,
    attention_probe_matrix,
    attention_extra_matrices,
    attention_final_matrix,
    tensor_entry_matrices,
    tensor_final_matrix,
    incoming_entry_matrices,
    incoming_switch_matrix,
    incoming_final_matrix,
):
    inner = ATTENTION_UNITS * UNIT_WIDTH
    row_count = lax.axis_size("row")
    seqs, residues, depth = homolog_tensor.shape
    own_residues = residues // row_count
    high, low = standardise(homolog_tensor)
    high = high.reshape(row_count, own_residues, seqs, depth)
    low = low.reshape(row_count, own_residues, seqs + 16, depth)
    high = lax.all_to_all(high, "row", split_axis=0, concat_axis=0)
    low = lax.all_to_all(low, "row", split_axis=0, concat_axis=0)
    others = jnp.concatenate(
        [attention_probe_matrix.T, attention_extra_matrices[:, inner:].T], axis=0
    )
    gated, turned = attention(high, attention_extra_matrices[:, :inner], others)
    left_piece, right_piece = alignment(
        high, low, turned, attention_final_matrix.T, tensor_entry_matrices.T
    )
    gated = lax.all_to_all(gated, "row", split_axis=0, concat_axis=0)
    gated = jnp.transpose(gated.reshape(residues, seqs, inner), (1, 0, 2))
    change = jnp.dot(
        gated.reshape(-1, inner), attention_final_matrix, preferred_element_type=F32
    )
    refreshed_homologs = homolog_tensor + change.reshape(homolog_tensor.shape)

    right = lax.all_gather(right_piece, "row")
    left = gather_turned_direct(left_piece)
    total = left.shape[-1]
    mid, gate, left_pair, right_pair = pair_update(
        left.reshape(-1, total),
        right.reshape(-1, total),
        spread_weights(tensor_final_matrix),
        couplings,
        paired_entries(incoming_entry_matrices),
        incoming_switch_matrix,
    )
    right_pair = lax.all_gather(right_pair, "row")
    left_pair = gather_turned(left_pair)
    pair_output = triangle(left_pair, right_pair, mid, gate, incoming_final_matrix)
    return (refreshed_homologs, pair_output)


def solution(mesh):
    in_specs = (
        P("row", "col", None),
        P("row", "col", None),
        P(),
        P(),
        P(),
        P(),
        P(),
        P(),
        P(),
        P(),
    )
    out_specs = (P("row", "col", None), P("row", "col", None))
    return jax.shard_map(body, mesh=mesh, in_specs=in_specs, out_specs=out_specs, check_vma=False)
```

```python
import functools

import jax
import jax.numpy as jnp
from jax import lax
from jax.experimental import pallas as pl
from jax.experimental.pallas import tpu as pltpu
from jax.sharding import PartitionSpec as P

FEATURE_DEPTH = 256
C_Z = 128
TENSOR_FEATURES = 32
C_TRI = 128
ATTENTION_UNITS = 8
UNIT_WIDTH = 32
EPS = 1e-05
GROUP = 4
F32 = jnp.float32
BF16 = jnp.bfloat16
NT = (((1,), (1,)), ((), ()))
VMEM_LIMIT = 56 * 1024 * 1024


def matmul(left, right):
    return jnp.dot(left, right, preferred_element_type=F32)


def matmul_nt(left, right):
    return lax.dot_general(left, right, NT, preferred_element_type=F32)


def sigmoid(values):
    return 1.0 / (1.0 + jnp.exp(-values))


def cost(microseconds):
    return pl.CostEstimate(
        flops=int(microseconds * 1e9), bytes_accessed=int(microseconds * 1e6), transcendentals=0
    )


def params(*semantics):
    return pltpu.CompilerParams(
        dimension_semantics=semantics or None, vmem_limit_bytes=VMEM_LIMIT
    )


def standardise_kernel(first_ref, second_ref, high_ref, low_ref):
    seqs, residues, lanes = first_ref.shape
    first_rows = first_ref.reshape(seqs * residues, lanes)
    second_rows = second_ref.reshape(seqs * residues, lanes)
    lane = lax.broadcasted_iota(jnp.int32, (seqs, 128), 1)
    spreads = jnp.zeros((seqs, 128), F32)
    for n in range(residues):
        rows = pl.ds(n, seqs, stride=residues)
        column = jnp.concatenate([first_rows[rows, :], second_rows[rows, :]], axis=1)
        centred = column - jnp.mean(column, axis=1, keepdims=True)
        variance = jnp.mean(centred * centred, axis=1, keepdims=True) + EPS
        scale = lax.rsqrt(variance)
        normed = centred * scale
        high = normed.astype(BF16)
        high_ref[n] = high
        low_ref[n, :seqs, :] = (normed - high.astype(F32)).astype(BF16)
        spreads = jnp.where(lane == n, variance * scale, spreads)
    spreads = spreads.T
    row = lax.broadcasted_iota(jnp.int32, (16, seqs), 0)
    for n in range(residues):
        spread = jnp.broadcast_to(spreads[n : n + 1, :], (16, seqs))
        coarse = spread.astype(BF16).astype(F32)
        kept = jnp.where(row == 0, coarse, jnp.where(row == 1, spread - coarse, 0.0))
        kept = jnp.concatenate([kept, jnp.zeros((16, 2 * lanes - seqs), F32)], axis=1)
        low_ref[n, seqs:, :] = kept.astype(BF16)


def standardise(block):
    seqs, residues, depth = block.shape
    half = depth // 2
    return pl.pallas_call(
        standardise_kernel,
        grid=(residues // 8,),
        in_specs=[
            pl.BlockSpec((seqs, 8, half), lambda g: (0, g, 0)),
            pl.BlockSpec((seqs, 8, half), lambda g: (0, g, 1)),
        ],
        out_specs=[
            pl.BlockSpec((8, seqs, depth), lambda g: (g, 0, 0)),
            pl.BlockSpec((8, seqs + 16, depth), lambda g: (g, 0, 0)),
        ],
        out_shape=[
            jax.ShapeDtypeStruct((residues, seqs, depth), BF16),
            jax.ShapeDtypeStruct((residues, seqs + 16, depth), BF16),
        ],
        compiler_params=params("arbitrary"),
        cost_estimate=cost(4),
        name="standardise",
    )(block, block)


def attention_kernel(normed_ref, key_ref, others_ref, gated_ref, turned_ref):
    blocks, _, seqs, depth = normed_ref.shape
    total = blocks * seqs
    inner = ATTENTION_UNITS * UNIT_WIDTH
    column = normed_ref[...].reshape(total, depth)
    key_rows = matmul(column, key_ref[...]).astype(BF16)
    projected = matmul_nt(others_ref[...], column)
    queries = (projected[:inner] * UNIT_WIDTH ** (-0.5)).astype(BF16)
    value_rows = projected[inner : 2 * inner].astype(BF16)
    gates = sigmoid(projected[2 * inner :])
    ones = jnp.ones((16, total), BF16)
    parts = []
    for h in range(ATTENTION_UNITS):
        low, high = h * UNIT_WIDTH, (h + 1) * UNIT_WIDTH
        pieces = [queries[low:high]]
        if low > 0:
            pieces.insert(0, jnp.zeros((low, total), BF16))
        if high < inner:
            pieces.append(jnp.zeros((inner - high, total), BF16))
        scores = matmul(key_rows, jnp.concatenate(pieces, axis=0))
        weights = jnp.exp(scores - jnp.max(scores, axis=0, keepdims=True)).astype(BF16)
        attended = matmul(jnp.concatenate([value_rows[low:high], ones], axis=0), weights)
        parts.append(
            attended[:UNIT_WIDTH] * (gates[low:high] / attended[UNIT_WIDTH : UNIT_WIDTH + 1])
        )
    gated = jnp.concatenate(parts, axis=0)
    turned_ref[0] = gated.astype(BF16)
    gated_ref[...] = gated.T.astype(BF16).reshape(gated_ref.shape)


def attention(normed, key_matrix, other_matrices):
    blocks, residues, seqs, depth = normed.shape
    total = blocks * seqs
    inner = ATTENTION_UNITS * UNIT_WIDTH
    return pl.pallas_call(
        attention_kernel,
        grid=(residues,),
        in_specs=[
            pl.BlockSpec((blocks, 1, seqs, depth), lambda n: (0, n, 0, 0)),
            pl.BlockSpec((depth, inner), lambda n: (0, 0)),
            pl.BlockSpec((3 * inner, depth), lambda n: (0, 0)),
        ],
        out_specs=[
            pl.BlockSpec((blocks, 1, seqs, inner), lambda n: (0, n, 0, 0)),
            pl.BlockSpec((1, inner, total), lambda n: (n, 0, 0)),
        ],
        out_shape=[
            jax.ShapeDtypeStruct((blocks, residues, seqs, inner), BF16),
            jax.ShapeDtypeStruct((residues, inner, total), BF16),
        ],
        compiler_params=params("arbitrary"),
        cost_estimate=cost(20),
        name="attention",
    )(normed, key_matrix, other_matrices)


def alignment_kernel(high_ref, low_ref, turned_ref, final_ref, entry_ref, left_ref, right_ref):
    blocks, _, seqs, depth = high_ref.shape
    total = blocks * seqs
    low = low_ref[:, 0, :seqs, :].reshape(total, depth)
    column = high_ref[...].reshape(total, depth).astype(F32) + low.astype(F32)
    spreads = []
    for block in range(blocks):
        kept = low_ref[block, 0, seqs:, :seqs].astype(F32)
        spreads.append(jnp.sum(kept, axis=0, keepdims=True))
    spread = jnp.concatenate(spreads, axis=1)
    updated = column.T * spread + matmul(final_ref[...], turned_ref[0])
    centred = updated - jnp.mean(updated, axis=0, keepdims=True)
    variance = jnp.mean(centred * centred, axis=0, keepdims=True)
    normed = (centred * lax.rsqrt(variance + EPS)).astype(BF16)
    projected = matmul(entry_ref[...], normed).astype(BF16)
    left_ref[0] = projected[:TENSOR_FEATURES]
    right_ref[0] = projected[TENSOR_FEATURES:]


def alignment(high, low, turned, final_matrix, entry_matrices):
    blocks, residues, seqs, depth = high.shape
    total = blocks * seqs
    side = jax.ShapeDtypeStruct((residues, TENSOR_FEATURES, total), BF16)
    side_spec = pl.BlockSpec((1, TENSOR_FEATURES, total), lambda n: (n, 0, 0))
    return pl.pallas_call(
        alignment_kernel,
        grid=(residues,),
        in_specs=[
            pl.BlockSpec((blocks, 1, seqs, depth), lambda n: (0, n, 0, 0)),
            pl.BlockSpec((blocks, 1, seqs + 16, depth), lambda n: (0, n, 0, 0)),
            pl.BlockSpec((1, depth, total), lambda n: (n, 0, 0)),
            pl.BlockSpec(final_matrix.shape, lambda n: (0, 0)),
            pl.BlockSpec(entry_matrices.shape, lambda n: (0, 0)),
        ],
        out_specs=[side_spec, side_spec],
        out_shape=[side, side],
        compiler_params=params("arbitrary"),
        cost_estimate=cost(6),
        name="alignment",
    )(high, low, turned, final_matrix, entry_matrices)


def pair_kernel(
    left_ref,
    right_ref,
    weights_ref,
    couplings_ref,
    entry_ref,
    switch_ref,
    mid_ref,
    gate_ref,
    sides_ref,
    outer_ref,
    spread_ref,
    sum_ref,
    rows_ref,
):
    features = TENSOR_FEATURES
    total = left_ref.shape[1]
    rows = left_ref.shape[0] // features
    columns = right_ref.shape[0] // features
    groups = columns // GROUP
    pairs = features // 2
    step = 512

    def outer_step(m, carry):
        target = pl.ds(pl.multiple_of(m * step, step), step)
        piece = left_ref[target, :]
        for g in range(0, groups, 2):
            wide = right_ref[g * 128 : (g + 2) * 128, :]
            outer = matmul_nt(piece, wide) * (1.0 / total)
            outer_ref[g, target, :] = outer[:, :128]
            outer_ref[g + 1, target, :] = outer[:, 128:]
        return carry

    lax.fori_loop(0, left_ref.shape[0] // step, outer_step, 0)

    spread_ref[...] = jnp.zeros_like(spread_ref)

    def channel_step(p, carry):
        pieces = []
        for g in range(groups):
            first = outer_ref[g, pl.ds(2 * p, rows, stride=features), :]
            second = outer_ref[g, pl.ds(2 * p + 1, rows, stride=features), :]
            pieces.append(jnp.concatenate([first, second], axis=1).astype(BF16))
        slot = lax.rem(p, 2)
        for half in range(2):
            source = pl.multiple_of((2 * p + half) * features, features)
            piece = weights_ref[pl.ds(source, features), :]
            for place in range(GROUP):
                low = half * 128 + place * features
                spread_ref[slot, low : low + features, place * C_Z : (place + 1) * C_Z] = piece
        update = matmul(jnp.concatenate(pieces, axis=0), spread_ref[slot])

        @pl.when(p == 0)
        def _():
            sum_ref[...] = update

        @pl.when(p > 0)
        def _():
            sum_ref[...] += update

        return carry

    lax.fori_loop(0, pairs, channel_step, 0)

    for b in range(columns):
        g, place = b // GROUP, b % GROUP
        mid = sum_ref[g * rows : (g + 1) * rows, place * C_Z : (place + 1) * C_Z]
        mid = mid + couplings_ref[pl.ds(b, rows, stride=columns), :]
        mid_ref[b] = mid
        centred = mid - jnp.mean(mid, axis=1, keepdims=True)
        variance = jnp.mean(centred * centred, axis=1, keepdims=True)
        normed = (centred * lax.rsqrt(variance + EPS)).astype(BF16)
        gate_ref[b] = sigmoid(matmul(normed, switch_ref[...]))
        blank = jnp.zeros_like(normed)
        twice = jnp.concatenate(
            [
                jnp.concatenate([normed, blank], axis=1),
                jnp.concatenate([blank, normed], axis=1),
            ],
            axis=0,
        )
        sides = matmul_nt(entry_ref[...], twice)
        rows_ref[b * C_TRI : (b + 1) * C_TRI, :] = sigmoid(sides[C_TRI:]) * sides[:C_TRI]

    def turn_step(c, carry):
        sides_ref[c] = rows_ref[pl.ds(c, columns, stride=C_TRI), :].astype(BF16)
        return carry

    lax.fori_loop(0, C_TRI, turn_step, 0)


def pair_update(left, right, weights, couplings, entry_matrices, switch_matrix):
    rows, columns, depth = couplings.shape
    whole = jax.ShapeDtypeStruct((columns, rows, depth), F32)
    vmem = pl.BlockSpec(memory_space=pltpu.VMEM)
    return pl.pallas_call(
        pair_kernel,
        in_specs=[vmem] * 6,
        out_specs=[vmem] * 3,
        out_shape=[whole, whole, jax.ShapeDtypeStruct((C_TRI, columns, 2 * rows), BF16)],
        scratch_shapes=[
            pltpu.VMEM((columns // GROUP, rows * TENSOR_FEATURES, 128), F32),
            pltpu.VMEM((2, 2 * 128, GROUP * depth), BF16),
            pltpu.VMEM((columns // GROUP * rows, GROUP * depth), F32),
            pltpu.VMEM((columns * C_TRI, 2 * rows), F32),
        ],
        compiler_params=params(),
        cost_estimate=cost(15),
        name="pair_update",
    )(left, right, weights, couplings.reshape(rows * columns, depth), entry_matrices, switch_matrix)


def product_kernel(sides_ref, out_ref, *, grid_rows, grid_columns):
    part, lanes = sides_ref.shape[2:]
    half = lanes // 2
    lane = lax.broadcasted_iota(jnp.int32, (grid_columns * part, lanes), 1)
    front = lane < half
    lefts, rights = [], []
    for r in range(0, grid_rows, 2):
        even, odd = [
            jnp.concatenate(
                [sides_ref[(r + e) * grid_columns + c, 0] for c in range(grid_columns)], axis=0
            )
            for e in range(2)
        ]
        lefts.append(jnp.where(front, even, pltpu.roll(odd, half, 1)))
        rights.append(jnp.where(front, pltpu.roll(even, half, 1), odd))
    product = matmul_nt(jnp.concatenate(rights, axis=1), jnp.concatenate(lefts, axis=1))
    product = product.astype(BF16)
    front = front[: part // 2]
    for c in range(grid_columns):
        for r in range(0, grid_rows, 2):
            block = product[c * part : (c + 1) * part, r * half : (r + 2) * half]
            top, bottom = block[: part // 2], block[part // 2 :]
            even = jnp.where(front, top, pltpu.roll(bottom, half, 1))
            out_ref[r * grid_columns + c, 0] = even
            odd = jnp.where(front, pltpu.roll(top, half, 1), bottom)
            out_ref[(r + 1) * grid_columns + c, 0] = odd


def triangle_product(sides, grid_rows, grid_columns):
    devices, channels, part, lanes = sides.shape
    return pl.pallas_call(
        functools.partial(product_kernel, grid_rows=grid_rows, grid_columns=grid_columns),
        grid=(channels,),
        in_specs=[pl.BlockSpec((devices, 1, part, lanes), lambda c: (0, c, 0, 0))],
        out_specs=pl.BlockSpec((devices, 1, part // 2, lanes), lambda c: (0, c, 0, 0)),
        out_shape=jax.ShapeDtypeStruct((devices, channels, part // 2, lanes), BF16),
        compiler_params=params("arbitrary"),
        cost_estimate=cost(3),
        name="triangle_product",
    )(sides)


def output_kernel(product_ref, mid_ref, gate_ref, final_ref, out_ref, wide_ref):
    channels, part, lanes = product_ref.shape
    columns, rows, _ = mid_ref.shape
    wide_ref[...] = product_ref[...].astype(F32).reshape(channels * part, lanes)
    for j in range(part):
        product = wide_ref[pl.ds(j, channels, stride=part), :]
        centred = product - jnp.mean(product, axis=0, keepdims=True)
        variance = jnp.mean(centred * centred, axis=0, keepdims=True)
        normed = (centred * lax.rsqrt(variance + EPS)).T.astype(BF16)
        update = matmul(normed, final_ref[...])
        for half in range(2):
            b = half * part + j
            piece = update[half * rows : (half + 1) * rows]
            out_ref[pl.ds(b, rows, stride=columns), :] = mid_ref[b] + gate_ref[b] * piece


def pair_result(product, mid, gate, final_matrix):
    channels, part, lanes = product.shape
    columns, rows, depth = mid.shape
    vmem = pl.BlockSpec(memory_space=pltpu.VMEM)
    out = pl.pallas_call(
        output_kernel,
        in_specs=[vmem] * 4,
        out_specs=vmem,
        out_shape=jax.ShapeDtypeStruct((rows * columns, depth), F32),
        scratch_shapes=[pltpu.VMEM((channels * part, lanes), F32)],
        compiler_params=params(),
        cost_estimate=cost(5),
        name="pair_result",
    )(product, mid, gate, final_matrix)
    return out.reshape(rows, columns, depth)


def swap_cores(block):
    count = lax.axis_size("col")
    return lax.ppermute(block, "col", [(c, c ^ 1) for c in range(count)])


def in_core_order(own, other):
    first = lax.rem(lax.axis_index("col"), 2) == 0
    return jnp.where(first, jnp.stack([own, other]), jnp.stack([other, own]))


def gather_turned_direct(block):
    rows, columns = lax.axis_size("row"), lax.axis_size("col")
    me = lax.axis_index("col") // 2
    arrived = []
    for shift in range(rows):
        moves = []
        for r in range(rows):
            for q in range(rows):
                for core in range(columns // rows):
                    source = r * columns + 2 * q + core
                    moves.append((source, q * columns + 2 * ((r + shift) % rows) + core))
        arrived.append(lax.ppermute(block, ("row", "col"), moves))
    arrived = jnp.stack(arrived)
    order = lax.rem(me - jnp.arange(rows) + rows, rows)
    own = jnp.take(arrived, order, axis=0)
    return in_core_order(own, swap_cores(own))


def gather_rows(block):
    rows = lax.axis_size("row")
    me = lax.axis_index("row")
    arrived = [block]
    for shift in range(1, rows):
        arrived.append(lax.ppermute(block, "row", [(r, r ^ shift) for r in range(rows)]))
    return jnp.take(jnp.stack(arrived), me ^ jnp.arange(rows), axis=0)


def paired_entries(matrices):
    turned = matrices.reshape(C_Z, 2, 2, C_TRI)
    return jnp.transpose(turned, (2, 3, 1, 0)).reshape(2 * C_TRI, 2 * C_Z)


def body(
    homolog_tensor,
    couplings,
    attention_probe_matrix,
    attention_extra_matrices,
    attention_final_matrix,
    tensor_entry_matrices,
    tensor_final_matrix,
    incoming_entry_matrices,
    incoming_switch_matrix,
    incoming_final_matrix,
):
    inner = ATTENTION_UNITS * UNIT_WIDTH
    row_count = lax.axis_size("row")
    seqs, residues, depth = homolog_tensor.shape
    own_residues = residues // row_count
    high, low = standardise(homolog_tensor)
    high = high.reshape(row_count, own_residues, seqs, depth)
    low = low.reshape(row_count, own_residues, seqs + 16, depth)
    high = lax.all_to_all(high, "row", split_axis=0, concat_axis=0)
    low = lax.all_to_all(low, "row", split_axis=0, concat_axis=0)
    others = jnp.concatenate(
        [attention_probe_matrix.T, attention_extra_matrices[:, inner:].T], axis=0
    )
    gated, turned = attention(high, attention_extra_matrices[:, :inner], others)
    left_piece, right_piece = alignment(
        high, low, turned, attention_final_matrix.T, tensor_entry_matrices.T
    )

    right = gather_rows(right_piece)
    left = gather_turned_direct(left_piece)
    left, right, gated = lax.optimization_barrier((left, right, gated))
    gated = lax.all_to_all(gated, "row", split_axis=0, concat_axis=0)
    total = left.shape[-1]
    mid, gate, sides = pair_update(
        left.reshape(-1, total),
        right.reshape(-1, total),
        tensor_final_matrix,
        couplings,
        paired_entries(incoming_entry_matrices),
        incoming_switch_matrix,
    )
    column_count = lax.axis_size("col")
    devices = row_count * column_count
    sides = sides.reshape(devices, C_TRI // devices, *sides.shape[1:])
    sides = lax.all_to_all(sides, ("row", "col"), split_axis=0, concat_axis=0)
    product = triangle_product(sides, row_count, column_count)

    gated = jnp.transpose(gated.reshape(residues, seqs, inner), (1, 0, 2))
    change = jnp.dot(
        gated.reshape(-1, inner), attention_final_matrix, preferred_element_type=F32
    )
    refreshed_homologs = homolog_tensor + change.reshape(homolog_tensor.shape)

    product = lax.all_to_all(product, ("row", "col"), split_axis=0, concat_axis=0)
    product = product.reshape(C_TRI, *product.shape[2:])
    pair_output = pair_result(product, mid, gate, incoming_final_matrix)
    return (refreshed_homologs, pair_output)


def solution(mesh):
    in_specs = (
        P("row", "col", None),
        P("row", "col", None),
        P(),
        P(),
        P(),
        P(),
        P(),
        P(),
        P(),
        P(),
    )
    out_specs = (P("row", "col", None), P("row", "col", None))
    return jax.shard_map(body, mesh=mesh, in_specs=in_specs, out_specs=out_specs, check_vma=False)
```

```python
import functools

import jax
import jax.numpy as jnp
from jax import lax
from jax.experimental import pallas as pl
from jax.experimental.pallas import tpu as pltpu
from jax.sharding import PartitionSpec as P

FEATURE_DEPTH = 256
C_Z = 128
TENSOR_FEATURES = 32
C_TRI = 128
ATTENTION_UNITS = 8
UNIT_WIDTH = 32
EPS = 1e-05
GROUP = 4
F32 = jnp.float32
BF16 = jnp.bfloat16
NT = (((1,), (1,)), ((), ()))
VMEM_LIMIT = 56 * 1024 * 1024


def matmul(left, right):
    return jnp.dot(left, right, preferred_element_type=F32)


def matmul_nt(left, right):
    return lax.dot_general(left, right, NT, preferred_element_type=F32)


def sigmoid(values):
    return 0.5 * jnp.tanh(0.5 * values) + 0.5


def cost(microseconds):
    return pl.CostEstimate(
        flops=int(microseconds * 1e9), bytes_accessed=int(microseconds * 1e6), transcendentals=0
    )


def params(*semantics):
    return pltpu.CompilerParams(
        dimension_semantics=semantics or None, vmem_limit_bytes=VMEM_LIMIT
    )


def standardise_kernel(first_ref, second_ref, high_ref, low_ref):
    seqs, residues, lanes = first_ref.shape
    first_rows = first_ref.reshape(seqs * residues, lanes)
    second_rows = second_ref.reshape(seqs * residues, lanes)
    lane = lax.broadcasted_iota(jnp.int32, (seqs, 128), 1)
    spreads = jnp.zeros((seqs, 128), F32)
    for n in range(residues):
        rows = pl.ds(n, seqs, stride=residues)
        column = jnp.concatenate([first_rows[rows, :], second_rows[rows, :]], axis=1)
        centred = column - jnp.mean(column, axis=1, keepdims=True)
        variance = jnp.mean(centred * centred, axis=1, keepdims=True) + EPS
        scale = lax.rsqrt(variance)
        normed = centred * scale
        high = normed.astype(BF16)
        high_ref[n] = high
        low_ref[n, :seqs, :] = (normed - high.astype(F32)).astype(BF16)
        spreads = jnp.where(lane == n, variance * scale, spreads)
    spreads = spreads.T
    row = lax.broadcasted_iota(jnp.int32, (16, seqs), 0)
    for n in range(residues):
        spread = jnp.broadcast_to(spreads[n : n + 1, :], (16, seqs))
        coarse = spread.astype(BF16).astype(F32)
        kept = jnp.where(row == 0, coarse, jnp.where(row == 1, spread - coarse, 0.0))
        kept = jnp.concatenate([kept, jnp.zeros((16, 2 * lanes - seqs), F32)], axis=1)
        low_ref[n, seqs:, :] = kept.astype(BF16)


def standardise(block):
    seqs, residues, depth = block.shape
    half = depth // 2
    return pl.pallas_call(
        standardise_kernel,
        grid=(residues // 8,),
        in_specs=[
            pl.BlockSpec((seqs, 8, half), lambda g: (0, g, 0)),
            pl.BlockSpec((seqs, 8, half), lambda g: (0, g, 1)),
        ],
        out_specs=[
            pl.BlockSpec((8, seqs, depth), lambda g: (g, 0, 0)),
            pl.BlockSpec((8, seqs + 16, depth), lambda g: (g, 0, 0)),
        ],
        out_shape=[
            jax.ShapeDtypeStruct((residues, seqs, depth), BF16),
            jax.ShapeDtypeStruct((residues, seqs + 16, depth), BF16),
        ],
        compiler_params=params("arbitrary"),
        cost_estimate=cost(4),
        name="standardise",
    )(block, block)


def attention_kernel(
    normed_ref, key_ref, others_ref, gated_ref, turned_ref, scores_ref, weights_ref
):
    blocks, _, seqs, depth = normed_ref.shape
    total = blocks * seqs
    inner = ATTENTION_UNITS * UNIT_WIDTH
    column = normed_ref[...].reshape(total, depth)
    key_rows = matmul(column, key_ref[...]).astype(BF16)
    projected = matmul_nt(others_ref[...], column)
    queries = (projected[:inner] * UNIT_WIDTH ** (-0.5)).astype(BF16)
    value_rows = projected[inner : 2 * inner].astype(BF16)
    gates = sigmoid(projected[2 * inner :])
    parts = []

    def score(h):
        low, high = h * UNIT_WIDTH, (h + 1) * UNIT_WIDTH
        pieces = [queries[low:high]]
        if low > 0:
            pieces.insert(0, jnp.zeros((low, total), BF16))
        if high < inner:
            pieces.append(jnp.zeros((inner - high, total), BF16))
        scores_ref[h] = matmul(key_rows, jnp.concatenate(pieces, axis=0))

    def weigh(h):
        for low in range(0, total, 128):
            scores = scores_ref[h, :, low : low + 128]
            weights = jnp.exp(scores - jnp.max(scores, axis=0, keepdims=True))
            scale = 1.0 / jnp.sum(weights, axis=0, keepdims=True)
            weights_ref[h, :, low : low + 128] = (weights * scale).astype(BF16)

    def attend(h):
        low, high = h * UNIT_WIDTH, (h + 1) * UNIT_WIDTH
        parts.append(matmul(value_rows[low:high], weights_ref[h]) * gates[low:high])

    for step in range(ATTENTION_UNITS + 2):
        if step < ATTENTION_UNITS:
            score(step)
        if 1 <= step <= ATTENTION_UNITS:
            weigh(step - 1)
        if step >= 2:
            attend(step - 2)
    gated = jnp.concatenate(parts, axis=0)
    turned_ref[0] = gated.astype(BF16)
    gated_ref[...] = gated.T.astype(BF16).reshape(gated_ref.shape)


def attention(normed, key_matrix, other_matrices):
    blocks, residues, seqs, depth = normed.shape
    total = blocks * seqs
    inner = ATTENTION_UNITS * UNIT_WIDTH
    return pl.pallas_call(
        attention_kernel,
        grid=(residues,),
        in_specs=[
            pl.BlockSpec((blocks, 1, seqs, depth), lambda n: (0, n, 0, 0)),
            pl.BlockSpec((depth, inner), lambda n: (0, 0)),
            pl.BlockSpec((3 * inner, depth), lambda n: (0, 0)),
        ],
        out_specs=[
            pl.BlockSpec((blocks, 1, seqs, inner), lambda n: (0, n, 0, 0)),
            pl.BlockSpec((1, inner, total), lambda n: (n, 0, 0)),
        ],
        out_shape=[
            jax.ShapeDtypeStruct((blocks, residues, seqs, inner), BF16),
            jax.ShapeDtypeStruct((residues, inner, total), BF16),
        ],
        scratch_shapes=[
            pltpu.VMEM((ATTENTION_UNITS, total, total), F32),
            pltpu.VMEM((ATTENTION_UNITS, total, total), BF16),
        ],
        compiler_params=params("arbitrary"),
        cost_estimate=cost(20),
        name="attention",
    )(normed, key_matrix, other_matrices)


def alignment_kernel(
    high_ref, low_ref, turned_ref, final_ref, entry_ref, left_ref, right_ref, rows_ref
):
    blocks, residues, seqs, depth = high_ref.shape
    total = blocks * seqs
    features = TENSOR_FEATURES
    step = pl.program_id(0)
    for n in range(residues):
        low = low_ref[:, n, :seqs, :].reshape(total, depth)
        column = high_ref[:, n].reshape(total, depth).astype(F32) + low.astype(F32)
        spreads = []
        for block in range(blocks):
            kept = low_ref[block, n, seqs:, :seqs].astype(F32)
            spreads.append(jnp.sum(kept, axis=0, keepdims=True))
        spread = jnp.concatenate(spreads, axis=1)
        updated = column.T * spread + matmul(final_ref[...], turned_ref[n])
        centred = updated - jnp.mean(updated, axis=0, keepdims=True)
        variance = jnp.mean(centred * centred, axis=0, keepdims=True)
        normed = (centred * lax.rsqrt(variance + EPS)).astype(BF16)
        projected = matmul(entry_ref[...], normed)
        right_ref[n] = projected[features:].astype(BF16)
        first = pl.multiple_of((step * residues + n) * features, features)
        for tile in range(total // 128):
            rows_ref[tile, pl.ds(first, features), :] = projected[
                :features, tile * 128 : (tile + 1) * 128
            ]

    @pl.when(step == pl.num_programs(0) - 1)
    def _():
        count = rows_ref.shape[1] // features
        together = max(1, 16 // count)
        for c in range(0, features, together):
            pieces = []
            for e in range(together):
                chosen = pl.ds(c + e, count, stride=features)
                tiles = [rows_ref[tile, chosen, :] for tile in range(total // 128)]
                pieces.append(jnp.concatenate(tiles, axis=1))
            piece = jnp.concatenate(pieces, axis=0).astype(BF16)
            left_ref[c * count : (c + together) * count, :] = piece


def alignment(high, low, turned, final_matrix, entry_matrices):
    blocks, residues, seqs, depth = high.shape
    total = blocks * seqs
    features = TENSOR_FEATURES
    return pl.pallas_call(
        alignment_kernel,
        grid=(residues // 2,),
        in_specs=[
            pl.BlockSpec((blocks, 2, seqs, depth), lambda n: (0, n, 0, 0)),
            pl.BlockSpec((blocks, 2, seqs + 16, depth), lambda n: (0, n, 0, 0)),
            pl.BlockSpec((2, depth, total), lambda n: (n, 0, 0)),
            pl.BlockSpec(final_matrix.shape, lambda n: (0, 0)),
            pl.BlockSpec(entry_matrices.shape, lambda n: (0, 0)),
        ],
        out_specs=[
            pl.BlockSpec((features * residues, total), lambda n: (0, 0)),
            pl.BlockSpec((2, features, total), lambda n: (n, 0, 0)),
        ],
        out_shape=[
            jax.ShapeDtypeStruct((features * residues, total), BF16),
            jax.ShapeDtypeStruct((residues, features, total), BF16),
        ],
        scratch_shapes=[pltpu.VMEM((total // 128, residues * features, 128), F32)],
        compiler_params=params("arbitrary"),
        cost_estimate=cost(6),
        name="alignment",
    )(high, low, turned, final_matrix, entry_matrices)


def pair_kernel(
    left_ref,
    right_ref,
    weights_ref,
    couplings_ref,
    entry_ref,
    switch_ref,
    mid_ref,
    gate_ref,
    *rest,
):
    *sides_refs, outer_ref, spread_ref, sum_ref, rows_ref = rest
    features = TENSOR_FEATURES
    total = left_ref.shape[1]
    rows = left_ref.shape[0] // features
    columns = right_ref.shape[0] // features
    groups = columns // GROUP
    step = 512
    together = spread_ref.shape[1] // 128

    def outer_step(m, carry):
        target = pl.ds(pl.multiple_of(m * step, step), step)
        piece = left_ref[target, :]
        for g in range(0, groups, 2):
            wide = right_ref[g * 128 : (g + 2) * 128, :]
            outer = matmul_nt(piece, wide) * (1.0 / total)
            outer_ref[target, g * 128 : (g + 2) * 128] = outer.astype(BF16)
        return carry

    lax.fori_loop(0, left_ref.shape[0] // step, outer_step, 0)

    spread_ref[...] = jnp.zeros_like(spread_ref)

    def channel_step(p, carry):
        slot = lax.rem(p, 2)
        for e in range(together):
            source = pl.multiple_of((p * together + e) * features, features)
            piece = weights_ref[pl.ds(source, features), :]
            for place in range(GROUP):
                low = e * 128 + place * features
                spread_ref[slot, low : low + features, place * C_Z : (place + 1) * C_Z] = piece
        pieces = []
        for g in range(groups):
            parts = []
            for e in range(together):
                source = pl.multiple_of((p * together + e) * rows, rows)
                parts.append(outer_ref[pl.ds(source, rows), g * 128 : (g + 1) * 128])
            pieces.append(jnp.concatenate(parts, axis=1))
        update = matmul(jnp.concatenate(pieces, axis=0), spread_ref[slot])

        @pl.when(p == 0)
        def _():
            sum_ref[...] = update

        @pl.when(p > 0)
        def _():
            sum_ref[...] += update

        return carry

    lax.fori_loop(0, features // together, channel_step, 0)

    for g in range(groups):
        normed = []
        for place in range(GROUP):
            b = g * GROUP + place
            mid = sum_ref[g * rows : (g + 1) * rows, place * C_Z : (place + 1) * C_Z]
            mid = mid + couplings_ref[pl.ds(b, rows, stride=columns), :]
            mid_ref[b] = mid
            centred = mid - jnp.mean(mid, axis=1, keepdims=True)
            variance = jnp.mean(centred * centred, axis=1, keepdims=True)
            normed.append((centred * lax.rsqrt(variance + EPS)).astype(BF16))
        gates = sigmoid(matmul(jnp.concatenate(normed, axis=0), switch_ref[...]))
        blank = jnp.zeros_like(normed[0])
        for place in range(0, GROUP, 2):
            twice = []
            for e in range(2):
                b = g * GROUP + place + e
                gate_ref[b] = gates[(place + e) * rows : (place + e + 1) * rows]
                twice.append(jnp.concatenate([normed[place + e], blank], axis=1))
                twice.append(jnp.concatenate([blank, normed[place + e]], axis=1))
            sides = matmul_nt(entry_ref[...], jnp.concatenate(twice, axis=0))
            sides = sigmoid(sides[C_TRI:]) * sides[:C_TRI]
            b = g * GROUP + place
            rows_ref[b * C_TRI : (b + 1) * C_TRI, :] = sides[:, : 2 * rows]
            rows_ref[(b + 1) * C_TRI : (b + 2) * C_TRI, :] = sides[:, 2 * rows :]

    share = C_TRI // len(sides_refs)
    for part, sides_ref in enumerate(sides_refs):

        def turn_step(c, carry, part=part, sides_ref=sides_ref):
            chosen = pl.ds(part * share + c, columns, stride=C_TRI)
            sides_ref[c] = rows_ref[chosen, :].astype(BF16)
            return carry

        lax.fori_loop(0, share, turn_step, 0, unroll=8)


def pair_update(left, right, weights, couplings, entry_matrices, switch_matrix, parts):
    rows, columns, depth = couplings.shape
    whole = jax.ShapeDtypeStruct((columns, rows, depth), F32)
    sides = jax.ShapeDtypeStruct((C_TRI // parts, columns, 2 * rows), BF16)
    vmem = pl.BlockSpec(memory_space=pltpu.VMEM)
    return pl.pallas_call(
        pair_kernel,
        in_specs=[vmem] * 6,
        out_specs=[vmem] * (2 + parts),
        out_shape=[whole, whole] + [sides] * parts,
        scratch_shapes=[
            pltpu.VMEM((rows * TENSOR_FEATURES, columns * TENSOR_FEATURES), BF16),
            pltpu.VMEM((2, 8 * 128, GROUP * depth), BF16),
            pltpu.VMEM((columns // GROUP * rows, GROUP * depth), F32),
            pltpu.VMEM((columns * C_TRI, 2 * rows), F32),
        ],
        compiler_params=params(),
        cost_estimate=cost(12),
        name="pair_update",
    )(left, right, weights, couplings.reshape(rows * columns, depth), entry_matrices, switch_matrix)


def product_kernel(sides_ref, out_ref, *, grid_rows, grid_columns):
    part, lanes = sides_ref.shape[2:]
    half = lanes // 2
    lane = lax.broadcasted_iota(jnp.int32, (grid_columns * part, lanes), 1)
    front = lane < half
    lefts, rights = [], []
    for r in range(0, grid_rows, 2):
        even, odd = [
            jnp.concatenate(
                [sides_ref[(r + e) * grid_columns + c, 0] for c in range(grid_columns)], axis=0
            )
            for e in range(2)
        ]
        lefts.append(jnp.where(front, even, pltpu.roll(odd, half, 1)))
        rights.append(jnp.where(front, pltpu.roll(even, half, 1), odd))
    product = matmul_nt(jnp.concatenate(rights, axis=1), jnp.concatenate(lefts, axis=1))
    product = product.astype(BF16)
    front = front[: part // 2]
    for c in range(grid_columns):
        for r in range(0, grid_rows, 2):
            block = product[c * part : (c + 1) * part, r * half : (r + 2) * half]
            top, bottom = block[: part // 2], block[part // 2 :]
            even = jnp.where(front, top, pltpu.roll(bottom, half, 1))
            out_ref[r * grid_columns + c, 0] = even
            odd = jnp.where(front, pltpu.roll(top, half, 1), bottom)
            out_ref[(r + 1) * grid_columns + c, 0] = odd


def triangle_product(sides, grid_rows, grid_columns):
    devices, channels, part, lanes = sides.shape
    return pl.pallas_call(
        functools.partial(product_kernel, grid_rows=grid_rows, grid_columns=grid_columns),
        grid=(channels,),
        in_specs=[pl.BlockSpec((devices, 1, part, lanes), lambda c: (0, c, 0, 0))],
        out_specs=pl.BlockSpec((devices, 1, part // 2, lanes), lambda c: (0, c, 0, 0)),
        out_shape=jax.ShapeDtypeStruct((devices, channels, part // 2, lanes), BF16),
        compiler_params=params("arbitrary"),
        cost_estimate=cost(3),
        name="triangle_product",
    )(sides)


def output_kernel(mid_ref, gate_ref, final_ref, *rest):
    *product_refs, out_ref, wide_ref = rest
    share, part, lanes = product_refs[0].shape
    channels = share * len(product_refs)
    columns, rows, _ = mid_ref.shape
    for e, product_ref in enumerate(product_refs):
        wide_ref[e * share * part : (e + 1) * share * part, :] = (
            product_ref[...].astype(F32).reshape(share * part, lanes)
        )
    for j in range(part):
        product = wide_ref[pl.ds(j, channels, stride=part), :]
        centred = product - jnp.mean(product, axis=0, keepdims=True)
        variance = jnp.mean(centred * centred, axis=0, keepdims=True)
        normed = (centred * lax.rsqrt(variance + EPS)).T.astype(BF16)
        update = matmul(normed, final_ref[...])
        for half in range(2):
            b = half * part + j
            piece = update[half * rows : (half + 1) * rows]
            out_ref[pl.ds(b, rows, stride=columns), :] = mid_ref[b] + gate_ref[b] * piece


def pair_result(products, mid, gate, final_matrix):
    _, part, lanes = products[0].shape
    columns, rows, depth = mid.shape
    vmem = pl.BlockSpec(memory_space=pltpu.VMEM)
    out = pl.pallas_call(
        output_kernel,
        in_specs=[vmem] * (3 + len(products)),
        out_specs=vmem,
        out_shape=jax.ShapeDtypeStruct((rows * columns, depth), F32),
        scratch_shapes=[pltpu.VMEM((C_TRI * part, lanes), F32)],
        compiler_params=params(),
        cost_estimate=cost(4),
        name="pair_result",
    )(mid, gate, final_matrix, *products)
    return out.reshape(rows, columns, depth)


def swap_cores(block):
    count = lax.axis_size("col")
    return lax.ppermute(block, "col", [(c, c ^ 1) for c in range(count)])


def in_core_order(own, other):
    first = lax.rem(lax.axis_index("col"), 2) == 0
    return jnp.where(first, jnp.stack([own, other]), jnp.stack([other, own]))


def gather_turned_direct(block):
    rows, columns = lax.axis_size("row"), lax.axis_size("col")
    me = lax.axis_index("col") // 2
    arrived = []
    for shift in range(rows):
        moves = []
        for r in range(rows):
            for q in range(rows):
                for core in range(columns // rows):
                    source = r * columns + 2 * q + core
                    moves.append((source, q * columns + 2 * ((r + shift) % rows) + core))
        arrived.append(lax.ppermute(block, ("row", "col"), moves))
    arrived = jnp.stack(arrived)
    order = lax.rem(me - jnp.arange(rows) + rows, rows)
    own = jnp.take(arrived, order, axis=0)
    return in_core_order(own, swap_cores(own))


def gather_rows(block):
    rows = lax.axis_size("row")
    me = lax.axis_index("row")
    arrived = [block]
    for shift in range(1, rows):
        arrived.append(lax.ppermute(block, "row", [(r, r ^ shift) for r in range(rows)]))
    return jnp.take(jnp.stack(arrived), me ^ jnp.arange(rows), axis=0)


def paired_entries(matrices):
    turned = matrices.reshape(C_Z, 2, 2, C_TRI)
    return jnp.transpose(turned, (2, 3, 1, 0)).reshape(2 * C_TRI, 2 * C_Z)


def body(
    homolog_tensor,
    couplings,
    attention_probe_matrix,
    attention_extra_matrices,
    attention_final_matrix,
    tensor_entry_matrices,
    tensor_final_matrix,
    incoming_entry_matrices,
    incoming_switch_matrix,
    incoming_final_matrix,
):
    inner = ATTENTION_UNITS * UNIT_WIDTH
    row_count = lax.axis_size("row")
    seqs, residues, depth = homolog_tensor.shape
    own_residues = residues // row_count
    high, low = standardise(homolog_tensor)
    high = high.reshape(row_count, own_residues, seqs, depth)
    low = low.reshape(row_count, own_residues, seqs + 16, depth)
    high = lax.all_to_all(high, "row", split_axis=0, concat_axis=0)
    low = lax.all_to_all(low, "row", split_axis=0, concat_axis=0)
    others = jnp.concatenate(
        [attention_probe_matrix.T, attention_extra_matrices[:, inner:].T], axis=0
    )
    gated, turned = attention(high, attention_extra_matrices[:, :inner], others)
    left_piece, right_piece = alignment(
        high, low, turned, attention_final_matrix.T, tensor_entry_matrices.T
    )

    right = gather_rows(right_piece)
    left = gather_turned_direct(left_piece)
    total = left.shape[-1]
    left = left.reshape(2, row_count, TENSOR_FEATURES, own_residues, total)
    left = jnp.transpose(left, (2, 0, 1, 3, 4)).reshape(-1, total)
    left, right, gated = lax.optimization_barrier((left, right.reshape(-1, total), gated))
    gated = lax.all_to_all(gated, "row", split_axis=0, concat_axis=0)
    column_count = lax.axis_size("col")
    devices = row_count * column_count
    channels = C_TRI // devices
    parts = 2 if channels % 2 == 0 else 1
    mid, gate, *sides = pair_update(
        left,
        right,
        tensor_final_matrix,
        couplings,
        paired_entries(incoming_entry_matrices),
        incoming_switch_matrix,
        parts,
    )
    gated, *sides = lax.optimization_barrier((gated, *sides))
    gated = jnp.transpose(gated.reshape(residues, seqs, inner), (1, 0, 2))
    change = jnp.dot(
        gated.reshape(-1, inner), attention_final_matrix, preferred_element_type=F32
    )
    refreshed_homologs = homolog_tensor + change.reshape(homolog_tensor.shape)

    everywhere = ("row", "col")
    sides = [side.reshape(devices, channels // parts, *side.shape[1:]) for side in sides]
    sides = [lax.all_to_all(side, everywhere, split_axis=0, concat_axis=0) for side in sides]
    products = []
    for side in sides:
        product = triangle_product(side, row_count, column_count)
        product = lax.all_to_all(product, everywhere, split_axis=0, concat_axis=0)
        products.append(product.reshape(C_TRI // parts, *product.shape[2:]))
    pair_output = pair_result(products, mid, gate, incoming_final_matrix)
    return (refreshed_homologs, pair_output)


def solution(mesh):
    in_specs = (
        P("row", "col", None),
        P("row", "col", None),
        P(),
        P(),
        P(),
        P(),
        P(),
        P(),
        P(),
        P(),
    )
    out_specs = (P("row", "col", None), P("row", "col", None))
    return jax.shard_map(body, mesh=mesh, in_specs=in_specs, out_specs=out_specs, check_vma=False)
```

```python
import functools

import jax
import jax.numpy as jnp
from jax import lax
from jax.experimental import pallas as pl
from jax.experimental.pallas import tpu as pltpu
from jax.sharding import PartitionSpec as P

FEATURE_DEPTH = 256
C_Z = 128
TENSOR_FEATURES = 32
C_TRI = 128
ATTENTION_UNITS = 8
UNIT_WIDTH = 32
EPS = 1e-05
GROUP = 4
F32 = jnp.float32
BF16 = jnp.bfloat16
NT = (((1,), (1,)), ((), ()))
MEGA = 1024 * 1024


def matmul(left, right):
    return jnp.dot(left, right, preferred_element_type=F32)


def matmul_nt(left, right):
    return lax.dot_general(left, right, NT, preferred_element_type=F32)


def sigmoid(values):
    return 0.5 * jnp.tanh(0.5 * values) + 0.5


def cost(microseconds):
    return pl.CostEstimate(
        flops=int(microseconds * 1e9), bytes_accessed=int(microseconds * 1e6), transcendentals=0
    )


def params(megabytes, *semantics):
    return pltpu.CompilerParams(
        dimension_semantics=semantics or None, vmem_limit_bytes=megabytes * MEGA
    )


def standardised_column(first_rows, second_rows, n, residues):
    seqs = first_rows.shape[0] // residues
    rows = pl.ds(n, seqs, stride=residues)
    column = jnp.concatenate([first_rows[rows, :], second_rows[rows, :]], axis=1)
    centred = column - jnp.mean(column, axis=1, keepdims=True)
    variance = jnp.mean(centred * centred, axis=1, keepdims=True) + EPS
    scale = lax.rsqrt(variance)
    return centred * scale, variance * scale


def high_kernel(first_ref, second_ref, high_ref):
    seqs, residues, lanes = first_ref.shape
    first_rows = first_ref.reshape(seqs * residues, lanes)
    second_rows = second_ref.reshape(seqs * residues, lanes)
    for n in range(residues):
        normed, _ = standardised_column(first_rows, second_rows, n, residues)
        high_ref[n] = normed.astype(BF16)


def low_kernel(first_ref, second_ref, low_ref):
    seqs, residues, lanes = first_ref.shape
    first_rows = first_ref.reshape(seqs * residues, lanes)
    second_rows = second_ref.reshape(seqs * residues, lanes)
    lane = lax.broadcasted_iota(jnp.int32, (seqs, 128), 1)
    spreads = jnp.zeros((seqs, 128), F32)
    for n in range(residues):
        normed, spread = standardised_column(first_rows, second_rows, n, residues)
        low_ref[n, :seqs, :] = (normed - normed.astype(BF16).astype(F32)).astype(BF16)
        spreads = jnp.where(lane == n, spread, spreads)
    spreads = spreads.T
    row = lax.broadcasted_iota(jnp.int32, (16, seqs), 0)
    for n in range(residues):
        spread = jnp.broadcast_to(spreads[n : n + 1, :], (16, seqs))
        coarse = spread.astype(BF16).astype(F32)
        kept = jnp.where(row == 0, coarse, jnp.where(row == 1, spread - coarse, 0.0))
        kept = jnp.concatenate([kept, jnp.zeros((16, 2 * lanes - seqs), F32)], axis=1)
        low_ref[n, seqs:, :] = kept.astype(BF16)


def standardise(block, kernel, extra):
    seqs, residues, depth = block.shape
    half = depth // 2
    return pl.pallas_call(
        kernel,
        grid=(residues // 8,),
        in_specs=[
            pl.BlockSpec((seqs, 8, half), lambda g: (0, g, 0)),
            pl.BlockSpec((seqs, 8, half), lambda g: (0, g, 1)),
        ],
        out_specs=pl.BlockSpec((8, seqs + extra, depth), lambda g: (g, 0, 0)),
        out_shape=jax.ShapeDtypeStruct((residues, seqs + extra, depth), BF16),
        compiler_params=params(12, "arbitrary"),
        cost_estimate=cost(3),
        name="standardise",
    )(block, block)


def attention_kernel(
    normed_ref, key_ref, others_ref, gated_ref, turned_ref, scores_ref, weights_ref
):
    blocks, residues, seqs, depth = normed_ref.shape
    total = blocks * seqs
    inner = ATTENTION_UNITS * UNIT_WIDTH
    columns = []
    for n in range(residues):
        column = normed_ref[:, n].reshape(total, depth)
        key_rows = matmul(column, key_ref[...]).astype(BF16)
        projected = matmul_nt(others_ref[...], column)
        queries = (projected[:inner] * UNIT_WIDTH ** (-0.5)).astype(BF16)
        value_rows = projected[inner : 2 * inner].astype(BF16)
        gates = sigmoid(projected[2 * inner :])
        columns.append((key_rows, queries, value_rows, gates))

    def score(n, h):
        key_rows, queries, _, _ = columns[n]
        low, high = h * UNIT_WIDTH, (h + 1) * UNIT_WIDTH
        pieces = [queries[low:high]]
        if low > 0:
            pieces.insert(0, jnp.zeros((low, total), BF16))
        if high < inner:
            pieces.append(jnp.zeros((inner - high, total), BF16))
        scores_ref[n, h] = matmul(key_rows, jnp.concatenate(pieces, axis=0))

    def weigh(n, h):
        for low in range(0, total, 128):
            scores = scores_ref[n, h, :, low : low + 128]
            weights = jnp.exp(scores - jnp.max(scores, axis=0, keepdims=True))
            scale = 1.0 / jnp.sum(weights, axis=0, keepdims=True)
            weights_ref[n, h, :, low : low + 128] = (weights * scale).astype(BF16)

    def attend(n, h):
        _, _, value_rows, gates = columns[n]
        rows = slice(h * UNIT_WIDTH, (h + 1) * UNIT_WIDTH)
        attended = matmul(value_rows[rows], weights_ref[n, h]) * gates[rows]
        turned_ref[n, rows, :] = attended.astype(BF16)

    units = [(n, h) for h in range(ATTENTION_UNITS) for n in range(residues)]
    for step in range(len(units) + 2):
        if step < len(units):
            score(*units[step])
        if 1 <= step <= len(units):
            weigh(*units[step - 1])
        if step >= 2:
            attend(*units[step - 2])
    for n in range(residues):
        gated_ref[:, n] = turned_ref[n].T.reshape(blocks, seqs, inner)


def attention(normed, key_matrix, other_matrices):
    blocks, residues, seqs, depth = normed.shape
    total = blocks * seqs
    inner = ATTENTION_UNITS * UNIT_WIDTH
    return pl.pallas_call(
        attention_kernel,
        grid=(residues // 2,),
        in_specs=[
            pl.BlockSpec((blocks, 2, seqs, depth), lambda n: (0, n, 0, 0)),
            pl.BlockSpec((depth, inner), lambda n: (0, 0)),
            pl.BlockSpec((3 * inner, depth), lambda n: (0, 0)),
        ],
        out_specs=[
            pl.BlockSpec((blocks, 2, seqs, inner), lambda n: (0, n, 0, 0)),
            pl.BlockSpec((2, inner, total), lambda n: (n, 0, 0)),
        ],
        out_shape=[
            jax.ShapeDtypeStruct((blocks, residues, seqs, inner), BF16),
            jax.ShapeDtypeStruct((residues, inner, total), BF16),
        ],
        scratch_shapes=[
            pltpu.VMEM((2, ATTENTION_UNITS, total, total), F32),
            pltpu.VMEM((2, ATTENTION_UNITS, total, total), BF16),
        ],
        compiler_params=params(40, "arbitrary"),
        cost_estimate=cost(14),
        name="attention",
    )(normed, key_matrix, other_matrices)


def alignment_kernel(
    high_ref, low_ref, turned_ref, final_ref, entry_ref, left_ref, right_ref, rows_ref
):
    blocks, residues, seqs, depth = high_ref.shape
    total = blocks * seqs
    features = TENSOR_FEATURES
    step = pl.program_id(0)
    for n in range(residues):
        low = low_ref[:, n, :seqs, :].reshape(total, depth)
        column = high_ref[:, n].reshape(total, depth).astype(F32) + low.astype(F32)
        spreads = []
        for block in range(blocks):
            kept = low_ref[block, n, seqs:, :seqs].astype(F32)
            spreads.append(jnp.sum(kept, axis=0, keepdims=True))
        spread = jnp.concatenate(spreads, axis=1)
        updated = column.T * spread + matmul(final_ref[...], turned_ref[n])
        centred = updated - jnp.mean(updated, axis=0, keepdims=True)
        variance = jnp.mean(centred * centred, axis=0, keepdims=True)
        normed = (centred * lax.rsqrt(variance + EPS)).astype(BF16)
        projected = matmul(entry_ref[...], normed)
        right_ref[n] = projected[features:].astype(BF16)
        first = pl.multiple_of((step * residues + n) * features, features)
        for tile in range(total // 128):
            rows_ref[tile, pl.ds(first, features), :] = projected[
                :features, tile * 128 : (tile + 1) * 128
            ]

    @pl.when(step == pl.num_programs(0) - 1)
    def _():
        count = rows_ref.shape[1] // features
        together = max(1, 16 // count)
        for c in range(0, features, together):
            pieces = []
            for e in range(together):
                chosen = pl.ds(c + e, count, stride=features)
                tiles = [rows_ref[tile, chosen, :] for tile in range(total // 128)]
                pieces.append(jnp.concatenate(tiles, axis=1))
            piece = jnp.concatenate(pieces, axis=0).astype(BF16)
            left_ref[c * count : (c + together) * count, :] = piece


def alignment(high, low, turned, final_matrix, entry_matrices):
    blocks, residues, seqs, depth = high.shape
    total = blocks * seqs
    features = TENSOR_FEATURES
    return pl.pallas_call(
        alignment_kernel,
        grid=(residues // 2,),
        in_specs=[
            pl.BlockSpec((blocks, 2, seqs, depth), lambda n: (0, n, 0, 0)),
            pl.BlockSpec((blocks, 2, seqs + 16, depth), lambda n: (0, n, 0, 0)),
            pl.BlockSpec((2, depth, total), lambda n: (n, 0, 0)),
            pl.BlockSpec(final_matrix.shape, lambda n: (0, 0)),
            pl.BlockSpec(entry_matrices.shape, lambda n: (0, 0)),
        ],
        out_specs=[
            pl.BlockSpec((features * residues, total), lambda n: (0, 0)),
            pl.BlockSpec((2, features, total), lambda n: (n, 0, 0)),
        ],
        out_shape=[
            jax.ShapeDtypeStruct((features * residues, total), BF16),
            jax.ShapeDtypeStruct((residues, features, total), BF16),
        ],
        scratch_shapes=[pltpu.VMEM((total // 128, residues * features, 128), F32)],
        compiler_params=params(20, "arbitrary"),
        cost_estimate=cost(6),
        name="alignment",
    )(high, low, turned, final_matrix, entry_matrices)


def pair_kernel(
    left_slots_ref,
    right_firsts_ref,
    own_ref,
    other_ref,
    *rest,
):
    weights_ref, couplings_ref, entry_ref, switch_ref, mid_ref, gate_ref, sides_ref = rest[-11:-4]
    outer_ref, spread_ref, sum_ref, rows_ref = rest[-4:]
    right_refs = rest[:-11]
    features = TENSOR_FEATURES
    slots, piece_rows, total = own_ref.shape
    residues = piece_rows // features
    rows = 2 * slots * residues
    share = right_refs[0].shape[0]
    columns = len(right_refs) * share
    groups = columns // GROUP
    wide = share * features
    together = spread_ref.shape[1] // 128

    for half, left_ref in enumerate((own_ref, other_ref)):
        piece = left_ref[...].reshape(slots * piece_rows, total)
        target = slice(half * slots * piece_rows, (half + 1) * slots * piece_rows)
        for p, right_ref in enumerate(right_refs):
            right = right_ref[...].reshape(wide, total)
            outer_ref[target, p * wide : (p + 1) * wide] = matmul_nt(piece, right) * (1.0 / total)

    spread_ref[...] = jnp.zeros_like(spread_ref)

    def channel_step(p, carry):
        slot = lax.rem(p, 2)
        for e in range(together):
            source = pl.multiple_of((p * together + e) * features, features)
            piece = weights_ref[pl.ds(source, features), :]
            for place in range(GROUP):
                low = e * 128 + place * features
                spread_ref[slot, low : low + features, place * C_Z : (place + 1) * C_Z] = piece
        pieces = []
        for g in range(groups):
            parts = []
            for e in range(together):
                channel = []
                for slot_number in range(2 * slots):
                    first = slot_number * piece_rows + (p * together + e) * residues
                    source = pl.ds(pl.multiple_of(first, residues), residues)
                    channel.append(outer_ref[source, g * 128 : (g + 1) * 128])
                parts.append(jnp.concatenate(channel, axis=0).astype(BF16))
            pieces.append(jnp.concatenate(parts, axis=1))
        update = matmul(jnp.concatenate(pieces, axis=0), spread_ref[slot])

        @pl.when(p == 0)
        def _():
            sum_ref[...] = update

        @pl.when(p > 0)
        def _():
            sum_ref[...] += update

        return carry

    lax.fori_loop(0, features // together, channel_step, 0)

    left_firsts = [left_slots_ref[j] * residues for j in range(2 * slots)]
    right_firsts = [right_firsts_ref[p] for p in range(len(right_refs))]
    for g in range(groups):
        normed, places = [], []
        for place in range(GROUP):
            p, n = divmod(g * GROUP + place, share)
            b = right_firsts[p] + n
            places.append(b)
            lanes = slice(place * C_Z, (place + 1) * C_Z)
            pieces = []
            for first in left_firsts:
                source = pl.ds(pl.multiple_of(g * rows + first, residues), residues)
                pieces.append(sum_ref[source, lanes])
            mid = jnp.concatenate(pieces, axis=0)
            mid = mid + couplings_ref[pl.ds(b, rows, stride=columns), :]
            mid_ref[b] = mid
            centred = mid - jnp.mean(mid, axis=1, keepdims=True)
            variance = jnp.mean(centred * centred, axis=1, keepdims=True)
            normed.append((centred * lax.rsqrt(variance + EPS)).astype(BF16))
        gates = sigmoid(matmul(jnp.concatenate(normed, axis=0), switch_ref[...]))
        blank = jnp.zeros_like(normed[0])
        for place in range(0, GROUP, 2):
            twice = []
            for e in range(2):
                gate_ref[places[place + e]] = gates[(place + e) * rows : (place + e + 1) * rows]
                twice.append(jnp.concatenate([normed[place + e], blank], axis=1))
                twice.append(jnp.concatenate([blank, normed[place + e]], axis=1))
            sides = matmul_nt(entry_ref[...], jnp.concatenate(twice, axis=0))
            sides = sigmoid(sides[C_TRI:]) * sides[:C_TRI]
            for e in range(2):
                first = pl.multiple_of(places[place + e] * C_TRI, C_TRI)
                rows_ref[pl.ds(first, C_TRI), :] = sides[:, e * 2 * rows : (e + 1) * 2 * rows]

    def turn_step(c, carry):
        sides_ref[c] = rows_ref[pl.ds(c, columns, stride=C_TRI), :].astype(BF16)
        return carry

    lax.fori_loop(0, C_TRI, turn_step, 0, unroll=8)


def pair_update(left_slots, right_firsts, left, rights, weights, couplings, entry, switch):
    rows, columns, depth = couplings.shape
    whole = jax.ShapeDtypeStruct((columns, rows, depth), F32)
    smem = pl.BlockSpec(memory_space=pltpu.SMEM)
    vmem = pl.BlockSpec(memory_space=pltpu.VMEM)
    return pl.pallas_call(
        pair_kernel,
        in_specs=[smem] * 2 + [vmem] * (6 + len(rights)),
        out_specs=[vmem] * 3,
        out_shape=[whole, whole, jax.ShapeDtypeStruct((C_TRI, columns, 2 * rows), BF16)],
        scratch_shapes=[
            pltpu.VMEM((rows * TENSOR_FEATURES, columns * TENSOR_FEATURES), F32),
            pltpu.VMEM((2, 8 * 128, GROUP * depth), BF16),
            pltpu.VMEM((columns // GROUP * rows, GROUP * depth), F32),
            pltpu.VMEM((columns * C_TRI, 2 * rows), F32),
        ],
        compiler_params=params(36),
        cost_estimate=cost(12),
        name="pair_update",
    )(
        left_slots,
        right_firsts,
        *left,
        *rights,
        weights,
        couplings.reshape(rows * columns, depth),
        entry,
        switch,
    )


def product_kernel(sides_ref, out_ref, *, grid_rows, grid_columns):
    channels, part, lanes = sides_ref.shape[1:]
    half = lanes // 2
    lane = lax.broadcasted_iota(jnp.int32, (grid_columns * part, lanes), 1)
    front = lane < half
    cut = front[: part // 2]
    for channel in range(channels):
        lefts, rights = [], []
        for r in range(0, grid_rows, 2):
            even, odd = [
                jnp.concatenate(
                    [sides_ref[(r + e) * grid_columns + c, channel] for c in range(grid_columns)],
                    axis=0,
                )
                for e in range(2)
            ]
            lefts.append(jnp.where(front, even, pltpu.roll(odd, half, 1)))
            rights.append(jnp.where(front, pltpu.roll(even, half, 1), odd))
        product = matmul_nt(jnp.concatenate(rights, axis=1), jnp.concatenate(lefts, axis=1))
        product = product.astype(BF16)
        for c in range(grid_columns):
            for r in range(0, grid_rows, 2):
                block = product[c * part : (c + 1) * part, r * half : (r + 2) * half]
                top, bottom = block[: part // 2], block[part // 2 :]
                even = jnp.where(cut, top, pltpu.roll(bottom, half, 1))
                out_ref[r * grid_columns + c, channel] = even
                odd = jnp.where(cut, pltpu.roll(top, half, 1), bottom)
                out_ref[(r + 1) * grid_columns + c, channel] = odd


def triangle_product(sides, grid_rows, grid_columns):
    devices, channels, part, lanes = sides.shape
    step = 2 if channels % 2 == 0 else 1
    return pl.pallas_call(
        functools.partial(product_kernel, grid_rows=grid_rows, grid_columns=grid_columns),
        grid=(channels // step,),
        in_specs=[pl.BlockSpec((devices, step, part, lanes), lambda c: (0, c, 0, 0))],
        out_specs=pl.BlockSpec((devices, step, part // 2, lanes), lambda c: (0, c, 0, 0)),
        out_shape=jax.ShapeDtypeStruct((devices, channels, part // 2, lanes), BF16),
        compiler_params=params(16, "arbitrary"),
        cost_estimate=cost(3),
        name="triangle_product",
    )(sides)


def output_kernel(product_ref, mid_ref, gate_ref, final_ref, out_ref, wide_ref):
    channels, part, lanes = product_ref.shape
    columns, rows, _ = mid_ref.shape
    wide_ref[...] = product_ref[...].astype(F32).reshape(channels * part, lanes)
    for j in range(part):
        product = wide_ref[pl.ds(j, channels, stride=part), :]
        centred = product - jnp.mean(product, axis=0, keepdims=True)
        variance = jnp.mean(centred * centred, axis=0, keepdims=True)
        normed = (centred * lax.rsqrt(variance + EPS)).T.astype(BF16)
        update = matmul(normed, final_ref[...])
        for half in range(2):
            b = half * part + j
            piece = update[half * rows : (half + 1) * rows]
            out_ref[pl.ds(b, rows, stride=columns), :] = mid_ref[b] + gate_ref[b] * piece


def pair_result(product, mid, gate, final_matrix):
    channels, part, lanes = product.shape
    columns, rows, depth = mid.shape
    vmem = pl.BlockSpec(memory_space=pltpu.VMEM)
    out = pl.pallas_call(
        output_kernel,
        in_specs=[vmem] * 4,
        out_specs=vmem,
        out_shape=jax.ShapeDtypeStruct((rows * columns, depth), F32),
        scratch_shapes=[pltpu.VMEM((channels * part, lanes), F32)],
        compiler_params=params(12),
        cost_estimate=cost(4),
        name="pair_result",
    )(product, mid, gate, final_matrix)
    return out.reshape(rows, columns, depth)


def swap_cores(block):
    count = lax.axis_size("col")
    return lax.ppermute(block, "col", [(c, c ^ 1) for c in range(count)])


def gather_turned(block):
    rows, columns = lax.axis_size("row"), lax.axis_size("col")
    me, core = lax.axis_index("col") // 2, lax.rem(lax.axis_index("col"), 2)
    arrived = []
    for shift in range(rows):
        moves = []
        for r in range(rows):
            for q in range(rows):
                for side in range(2):
                    source = r * columns + 2 * q + side
                    moves.append((source, q * columns + 2 * ((r + shift) % rows) + side))
        arrived.append(lax.ppermute(block, ("row", "col"), moves))
    own = jnp.stack(arrived)
    other = swap_cores(own)
    shifts = lax.rem(me - jnp.arange(rows, dtype=jnp.int32) + rows, rows)
    residues = block.shape[0] // TENSOR_FEATURES
    if residues % 8 == 0:
        return (own, other), jnp.concatenate([shifts + core * rows, shifts + (1 - core) * rows])
    own, other = jnp.take(own, shifts, axis=0), jnp.take(other, shifts, axis=0)
    joined = 8 // residues
    ordered = []
    for side in (jnp.where(core == 0, own, other), jnp.where(core == 0, other, own)):
        side = side.reshape(rows // joined, joined, TENSOR_FEATURES, residues, -1)
        side = jnp.transpose(side, (0, 2, 1, 3, 4))
        ordered.append(side.reshape(rows // joined, joined * block.shape[0], -1))
    return tuple(ordered), jnp.arange(2 * rows // joined, dtype=jnp.int32)


def exchange_rows(pieces):
    rows = lax.axis_size("row")
    arrived = [pieces[0]]
    for shift in range(1, rows):
        moves = [(r, r ^ shift) for r in range(rows)]
        arrived.append(lax.ppermute(pieces[shift], "row", moves))
    return arrived, lax.axis_index("row") ^ jnp.arange(rows, dtype=jnp.int32)


def paired_entries(matrices):
    turned = matrices.reshape(C_Z, 2, 2, C_TRI)
    return jnp.transpose(turned, (2, 3, 1, 0)).reshape(2 * C_TRI, 2 * C_Z)


def body(
    homolog_tensor,
    couplings,
    attention_probe_matrix,
    attention_extra_matrices,
    attention_final_matrix,
    tensor_entry_matrices,
    tensor_final_matrix,
    incoming_entry_matrices,
    incoming_switch_matrix,
    incoming_final_matrix,
):
    inner = ATTENTION_UNITS * UNIT_WIDTH
    row_count = lax.axis_size("row")
    seqs, residues, depth = homolog_tensor.shape
    own_residues = residues // row_count
    high = standardise(homolog_tensor, high_kernel, 0)
    high = high.reshape(row_count, own_residues, seqs, depth)
    low = standardise(homolog_tensor, low_kernel, 16)
    low = low.reshape(row_count, own_residues, seqs + 16, depth)
    high = lax.all_to_all(high, "row", split_axis=0, concat_axis=0)
    low = lax.all_to_all(low, "row", split_axis=0, concat_axis=0)
    others = jnp.concatenate(
        [attention_probe_matrix.T, attention_extra_matrices[:, inner:].T], axis=0
    )
    gated, turned = attention(high, attention_extra_matrices[:, :inner], others)
    left_piece, right_piece = alignment(
        high, low, turned, attention_final_matrix.T, tensor_entry_matrices.T
    )


    rights, sources = exchange_rows([right_piece] * row_count)
    left, left_slots = gather_turned(left_piece)
    mid, gate, sides = pair_update(
        left_slots,
        sources * own_residues,
        left,
        rights,
        tensor_final_matrix,
        couplings,
        paired_entries(incoming_entry_matrices),
        incoming_switch_matrix,
    )
    gated, sides = lax.optimization_barrier((gated, sides))

    everywhere = ("row", "col")
    column_count = lax.axis_size("col")
    devices = row_count * column_count
    sides = sides.reshape(devices, C_TRI // devices, *sides.shape[1:])
    sides = lax.all_to_all(sides, everywhere, split_axis=0, concat_axis=0)

    pieces = [
        lax.dynamic_index_in_dim(gated, sources[shift], keepdims=False)
        for shift in range(row_count)
    ]
    pieces, sources = exchange_rows(pieces)
    gated = jnp.take(jnp.stack(pieces), sources, axis=0)
    gated = jnp.transpose(gated.reshape(residues, seqs, inner), (1, 0, 2))
    change = jnp.dot(
        gated.reshape(-1, inner), attention_final_matrix, preferred_element_type=F32
    )
    refreshed_homologs = homolog_tensor + change.reshape(homolog_tensor.shape)

    product = triangle_product(sides, row_count, column_count)
    product = lax.all_to_all(product, everywhere, split_axis=0, concat_axis=0)
    product = product.reshape(C_TRI, *product.shape[2:])
    pair_output = pair_result(product, mid, gate, incoming_final_matrix)
    return (refreshed_homologs, pair_output)


def solution(mesh):
    in_specs = (
        P("row", "col", None),
        P("row", "col", None),
        P(),
        P(),
        P(),
        P(),
        P(),
        P(),
        P(),
        P(),
    )
    out_specs = (P("row", "col", None), P("row", "col", None))
    return jax.shard_map(body, mesh=mesh, in_specs=in_specs, out_specs=out_specs, check_vma=False)
```

```python
import functools

import jax
import jax.numpy as jnp
from jax import lax
from jax.experimental import pallas as pl
from jax.experimental.pallas import tpu as pltpu
from jax.sharding import PartitionSpec as P

FEATURE_DEPTH = 256
C_Z = 128
TENSOR_FEATURES = 32
C_TRI = 128
ATTENTION_UNITS = 8
UNIT_WIDTH = 32
EPS = 1e-05
GROUP = 4
F32 = jnp.float32
BF16 = jnp.bfloat16
NT = (((1,), (1,)), ((), ()))
VMEM_LIMIT = 56 * 1024 * 1024


def matmul(left, right):
    return jnp.dot(left, right, preferred_element_type=F32)


def matmul_nt(left, right):
    return lax.dot_general(left, right, NT, preferred_element_type=F32)


def sigmoid(values):
    return 0.5 * jnp.tanh(0.5 * values) + 0.5


def cost(microseconds):
    return pl.CostEstimate(
        flops=int(microseconds * 1e9), bytes_accessed=int(microseconds * 1e6), transcendentals=0
    )


def params(*semantics):
    return pltpu.CompilerParams(
        dimension_semantics=semantics or None, vmem_limit_bytes=VMEM_LIMIT
    )


def standardise_kernel(first_ref, second_ref, out_ref):
    seqs, residues, lanes = first_ref.shape
    cuts, height, _ = out_ref.shape
    own = (height - 16) // seqs
    first_rows = first_ref.reshape(seqs * residues, lanes)
    second_rows = second_ref.reshape(seqs * residues, lanes)
    lane = lax.broadcasted_iota(jnp.int32, (seqs, 128), 1)
    for cut in range(cuts):
        spreads = jnp.zeros((seqs, 128), F32)
        for n in range(own):
            rows = pl.ds(cut * own + n, seqs, stride=residues)
            column = jnp.concatenate([first_rows[rows, :], second_rows[rows, :]], axis=1)
            centred = column - jnp.mean(column, axis=1, keepdims=True)
            variance = jnp.mean(centred * centred, axis=1, keepdims=True) + EPS
            scale = lax.rsqrt(variance)
            out_ref[cut, n * seqs : (n + 1) * seqs, :] = (centred * scale).astype(BF16)
            spreads = jnp.where(lane == n, variance * scale, spreads)
        spreads = spreads.T[:8, :]
        coarse = spreads.astype(BF16).astype(F32)
        kept = jnp.concatenate([coarse, spreads - coarse], axis=0)
        kept = jnp.concatenate([kept, jnp.zeros((16, 2 * lanes - seqs), F32)], axis=1)
        out_ref[cut, own * seqs :, :] = kept.astype(BF16)


def standardise(block, cuts):
    seqs, residues, depth = block.shape
    half = depth // 2
    own = residues // cuts
    height = own * seqs + 16
    return pl.pallas_call(
        standardise_kernel,
        grid=(residues // 8,),
        in_specs=[
            pl.BlockSpec((seqs, 8, half), lambda g: (0, g, 0)),
            pl.BlockSpec((seqs, 8, half), lambda g: (0, g, 1)),
        ],
        out_specs=pl.BlockSpec((8 // own, height, depth), lambda g: (g, 0, 0)),
        out_shape=jax.ShapeDtypeStruct((cuts, height, depth), BF16),
        compiler_params=params("arbitrary"),
        cost_estimate=cost(3),
        name="standardise",
    )(block, block)


def attention_kernel(
    normed_ref, key_ref, others_ref, gated_ref, turned_ref, scores_ref, weights_ref
):
    blocks, residues, seqs, _ = gated_ref.shape
    depth = normed_ref.shape[2]
    total = blocks * seqs
    inner = ATTENTION_UNITS * UNIT_WIDTH
    ring = scores_ref.shape[0]
    columns = []
    for n in range(residues):
        column = normed_ref[:, n * seqs : (n + 1) * seqs, :].reshape(total, depth)
        key_rows = matmul(column, key_ref[...]).astype(BF16)
        projected = matmul_nt(others_ref[...], column)
        queries = (projected[:inner] * UNIT_WIDTH ** (-0.5)).astype(BF16)
        value_rows = projected[inner : 2 * inner].astype(BF16)
        gates = sigmoid(projected[2 * inner :])
        columns.append((key_rows, queries, value_rows, gates))
    units = [(n, h) for h in range(ATTENTION_UNITS) for n in range(residues)]

    def score(unit):
        n, h = units[unit]
        key_rows, queries, _, _ = columns[n]
        low, high = h * UNIT_WIDTH, (h + 1) * UNIT_WIDTH
        pieces = [queries[low:high]]
        if low > 0:
            pieces.insert(0, jnp.zeros((low, total), BF16))
        if high < inner:
            pieces.append(jnp.zeros((inner - high, total), BF16))
        scores_ref[unit % ring] = matmul(key_rows, jnp.concatenate(pieces, axis=0))

    def weigh(unit):
        for low in range(0, total, 128):
            scores = scores_ref[unit % ring, :, low : low + 128]
            weights = jnp.exp(scores - jnp.max(scores, axis=0, keepdims=True))
            scale = 1.0 / jnp.sum(weights, axis=0, keepdims=True)
            weights_ref[unit % ring, :, low : low + 128] = (weights * scale).astype(BF16)

    def attend(unit):
        n, h = units[unit]
        _, _, value_rows, gates = columns[n]
        rows = slice(h * UNIT_WIDTH, (h + 1) * UNIT_WIDTH)
        attended = matmul(value_rows[rows], weights_ref[unit % ring]) * gates[rows]
        turned_ref[n, rows, :] = attended.astype(BF16)

    for step in range(len(units) + 2):
        if step < len(units):
            score(step)
        if 1 <= step <= len(units):
            weigh(step - 1)
        if step >= 2:
            attend(step - 2)
    for n in range(residues):
        gated_ref[:, n] = turned_ref[n].T.reshape(blocks, seqs, inner)


def attention(normed, key_matrix, other_matrices, residues):
    blocks, height, depth = normed.shape
    seqs = (height - 16) // residues
    total = blocks * seqs
    inner = ATTENTION_UNITS * UNIT_WIDTH
    step = 4
    return pl.pallas_call(
        attention_kernel,
        grid=(residues // step,),
        in_specs=[
            pl.BlockSpec((blocks, step * seqs, depth), lambda n: (0, n, 0)),
            pl.BlockSpec((depth, inner), lambda n: (0, 0)),
            pl.BlockSpec((3 * inner, depth), lambda n: (0, 0)),
        ],
        out_specs=[
            pl.BlockSpec((blocks, step, seqs, inner), lambda n: (0, n, 0, 0)),
            pl.BlockSpec((step, inner, total), lambda n: (n, 0, 0)),
        ],
        out_shape=[
            jax.ShapeDtypeStruct((blocks, residues, seqs, inner), BF16),
            jax.ShapeDtypeStruct((residues, inner, total), BF16),
        ],
        scratch_shapes=[
            pltpu.VMEM((4, total, total), F32),
            pltpu.VMEM((4, total, total), BF16),
        ],
        compiler_params=params("arbitrary"),
        cost_estimate=cost(10),
        name="attention",
    )(normed, key_matrix, other_matrices)


def alignment_kernel(
    normed_ref, spread_ref, turned_ref, final_ref, entry_ref, left_ref, right_ref, rows_ref
):
    blocks, _, depth = normed_ref.shape
    residues, _, total = turned_ref.shape
    seqs = total // blocks
    features = TENSOR_FEATURES
    step = pl.program_id(0)
    for n in range(residues):
        column = normed_ref[:, n * seqs : (n + 1) * seqs, :].reshape(total, depth)
        spreads = []
        for block in range(blocks):
            kept = spread_ref[block, :, :seqs].astype(F32)
            row = lax.broadcasted_iota(jnp.int32, kept.shape, 0)
            chosen = lax.rem(row, 8) == step * residues + n
            spreads.append(jnp.sum(jnp.where(chosen, kept, 0.0), axis=0, keepdims=True))
        spread = jnp.concatenate(spreads, axis=1)
        updated = column.T.astype(F32) * spread + matmul(final_ref[...], turned_ref[n])
        centred = updated - jnp.mean(updated, axis=0, keepdims=True)
        variance = jnp.mean(centred * centred, axis=0, keepdims=True)
        normed = (centred * lax.rsqrt(variance + EPS)).astype(BF16)
        projected = matmul(entry_ref[...], normed)
        right_ref[n] = projected[features:].astype(BF16)
        first = pl.multiple_of((step * residues + n) * features, features)
        for tile in range(total // 128):
            rows_ref[tile, pl.ds(first, features), :] = projected[
                :features, tile * 128 : (tile + 1) * 128
            ]

    @pl.when(step == pl.num_programs(0) - 1)
    def _():
        count = rows_ref.shape[1] // features
        together = max(1, 16 // count)
        for c in range(0, features, together):
            pieces = []
            for e in range(together):
                chosen = pl.ds(c + e, count, stride=features)
                tiles = [rows_ref[tile, chosen, :] for tile in range(total // 128)]
                pieces.append(jnp.concatenate(tiles, axis=1))
            piece = jnp.concatenate(pieces, axis=0).astype(BF16)
            left_ref[c * count : (c + together) * count, :] = piece


def alignment(normed, turned, final_matrix, entry_matrices):
    blocks, height, depth = normed.shape
    residues, _, total = turned.shape
    seqs = total // blocks
    features = TENSOR_FEATURES
    step = 4
    return pl.pallas_call(
        alignment_kernel,
        grid=(residues // step,),
        in_specs=[
            pl.BlockSpec((blocks, step * seqs, depth), lambda n: (0, n, 0)),
            pl.BlockSpec((blocks, 16, depth), lambda n: (0, height // 16 - 1, 0)),
            pl.BlockSpec((step, depth, total), lambda n: (n, 0, 0)),
            pl.BlockSpec(final_matrix.shape, lambda n: (0, 0)),
            pl.BlockSpec(entry_matrices.shape, lambda n: (0, 0)),
        ],
        out_specs=[
            pl.BlockSpec((features * residues, total), lambda n: (0, 0)),
            pl.BlockSpec((step, features, total), lambda n: (n, 0, 0)),
        ],
        out_shape=[
            jax.ShapeDtypeStruct((features * residues, total), BF16),
            jax.ShapeDtypeStruct((residues, features, total), BF16),
        ],
        scratch_shapes=[pltpu.VMEM((total // 128, residues * features, 128), F32)],
        compiler_params=params("arbitrary"),
        cost_estimate=cost(4),
        name="alignment",
    )(normed, normed, turned, final_matrix, entry_matrices)


def pair_kernel(
    left_slots_ref,
    right_firsts_ref,
    own_ref,
    other_ref,
    *rest,
):
    weights_ref, entry_ref, switch_ref, couplings_hbm, mid_hbm, gate_hbm, sides_hbm = rest[-16:-9]
    outer_ref, spread_ref, sum_ref, rows_ref, couplings_ref = rest[-9:-4]
    mid_ref, gate_ref, sides_ref, copied = rest[-4:]
    right_refs = rest[:-16]
    fetched = pltpu.make_async_copy(couplings_hbm, couplings_ref, copied.at[0])
    fetched.start()
    copies = []

    def send(source, target):
        copies.append(pltpu.make_async_copy(source, target, copied.at[len(copies) + 1]))
        copies[-1].start()

    features = TENSOR_FEATURES
    slots, piece_rows, total = own_ref.shape
    residues = piece_rows // features
    rows = 2 * slots * residues
    share = right_refs[0].shape[0]
    columns = len(right_refs) * share
    groups = columns // GROUP
    wide = share * features
    together = spread_ref.shape[1] // 128

    for half, left_ref in enumerate((own_ref, other_ref)):
        piece = left_ref[...].reshape(slots * piece_rows, total)
        target = slice(half * slots * piece_rows, (half + 1) * slots * piece_rows)
        for p, right_ref in enumerate(right_refs):
            right = right_ref[...].reshape(wide, total)
            outer_ref[target, p * wide : (p + 1) * wide] = matmul_nt(piece, right) * (1.0 / total)

    spread_ref[...] = jnp.zeros_like(spread_ref)

    def channel_step(p, carry):
        slot = lax.rem(p, 2)
        for e in range(together):
            source = pl.multiple_of((p * together + e) * features, features)
            piece = weights_ref[pl.ds(source, features), :]
            for place in range(GROUP):
                low = e * 128 + place * features
                spread_ref[slot, low : low + features, place * C_Z : (place + 1) * C_Z] = piece
        pieces = []
        for g in range(groups):
            parts = []
            for e in range(together):
                channel = []
                for slot_number in range(2 * slots):
                    first = slot_number * piece_rows + (p * together + e) * residues
                    source = pl.ds(pl.multiple_of(first, residues), residues)
                    channel.append(outer_ref[source, g * 128 : (g + 1) * 128])
                parts.append(jnp.concatenate(channel, axis=0).astype(BF16))
            pieces.append(jnp.concatenate(parts, axis=1))
        update = matmul(jnp.concatenate(pieces, axis=0), spread_ref[slot])

        @pl.when(p == 0)
        def _():
            sum_ref[...] = update

        @pl.when(p > 0)
        def _():
            sum_ref[...] += update

        return carry

    lax.fori_loop(0, features // together, channel_step, 0)

    left_firsts = [left_slots_ref[j] * residues for j in range(2 * slots)]
    right_firsts = [right_firsts_ref[p] for p in range(len(right_refs))]
    fetched.wait()
    for g in range(groups):
        normed, places = [], []
        for place in range(GROUP):
            p, n = divmod(g * GROUP + place, share)
            b = right_firsts[p] + n
            places.append(b)
            lanes = slice(place * C_Z, (place + 1) * C_Z)
            pieces = []
            for first in left_firsts:
                source = pl.ds(pl.multiple_of(g * rows + first, residues), residues)
                pieces.append(sum_ref[source, lanes])
            mid = jnp.concatenate(pieces, axis=0)
            mid = mid + couplings_ref[pl.ds(b, rows, stride=columns), :]
            mid_ref[g * GROUP + place] = mid
            centred = mid - jnp.mean(mid, axis=1, keepdims=True)
            variance = jnp.mean(centred * centred, axis=1, keepdims=True)
            normed.append((centred * lax.rsqrt(variance + EPS)).astype(BF16))
        gates = sigmoid(matmul(jnp.concatenate(normed, axis=0), switch_ref[...]))
        blank = jnp.zeros_like(normed[0])
        for place in range(0, GROUP, 2):
            twice = []
            for e in range(2):
                part = gates[(place + e) * rows : (place + e + 1) * rows]
                gate_ref[g * GROUP + place + e] = part
                twice.append(jnp.concatenate([normed[place + e], blank], axis=1))
                twice.append(jnp.concatenate([blank, normed[place + e]], axis=1))
            sides = matmul_nt(entry_ref[...], jnp.concatenate(twice, axis=0))
            sides = sigmoid(sides[C_TRI:]) * sides[:C_TRI]
            for e in range(2):
                first = pl.multiple_of(places[place + e] * C_TRI, C_TRI)
                rows_ref[pl.ds(first, C_TRI), :] = sides[:, e * 2 * rows : (e + 1) * 2 * rows]

        if (g + 1) * GROUP % share == 0:
            p = (g + 1) * GROUP // share - 1
            source, target = pl.ds(p * share, share), pl.ds(right_firsts[p], share)
            send(mid_ref.at[source], mid_hbm.at[target])
            send(gate_ref.at[source], gate_hbm.at[target])

    cut = C_TRI // 4
    for part in range(4):

        def turn_step(c, carry):
            sides_ref[c] = rows_ref[pl.ds(c, columns, stride=C_TRI), :].astype(BF16)
            return carry

        lax.fori_loop(part * cut, (part + 1) * cut, turn_step, 0, unroll=8)
        chosen = pl.ds(part * cut, cut)
        send(sides_ref.at[chosen], sides_hbm.at[chosen])
    for copy in copies:
        copy.wait()


def pair_update(left_slots, right_firsts, left, rights, weights, couplings, entry, switch):
    rows, columns, depth = couplings.shape
    whole = jax.ShapeDtypeStruct((columns, rows, depth), F32)
    sides = jax.ShapeDtypeStruct((C_TRI, columns, 2 * rows), BF16)
    smem = pl.BlockSpec(memory_space=pltpu.SMEM)
    vmem = pl.BlockSpec(memory_space=pltpu.VMEM)
    anywhere = pl.BlockSpec(memory_space=pl.ANY)
    return pl.pallas_call(
        pair_kernel,
        in_specs=[smem] * 2 + [vmem] * (5 + len(rights)) + [anywhere],
        out_specs=[anywhere] * 3,
        out_shape=[whole, whole, sides],
        scratch_shapes=[
            pltpu.VMEM((rows * TENSOR_FEATURES, columns * TENSOR_FEATURES), F32),
            pltpu.VMEM((2, 8 * 128, GROUP * depth), BF16),
            pltpu.VMEM((columns // GROUP * rows, GROUP * depth), F32),
            pltpu.VMEM((columns * C_TRI, 2 * rows), F32),
            pltpu.VMEM((rows * columns, depth), F32),
            pltpu.VMEM(whole.shape, F32),
            pltpu.VMEM(whole.shape, F32),
            pltpu.VMEM(sides.shape, BF16),
            pltpu.SemaphoreType.DMA((2 * len(rights) + 5,)),
        ],
        compiler_params=params(),
        cost_estimate=cost(12),
        name="pair_update",
    )(
        left_slots,
        right_firsts,
        *left,
        *rights,
        weights,
        entry,
        switch,
        couplings.reshape(rows * columns, depth),
    )


def product_kernel(sides_ref, out_ref, *, grid_rows, grid_columns):
    channels, part, lanes = sides_ref.shape[1:]
    half = lanes // 2
    lane = lax.broadcasted_iota(jnp.int32, (grid_columns * part, lanes), 1)
    front = lane < half
    cut = front[: part // 2]
    for channel in range(channels):
        lefts, rights = [], []
        for r in range(0, grid_rows, 2):
            even, odd = [
                jnp.concatenate(
                    [sides_ref[(r + e) * grid_columns + c, channel] for c in range(grid_columns)],
                    axis=0,
                )
                for e in range(2)
            ]
            lefts.append(jnp.where(front, even, pltpu.roll(odd, half, 1)))
            rights.append(jnp.where(front, pltpu.roll(even, half, 1), odd))
        product = matmul_nt(jnp.concatenate(rights, axis=1), jnp.concatenate(lefts, axis=1))
        product = product.astype(BF16)
        for c in range(grid_columns):
            for r in range(0, grid_rows, 2):
                block = product[c * part : (c + 1) * part, r * half : (r + 2) * half]
                top, bottom = block[: part // 2], block[part // 2 :]
                even = jnp.where(cut, top, pltpu.roll(bottom, half, 1))
                out_ref[r * grid_columns + c, channel] = even
                odd = jnp.where(cut, pltpu.roll(top, half, 1), bottom)
                out_ref[(r + 1) * grid_columns + c, channel] = odd


def triangle_product(sides, grid_rows, grid_columns):
    devices, channels, part, lanes = sides.shape
    step = 2 if channels % 2 == 0 else 1
    return pl.pallas_call(
        functools.partial(product_kernel, grid_rows=grid_rows, grid_columns=grid_columns),
        grid=(channels // step,),
        in_specs=[pl.BlockSpec((devices, step, part, lanes), lambda c: (0, c, 0, 0))],
        out_specs=pl.BlockSpec((devices, step, part // 2, lanes), lambda c: (0, c, 0, 0)),
        out_shape=jax.ShapeDtypeStruct((devices, channels, part // 2, lanes), BF16),
        compiler_params=params("arbitrary"),
        cost_estimate=cost(3),
        name="triangle_product",
    )(sides)


def output_kernel(product_ref, mid_ref, gate_ref, final_ref, out_ref, wide_ref):
    channels, part, lanes = product_ref.shape
    _, own, rows, depth = mid_ref.shape
    out_rows = out_ref.reshape(rows * 2 * own, depth)
    step = pl.program_id(0)

    @pl.when(step == 0)
    def _():
        wide_ref[...] = product_ref[...].astype(F32).reshape(channels * part, lanes)

    for j in range(own):
        product = wide_ref[pl.ds(step * own + j, channels, stride=part), :]
        centred = product - jnp.mean(product, axis=0, keepdims=True)
        variance = jnp.mean(centred * centred, axis=0, keepdims=True)
        normed = (centred * lax.rsqrt(variance + EPS)).astype(BF16).T
        update = matmul(normed, final_ref[...])
        for half in range(2):
            piece = update[half * rows : (half + 1) * rows]
            piece = mid_ref[half, j] + gate_ref[half, j] * piece
            out_rows[pl.ds(half * own + j, rows, stride=2 * own), :] = piece


def pair_result(product, mid, gate, final_matrix):
    channels, part, lanes = product.shape
    columns, rows, depth = mid.shape
    own = 8
    whole = pl.BlockSpec((2, own, rows, depth), lambda j: (0, j, 0, 0))
    out = pl.pallas_call(
        output_kernel,
        grid=(part // own,),
        in_specs=[
            pl.BlockSpec(product.shape, lambda j: (0, 0, 0)),
            whole,
            whole,
            pl.BlockSpec(final_matrix.shape, lambda j: (0, 0)),
        ],
        out_specs=pl.BlockSpec((rows, 2, own, depth), lambda j: (0, 0, j, 0)),
        out_shape=jax.ShapeDtypeStruct((rows, 2, part, depth), F32),
        scratch_shapes=[pltpu.VMEM((channels * part, lanes), F32)],
        compiler_params=params("arbitrary"),
        cost_estimate=cost(4),
        name="pair_result",
    )(
        product,
        mid.reshape(2, part, rows, depth),
        gate.reshape(2, part, rows, depth),
        final_matrix,
    )
    return out.reshape(rows, columns, depth)


def swap_cores(block):
    count = lax.axis_size("col")
    return lax.ppermute(block, "col", [(c, c ^ 1) for c in range(count)])


def gather_turned(block):
    rows, columns = lax.axis_size("row"), lax.axis_size("col")
    arrived = []
    for shift in range(rows):
        moves = []
        for r in range(rows):
            for q in range(rows):
                for side in range(2):
                    source = r * columns + 2 * q + side
                    moves.append((source, q * columns + 2 * ((r + shift) % rows) + side))
        arrived.append(lax.ppermute(block, ("row", "col"), moves))
    return jnp.stack(arrived)


def both_cores(own):
    rows = lax.axis_size("row")
    me, core = lax.axis_index("col") // 2, lax.rem(lax.axis_index("col"), 2)
    other = swap_cores(own)
    shifts = lax.rem(me - jnp.arange(rows, dtype=jnp.int32) + rows, rows)
    residues = own.shape[1] // TENSOR_FEATURES
    if residues % 8 == 0:
        return (own, other), jnp.concatenate([shifts + core * rows, shifts + (1 - core) * rows])
    own, other = jnp.take(own, shifts, axis=0), jnp.take(other, shifts, axis=0)
    joined = 8 // residues
    ordered = []
    for side in (jnp.where(core == 0, own, other), jnp.where(core == 0, other, own)):
        side = side.reshape(rows // joined, joined, TENSOR_FEATURES, residues, -1)
        side = jnp.transpose(side, (0, 2, 1, 3, 4))
        ordered.append(side.reshape(rows // joined, joined * own.shape[1], -1))
    return tuple(ordered), jnp.arange(2 * rows // joined, dtype=jnp.int32)


def exchange_rows(pieces):
    rows = lax.axis_size("row")
    arrived = [pieces[0]]
    for shift in range(1, rows):
        moves = [(r, r ^ shift) for r in range(rows)]
        arrived.append(lax.ppermute(pieces[shift], "row", moves))
    return arrived, lax.axis_index("row") ^ jnp.arange(rows, dtype=jnp.int32)


def paired_entries(matrices):
    turned = matrices.reshape(C_Z, 2, 2, C_TRI)
    return jnp.transpose(turned, (2, 3, 1, 0)).reshape(2 * C_TRI, 2 * C_Z)


def body(
    homolog_tensor,
    couplings,
    attention_probe_matrix,
    attention_extra_matrices,
    attention_final_matrix,
    tensor_entry_matrices,
    tensor_final_matrix,
    incoming_entry_matrices,
    incoming_switch_matrix,
    incoming_final_matrix,
):
    inner = ATTENTION_UNITS * UNIT_WIDTH
    row_count = lax.axis_size("row")
    seqs, residues, depth = homolog_tensor.shape
    own_residues = residues // row_count
    normed = standardise(homolog_tensor, row_count)
    normed = lax.all_to_all(normed, "row", split_axis=0, concat_axis=0)
    others = jnp.concatenate(
        [attention_probe_matrix.T, attention_extra_matrices[:, inner:].T], axis=0
    )
    gated, turned = attention(
        normed, attention_extra_matrices[:, :inner], others, own_residues
    )
    left_piece, right_piece = alignment(
        normed, turned, attention_final_matrix.T, tensor_entry_matrices.T
    )

    rights, sources = exchange_rows([right_piece] * row_count)
    own = gather_turned(left_piece)
    own, rights, gated = lax.optimization_barrier((own, rights, gated))
    gated = lax.all_to_all(gated, "row", split_axis=0, concat_axis=0)
    left, left_slots = both_cores(own)
    mid, gate, sides = pair_update(
        left_slots,
        sources * own_residues,
        left,
        rights,
        tensor_final_matrix,
        couplings,
        paired_entries(incoming_entry_matrices),
        incoming_switch_matrix,
    )
    gated, sides = lax.optimization_barrier((gated, sides))
    gated = jnp.transpose(gated.reshape(residues, seqs, inner), (1, 0, 2))
    change = jnp.dot(
        gated.reshape(-1, inner), attention_final_matrix, preferred_element_type=F32
    )
    refreshed_homologs = homolog_tensor + change.reshape(homolog_tensor.shape)

    everywhere = ("row", "col")
    column_count = lax.axis_size("col")
    devices = row_count * column_count
    sides = sides.reshape(devices, C_TRI // devices, *sides.shape[1:])
    sides = lax.all_to_all(sides, everywhere, split_axis=0, concat_axis=0)
    product = triangle_product(sides, row_count, column_count)
    product = lax.all_to_all(product, everywhere, split_axis=0, concat_axis=0)
    product = product.reshape(C_TRI, *product.shape[2:])
    pair_output = pair_result(product, mid, gate, incoming_final_matrix)
    return (refreshed_homologs, pair_output)


def solution(mesh):
    in_specs = (
        P("row", "col", None),
        P("row", "col", None),
        P(),
        P(),
        P(),
        P(),
        P(),
        P(),
        P(),
        P(),
    )
    out_specs = (P("row", "col", None), P("row", "col", None))
    return jax.shard_map(body, mesh=mesh, in_specs=in_specs, out_specs=out_specs, check_vma=False)
```

```python
import functools

import jax
import jax.numpy as jnp
from jax import lax
from jax.experimental import pallas as pl
from jax.experimental.pallas import tpu as pltpu
from jax.sharding import PartitionSpec as P

FEATURE_DEPTH = 256
C_Z = 128
TENSOR_FEATURES = 32
C_TRI = 128
ATTENTION_UNITS = 8
UNIT_WIDTH = 32
EPS = 1e-05
GROUP = 4
F32 = jnp.float32
BF16 = jnp.bfloat16
NT = (((1,), (1,)), ((), ()))
VMEM_LIMIT = 56 * 1024 * 1024


def matmul(left, right):
    return jnp.dot(left, right, preferred_element_type=F32)


def matmul_nt(left, right):
    return lax.dot_general(left, right, NT, preferred_element_type=F32)


def sigmoid(values):
    return 0.5 * jnp.tanh(0.5 * values) + 0.5


def cost(microseconds):
    return pl.CostEstimate(
        flops=int(microseconds * 1e9), bytes_accessed=int(microseconds * 1e6), transcendentals=0
    )


def params(*semantics):
    return pltpu.CompilerParams(
        dimension_semantics=semantics or None, vmem_limit_bytes=VMEM_LIMIT
    )


def standardised_column(first_rows, second_rows, n, residues):
    seqs = first_rows.shape[0] // residues
    rows = pl.ds(n, seqs, stride=residues)
    column = jnp.concatenate([first_rows[rows, :], second_rows[rows, :]], axis=1)
    centred = column - jnp.mean(column, axis=1, keepdims=True)
    variance = jnp.mean(centred * centred, axis=1, keepdims=True) + EPS
    scale = lax.rsqrt(variance)
    return centred * scale, variance * scale


def high_kernel(first_ref, second_ref, high_ref):
    seqs, residues, lanes = first_ref.shape
    first_rows = first_ref.reshape(seqs * residues, lanes)
    second_rows = second_ref.reshape(seqs * residues, lanes)
    for n in range(residues):
        normed, _ = standardised_column(first_rows, second_rows, n, residues)
        high_ref[n] = normed.astype(BF16)


def standardise_high(block):
    seqs, residues, depth = block.shape
    half = depth // 2
    step = 16
    return pl.pallas_call(
        high_kernel,
        grid=(seqs // step,),
        in_specs=[
            pl.BlockSpec((step, residues, half), lambda s: (s, 0, 0)),
            pl.BlockSpec((step, residues, half), lambda s: (s, 0, 1)),
        ],
        out_specs=pl.BlockSpec((residues, step, depth), lambda s: (0, s, 0)),
        out_shape=jax.ShapeDtypeStruct((residues, seqs, depth), BF16),
        compiler_params=params("arbitrary"),
        cost_estimate=cost(3),
        name="standardise_high",
    )(block, block)


def low_kernel(first_ref, second_ref, low_ref):
    seqs, residues, lanes = first_ref.shape
    first_rows = first_ref.reshape(seqs * residues, lanes)
    second_rows = second_ref.reshape(seqs * residues, lanes)
    lane = lax.broadcasted_iota(jnp.int32, (seqs, 128), 1)
    spreads = jnp.zeros((seqs, 128), F32)
    for n in range(residues):
        normed, spread = standardised_column(first_rows, second_rows, n, residues)
        low_ref[n, :seqs, :] = (normed - normed.astype(BF16).astype(F32)).astype(BF16)
        spreads = jnp.where(lane == n, spread, spreads)
    spreads = spreads.T
    row = lax.broadcasted_iota(jnp.int32, (16, seqs), 0)
    for n in range(residues):
        spread = jnp.broadcast_to(spreads[n : n + 1, :], (16, seqs))
        coarse = spread.astype(BF16).astype(F32)
        kept = jnp.where(row == 0, coarse, jnp.where(row == 1, spread - coarse, 0.0))
        kept = jnp.concatenate([kept, jnp.zeros((16, 2 * lanes - seqs), F32)], axis=1)
        low_ref[n, seqs:, :] = kept.astype(BF16)


def standardise_low(block):
    seqs, residues, depth = block.shape
    half = depth // 2
    return pl.pallas_call(
        low_kernel,
        grid=(residues // 8,),
        in_specs=[
            pl.BlockSpec((seqs, 8, half), lambda g: (0, g, 0)),
            pl.BlockSpec((seqs, 8, half), lambda g: (0, g, 1)),
        ],
        out_specs=pl.BlockSpec((8, seqs + 16, depth), lambda g: (g, 0, 0)),
        out_shape=jax.ShapeDtypeStruct((residues, seqs + 16, depth), BF16),
        compiler_params=params("arbitrary"),
        cost_estimate=cost(3),
        name="standardise_low",
    )(block, block)


def attention_kernel(sources_ref, normed_ref, key_ref, others_ref, turned_ref, *rest):
    *gated_refs, scores_ref, weights_ref, back_ref = rest
    blocks, residues, seqs, depth = normed_ref.shape
    total = blocks * seqs
    inner = ATTENTION_UNITS * UNIT_WIDTH
    ring = scores_ref.shape[0]
    columns = []
    for n in range(residues):
        column = normed_ref[:, n].reshape(total, depth)
        key_rows = matmul(column, key_ref[...]).astype(BF16)
        projected = matmul_nt(others_ref[...], column)
        queries = (projected[:inner] * UNIT_WIDTH ** (-0.5)).astype(BF16)
        value_rows = projected[inner : 2 * inner].astype(BF16)
        gates = sigmoid(projected[2 * inner :])
        columns.append((key_rows, queries, value_rows, gates))
    units = [(n, h) for h in range(ATTENTION_UNITS) for n in range(residues)]

    def score(unit):
        n, h = units[unit]
        key_rows, queries, _, _ = columns[n]
        rows = slice(h * UNIT_WIDTH, (h + 1) * UNIT_WIDTH)
        scores_ref[unit % ring] = matmul(key_rows[:, rows], queries[rows])

    def weigh(unit):
        for low in range(0, total, 128):
            scores = scores_ref[unit % ring, :, low : low + 128]
            weights = jnp.exp(scores - jnp.max(scores, axis=0, keepdims=True))
            scale = 1.0 / jnp.sum(weights, axis=0, keepdims=True)
            weights_ref[unit % ring, :, low : low + 128] = (weights * scale).astype(BF16)

    def attend(unit):
        n, h = units[unit]
        _, _, value_rows, gates = columns[n]
        rows = slice(h * UNIT_WIDTH, (h + 1) * UNIT_WIDTH)
        attended = matmul(value_rows[rows], weights_ref[unit % ring]) * gates[rows]
        turned_ref[n, rows, :] = attended.astype(BF16)

    for step in range(len(units) + 2):
        if step < len(units):
            score(step)
        if 1 <= step <= len(units):
            weigh(step - 1)
        if step >= 2:
            attend(step - 2)
    for n in range(residues):
        back_ref[n] = turned_ref[n].T
        for shift, gated_ref in enumerate(gated_refs):
            first = pl.multiple_of(sources_ref[shift] * seqs, seqs)
            gated_ref[n] = back_ref[n, pl.ds(first, seqs), :]


def attention(sources, normed, key_matrix, other_matrices):
    blocks, residues, seqs, depth = normed.shape
    total = blocks * seqs
    inner = ATTENTION_UNITS * UNIT_WIDTH
    step = 2
    gated = jax.ShapeDtypeStruct((residues, seqs, inner), BF16)
    gated_spec = pl.BlockSpec((step, seqs, inner), lambda n: (n, 0, 0))
    return pl.pallas_call(
        attention_kernel,
        grid=(residues // step,),
        in_specs=[
            pl.BlockSpec(memory_space=pltpu.SMEM),
            pl.BlockSpec((blocks, step, seqs, depth), lambda n: (0, n, 0, 0)),
            pl.BlockSpec((depth, inner), lambda n: (0, 0)),
            pl.BlockSpec((3 * inner, depth), lambda n: (0, 0)),
        ],
        out_specs=[pl.BlockSpec((step, inner, total), lambda n: (n, 0, 0))]
        + [gated_spec] * blocks,
        out_shape=[jax.ShapeDtypeStruct((residues, inner, total), BF16)] + [gated] * blocks,
        scratch_shapes=[
            pltpu.VMEM((4, total, total), F32),
            pltpu.VMEM((4, total, total), BF16),
            pltpu.VMEM((step, total, inner), BF16),
        ],
        compiler_params=params("arbitrary"),
        cost_estimate=cost(10),
        name="attention",
    )(sources, normed, key_matrix, other_matrices)


def alignment_kernel(
    high_ref, low_ref, turned_ref, final_ref, entry_ref, left_ref, right_ref, rows_ref
):
    blocks, residues, seqs, depth = high_ref.shape
    total = blocks * seqs
    features = TENSOR_FEATURES
    step = pl.program_id(0)
    for n in range(residues):
        low = low_ref[:, n, :seqs, :].reshape(total, depth)
        column = high_ref[:, n].reshape(total, depth).astype(F32) + low.astype(F32)
        spreads = []
        for block in range(blocks):
            kept = low_ref[block, n, seqs:, :seqs].astype(F32)
            spreads.append(jnp.sum(kept, axis=0, keepdims=True))
        spread = jnp.concatenate(spreads, axis=1)
        updated = column.T * spread + matmul(final_ref[...], turned_ref[n])
        centred = updated - jnp.mean(updated, axis=0, keepdims=True)
        variance = jnp.mean(centred * centred, axis=0, keepdims=True)
        normed = (centred * lax.rsqrt(variance + EPS)).astype(BF16)
        projected = matmul(entry_ref[...], normed)
        right_ref[n] = projected[features:].astype(BF16)
        first = pl.multiple_of((step * residues + n) * features, features)
        for tile in range(total // 128):
            rows_ref[tile, pl.ds(first, features), :] = projected[
                :features, tile * 128 : (tile + 1) * 128
            ]

    @pl.when(step == pl.num_programs(0) - 1)
    def _():
        count = rows_ref.shape[1] // features
        together = max(1, 16 // count)
        for c in range(0, features, together):
            pieces = []
            for e in range(together):
                chosen = pl.ds(c + e, count, stride=features)
                tiles = [rows_ref[tile, chosen, :] for tile in range(total // 128)]
                pieces.append(jnp.concatenate(tiles, axis=1))
            piece = jnp.concatenate(pieces, axis=0).astype(BF16)
            left_ref[c * count : (c + together) * count, :] = piece


def alignment(high, low, turned, final_matrix, entry_matrices):
    blocks, residues, seqs, depth = high.shape
    total = blocks * seqs
    features = TENSOR_FEATURES
    return pl.pallas_call(
        alignment_kernel,
        grid=(residues // 2,),
        in_specs=[
            pl.BlockSpec((blocks, 2, seqs, depth), lambda n: (0, n, 0, 0)),
            pl.BlockSpec((blocks, 2, seqs + 16, depth), lambda n: (0, n, 0, 0)),
            pl.BlockSpec((2, depth, total), lambda n: (n, 0, 0)),
            pl.BlockSpec(final_matrix.shape, lambda n: (0, 0)),
            pl.BlockSpec(entry_matrices.shape, lambda n: (0, 0)),
        ],
        out_specs=[
            pl.BlockSpec((features * residues, total), lambda n: (0, 0)),
            pl.BlockSpec((2, features, total), lambda n: (n, 0, 0)),
        ],
        out_shape=[
            jax.ShapeDtypeStruct((features * residues, total), BF16),
            jax.ShapeDtypeStruct((residues, features, total), BF16),
        ],
        scratch_shapes=[pltpu.VMEM((total // 128, residues * features, 128), F32)],
        compiler_params=params("arbitrary"),
        cost_estimate=cost(4),
        name="alignment",
    )(high, low, turned, final_matrix, entry_matrices)


def pair_kernel(
    left_slots_ref,
    right_firsts_ref,
    own_ref,
    other_ref,
    *rest,
):
    weights_ref, entry_ref, switch_ref, couplings_hbm, mid_hbm, gate_hbm, sides_hbm = rest[-16:-9]
    outer_ref, spread_ref, sum_ref, rows_ref, couplings_ref = rest[-9:-4]
    mid_ref, gate_ref, sides_ref, copied = rest[-4:]
    right_refs = rest[:-16]
    fetched = pltpu.make_async_copy(couplings_hbm, couplings_ref, copied.at[0])
    fetched.start()
    copies = []

    def send(source, target):
        copies.append(pltpu.make_async_copy(source, target, copied.at[len(copies) + 1]))
        copies[-1].start()

    features = TENSOR_FEATURES
    slots, piece_rows, total = own_ref.shape
    residues = piece_rows // features
    rows = 2 * slots * residues
    share = right_refs[0].shape[0]
    columns = len(right_refs) * share
    groups = columns // GROUP
    wide = share * features
    together = spread_ref.shape[1] // 128

    for half, left_ref in enumerate((own_ref, other_ref)):
        piece = left_ref[...].reshape(slots * piece_rows, total)
        target = slice(half * slots * piece_rows, (half + 1) * slots * piece_rows)
        for p, right_ref in enumerate(right_refs):
            right = right_ref[...].reshape(wide, total)
            outer_ref[target, p * wide : (p + 1) * wide] = matmul_nt(piece, right) * (1.0 / total)

    spread_ref[...] = jnp.zeros_like(spread_ref)

    def channel_step(p, carry):
        slot = lax.rem(p, 2)
        for e in range(together):
            source = pl.multiple_of((p * together + e) * features, features)
            piece = weights_ref[pl.ds(source, features), :]
            for place in range(GROUP):
                low = e * 128 + place * features
                spread_ref[slot, low : low + features, place * C_Z : (place + 1) * C_Z] = piece
        pieces = []
        for g in range(groups):
            parts = []
            for e in range(together):
                channel = []
                for slot_number in range(2 * slots):
                    first = slot_number * piece_rows + (p * together + e) * residues
                    source = pl.ds(pl.multiple_of(first, residues), residues)
                    channel.append(outer_ref[source, g * 128 : (g + 1) * 128])
                parts.append(jnp.concatenate(channel, axis=0).astype(BF16))
            pieces.append(jnp.concatenate(parts, axis=1))
        update = matmul(jnp.concatenate(pieces, axis=0), spread_ref[slot])

        @pl.when(p == 0)
        def _():
            sum_ref[...] = update

        @pl.when(p > 0)
        def _():
            sum_ref[...] += update

        return carry

    lax.fori_loop(0, features // together, channel_step, 0)

    left_firsts = [left_slots_ref[j] * residues for j in range(2 * slots)]
    right_firsts = [right_firsts_ref[p] for p in range(len(right_refs))]
    fetched.wait()
    for g in range(groups):
        normed, places = [], []
        for place in range(GROUP):
            p, n = divmod(g * GROUP + place, share)
            b = right_firsts[p] + n
            places.append(b)
            lanes = slice(place * C_Z, (place + 1) * C_Z)
            pieces = []
            for first in left_firsts:
                source = pl.ds(pl.multiple_of(g * rows + first, residues), residues)
                pieces.append(sum_ref[source, lanes])
            mid = jnp.concatenate(pieces, axis=0)
            mid = mid + couplings_ref[pl.ds(b, rows, stride=columns), :]
            mid_ref[g * GROUP + place] = mid
            centred = mid - jnp.mean(mid, axis=1, keepdims=True)
            variance = jnp.mean(centred * centred, axis=1, keepdims=True)
            normed.append((centred * lax.rsqrt(variance + EPS)).astype(BF16))
        gates = sigmoid(matmul(jnp.concatenate(normed, axis=0), switch_ref[...]))
        blank = jnp.zeros_like(normed[0])
        for place in range(0, GROUP, 2):
            twice = []
            for e in range(2):
                part = gates[(place + e) * rows : (place + e + 1) * rows]
                gate_ref[g * GROUP + place + e] = part
                twice.append(jnp.concatenate([normed[place + e], blank], axis=1))
                twice.append(jnp.concatenate([blank, normed[place + e]], axis=1))
            sides = matmul_nt(entry_ref[...], jnp.concatenate(twice, axis=0))
            sides = sigmoid(sides[C_TRI:]) * sides[:C_TRI]
            for e in range(2):
                first = pl.multiple_of(places[place + e] * C_TRI, C_TRI)
                rows_ref[pl.ds(first, C_TRI), :] = sides[:, e * 2 * rows : (e + 1) * 2 * rows]

        if (g + 1) * GROUP % share == 0:
            p = (g + 1) * GROUP // share - 1
            source, target = pl.ds(p * share, share), pl.ds(right_firsts[p], share)
            send(mid_ref.at[source], mid_hbm.at[target])
            send(gate_ref.at[source], gate_hbm.at[target])

    cut = C_TRI // 4
    for part in range(4):

        def turn_step(c, carry):
            sides_ref[c] = rows_ref[pl.ds(c, columns, stride=C_TRI), :].astype(BF16)
            return carry

        lax.fori_loop(part * cut, (part + 1) * cut, turn_step, 0, unroll=8)
        chosen = pl.ds(part * cut, cut)
        send(sides_ref.at[chosen], sides_hbm.at[chosen])
    for copy in copies:
        copy.wait()


def pair_update(left_slots, right_firsts, left, rights, weights, couplings, entry, switch):
    rows, columns, depth = couplings.shape
    whole = jax.ShapeDtypeStruct((columns, rows, depth), F32)
    sides = jax.ShapeDtypeStruct((C_TRI, columns, 2 * rows), BF16)
    smem = pl.BlockSpec(memory_space=pltpu.SMEM)
    vmem = pl.BlockSpec(memory_space=pltpu.VMEM)
    anywhere = pl.BlockSpec(memory_space=pl.ANY)
    return pl.pallas_call(
        pair_kernel,
        in_specs=[smem] * 2 + [vmem] * (5 + len(rights)) + [anywhere],
        out_specs=[anywhere] * 3,
        out_shape=[whole, whole, sides],
        scratch_shapes=[
            pltpu.VMEM((rows * TENSOR_FEATURES, columns * TENSOR_FEATURES), F32),
            pltpu.VMEM((2, 8 * 128, GROUP * depth), BF16),
            pltpu.VMEM((columns // GROUP * rows, GROUP * depth), F32),
            pltpu.VMEM((columns * C_TRI, 2 * rows), F32),
            pltpu.VMEM((rows * columns, depth), F32),
            pltpu.VMEM(whole.shape, F32),
            pltpu.VMEM(whole.shape, F32),
            pltpu.VMEM(sides.shape, BF16),
            pltpu.SemaphoreType.DMA((2 * len(rights) + 5,)),
        ],
        compiler_params=params(),
        cost_estimate=cost(12),
        name="pair_update",
    )(
        left_slots,
        right_firsts,
        *left,
        *rights,
        weights,
        entry,
        switch,
        couplings.reshape(rows * columns, depth),
    )


def product_kernel(sides_ref, out_ref, *, grid_rows, grid_columns):
    channels, part, lanes = sides_ref.shape[1:]
    half = lanes // 2
    lane = lax.broadcasted_iota(jnp.int32, (grid_columns * part, lanes), 1)
    front = lane < half
    cut = front[: part // 2]
    for channel in range(channels):
        lefts, rights = [], []
        for r in range(0, grid_rows, 2):
            even, odd = [
                jnp.concatenate(
                    [sides_ref[(r + e) * grid_columns + c, channel] for c in range(grid_columns)],
                    axis=0,
                )
                for e in range(2)
            ]
            lefts.append(jnp.where(front, even, pltpu.roll(odd, half, 1)))
            rights.append(jnp.where(front, pltpu.roll(even, half, 1), odd))
        product = matmul_nt(jnp.concatenate(rights, axis=1), jnp.concatenate(lefts, axis=1))
        product = product.astype(BF16)
        for c in range(grid_columns):
            for r in range(0, grid_rows, 2):
                block = product[c * part : (c + 1) * part, r * half : (r + 2) * half]
                top, bottom = block[: part // 2], block[part // 2 :]
                even = jnp.where(cut, top, pltpu.roll(bottom, half, 1))
                out_ref[r * grid_columns + c, channel] = even
                odd = jnp.where(cut, pltpu.roll(top, half, 1), bottom)
                out_ref[(r + 1) * grid_columns + c, channel] = odd


def triangle_product(sides, grid_rows, grid_columns):
    devices, channels, part, lanes = sides.shape
    step = 2 if channels % 2 == 0 else 1
    return pl.pallas_call(
        functools.partial(product_kernel, grid_rows=grid_rows, grid_columns=grid_columns),
        grid=(channels // step,),
        in_specs=[pl.BlockSpec((devices, step, part, lanes), lambda c: (0, c, 0, 0))],
        out_specs=pl.BlockSpec((devices, step, part // 2, lanes), lambda c: (0, c, 0, 0)),
        out_shape=jax.ShapeDtypeStruct((devices, channels, part // 2, lanes), BF16),
        compiler_params=params("arbitrary"),
        cost_estimate=cost(3),
        name="triangle_product",
    )(sides)


def output_kernel(product_ref, mid_ref, gate_ref, final_ref, out_ref, wide_ref):
    channels, part, lanes = product_ref.shape
    _, own, rows, depth = mid_ref.shape
    out_rows = out_ref.reshape(rows * 2 * own, depth)
    step = pl.program_id(0)

    @pl.when(step == 0)
    def _():
        wide_ref[...] = product_ref[...].astype(F32).reshape(channels * part, lanes)

    for j in range(own):
        product = wide_ref[pl.ds(step * own + j, channels, stride=part), :]
        centred = product - jnp.mean(product, axis=0, keepdims=True)
        variance = jnp.mean(centred * centred, axis=0, keepdims=True)
        normed = (centred * lax.rsqrt(variance + EPS)).astype(BF16).T
        update = matmul(normed, final_ref[...])
        for half in range(2):
            piece = update[half * rows : (half + 1) * rows]
            piece = mid_ref[half, j] + gate_ref[half, j] * piece
            out_rows[pl.ds(half * own + j, rows, stride=2 * own), :] = piece


def pair_result(product, mid, gate, final_matrix):
    channels, part, lanes = product.shape
    columns, rows, depth = mid.shape
    own = 8
    whole = pl.BlockSpec((2, own, rows, depth), lambda j: (0, j, 0, 0))
    out = pl.pallas_call(
        output_kernel,
        grid=(part // own,),
        in_specs=[
            pl.BlockSpec(product.shape, lambda j: (0, 0, 0)),
            whole,
            whole,
            pl.BlockSpec(final_matrix.shape, lambda j: (0, 0)),
        ],
        out_specs=pl.BlockSpec((rows, 2, own, depth), lambda j: (0, 0, j, 0)),
        out_shape=jax.ShapeDtypeStruct((rows, 2, part, depth), F32),
        scratch_shapes=[pltpu.VMEM((channels * part, lanes), F32)],
        compiler_params=params("arbitrary"),
        cost_estimate=cost(4),
        name="pair_result",
    )(
        product,
        mid.reshape(2, part, rows, depth),
        gate.reshape(2, part, rows, depth),
        final_matrix,
    )
    return out.reshape(rows, columns, depth)


def swap_cores(block):
    count = lax.axis_size("col")
    return lax.ppermute(block, "col", [(c, c ^ 1) for c in range(count)])


def gather_turned(block):
    rows, columns = lax.axis_size("row"), lax.axis_size("col")
    arrived = []
    for shift in range(rows):
        moves = []
        for r in range(rows):
            for q in range(rows):
                for side in range(2):
                    source = r * columns + 2 * q + side
                    moves.append((source, q * columns + 2 * ((r + shift) % rows) + side))
        arrived.append(lax.ppermute(block, ("row", "col"), moves))
    return jnp.stack(arrived)


def both_cores(own):
    rows = lax.axis_size("row")
    core = lax.rem(lax.axis_index("col"), 2)
    other = swap_cores(own)
    residues = own.shape[1] // TENSOR_FEATURES
    if residues % 8 == 0:
        return own, other
    order = left_order(rows)
    own, other = jnp.take(own, order, axis=0), jnp.take(other, order, axis=0)
    joined = 8 // residues
    ordered = []
    for side in (jnp.where(core == 0, own, other), jnp.where(core == 0, other, own)):
        side = side.reshape(rows // joined, joined, TENSOR_FEATURES, residues, -1)
        side = jnp.transpose(side, (0, 2, 1, 3, 4))
        ordered.append(side.reshape(rows // joined, joined * own.shape[1], -1))
    return tuple(ordered)


def left_order(rows):
    me = lax.axis_index("col") // 2
    return lax.rem(me - jnp.arange(rows, dtype=jnp.int32) + rows, rows)


def left_groups(rows, residues):
    if residues % 8:
        return jnp.arange(2 * rows * residues // 8, dtype=jnp.int32)
    core = lax.rem(lax.axis_index("col"), 2)
    order = left_order(rows)
    return jnp.concatenate([order + core * rows, order + (1 - core) * rows])


def exchange_rows(pieces):
    arrived = [pieces[0]]
    for shift in range(1, len(pieces)):
        moves = [(r, r ^ shift) for r in range(len(pieces))]
        arrived.append(lax.ppermute(pieces[shift], "row", moves))
    return arrived


def paired_entries(matrices):
    turned = matrices.reshape(C_Z, 2, 2, C_TRI)
    return jnp.transpose(turned, (2, 3, 1, 0)).reshape(2 * C_TRI, 2 * C_Z)


def body(
    homolog_tensor,
    couplings,
    attention_probe_matrix,
    attention_extra_matrices,
    attention_final_matrix,
    tensor_entry_matrices,
    tensor_final_matrix,
    incoming_entry_matrices,
    incoming_switch_matrix,
    incoming_final_matrix,
):
    inner = ATTENTION_UNITS * UNIT_WIDTH
    row_count = lax.axis_size("row")
    seqs, residues, depth = homolog_tensor.shape
    own_residues = residues // row_count
    high = standardise_high(homolog_tensor)
    high = high.reshape(row_count, own_residues, seqs, depth)
    high = lax.all_to_all(high, "row", split_axis=0, concat_axis=0)
    low = standardise_low(homolog_tensor)
    low = low.reshape(row_count, own_residues, seqs + 16, depth)
    others = jnp.concatenate(
        [attention_probe_matrix.T, attention_extra_matrices[:, inner:].T], axis=0
    )
    entries = paired_entries(incoming_entry_matrices)
    sources = lax.axis_index("row") ^ jnp.arange(row_count, dtype=jnp.int32)
    firsts = sources * own_residues
    slots = left_groups(row_count, own_residues)
    high, low, others, entries, sources, firsts, slots = lax.optimization_barrier(
        (high, low, others, entries, sources, firsts, slots)
    )
    low = lax.all_to_all(low, "row", split_axis=0, concat_axis=0)
    turned, *gated = attention(sources, high, attention_extra_matrices[:, :inner], others)
    left_piece, right_piece = alignment(
        high, low, turned, attention_final_matrix.T, tensor_entry_matrices.T
    )

    rights = exchange_rows([right_piece] * row_count)
    own = gather_turned(left_piece)
    own, rights = lax.optimization_barrier((own, rights))
    mid, gate, sides = pair_update(
        slots,
        firsts,
        both_cores(own),
        rights,
        tensor_final_matrix,
        couplings,
        entries,
        incoming_switch_matrix,
    )
    gated, sides = lax.optimization_barrier((gated, sides))
    gated = exchange_rows(gated)

    everywhere = ("row", "col")
    column_count = lax.axis_size("col")
    devices = row_count * column_count
    sides = sides.reshape(devices, C_TRI // devices, *sides.shape[1:])
    sides = lax.all_to_all(sides, everywhere, split_axis=0, concat_axis=0)
    gated, sides = lax.optimization_barrier((gated, sides))
    product = triangle_product(sides, row_count, column_count)
    product = lax.all_to_all(product, everywhere, split_axis=0, concat_axis=0)

    gated = jnp.take(jnp.stack(gated), sources, axis=0)
    gated = jnp.transpose(gated.reshape(residues, seqs, inner), (1, 0, 2))
    change = jnp.dot(
        gated.reshape(-1, inner), attention_final_matrix, preferred_element_type=F32
    )
    refreshed_homologs = homolog_tensor + change.reshape(homolog_tensor.shape)
    product = product.reshape(C_TRI, *product.shape[2:])
    pair_output = pair_result(product, mid, gate, incoming_final_matrix)
    return (refreshed_homologs, pair_output)


def solution(mesh):
    in_specs = (
        P("row", "col", None),
        P("row", "col", None),
        P(),
        P(),
        P(),
        P(),
        P(),
        P(),
        P(),
        P(),
    )
    out_specs = (P("row", "col", None), P("row", "col", None))
    return jax.shard_map(body, mesh=mesh, in_specs=in_specs, out_specs=out_specs, check_vma=False)
```

```python
import functools

import jax
import jax.numpy as jnp
from jax import lax
from jax.experimental import pallas as pl
from jax.experimental.pallas import tpu as pltpu
from jax.sharding import PartitionSpec as P

FEATURE_DEPTH = 256
C_Z = 128
TENSOR_FEATURES = 32
C_TRI = 128
ATTENTION_UNITS = 8
UNIT_WIDTH = 32
EPS = 1e-05
GROUP = 4
F32 = jnp.float32
BF16 = jnp.bfloat16
NT = (((1,), (1,)), ((), ()))


def matmul(left, right):
    return jnp.dot(left, right, preferred_element_type=F32)


def matmul_nt(left, right):
    return lax.dot_general(left, right, NT, preferred_element_type=F32)


def sigmoid(values):
    return 0.5 * jnp.tanh(0.5 * values) + 0.5


def cost(microseconds):
    return pl.CostEstimate(
        flops=int(microseconds * 1e9), bytes_accessed=int(microseconds * 1e6), transcendentals=0
    )


def params(megabytes, *semantics):
    return pltpu.CompilerParams(
        dimension_semantics=semantics or None, vmem_limit_bytes=megabytes * 1024 * 1024
    )


def fold(values, combine):
    while values.shape[0] > 8:
        half = values.shape[0] // 2
        values = combine(values[:half], values[half:])
    return values


def top_rows(values):
    return jnp.max(fold(values, jnp.maximum), axis=0, keepdims=True)


def sum_rows(values):
    return jnp.sum(fold(values, jnp.add), axis=0, keepdims=True)


def normalise_rows(values):
    count = values.shape[0]
    centred = values - sum_rows(values) * (1.0 / count)
    variance = sum_rows(centred * centred) * (1.0 / count)
    return (centred * lax.rsqrt(variance + EPS)).astype(BF16)


def standardised_column(first_rows, second_rows, n, residues):
    seqs = first_rows.shape[0] // residues
    rows = pl.ds(n, seqs, stride=residues)
    column = jnp.concatenate([first_rows[rows, :], second_rows[rows, :]], axis=1)
    centred = column - jnp.mean(column, axis=1, keepdims=True)
    variance = jnp.mean(centred * centred, axis=1, keepdims=True) + EPS
    scale = lax.rsqrt(variance)
    return centred * scale, variance * scale


def high_kernel(block_hbm, high_hbm, first_ref, second_ref, high_ref, fetched, sent):
    seqs, residues, lanes = first_ref.shape
    step = 16
    fetches, sends = [], []
    for s in range(0, seqs, step):
        chosen = pl.ds(s, step)
        for half, ref in enumerate((first_ref, second_ref)):
            source = block_hbm.at[chosen, :, pl.ds(half * lanes, lanes)]
            fetches.append(
                pltpu.make_async_copy(source, ref.at[chosen], fetched.at[len(fetches)])
            )
            fetches[-1].start()
    for part in range(seqs // step):
        chosen = pl.ds(part * step, step)
        fetches[2 * part].wait()
        fetches[2 * part + 1].wait()
        first_rows = first_ref.at[chosen].reshape(step * residues, lanes)
        second_rows = second_ref.at[chosen].reshape(step * residues, lanes)
        for n in range(residues):
            normed, _ = standardised_column(first_rows, second_rows, n, residues)
            high_ref[n, chosen, :] = normed.astype(BF16)
        sends.append(
            pltpu.make_async_copy(
                high_ref.at[:, chosen], high_hbm.at[:, chosen], sent.at[part]
            )
        )
        sends[-1].start()
    for send in sends:
        send.wait()


def standardise_high(block):
    seqs, residues, depth = block.shape
    half = depth // 2
    anywhere = pl.BlockSpec(memory_space=pltpu.HBM)
    return pl.pallas_call(
        high_kernel,
        in_specs=[anywhere],
        out_specs=anywhere,
        out_shape=pltpu.HBM((residues, seqs, depth), BF16),
        scratch_shapes=[
            pltpu.VMEM((seqs, residues, half), F32),
            pltpu.VMEM((seqs, residues, half), F32),
            pltpu.VMEM((residues, seqs, depth), BF16),
            pltpu.SemaphoreType.DMA((seqs // 8,)),
            pltpu.SemaphoreType.DMA((seqs // 16,)),
        ],
        compiler_params=params(10),
        cost_estimate=cost(3),
        name="standardise_high",
    )(pltpu.with_memory_space_constraint(block, pltpu.HBM))


def low_kernel(first_ref, second_ref, low_ref):
    seqs, residues, lanes = first_ref.shape
    first_rows = first_ref.reshape(seqs * residues, lanes)
    second_rows = second_ref.reshape(seqs * residues, lanes)
    lane = lax.broadcasted_iota(jnp.int32, (seqs, 128), 1)
    spreads = jnp.zeros((seqs, 128), F32)
    for n in range(residues):
        normed, spread = standardised_column(first_rows, second_rows, n, residues)
        low_ref[n, :seqs, :] = (normed - normed.astype(BF16).astype(F32)).astype(BF16)
        spreads = jnp.where(lane == n, spread, spreads)
    spreads = spreads.T
    row = lax.broadcasted_iota(jnp.int32, (16, seqs), 0)
    for n in range(residues):
        spread = jnp.broadcast_to(spreads[n : n + 1, :], (16, seqs))
        coarse = spread.astype(BF16).astype(F32)
        kept = jnp.where(row == 0, coarse, jnp.where(row == 1, spread - coarse, 0.0))
        kept = jnp.concatenate([kept, jnp.zeros((16, 2 * lanes - seqs), F32)], axis=1)
        low_ref[n, seqs:, :] = kept.astype(BF16)


def standardise_low(block):
    seqs, residues, depth = block.shape
    half = depth // 2
    return pl.pallas_call(
        low_kernel,
        grid=(residues // 8,),
        in_specs=[
            pl.BlockSpec((seqs, 8, half), lambda g: (0, g, 0)),
            pl.BlockSpec((seqs, 8, half), lambda g: (0, g, 1)),
        ],
        out_specs=pl.BlockSpec((8, seqs + 16, depth), lambda g: (g, 0, 0)),
        out_shape=pltpu.HBM((residues, seqs + 16, depth), BF16),
        compiler_params=params(10, "arbitrary"),
        cost_estimate=cost(3),
        name="standardise_low",
    )(block, block)


def attention_kernel(sources_ref, normed_ref, key_ref, others_ref, turned_ref, *rest):
    *gated_refs, scores_ref, weights_ref, back_ref = rest
    blocks, residues, seqs, depth = normed_ref.shape
    total = blocks * seqs
    inner = ATTENTION_UNITS * UNIT_WIDTH
    ring = scores_ref.shape[0]
    columns = []
    for n in range(residues):
        column = normed_ref[:, n].reshape(total, depth)
        key_rows = matmul(column, key_ref[...]).astype(BF16)
        projected = matmul_nt(others_ref[...], column)
        queries = (projected[:inner] * UNIT_WIDTH ** (-0.5)).astype(BF16)
        value_rows = projected[inner : 2 * inner].astype(BF16)
        gates = sigmoid(projected[2 * inner :])
        columns.append((key_rows, queries, value_rows, gates))
    units = [(n, h) for h in range(ATTENTION_UNITS) for n in range(residues)]

    def score(unit):
        n, h = units[unit]
        key_rows, queries, _, _ = columns[n]
        low, high = h * UNIT_WIDTH, (h + 1) * UNIT_WIDTH
        pieces = [queries[low:high]]
        if low > 0:
            pieces.insert(0, jnp.zeros((low, total), BF16))
        if high < inner:
            pieces.append(jnp.zeros((inner - high, total), BF16))
        scores_ref[unit % ring] = matmul(key_rows, jnp.concatenate(pieces, axis=0))

    def weigh(unit):
        for low in range(0, total, 128):
            scores = scores_ref[unit % ring, :, low : low + 128]
            weights = jnp.exp(scores - top_rows(scores))
            scale = 1.0 / sum_rows(weights)
            weights_ref[unit % ring, :, low : low + 128] = (weights * scale).astype(BF16)

    def attend(unit):
        n, h = units[unit]
        _, _, value_rows, gates = columns[n]
        rows = slice(h * UNIT_WIDTH, (h + 1) * UNIT_WIDTH)
        attended = matmul(value_rows[rows], weights_ref[unit % ring]) * gates[rows]
        turned_ref[n, rows, :] = attended.astype(BF16)

    for step in range(len(units) + 2):
        if step < len(units):
            score(step)
        if 1 <= step <= len(units):
            weigh(step - 1)
        if step >= 2:
            attend(step - 2)
    for n in range(residues):
        back_ref[n] = turned_ref[n].T
        for shift, gated_ref in enumerate(gated_refs):
            first = pl.multiple_of(sources_ref[shift] * seqs, seqs)
            gated_ref[n] = back_ref[n, pl.ds(first, seqs), :]


def attention(sources, normed, key_matrix, other_matrices):
    blocks, residues, seqs, depth = normed.shape
    total = blocks * seqs
    inner = ATTENTION_UNITS * UNIT_WIDTH
    step = 2
    gated = jax.ShapeDtypeStruct((residues, seqs, inner), BF16)
    gated_spec = pl.BlockSpec((step, seqs, inner), lambda n: (n, 0, 0))
    return pl.pallas_call(
        attention_kernel,
        grid=(residues // step,),
        in_specs=[
            pl.BlockSpec(memory_space=pltpu.SMEM),
            pl.BlockSpec((blocks, step, seqs, depth), lambda n: (0, n, 0, 0)),
            pl.BlockSpec((depth, inner), lambda n: (0, 0)),
            pl.BlockSpec((3 * inner, depth), lambda n: (0, 0)),
        ],
        out_specs=[pl.BlockSpec((step, inner, total), lambda n: (n, 0, 0))]
        + [gated_spec] * blocks,
        out_shape=[jax.ShapeDtypeStruct((residues, inner, total), BF16)] + [gated] * blocks,
        scratch_shapes=[
            pltpu.VMEM((4, total, total), F32),
            pltpu.VMEM((4, total, total), BF16),
            pltpu.VMEM((step, total, inner), BF16),
        ],
        compiler_params=params(8 + (total // 128) ** 2, "arbitrary"),
        cost_estimate=cost(10),
        name="attention",
    )(sources, normed, key_matrix, other_matrices)


def alignment_kernel(
    high_ref, low_ref, turned_ref, final_ref, entry_ref, left_ref, right_ref, rows_ref
):
    blocks, residues, seqs, depth = high_ref.shape
    total = blocks * seqs
    features = TENSOR_FEATURES
    step = pl.program_id(0)
    for n in range(residues):
        low = low_ref[:, n, :seqs, :].reshape(total, depth)
        column = high_ref[:, n].reshape(total, depth).astype(F32) + low.astype(F32)
        spreads = []
        for block in range(blocks):
            kept = low_ref[block, n, seqs:, :seqs].astype(F32)
            spreads.append(jnp.sum(kept, axis=0, keepdims=True))
        spread = jnp.concatenate(spreads, axis=1)
        updated = column.T * spread + matmul(final_ref[...], turned_ref[n])
        projected = matmul(entry_ref[...], normalise_rows(updated))
        right_ref[n] = projected[features:].astype(BF16)
        first = pl.multiple_of((step * residues + n) * features, features)
        for tile in range(total // 128):
            rows_ref[tile, pl.ds(first, features), :] = projected[
                :features, tile * 128 : (tile + 1) * 128
            ]

    @pl.when(step == pl.num_programs(0) - 1)
    def _():
        count = rows_ref.shape[1] // features
        together = max(1, 16 // count)
        for c in range(0, features, together):
            pieces = []
            for e in range(together):
                chosen = pl.ds(c + e, count, stride=features)
                tiles = [rows_ref[tile, chosen, :] for tile in range(total // 128)]
                pieces.append(jnp.concatenate(tiles, axis=1))
            piece = jnp.concatenate(pieces, axis=0).astype(BF16)
            left_ref[c * count : (c + together) * count, :] = piece


def alignment(high, low, turned, final_matrix, entry_matrices):
    blocks, residues, seqs, depth = high.shape
    total = blocks * seqs
    features = TENSOR_FEATURES
    return pl.pallas_call(
        alignment_kernel,
        grid=(residues // 2,),
        in_specs=[
            pl.BlockSpec((blocks, 2, seqs, depth), lambda n: (0, n, 0, 0)),
            pl.BlockSpec((blocks, 2, seqs + 16, depth), lambda n: (0, n, 0, 0)),
            pl.BlockSpec((2, depth, total), lambda n: (n, 0, 0)),
            pl.BlockSpec(final_matrix.shape, lambda n: (0, 0)),
            pl.BlockSpec(entry_matrices.shape, lambda n: (0, 0)),
        ],
        out_specs=[
            pl.BlockSpec((features * residues, total), lambda n: (0, 0)),
            pl.BlockSpec((2, features, total), lambda n: (n, 0, 0)),
        ],
        out_shape=[
            jax.ShapeDtypeStruct((features * residues, total), BF16),
            jax.ShapeDtypeStruct((residues, features, total), BF16),
        ],
        scratch_shapes=[pltpu.VMEM((total // 128, residues * features, 128), F32)],
        compiler_params=params(16, "arbitrary"),
        cost_estimate=cost(4),
        name="alignment",
    )(high, low, turned, final_matrix, entry_matrices)


def pair_kernel(
    left_slots_ref,
    right_firsts_ref,
    own_ref,
    other_ref,
    *rest,
):
    weights_ref, entry_ref, switch_ref, couplings_hbm, mid_hbm, gate_hbm, sides_hbm = rest[-16:-9]
    outer_ref, spread_ref, sum_ref, rows_ref, couplings_ref = rest[-9:-4]
    mid_ref, gate_ref, sides_ref, copied = rest[-4:]
    right_refs = rest[:-16]
    fetched = pltpu.make_async_copy(couplings_hbm, couplings_ref, copied.at[0])
    fetched.start()
    copies = []

    def send(source, target):
        copies.append(pltpu.make_async_copy(source, target, copied.at[len(copies) + 1]))
        copies[-1].start()

    features = TENSOR_FEATURES
    slots, piece_rows, total = own_ref.shape
    residues = piece_rows // features
    rows = 2 * slots * residues
    share = right_refs[0].shape[0]
    columns = len(right_refs) * share
    groups = columns // GROUP
    wide = share * features
    together = spread_ref.shape[1] // 128

    for half, left_ref in enumerate((own_ref, other_ref)):
        piece = left_ref[...].reshape(slots * piece_rows, total)
        target = slice(half * slots * piece_rows, (half + 1) * slots * piece_rows)
        for p, right_ref in enumerate(right_refs):
            right = right_ref[...].reshape(wide, total)
            outer_ref[target, p * wide : (p + 1) * wide] = matmul_nt(piece, right) * (1.0 / total)

    spread_ref[...] = jnp.zeros_like(spread_ref)

    def channel_step(p, carry):
        slot = lax.rem(p, 2)
        for e in range(together):
            source = pl.multiple_of((p * together + e) * features, features)
            piece = weights_ref[pl.ds(source, features), :]
            for place in range(GROUP):
                low = e * 128 + place * features
                spread_ref[slot, low : low + features, place * C_Z : (place + 1) * C_Z] = piece
        pieces = []
        for g in range(groups):
            parts = []
            for e in range(together):
                channel = []
                for slot_number in range(2 * slots):
                    first = slot_number * piece_rows + (p * together + e) * residues
                    source = pl.ds(pl.multiple_of(first, residues), residues)
                    channel.append(outer_ref[source, g * 128 : (g + 1) * 128])
                parts.append(jnp.concatenate(channel, axis=0).astype(BF16))
            pieces.append(jnp.concatenate(parts, axis=1))
        update = matmul(jnp.concatenate(pieces, axis=0), spread_ref[slot])

        @pl.when(p == 0)
        def _():
            sum_ref[...] = update

        @pl.when(p > 0)
        def _():
            sum_ref[...] += update

        return carry

    lax.fori_loop(0, features // together, channel_step, 0)

    left_firsts = [left_slots_ref[j] * residues for j in range(2 * slots)]
    right_firsts = [right_firsts_ref[p] for p in range(len(right_refs))]
    fetched.wait()
    for g in range(groups):
        normed, places = [], []
        for place in range(GROUP):
            p, n = divmod(g * GROUP + place, share)
            b = right_firsts[p] + n
            places.append(b)
            lanes = slice(place * C_Z, (place + 1) * C_Z)
            pieces = []
            for first in left_firsts:
                source = pl.ds(pl.multiple_of(g * rows + first, residues), residues)
                pieces.append(sum_ref[source, lanes])
            mid = jnp.concatenate(pieces, axis=0)
            mid = mid + couplings_ref[pl.ds(b, rows, stride=columns), :]
            mid_ref[g * GROUP + place] = mid
            centred = mid - jnp.mean(mid, axis=1, keepdims=True)
            variance = jnp.mean(centred * centred, axis=1, keepdims=True)
            normed.append((centred * lax.rsqrt(variance + EPS)).astype(BF16))
        gates = sigmoid(matmul(jnp.concatenate(normed, axis=0), switch_ref[...]))
        blank = jnp.zeros_like(normed[0])
        for place in range(0, GROUP, 2):
            twice = []
            for e in range(2):
                part = gates[(place + e) * rows : (place + e + 1) * rows]
                gate_ref[g * GROUP + place + e] = part
                twice.append(jnp.concatenate([normed[place + e], blank], axis=1))
                twice.append(jnp.concatenate([blank, normed[place + e]], axis=1))
            sides = matmul_nt(entry_ref[...], jnp.concatenate(twice, axis=0))
            sides = sigmoid(sides[C_TRI:]) * sides[:C_TRI]
            for e in range(2):
                first = pl.multiple_of(places[place + e] * C_TRI, C_TRI)
                rows_ref[pl.ds(first, C_TRI), :] = sides[:, e * 2 * rows : (e + 1) * 2 * rows]

        if (g + 1) * GROUP % share == 0:
            p = (g + 1) * GROUP // share - 1
            source, target = pl.ds(p * share, share), pl.ds(right_firsts[p], share)
            send(mid_ref.at[source], mid_hbm.at[target])
            send(gate_ref.at[source], gate_hbm.at[target])

    cut = C_TRI // 4
    for part in range(4):

        def turn_step(c, carry):
            sides_ref[c] = rows_ref[pl.ds(c, columns, stride=C_TRI), :].astype(BF16)
            return carry

        lax.fori_loop(part * cut, (part + 1) * cut, turn_step, 0, unroll=8)
        chosen = pl.ds(part * cut, cut)
        send(sides_ref.at[chosen], sides_hbm.at[chosen])
    for copy in copies:
        copy.wait()


def pair_update(left_slots, right_firsts, left, rights, weights, couplings, entry, switch):
    rows, columns, depth = couplings.shape
    whole = jax.ShapeDtypeStruct((columns, rows, depth), F32)
    sides = jax.ShapeDtypeStruct((C_TRI, columns, 2 * rows), BF16)
    smem = pl.BlockSpec(memory_space=pltpu.SMEM)
    vmem = pl.BlockSpec(memory_space=pltpu.VMEM)
    anywhere = pl.BlockSpec(memory_space=pl.ANY)
    return pl.pallas_call(
        pair_kernel,
        in_specs=[smem] * 2 + [vmem] * (5 + len(rights)) + [anywhere],
        out_specs=[anywhere] * 3,
        out_shape=[whole, whole, pltpu.HBM(sides.shape, BF16)],
        scratch_shapes=[
            pltpu.VMEM((rows * TENSOR_FEATURES, columns * TENSOR_FEATURES), F32),
            pltpu.VMEM((2, 8 * 128, GROUP * depth), BF16),
            pltpu.VMEM((columns // GROUP * rows, GROUP * depth), F32),
            pltpu.VMEM((columns * C_TRI, 2 * rows), F32),
            pltpu.VMEM((rows * columns, depth), F32),
            pltpu.VMEM(whole.shape, F32),
            pltpu.VMEM(whole.shape, F32),
            pltpu.VMEM(sides.shape, BF16),
            pltpu.SemaphoreType.DMA((2 * len(rights) + 5,)),
        ],
        compiler_params=params(28),
        cost_estimate=cost(12),
        name="pair_update",
    )(
        left_slots,
        right_firsts,
        *left,
        *rights,
        weights,
        entry,
        switch,
        couplings.reshape(rows * columns, depth),
    )


def product_kernel(sides_ref, out_ref, *, grid_rows, grid_columns):
    channels, part, lanes = sides_ref.shape[1:]
    half = lanes // 2
    lane = lax.broadcasted_iota(jnp.int32, (grid_columns * part, lanes), 1)
    front = lane < half
    cut = front[: part // 2]
    for channel in range(channels):
        lefts, rights = [], []
        for r in range(0, grid_rows, 2):
            even, odd = [
                jnp.concatenate(
                    [sides_ref[(r + e) * grid_columns + c, channel] for c in range(grid_columns)],
                    axis=0,
                )
                for e in range(2)
            ]
            lefts.append(jnp.where(front, even, pltpu.roll(odd, half, 1)))
            rights.append(jnp.where(front, pltpu.roll(even, half, 1), odd))
        product = matmul_nt(jnp.concatenate(rights, axis=1), jnp.concatenate(lefts, axis=1))
        product = product.astype(BF16)
        for c in range(grid_columns):
            for r in range(0, grid_rows, 2):
                block = product[c * part : (c + 1) * part, r * half : (r + 2) * half]
                top, bottom = block[: part // 2], block[part // 2 :]
                even = jnp.where(cut, top, pltpu.roll(bottom, half, 1))
                out_ref[r * grid_columns + c, channel] = even
                odd = jnp.where(cut, pltpu.roll(top, half, 1), bottom)
                out_ref[(r + 1) * grid_columns + c, channel] = odd


def triangle_product(sides, grid_rows, grid_columns):
    devices, channels, part, lanes = sides.shape
    step = 2 if channels % 2 == 0 else 1
    return pl.pallas_call(
        functools.partial(product_kernel, grid_rows=grid_rows, grid_columns=grid_columns),
        grid=(channels // step,),
        in_specs=[pl.BlockSpec((devices, step, part, lanes), lambda c: (0, c, 0, 0))],
        out_specs=pl.BlockSpec((devices, step, part // 2, lanes), lambda c: (0, c, 0, 0)),
        out_shape=pltpu.HBM((devices, channels, part // 2, lanes), BF16),
        compiler_params=params(8, "arbitrary"),
        cost_estimate=cost(3),
        name="triangle_product",
    )(sides)


def output_kernel(product_ref, mid_ref, gate_ref, final_ref, out_ref, wide_ref):
    channels, part, lanes = product_ref.shape
    _, own, rows, depth = mid_ref.shape
    out_rows = out_ref.reshape(rows * 2 * own, depth)
    step = pl.program_id(0)

    @pl.when(step == 0)
    def _():
        wide_ref[...] = product_ref[...].astype(F32).reshape(channels * part, lanes)

    for j in range(own):
        product = wide_ref[pl.ds(step * own + j, channels, stride=part), :]
        update = matmul(normalise_rows(product).T, final_ref[...])
        for half in range(2):
            piece = update[half * rows : (half + 1) * rows]
            piece = mid_ref[half, j] + gate_ref[half, j] * piece
            out_rows[pl.ds(half * own + j, rows, stride=2 * own), :] = piece


def pair_result(product, mid, gate, final_matrix):
    channels, part, lanes = product.shape
    columns, rows, depth = mid.shape
    own = 8
    whole = pl.BlockSpec((2, own, rows, depth), lambda j: (0, j, 0, 0))
    out = pl.pallas_call(
        output_kernel,
        grid=(part // own,),
        in_specs=[
            pl.BlockSpec(product.shape, lambda j: (0, 0, 0)),
            whole,
            whole,
            pl.BlockSpec(final_matrix.shape, lambda j: (0, 0)),
        ],
        out_specs=pl.BlockSpec((rows, 2, own, depth), lambda j: (0, 0, j, 0)),
        out_shape=jax.ShapeDtypeStruct((rows, 2, part, depth), F32),
        scratch_shapes=[pltpu.VMEM((channels * part, lanes), F32)],
        compiler_params=params(12, "arbitrary"),
        cost_estimate=cost(4),
        name="pair_result",
    )(
        product,
        mid.reshape(2, part, rows, depth),
        gate.reshape(2, part, rows, depth),
        final_matrix,
    )
    return out.reshape(rows, columns, depth)


def swap_cores(block):
    count = lax.axis_size("col")
    return lax.ppermute(block, "col", [(c, c ^ 1) for c in range(count)])


def gather_turned(block):
    rows, columns = lax.axis_size("row"), lax.axis_size("col")
    arrived = []
    for shift in range(rows):
        moves = []
        for r in range(rows):
            for q in range(rows):
                for side in range(2):
                    source = r * columns + 2 * q + side
                    moves.append((source, q * columns + 2 * ((r + shift) % rows) + side))
        arrived.append(lax.ppermute(block, ("row", "col"), moves))
    return jnp.stack(arrived)


def both_cores(own):
    rows = lax.axis_size("row")
    core = lax.rem(lax.axis_index("col"), 2)
    other = swap_cores(own)
    residues = own.shape[1] // TENSOR_FEATURES
    if residues % 8 == 0:
        return own, other
    order = left_order(rows)
    own, other = jnp.take(own, order, axis=0), jnp.take(other, order, axis=0)
    joined = 8 // residues
    ordered = []
    for side in (jnp.where(core == 0, own, other), jnp.where(core == 0, other, own)):
        side = side.reshape(rows // joined, joined, TENSOR_FEATURES, residues, -1)
        side = jnp.transpose(side, (0, 2, 1, 3, 4))
        ordered.append(side.reshape(rows // joined, joined * own.shape[1], -1))
    return tuple(ordered)


def left_order(rows):
    me = lax.axis_index("col") // 2
    return lax.rem(me - jnp.arange(rows, dtype=jnp.int32) + rows, rows)


def left_groups(rows, residues):
    if residues % 8:
        return jnp.arange(2 * rows * residues // 8, dtype=jnp.int32)
    core = lax.rem(lax.axis_index("col"), 2)
    order = left_order(rows)
    return jnp.concatenate([order + core * rows, order + (1 - core) * rows])


def exchange_rows(pieces):
    arrived = [pieces[0]]
    for shift in range(1, len(pieces)):
        moves = [(r, r ^ shift) for r in range(len(pieces))]
        arrived.append(lax.ppermute(pieces[shift], "row", moves))
    return arrived


def paired_entries(matrices):
    turned = matrices.reshape(C_Z, 2, 2, C_TRI)
    return jnp.transpose(turned, (2, 3, 1, 0)).reshape(2 * C_TRI, 2 * C_Z)


def body(
    homolog_tensor,
    couplings,
    attention_probe_matrix,
    attention_extra_matrices,
    attention_final_matrix,
    tensor_entry_matrices,
    tensor_final_matrix,
    incoming_entry_matrices,
    incoming_switch_matrix,
    incoming_final_matrix,
):
    inner = ATTENTION_UNITS * UNIT_WIDTH
    row_count = lax.axis_size("row")
    seqs, residues, depth = homolog_tensor.shape
    own_residues = residues // row_count
    high = standardise_high(homolog_tensor)
    high = high.reshape(row_count, own_residues, seqs, depth)
    high = lax.all_to_all(high, "row", split_axis=0, concat_axis=0)
    low = standardise_low(homolog_tensor)
    low = low.reshape(row_count, own_residues, seqs + 16, depth)
    others = jnp.concatenate(
        [attention_probe_matrix.T, attention_extra_matrices[:, inner:].T], axis=0
    )
    entries = paired_entries(incoming_entry_matrices)
    sources = lax.axis_index("row") ^ jnp.arange(row_count, dtype=jnp.int32)
    firsts = sources * own_residues
    slots = left_groups(row_count, own_residues)
    high, low, others, entries, sources, firsts, slots = lax.optimization_barrier(
        (high, low, others, entries, sources, firsts, slots)
    )
    low = lax.all_to_all(low, "row", split_axis=0, concat_axis=0)
    turned, *gated = attention(sources, high, attention_extra_matrices[:, :inner], others)
    left_piece, right_piece = alignment(
        high, low, turned, attention_final_matrix.T, tensor_entry_matrices.T
    )

    rights = exchange_rows([right_piece] * row_count)
    own = gather_turned(left_piece)
    own, rights = lax.optimization_barrier((own, rights))
    mid, gate, sides = pair_update(
        slots,
        firsts,
        both_cores(own),
        rights,
        tensor_final_matrix,
        couplings,
        entries,
        incoming_switch_matrix,
    )
    gated, sides = lax.optimization_barrier((gated, sides))
    gated = exchange_rows(gated)

    everywhere = ("row", "col")
    column_count = lax.axis_size("col")
    devices = row_count * column_count
    sides = sides.reshape(devices, C_TRI // devices, *sides.shape[1:])
    sides = lax.all_to_all(sides, everywhere, split_axis=0, concat_axis=0)
    gated, sides = lax.optimization_barrier((gated, sides))
    product = triangle_product(sides, row_count, column_count)
    product = lax.all_to_all(product, everywhere, split_axis=0, concat_axis=0)

    gated = jnp.take(jnp.stack(gated), sources, axis=0)
    gated = jnp.transpose(gated.reshape(residues, seqs, inner), (1, 0, 2))
    change = jnp.dot(
        gated.reshape(-1, inner), attention_final_matrix, preferred_element_type=F32
    )
    refreshed_homologs = homolog_tensor + change.reshape(homolog_tensor.shape)
    product = product.reshape(C_TRI, *product.shape[2:])
    pair_output = pair_result(product, mid, gate, incoming_final_matrix)
    return (refreshed_homologs, pair_output)


def solution(mesh):
    in_specs = (
        P("row", "col", None),
        P("row", "col", None),
        P(),
        P(),
        P(),
        P(),
        P(),
        P(),
        P(),
        P(),
    )
    out_specs = (P("row", "col", None), P("row", "col", None))
    return jax.shard_map(body, mesh=mesh, in_specs=in_specs, out_specs=out_specs, check_vma=False)
```

```python
import functools

import jax
import jax.numpy as jnp
from jax import lax
from jax.experimental import pallas as pl
from jax.experimental.pallas import tpu as pltpu
from jax.sharding import PartitionSpec as P

FEATURE_DEPTH = 256
C_Z = 128
TENSOR_FEATURES = 32
C_TRI = 128
ATTENTION_UNITS = 8
UNIT_WIDTH = 32
EPS = 1e-05
GROUP = 4
F32 = jnp.float32
BF16 = jnp.bfloat16
NT = (((1,), (1,)), ((), ()))


def matmul(left, right):
    return jnp.dot(left, right, preferred_element_type=F32)


def matmul_nt(left, right):
    return lax.dot_general(left, right, NT, preferred_element_type=F32)


def sigmoid(values):
    return 0.5 * jnp.tanh(0.5 * values) + 0.5


def cost(microseconds):
    return pl.CostEstimate(
        flops=int(microseconds * 1e9), bytes_accessed=int(microseconds * 1e6), transcendentals=0
    )


def params(megabytes, *semantics):
    return pltpu.CompilerParams(
        dimension_semantics=semantics or None, vmem_limit_bytes=megabytes * 1024 * 1024
    )


def fold(values, combine):
    while values.shape[0] > 8:
        half = values.shape[0] // 2
        values = combine(values[:half], values[half:])
    return values


def top_rows(values):
    return jnp.max(fold(values, jnp.maximum), axis=0, keepdims=True)


def sum_rows(values):
    return jnp.sum(fold(values, jnp.add), axis=0, keepdims=True)


def normalise_rows(values):
    count = values.shape[0]
    centred = values - sum_rows(values) * (1.0 / count)
    variance = sum_rows(centred * centred) * (1.0 / count)
    return (centred * lax.rsqrt(variance + EPS)).astype(BF16)


def standardised_column(first_rows, second_rows, n, residues):
    seqs = first_rows.shape[0] // residues
    rows = pl.ds(n, seqs, stride=residues)
    column = jnp.concatenate([first_rows[rows, :], second_rows[rows, :]], axis=1)
    centred = column - jnp.mean(column, axis=1, keepdims=True)
    variance = jnp.mean(centred * centred, axis=1, keepdims=True) + EPS
    scale = lax.rsqrt(variance)
    return centred * scale, variance * scale


def high_kernel(sources_ref, block_hbm, *rest):
    *pieces_hbm, first_ref, second_ref, high_ref, fetched, sent = rest
    seqs, residues, lanes = first_ref.shape
    own = residues // len(pieces_hbm)
    step = 16
    fetches, sends = [], []
    for s in range(0, seqs, step):
        chosen = pl.ds(s, step)
        for half, ref in enumerate((first_ref, second_ref)):
            source = block_hbm.at[chosen, :, pl.ds(half * lanes, lanes)]
            fetches.append(
                pltpu.make_async_copy(source, ref.at[chosen], fetched.at[len(fetches)])
            )
            fetches[-1].start()
    for part in range(seqs // step):
        chosen = pl.ds(part * step, step)
        fetches[2 * part].wait()
        fetches[2 * part + 1].wait()
        first_rows = first_ref.at[chosen].reshape(step * residues, lanes)
        second_rows = second_ref.at[chosen].reshape(step * residues, lanes)
        for n in range(residues):
            normed, _ = standardised_column(first_rows, second_rows, n, residues)
            high_ref[part, n] = normed.astype(BF16)
        for p, piece_hbm in enumerate(pieces_hbm):
            source = high_ref.at[part, pl.ds(sources_ref[p] * own, own)]
            sends.append(
                pltpu.make_async_copy(source, piece_hbm.at[:, chosen], sent.at[len(sends)])
            )
            sends[-1].start()
    for send in sends:
        send.wait()


def standardise_high(sources, block):
    seqs, residues, depth = block.shape
    half = depth // 2
    count = sources.shape[0]
    hbm = pl.BlockSpec(memory_space=pltpu.HBM)
    return pl.pallas_call(
        high_kernel,
        in_specs=[pl.BlockSpec(memory_space=pltpu.SMEM), hbm],
        out_specs=[hbm] * count,
        out_shape=[pltpu.HBM((residues // count, seqs, depth), BF16)] * count,
        scratch_shapes=[
            pltpu.VMEM((seqs, residues, half), F32),
            pltpu.VMEM((seqs, residues, half), F32),
            pltpu.VMEM((seqs // 16, residues, 16, depth), BF16),
            pltpu.SemaphoreType.DMA((seqs // 8,)),
            pltpu.SemaphoreType.DMA((seqs // 16 * count,)),
        ],
        compiler_params=params(10),
        cost_estimate=cost(3),
        name="standardise_high",
    )(sources, pltpu.with_memory_space_constraint(block, pltpu.HBM))


def low_kernel(sources_ref, first_ref, second_ref, *rest):
    *pieces_hbm, low_ref, sent = rest
    seqs, residues, lanes = first_ref.shape
    own = residues // len(pieces_hbm)
    first_rows = first_ref.reshape(seqs * residues, lanes)
    second_rows = second_ref.reshape(seqs * residues, lanes)
    lane = lax.broadcasted_iota(jnp.int32, (seqs, 128), 1)
    spreads = jnp.zeros((seqs, 128), F32)
    for n in range(residues):
        normed, spread = standardised_column(first_rows, second_rows, n, residues)
        low_ref[n, :seqs, :] = (normed - normed.astype(BF16).astype(F32)).astype(BF16)
        spreads = jnp.where(lane == n, spread, spreads)
    spreads = spreads.T
    row = lax.broadcasted_iota(jnp.int32, (16, seqs), 0)
    for n in range(residues):
        spread = jnp.broadcast_to(spreads[n : n + 1, :], (16, seqs))
        coarse = spread.astype(BF16).astype(F32)
        kept = jnp.where(row == 0, coarse, jnp.where(row == 1, spread - coarse, 0.0))
        kept = jnp.concatenate([kept, jnp.zeros((16, 2 * lanes - seqs), F32)], axis=1)
        low_ref[n, seqs:, :] = kept.astype(BF16)
    sends = []
    for p, piece_hbm in enumerate(pieces_hbm):
        source = low_ref.at[pl.ds(sources_ref[p] * own, own)]
        sends.append(pltpu.make_async_copy(source, piece_hbm, sent.at[p]))
        sends[-1].start()
    for send in sends:
        send.wait()


def standardise_low(sources, block):
    seqs, residues, depth = block.shape
    half = depth // 2
    count = sources.shape[0]
    hbm = pl.BlockSpec(memory_space=pltpu.HBM)
    return pl.pallas_call(
        low_kernel,
        grid=(1,),
        in_specs=[
            pl.BlockSpec(memory_space=pltpu.SMEM),
            pl.BlockSpec((seqs, residues, half), lambda g: (0, 0, 0)),
            pl.BlockSpec((seqs, residues, half), lambda g: (0, 0, 1)),
        ],
        out_specs=[hbm] * count,
        out_shape=[pltpu.HBM((residues // count, seqs + 16, depth), BF16)] * count,
        scratch_shapes=[
            pltpu.VMEM((residues, seqs + 16, depth), BF16),
            pltpu.SemaphoreType.DMA((count,)),
        ],
        compiler_params=params(14, "arbitrary"),
        cost_estimate=cost(4),
        name="standardise_low",
    )(sources, block, block)


def attention_kernel(key_ref, others_ref, *rest):
    *refs, scores_ref, weights_ref = rest
    blocks = len(refs) // 2
    normed_refs, turned_ref, gated_refs = refs[:blocks], refs[blocks], refs[blocks + 1 :]
    residues, seqs, _ = normed_refs[0].shape
    total = blocks * seqs
    inner = ATTENTION_UNITS * UNIT_WIDTH
    ring = scores_ref.shape[0]
    columns = []
    for n in range(residues):
        column = jnp.concatenate([ref[n] for ref in normed_refs], axis=0)
        key_rows = matmul(column, key_ref[...]).astype(BF16)
        projected = matmul_nt(others_ref[...], column)
        queries = (projected[:inner] * UNIT_WIDTH ** (-0.5)).astype(BF16)
        value_rows = projected[inner : 2 * inner].astype(BF16)
        gates = sigmoid(projected[2 * inner :])
        columns.append((key_rows, queries, value_rows, gates))
    units = [(n, h) for h in range(ATTENTION_UNITS) for n in range(residues)]

    def score(unit):
        n, h = units[unit]
        key_rows, queries, _, _ = columns[n]
        low, high = h * UNIT_WIDTH, (h + 1) * UNIT_WIDTH
        pieces = [queries[low:high]]
        if low > 0:
            pieces.insert(0, jnp.zeros((low, total), BF16))
        if high < inner:
            pieces.append(jnp.zeros((inner - high, total), BF16))
        scores_ref[unit % ring] = matmul(key_rows, jnp.concatenate(pieces, axis=0))

    def weigh(unit):
        for low in range(0, total, 128):
            scores = scores_ref[unit % ring, :, low : low + 128]
            weights = jnp.exp(scores - top_rows(scores))
            scale = 1.0 / sum_rows(weights)
            weights_ref[unit % ring, :, low : low + 128] = (weights * scale).astype(BF16)

    def attend(unit):
        n, h = units[unit]
        _, _, value_rows, gates = columns[n]
        rows = slice(h * UNIT_WIDTH, (h + 1) * UNIT_WIDTH)
        attended = matmul(value_rows[rows], weights_ref[unit % ring]) * gates[rows]
        turned_ref[n, rows, :] = attended.astype(BF16)

    for step in range(len(units) + 2):
        if step < len(units):
            score(step)
        if 1 <= step <= len(units):
            weigh(step - 1)
        if step >= 2:
            attend(step - 2)
    for n in range(residues):
        back = turned_ref[n].T
        for block, gated_ref in enumerate(gated_refs):
            gated_ref[n] = back[block * seqs : (block + 1) * seqs]


def attention(normed, key_matrix, other_matrices):
    blocks = len(normed)
    residues, seqs, depth = normed[0].shape
    total = blocks * seqs
    inner = ATTENTION_UNITS * UNIT_WIDTH
    step = 2
    return pl.pallas_call(
        attention_kernel,
        grid=(residues // step,),
        in_specs=[
            pl.BlockSpec((depth, inner), lambda n: (0, 0)),
            pl.BlockSpec((3 * inner, depth), lambda n: (0, 0)),
        ]
        + [pl.BlockSpec((step, seqs, depth), lambda n: (n, 0, 0))] * blocks,
        out_specs=[pl.BlockSpec((step, inner, total), lambda n: (n, 0, 0))]
        + [pl.BlockSpec((step, seqs, inner), lambda n: (n, 0, 0))] * blocks,
        out_shape=[jax.ShapeDtypeStruct((residues, inner, total), BF16)]
        + [pltpu.HBM((residues, seqs, inner), BF16)] * blocks,
        scratch_shapes=[
            pltpu.VMEM((4, total, total), F32),
            pltpu.VMEM((4, total, total), BF16),
        ],
        compiler_params=params(8 + (total // 128) ** 2, "arbitrary"),
        cost_estimate=cost(10),
        name="attention",
    )(key_matrix, other_matrices, *normed)


def alignment_kernel(sources_ref, turned_ref, final_ref, entry_ref, *rest):
    *refs, left_ref, right_ref, rows_ref = rest
    blocks = len(refs) // 2
    high_refs, low_refs = refs[:blocks], refs[blocks:]
    residues, seqs, depth = high_refs[0].shape
    total = blocks * seqs
    features = TENSOR_FEATURES
    step = pl.program_id(0)
    for n in range(residues):
        column = jnp.concatenate([ref[n] for ref in high_refs], axis=0).astype(F32)
        column = column + jnp.concatenate(
            [ref[n, :seqs, :] for ref in low_refs], axis=0
        ).astype(F32)
        spreads = []
        for ref in low_refs:
            kept = ref[n, seqs:, :seqs].astype(F32)
            spreads.append(jnp.sum(kept, axis=0, keepdims=True))
        spread = jnp.concatenate(spreads, axis=1)
        updated = column.T * spread + matmul(final_ref[...], turned_ref[n])
        projected = matmul(entry_ref[...], normalise_rows(updated))
        me = sources_ref[0]
        tiles = [projected[:, low : low + 128] for low in range(0, total, 128)]
        odd = lax.rem(me, 2) == 1
        tiles = [jnp.where(odd, pltpu.roll(tile, seqs, 1), tile) for tile in tiles]
        width = 1
        while width < len(tiles):
            crossed = lax.rem(lax.div(me, 2 * width), 2) == 1
            tiles = [
                jnp.where(crossed, tiles[t ^ width], tiles[t]) for t in range(len(tiles))
            ]
            width *= 2
        first = pl.multiple_of((step * residues + n) * features, features)
        for t, tile in enumerate(tiles):
            right_ref[n, :, t * 128 : (t + 1) * 128] = tile[features:].astype(BF16)
            rows_ref[t, pl.ds(first, features), :] = tile[:features]

    @pl.when(step == pl.num_programs(0) - 1)
    def _():
        count = rows_ref.shape[1] // features
        together = max(1, 16 // count)
        for c in range(0, features, together):
            pieces = []
            for e in range(together):
                chosen = pl.ds(c + e, count, stride=features)
                tiles = [rows_ref[tile, chosen, :] for tile in range(total // 128)]
                pieces.append(jnp.concatenate(tiles, axis=1))
            piece = jnp.concatenate(pieces, axis=0).astype(BF16)
            left_ref[c * count : (c + together) * count, :] = piece


def alignment(sources, high, low, turned, final_matrix, entry_matrices):
    blocks = len(high)
    residues, seqs, depth = high[0].shape
    total = blocks * seqs
    features = TENSOR_FEATURES
    return pl.pallas_call(
        alignment_kernel,
        grid=(residues // 2,),
        in_specs=[
            pl.BlockSpec(memory_space=pltpu.SMEM),
            pl.BlockSpec((2, depth, total), lambda n: (n, 0, 0)),
            pl.BlockSpec(final_matrix.shape, lambda n: (0, 0)),
            pl.BlockSpec(entry_matrices.shape, lambda n: (0, 0)),
        ]
        + [pl.BlockSpec((2, seqs, depth), lambda n: (n, 0, 0))] * blocks
        + [pl.BlockSpec((2, seqs + 16, depth), lambda n: (n, 0, 0))] * blocks,
        out_specs=[
            pl.BlockSpec((features * residues, total), lambda n: (0, 0)),
            pl.BlockSpec((2, features, total), lambda n: (n, 0, 0)),
        ],
        out_shape=[
            jax.ShapeDtypeStruct((features * residues, total), BF16),
            jax.ShapeDtypeStruct((residues, features, total), BF16),
        ],
        scratch_shapes=[pltpu.VMEM((total // 128, residues * features, 128), F32)],
        compiler_params=params(16, "arbitrary"),
        cost_estimate=cost(4),
        name="alignment",
    )(sources, turned, final_matrix, entry_matrices, *high, *low)


def pair_kernel(
    left_slots_ref,
    right_firsts_ref,
    own_ref,
    other_ref,
    *rest,
):
    weights_ref, entry_ref, switch_ref, couplings_hbm, mid_hbm, gate_hbm, sides_hbm = rest[-16:-9]
    outer_ref, spread_ref, sum_ref, rows_ref, couplings_ref = rest[-9:-4]
    mid_ref, gate_ref, sides_ref, copied = rest[-4:]
    right_refs = rest[:-16]
    fetched = pltpu.make_async_copy(couplings_hbm, couplings_ref, copied.at[0])
    fetched.start()
    copies = []

    def send(source, target):
        copies.append(pltpu.make_async_copy(source, target, copied.at[len(copies) + 1]))
        copies[-1].start()

    features = TENSOR_FEATURES
    slots, piece_rows, total = own_ref.shape
    residues = piece_rows // features
    rows = 2 * slots * residues
    share = right_refs[0].shape[0]
    columns = len(right_refs) * share
    groups = columns // GROUP
    wide = share * features
    together = spread_ref.shape[1] // 128

    for half, left_ref in enumerate((own_ref, other_ref)):
        piece = left_ref[...].reshape(slots * piece_rows, total)
        target = slice(half * slots * piece_rows, (half + 1) * slots * piece_rows)
        for p, right_ref in enumerate(right_refs):
            right = right_ref[...].reshape(wide, total)
            outer_ref[target, p * wide : (p + 1) * wide] = matmul_nt(piece, right) * (1.0 / total)

    spread_ref[...] = jnp.zeros_like(spread_ref)

    def channel_step(p, carry):
        slot = lax.rem(p, 2)
        for e in range(together):
            source = pl.multiple_of((p * together + e) * features, features)
            piece = weights_ref[pl.ds(source, features), :]
            for place in range(GROUP):
                low = e * 128 + place * features
                spread_ref[slot, low : low + features, place * C_Z : (place + 1) * C_Z] = piece
        pieces = []
        for g in range(groups):
            parts = []
            for e in range(together):
                channel = []
                for slot_number in range(2 * slots):
                    first = slot_number * piece_rows + (p * together + e) * residues
                    source = pl.ds(pl.multiple_of(first, residues), residues)
                    channel.append(outer_ref[source, g * 128 : (g + 1) * 128])
                parts.append(jnp.concatenate(channel, axis=0).astype(BF16))
            pieces.append(jnp.concatenate(parts, axis=1))
        update = matmul(jnp.concatenate(pieces, axis=0), spread_ref[slot])

        @pl.when(p == 0)
        def _():
            sum_ref[...] = update

        @pl.when(p > 0)
        def _():
            sum_ref[...] += update

        return carry

    lax.fori_loop(0, features // together, channel_step, 0)

    left_firsts = [left_slots_ref[j] * residues for j in range(2 * slots)]
    right_firsts = [right_firsts_ref[p] for p in range(len(right_refs))]
    fetched.wait()
    for g in range(groups):
        normed, places = [], []
        for place in range(GROUP):
            p, n = divmod(g * GROUP + place, share)
            b = right_firsts[p] + n
            places.append(b)
            lanes = slice(place * C_Z, (place + 1) * C_Z)
            pieces = []
            for first in left_firsts:
                source = pl.ds(pl.multiple_of(g * rows + first, residues), residues)
                pieces.append(sum_ref[source, lanes])
            mid = jnp.concatenate(pieces, axis=0)
            mid = mid + couplings_ref[pl.ds(b, rows, stride=columns), :]
            mid_ref[g * GROUP + place] = mid
            centred = mid - jnp.mean(mid, axis=1, keepdims=True)
            variance = jnp.mean(centred * centred, axis=1, keepdims=True)
            normed.append((centred * lax.rsqrt(variance + EPS)).astype(BF16))
        gates = sigmoid(matmul(jnp.concatenate(normed, axis=0), switch_ref[...]))
        blank = jnp.zeros_like(normed[0])
        for place in range(0, GROUP, 2):
            twice = []
            for e in range(2):
                part = gates[(place + e) * rows : (place + e + 1) * rows]
                gate_ref[g * GROUP + place + e] = part
                twice.append(jnp.concatenate([normed[place + e], blank], axis=1))
                twice.append(jnp.concatenate([blank, normed[place + e]], axis=1))
            sides = matmul_nt(entry_ref[...], jnp.concatenate(twice, axis=0))
            sides = sigmoid(sides[C_TRI:]) * sides[:C_TRI]
            for e in range(2):
                first = pl.multiple_of(places[place + e] * C_TRI, C_TRI)
                rows_ref[pl.ds(first, C_TRI), :] = sides[:, e * 2 * rows : (e + 1) * 2 * rows]

        if (g + 1) * GROUP % share == 0:
            p = (g + 1) * GROUP // share - 1
            source, target = pl.ds(p * share, share), pl.ds(right_firsts[p], share)
            send(mid_ref.at[source], mid_hbm.at[target])
            send(gate_ref.at[source], gate_hbm.at[target])

    cut = C_TRI // 4
    for part in range(4):

        def turn_step(c, carry):
            sides_ref[c] = rows_ref[pl.ds(c, columns, stride=C_TRI), :].astype(BF16)
            return carry

        lax.fori_loop(part * cut, (part + 1) * cut, turn_step, 0, unroll=8)
        chosen = pl.ds(part * cut, cut)
        send(sides_ref.at[chosen], sides_hbm.at[chosen])
    for copy in copies:
        copy.wait()


def pair_update(left_slots, right_firsts, left, rights, weights, couplings, entry, switch):
    rows, columns, depth = couplings.shape
    whole = jax.ShapeDtypeStruct((columns, rows, depth), F32)
    sides = jax.ShapeDtypeStruct((C_TRI, columns, 2 * rows), BF16)
    smem = pl.BlockSpec(memory_space=pltpu.SMEM)
    vmem = pl.BlockSpec(memory_space=pltpu.VMEM)
    anywhere = pl.BlockSpec(memory_space=pl.ANY)
    return pl.pallas_call(
        pair_kernel,
        in_specs=[smem] * 2 + [vmem] * (5 + len(rights)) + [anywhere],
        out_specs=[anywhere] * 3,
        out_shape=[pltpu.HBM(whole.shape, F32)] * 2 + [pltpu.HBM(sides.shape, BF16)],
        scratch_shapes=[
            pltpu.VMEM((rows * TENSOR_FEATURES, columns * TENSOR_FEATURES), F32),
            pltpu.VMEM((2, 8 * 128, GROUP * depth), BF16),
            pltpu.VMEM((columns // GROUP * rows, GROUP * depth), F32),
            pltpu.VMEM((columns * C_TRI, 2 * rows), F32),
            pltpu.VMEM((rows * columns, depth), F32),
            pltpu.VMEM(whole.shape, F32),
            pltpu.VMEM(whole.shape, F32),
            pltpu.VMEM(sides.shape, BF16),
            pltpu.SemaphoreType.DMA((2 * len(rights) + 5,)),
        ],
        compiler_params=params(28),
        cost_estimate=cost(12),
        name="pair_update",
    )(
        left_slots,
        right_firsts,
        *left,
        *rights,
        weights,
        entry,
        switch,
        couplings.reshape(rows * columns, depth),
    )


def product_kernel(sides_ref, out_ref, *, grid_rows, grid_columns):
    channels, part, lanes = sides_ref.shape[1:]
    half = lanes // 2
    lane = lax.broadcasted_iota(jnp.int32, (grid_columns * part, lanes), 1)
    front = lane < half
    cut = front[: part // 2]
    for channel in range(channels):
        lefts, rights = [], []
        for r in range(0, grid_rows, 2):
            even, odd = [
                jnp.concatenate(
                    [sides_ref[(r + e) * grid_columns + c, channel] for c in range(grid_columns)],
                    axis=0,
                )
                for e in range(2)
            ]
            lefts.append(jnp.where(front, even, pltpu.roll(odd, half, 1)))
            rights.append(jnp.where(front, pltpu.roll(even, half, 1), odd))
        product = matmul_nt(jnp.concatenate(rights, axis=1), jnp.concatenate(lefts, axis=1))
        product = product.astype(BF16)
        for c in range(grid_columns):
            for r in range(0, grid_rows, 2):
                block = product[c * part : (c + 1) * part, r * half : (r + 2) * half]
                top, bottom = block[: part // 2], block[part // 2 :]
                even = jnp.where(cut, top, pltpu.roll(bottom, half, 1))
                out_ref[r * grid_columns + c, channel] = even
                odd = jnp.where(cut, pltpu.roll(top, half, 1), bottom)
                out_ref[(r + 1) * grid_columns + c, channel] = odd


def triangle_product(sides, grid_rows, grid_columns):
    devices, channels, part, lanes = sides.shape
    step = 2 if channels % 2 == 0 else 1
    return pl.pallas_call(
        functools.partial(product_kernel, grid_rows=grid_rows, grid_columns=grid_columns),
        grid=(channels // step,),
        in_specs=[pl.BlockSpec((devices, step, part, lanes), lambda c: (0, c, 0, 0))],
        out_specs=pl.BlockSpec((devices, step, part // 2, lanes), lambda c: (0, c, 0, 0)),
        out_shape=pltpu.HBM((devices, channels, part // 2, lanes), BF16),
        compiler_params=params(8, "arbitrary"),
        cost_estimate=cost(3),
        name="triangle_product",
    )(sides)


def output_kernel(product_ref, mid_ref, gate_ref, final_ref, out_ref, wide_ref):
    channels, part, lanes = product_ref.shape
    _, own, rows, depth = mid_ref.shape
    out_rows = out_ref.reshape(rows * 2 * own, depth)
    step = pl.program_id(0)

    @pl.when(step == 0)
    def _():
        wide_ref[...] = product_ref[...].astype(F32).reshape(channels * part, lanes)

    for j in range(own):
        product = wide_ref[pl.ds(step * own + j, channels, stride=part), :]
        update = matmul(normalise_rows(product).T, final_ref[...])
        for half in range(2):
            piece = update[half * rows : (half + 1) * rows]
            piece = mid_ref[half, j] + gate_ref[half, j] * piece
            out_rows[pl.ds(half * own + j, rows, stride=2 * own), :] = piece


def pair_result(product, mid, gate, final_matrix):
    channels, part, lanes = product.shape
    columns, rows, depth = mid.shape
    own = 8
    whole = pl.BlockSpec((2, own, rows, depth), lambda j: (0, j, 0, 0))
    out = pl.pallas_call(
        output_kernel,
        grid=(part // own,),
        in_specs=[
            pl.BlockSpec(product.shape, lambda j: (0, 0, 0)),
            whole,
            whole,
            pl.BlockSpec(final_matrix.shape, lambda j: (0, 0)),
        ],
        out_specs=pl.BlockSpec((rows, 2, own, depth), lambda j: (0, 0, j, 0)),
        out_shape=jax.ShapeDtypeStruct((rows, 2, part, depth), F32),
        scratch_shapes=[pltpu.VMEM((channels * part, lanes), F32)],
        compiler_params=params(12, "arbitrary"),
        cost_estimate=cost(4),
        name="pair_result",
    )(
        product,
        pltpu.with_memory_space_constraint(mid.reshape(2, part, rows, depth), pltpu.HBM),
        pltpu.with_memory_space_constraint(gate.reshape(2, part, rows, depth), pltpu.HBM),
        final_matrix,
    )
    return out.reshape(rows, columns, depth)


def swap_cores(block):
    count = lax.axis_size("col")
    return lax.ppermute(block, "col", [(c, c ^ 1) for c in range(count)])


def gather_turned(block):
    rows, columns = lax.axis_size("row"), lax.axis_size("col")
    arrived = []
    for shift in range(rows):
        moves = []
        for r in range(rows):
            for q in range(rows):
                for side in range(2):
                    source = r * columns + 2 * q + side
                    moves.append((source, q * columns + 2 * ((r + shift) % rows) + side))
        arrived.append(lax.ppermute(block, ("row", "col"), moves))
    return jnp.stack(arrived)


def both_cores(own):
    rows = lax.axis_size("row")
    core = lax.rem(lax.axis_index("col"), 2)
    other = swap_cores(own)
    residues = own.shape[1] // TENSOR_FEATURES
    if residues % 8 == 0:
        return own, other
    order = left_order(rows)
    own, other = jnp.take(own, order, axis=0), jnp.take(other, order, axis=0)
    joined = 8 // residues
    ordered = []
    for side in (jnp.where(core == 0, own, other), jnp.where(core == 0, other, own)):
        side = side.reshape(rows // joined, joined, TENSOR_FEATURES, residues, -1)
        side = jnp.transpose(side, (0, 2, 1, 3, 4))
        ordered.append(side.reshape(rows // joined, joined * own.shape[1], -1))
    return tuple(ordered)


def left_order(rows):
    me = lax.axis_index("col") // 2
    return lax.rem(me - jnp.arange(rows, dtype=jnp.int32) + rows, rows)


def left_groups(rows, residues):
    if residues % 8:
        return jnp.arange(2 * rows * residues // 8, dtype=jnp.int32)
    core = lax.rem(lax.axis_index("col"), 2)
    order = left_order(rows)
    return jnp.concatenate([order + core * rows, order + (1 - core) * rows])


def exchange_rows(pieces):
    arrived = [pieces[0]]
    for shift in range(1, len(pieces)):
        moves = [(r, r ^ shift) for r in range(len(pieces))]
        arrived.append(lax.ppermute(pieces[shift], "row", moves))
    return arrived


def paired_entries(matrices):
    turned = matrices.reshape(C_Z, 2, 2, C_TRI)
    return jnp.transpose(turned, (2, 3, 1, 0)).reshape(2 * C_TRI, 2 * C_Z)


def body(
    homolog_tensor,
    couplings,
    attention_probe_matrix,
    attention_extra_matrices,
    attention_final_matrix,
    tensor_entry_matrices,
    tensor_final_matrix,
    incoming_entry_matrices,
    incoming_switch_matrix,
    incoming_final_matrix,
):
    inner = ATTENTION_UNITS * UNIT_WIDTH
    row_count = lax.axis_size("row")
    seqs, residues, depth = homolog_tensor.shape
    own_residues = residues // row_count
    sources = lax.axis_index("row") ^ jnp.arange(row_count, dtype=jnp.int32)
    high = exchange_rows(standardise_high(sources, homolog_tensor))
    low = standardise_low(sources, homolog_tensor)
    others = jnp.concatenate(
        [attention_probe_matrix.T, attention_extra_matrices[:, inner:].T], axis=0
    )
    early = (
        attention_extra_matrices[:, :inner],
        others,
        attention_final_matrix.T,
        tensor_entry_matrices.T,
        paired_entries(incoming_entry_matrices),
        sources * own_residues,
        left_groups(row_count, own_residues),
    )
    high, low, early = lax.optimization_barrier((high, low, early))
    key_matrix, others, final_turned, tensor_turned, entries, firsts, slots = early
    low = exchange_rows(low)
    turned, *gated = attention(high, key_matrix, others)
    left_piece, right_piece = alignment(
        sources, high, low, turned, final_turned, tensor_turned
    )

    rights = exchange_rows([right_piece] * row_count)
    own = gather_turned(left_piece)
    own, rights = lax.optimization_barrier((own, rights))
    mid, gate, sides = pair_update(
        slots,
        firsts,
        both_cores(own),
        rights,
        tensor_final_matrix,
        couplings,
        entries,
        incoming_switch_matrix,
    )
    gated, sides = lax.optimization_barrier((gated, sides))
    gated = exchange_rows(gated)

    everywhere = ("row", "col")
    column_count = lax.axis_size("col")
    devices = row_count * column_count
    sides = sides.reshape(devices, C_TRI // devices, *sides.shape[1:])
    sides = lax.all_to_all(sides, everywhere, split_axis=0, concat_axis=0)
    gated, sides = lax.optimization_barrier((gated, sides))
    product = triangle_product(sides, row_count, column_count)
    product = lax.all_to_all(product, everywhere, split_axis=0, concat_axis=0)

    gated = jnp.take(jnp.stack(gated), sources, axis=0)
    gated = jnp.transpose(gated.reshape(residues, seqs, inner), (1, 0, 2))
    change = jnp.dot(
        gated.reshape(-1, inner), attention_final_matrix, preferred_element_type=F32
    )
    refreshed_homologs = homolog_tensor + change.reshape(homolog_tensor.shape)
    product = product.reshape(C_TRI, *product.shape[2:])
    pair_output = pair_result(product, mid, gate, incoming_final_matrix)
    return (refreshed_homologs, pair_output)


def solution(mesh):
    in_specs = (
        P("row", "col", None),
        P("row", "col", None),
        P(),
        P(),
        P(),
        P(),
        P(),
        P(),
        P(),
        P(),
    )
    out_specs = (P("row", "col", None), P("row", "col", None))
    return jax.shard_map(body, mesh=mesh, in_specs=in_specs, out_specs=out_specs, check_vma=False)
```

```python
import functools

import jax
import jax.numpy as jnp
from jax import lax
from jax.experimental import pallas as pl
from jax.experimental.pallas import tpu as pltpu
from jax.sharding import PartitionSpec as P

FEATURE_DEPTH = 256
C_Z = 128
TENSOR_FEATURES = 32
C_TRI = 128
ATTENTION_UNITS = 8
UNIT_WIDTH = 32
EPS = 1e-05
GROUP = 4
F32 = jnp.float32
BF16 = jnp.bfloat16
NT = (((1,), (1,)), ((), ()))


def matmul(left, right):
    return jnp.dot(left, right, preferred_element_type=F32)


def matmul_nt(left, right):
    return lax.dot_general(left, right, NT, preferred_element_type=F32)


def sigmoid(values):
    return 0.5 * jnp.tanh(0.5 * values) + 0.5


def cost(microseconds):
    return pl.CostEstimate(
        flops=int(microseconds * 1e9), bytes_accessed=int(microseconds * 1e6), transcendentals=0
    )


def params(megabytes, *semantics):
    return pltpu.CompilerParams(
        dimension_semantics=semantics or None, vmem_limit_bytes=megabytes * 1024 * 1024
    )


def fold(values, combine):
    while values.shape[0] > 8:
        half = values.shape[0] // 2
        values = combine(values[:half], values[half:])
    return values


def top_rows(values):
    return jnp.max(fold(values, jnp.maximum), axis=0, keepdims=True)


def sum_rows(values):
    return jnp.sum(fold(values, jnp.add), axis=0, keepdims=True)


def normalise_rows(values):
    count = values.shape[0]
    centred = values - sum_rows(values) * (1.0 / count)
    variance = sum_rows(centred * centred) * (1.0 / count)
    return (centred * lax.rsqrt(variance + EPS)).astype(BF16)


def standardised_column(first_rows, second_rows, n, residues):
    seqs = first_rows.shape[0] // residues
    rows = pl.ds(n, seqs, stride=residues)
    column = jnp.concatenate([first_rows[rows, :], second_rows[rows, :]], axis=1)
    centred = column - jnp.mean(column, axis=1, keepdims=True)
    variance = jnp.mean(centred * centred, axis=1, keepdims=True) + EPS
    scale = lax.rsqrt(variance)
    return centred * scale, variance * scale


def high_kernel(sources_ref, block_hbm, *rest):
    *pieces_hbm, first_ref, second_ref, high_ref, fetched, sent = rest
    seqs, residues, lanes = first_ref.shape
    own = residues // len(pieces_hbm)
    step = 16
    fetches, sends = [], []
    for s in range(0, seqs, step):
        chosen = pl.ds(s, step)
        for half, ref in enumerate((first_ref, second_ref)):
            source = block_hbm.at[chosen, :, pl.ds(half * lanes, lanes)]
            fetches.append(
                pltpu.make_async_copy(source, ref.at[chosen], fetched.at[len(fetches)])
            )
            fetches[-1].start()
    for part in range(seqs // step):
        chosen = pl.ds(part * step, step)
        fetches[2 * part].wait()
        fetches[2 * part + 1].wait()
        first_rows = first_ref.at[chosen].reshape(step * residues, lanes)
        second_rows = second_ref.at[chosen].reshape(step * residues, lanes)
        for n in range(residues):
            normed, _ = standardised_column(first_rows, second_rows, n, residues)
            high_ref[part, n] = normed.astype(BF16)
        for p, piece_hbm in enumerate(pieces_hbm):
            source = high_ref.at[part, pl.ds(sources_ref[p] * own, own)]
            sends.append(
                pltpu.make_async_copy(source, piece_hbm.at[:, chosen], sent.at[len(sends)])
            )
            sends[-1].start()
    for send in sends:
        send.wait()


def standardise_high(sources, block):
    seqs, residues, depth = block.shape
    half = depth // 2
    count = sources.shape[0]
    hbm = pl.BlockSpec(memory_space=pltpu.HBM)
    return pl.pallas_call(
        high_kernel,
        in_specs=[pl.BlockSpec(memory_space=pltpu.SMEM), hbm],
        out_specs=[hbm] * count,
        out_shape=[pltpu.HBM((residues // count, seqs, depth), BF16)] * count,
        scratch_shapes=[
            pltpu.VMEM((seqs, residues, half), F32),
            pltpu.VMEM((seqs, residues, half), F32),
            pltpu.VMEM((seqs // 16, residues, 16, depth), BF16),
            pltpu.SemaphoreType.DMA((seqs // 8,)),
            pltpu.SemaphoreType.DMA((seqs // 16 * count,)),
        ],
        compiler_params=params(10),
        cost_estimate=cost(3),
        name="standardise_high",
    )(sources, pltpu.with_memory_space_constraint(block, pltpu.HBM))


def low_kernel(sources_ref, first_ref, second_ref, *rest):
    *pieces_hbm, low_ref, sent = rest
    seqs, residues, lanes = first_ref.shape
    own = residues // len(pieces_hbm)
    first_rows = first_ref.reshape(seqs * residues, lanes)
    second_rows = second_ref.reshape(seqs * residues, lanes)
    lane = lax.broadcasted_iota(jnp.int32, (seqs, 128), 1)
    for p in range(len(pieces_hbm)):
        spreads = jnp.zeros((seqs, 128), F32)
        for n in range(own):
            normed, spread = standardised_column(first_rows, second_rows, p * own + n, residues)
            left = (normed - normed.astype(BF16).astype(F32)).astype(BF16)
            low_ref[p, n * seqs : (n + 1) * seqs, :] = left
            spreads = jnp.where(lane == n, spread, spreads)
        spreads = spreads.T[:8, :]
        coarse = spreads.astype(BF16).astype(F32)
        kept = jnp.concatenate([coarse, spreads - coarse], axis=0)
        kept = jnp.concatenate([kept, jnp.zeros((16, 2 * lanes - seqs), F32)], axis=1)
        low_ref[p, own * seqs :, :] = kept.astype(BF16)
    sends = []
    for p, piece_hbm in enumerate(pieces_hbm):
        source = low_ref.at[sources_ref[p]]
        sends.append(pltpu.make_async_copy(source, piece_hbm, sent.at[p]))
        sends[-1].start()
    for send in sends:
        send.wait()


def standardise_low(sources, block):
    seqs, residues, depth = block.shape
    half = depth // 2
    count = sources.shape[0]
    height = residues // count * seqs + 16
    hbm = pl.BlockSpec(memory_space=pltpu.HBM)
    return pl.pallas_call(
        low_kernel,
        grid=(1,),
        in_specs=[
            pl.BlockSpec(memory_space=pltpu.SMEM),
            pl.BlockSpec((seqs, residues, half), lambda g: (0, 0, 0)),
            pl.BlockSpec((seqs, residues, half), lambda g: (0, 0, 1)),
        ],
        out_specs=[hbm] * count,
        out_shape=[pltpu.HBM((height, depth), BF16)] * count,
        scratch_shapes=[
            pltpu.VMEM((count, height, depth), BF16),
            pltpu.SemaphoreType.DMA((count,)),
        ],
        compiler_params=params(14, "arbitrary"),
        cost_estimate=cost(4),
        name="standardise_low",
    )(sources, block, block)


def attention_kernel(key_ref, others_ref, *rest):
    *refs, scores_ref, weights_ref = rest
    blocks = len(refs) // 2
    normed_refs, turned_ref, gated_refs = refs[:blocks], refs[blocks], refs[blocks + 1 :]
    residues, seqs, _ = normed_refs[0].shape
    total = blocks * seqs
    inner = ATTENTION_UNITS * UNIT_WIDTH
    ring = scores_ref.shape[0]
    columns = []

    def project(n):
        column = jnp.concatenate([ref[n] for ref in normed_refs], axis=0)
        key_rows = matmul(column, key_ref[...]).astype(BF16)
        projected = matmul_nt(others_ref[...], column)
        queries = (projected[:inner] * UNIT_WIDTH ** (-0.5)).astype(BF16)
        value_rows = projected[inner : 2 * inner].astype(BF16)
        gates = sigmoid(projected[2 * inner :])
        columns.append((key_rows, queries, value_rows, gates))
    units = [(n, h) for n in range(residues) for h in range(ATTENTION_UNITS)]

    def score(unit):
        n, h = units[unit]
        key_rows, queries, _, _ = columns[n]
        low, high = h * UNIT_WIDTH, (h + 1) * UNIT_WIDTH
        pieces = [queries[low:high]]
        if low > 0:
            pieces.insert(0, jnp.zeros((low, total), BF16))
        if high < inner:
            pieces.append(jnp.zeros((inner - high, total), BF16))
        scores_ref[unit % ring] = matmul(key_rows, jnp.concatenate(pieces, axis=0))

    def weigh(unit):
        for low in range(0, total, 128):
            scores = scores_ref[unit % ring, :, low : low + 128]
            weights = jnp.exp(scores - top_rows(scores))
            scale = 1.0 / sum_rows(weights)
            weights_ref[unit % ring, :, low : low + 128] = (weights * scale).astype(BF16)

    def attend(unit):
        n, h = units[unit]
        _, _, value_rows, gates = columns[n]
        rows = slice(h * UNIT_WIDTH, (h + 1) * UNIT_WIDTH)
        attended = matmul(value_rows[rows], weights_ref[unit % ring]) * gates[rows]
        turned_ref[n, rows, :] = attended.astype(BF16)

    def turn_back(n):
        back = turned_ref[n].T
        for block, gated_ref in enumerate(gated_refs):
            gated_ref[n] = back[block * seqs : (block + 1) * seqs]

    project(0)
    for step in range(len(units) + 2):
        if step < len(units):
            score(step)
            n, h = units[step]
            if h == ATTENTION_UNITS // 2 and n + 1 < residues:
                project(n + 1)
        if 1 <= step <= len(units):
            weigh(step - 1)
        if step >= 2:
            attend(step - 2)
            n, h = units[step - 2]
            if h == ATTENTION_UNITS - 1:
                turn_back(n)


def attention(normed, key_matrix, other_matrices):
    blocks = len(normed)
    residues, seqs, depth = normed[0].shape
    total = blocks * seqs
    inner = ATTENTION_UNITS * UNIT_WIDTH
    step = 4
    return pl.pallas_call(
        attention_kernel,
        grid=(residues // step,),
        in_specs=[
            pl.BlockSpec((depth, inner), lambda n: (0, 0)),
            pl.BlockSpec((3 * inner, depth), lambda n: (0, 0)),
        ]
        + [pl.BlockSpec((step, seqs, depth), lambda n: (n, 0, 0))] * blocks,
        out_specs=[pl.BlockSpec((step, inner, total), lambda n: (n, 0, 0))]
        + [pl.BlockSpec((step, seqs, inner), lambda n: (n, 0, 0))] * blocks,
        out_shape=[jax.ShapeDtypeStruct((residues, inner, total), BF16)]
        + [pltpu.HBM((residues, seqs, inner), BF16)] * blocks,
        scratch_shapes=[
            pltpu.VMEM((4, total, total), F32),
            pltpu.VMEM((4, total, total), BF16),
        ],
        compiler_params=params(12 + (total // 128) ** 2, "arbitrary"),
        cost_estimate=cost(10),
        name="attention",
    )(key_matrix, other_matrices, *normed)


def alignment_kernel(sources_ref, turned_ref, final_ref, entry_ref, *rest):
    *refs, left_ref, right_ref, rows_ref = rest
    blocks = len(refs) // 3
    high_refs, low_refs, spread_refs = refs[:blocks], refs[blocks : 2 * blocks], refs[2 * blocks :]
    residues, seqs, depth = high_refs[0].shape
    total = blocks * seqs
    features = TENSOR_FEATURES
    step = pl.program_id(0)
    for n in range(residues):
        column = jnp.concatenate([ref[n] for ref in high_refs], axis=0).astype(F32)
        column = column + jnp.concatenate(
            [ref[n * seqs : (n + 1) * seqs, :] for ref in low_refs], axis=0
        ).astype(F32)
        spreads = []
        for ref in spread_refs:
            kept = ref[:, :seqs].astype(F32)
            row = lax.broadcasted_iota(jnp.int32, kept.shape, 0)
            chosen = lax.rem(row, 8) == step * residues + n
            spreads.append(jnp.sum(jnp.where(chosen, kept, 0.0), axis=0, keepdims=True))
        spread = jnp.concatenate(spreads, axis=1)
        updated = column.T * spread + matmul(final_ref[...], turned_ref[n])
        projected = matmul(entry_ref[...], normalise_rows(updated))
        me = sources_ref[0]
        tiles = [projected[:, low : low + 128] for low in range(0, total, 128)]
        odd = lax.rem(me, 2) == 1
        tiles = [jnp.where(odd, pltpu.roll(tile, seqs, 1), tile) for tile in tiles]
        width = 1
        while width < len(tiles):
            crossed = lax.rem(lax.div(me, 2 * width), 2) == 1
            tiles = [
                jnp.where(crossed, tiles[t ^ width], tiles[t]) for t in range(len(tiles))
            ]
            width *= 2
        first = pl.multiple_of((step * residues + n) * features, features)
        for t, tile in enumerate(tiles):
            right_ref[n, :, t * 128 : (t + 1) * 128] = tile[features:].astype(BF16)
            rows_ref[t, pl.ds(first, features), :] = tile[:features]

    @pl.when(step == pl.num_programs(0) - 1)
    def _():
        count = rows_ref.shape[1] // features
        together = max(1, 16 // count)
        for c in range(0, features, together):
            pieces = []
            for e in range(together):
                chosen = pl.ds(c + e, count, stride=features)
                tiles = [rows_ref[tile, chosen, :] for tile in range(total // 128)]
                pieces.append(jnp.concatenate(tiles, axis=1))
            piece = jnp.concatenate(pieces, axis=0).astype(BF16)
            left_ref[c * count : (c + together) * count, :] = piece


def alignment(sources, high, low, turned, final_matrix, entry_matrices):
    blocks = len(high)
    residues, seqs, depth = high[0].shape
    total = blocks * seqs
    features = TENSOR_FEATURES
    step = 4
    height = residues * seqs + 16
    return pl.pallas_call(
        alignment_kernel,
        grid=(residues // step,),
        in_specs=[
            pl.BlockSpec(memory_space=pltpu.SMEM),
            pl.BlockSpec((step, depth, total), lambda n: (n, 0, 0)),
            pl.BlockSpec(final_matrix.shape, lambda n: (0, 0)),
            pl.BlockSpec(entry_matrices.shape, lambda n: (0, 0)),
        ]
        + [pl.BlockSpec((step, seqs, depth), lambda n: (n, 0, 0))] * blocks
        + [pl.BlockSpec((step * seqs, depth), lambda n: (n, 0))] * blocks
        + [pl.BlockSpec((16, depth), lambda n: (height // 16 - 1, 0))] * blocks,
        out_specs=[
            pl.BlockSpec((features * residues, total), lambda n: (0, 0)),
            pl.BlockSpec((step, features, total), lambda n: (n, 0, 0)),
        ],
        out_shape=[
            jax.ShapeDtypeStruct((features * residues, total), BF16),
            jax.ShapeDtypeStruct((residues, features, total), BF16),
        ],
        scratch_shapes=[pltpu.VMEM((total // 128, residues * features, 128), F32)],
        compiler_params=params(16, "arbitrary"),
        cost_estimate=cost(4),
        name="alignment",
    )(sources, turned, final_matrix, entry_matrices, *high, *low, *low)


def pair_kernel(
    left_slots_ref,
    right_firsts_ref,
    own_ref,
    other_ref,
    *rest,
):
    weights_ref, entry_ref, switch_ref, couplings_hbm, mid_hbm, gate_hbm, sides_hbm = rest[-16:-9]
    outer_ref, spread_ref, sum_ref, rows_ref, couplings_ref = rest[-9:-4]
    mid_ref, gate_ref, sides_ref, copied = rest[-4:]
    right_refs = rest[:-16]
    fetched = pltpu.make_async_copy(couplings_hbm, couplings_ref, copied.at[0])
    fetched.start()
    copies = []

    def send(source, target):
        copies.append(pltpu.make_async_copy(source, target, copied.at[len(copies) + 1]))
        copies[-1].start()

    features = TENSOR_FEATURES
    slots, piece_rows, total = own_ref.shape
    residues = piece_rows // features
    rows = 2 * slots * residues
    share = right_refs[0].shape[0]
    columns = len(right_refs) * share
    groups = columns // GROUP
    wide = share * features
    together = spread_ref.shape[1] // 128

    for half, left_ref in enumerate((own_ref, other_ref)):
        piece = left_ref[...].reshape(slots * piece_rows, total)
        target = slice(half * slots * piece_rows, (half + 1) * slots * piece_rows)
        for p, right_ref in enumerate(right_refs):
            right = right_ref[...].reshape(wide, total)
            outer_ref[target, p * wide : (p + 1) * wide] = matmul_nt(piece, right) * (1.0 / total)

    spread_ref[...] = jnp.zeros_like(spread_ref)

    def channel_step(p, carry):
        slot = lax.rem(p, 2)
        for e in range(together):
            source = pl.multiple_of((p * together + e) * features, features)
            piece = weights_ref[pl.ds(source, features), :]
            for place in range(GROUP):
                low = e * 128 + place * features
                spread_ref[slot, low : low + features, place * C_Z : (place + 1) * C_Z] = piece
        pieces = []
        for g in range(groups):
            parts = []
            for e in range(together):
                channel = []
                for slot_number in range(2 * slots):
                    first = slot_number * piece_rows + (p * together + e) * residues
                    source = pl.ds(pl.multiple_of(first, residues), residues)
                    channel.append(outer_ref[source, g * 128 : (g + 1) * 128])
                parts.append(jnp.concatenate(channel, axis=0).astype(BF16))
            pieces.append(jnp.concatenate(parts, axis=1))
        update = matmul(jnp.concatenate(pieces, axis=0), spread_ref[slot])

        @pl.when(p == 0)
        def _():
            sum_ref[...] = update

        @pl.when(p > 0)
        def _():
            sum_ref[...] += update

        return carry

    lax.fori_loop(0, features // together, channel_step, 0)

    left_firsts = [left_slots_ref[j] * residues for j in range(2 * slots)]
    right_firsts = [right_firsts_ref[p] for p in range(len(right_refs))]
    fetched.wait()
    for g in range(groups):
        normed, places = [], []
        for place in range(GROUP):
            p, n = divmod(g * GROUP + place, share)
            b = right_firsts[p] + n
            places.append(b)
            lanes = slice(place * C_Z, (place + 1) * C_Z)
            pieces = []
            for first in left_firsts:
                source = pl.ds(pl.multiple_of(g * rows + first, residues), residues)
                pieces.append(sum_ref[source, lanes])
            mid = jnp.concatenate(pieces, axis=0)
            mid = mid + couplings_ref[pl.ds(b, rows, stride=columns), :]
            mid_ref[g * GROUP + place] = mid
            centred = mid - jnp.mean(mid, axis=1, keepdims=True)
            variance = jnp.mean(centred * centred, axis=1, keepdims=True)
            normed.append((centred * lax.rsqrt(variance + EPS)).astype(BF16))
        gates = sigmoid(matmul(jnp.concatenate(normed, axis=0), switch_ref[...]))
        blank = jnp.zeros_like(normed[0])
        for place in range(0, GROUP, 2):
            twice = []
            for e in range(2):
                part = gates[(place + e) * rows : (place + e + 1) * rows]
                gate_ref[g * GROUP + place + e] = part
                twice.append(jnp.concatenate([normed[place + e], blank], axis=1))
                twice.append(jnp.concatenate([blank, normed[place + e]], axis=1))
            sides = matmul_nt(entry_ref[...], jnp.concatenate(twice, axis=0))
            sides = sigmoid(sides[C_TRI:]) * sides[:C_TRI]
            for e in range(2):
                first = pl.multiple_of(places[place + e] * C_TRI, C_TRI)
                rows_ref[pl.ds(first, C_TRI), :] = sides[:, e * 2 * rows : (e + 1) * 2 * rows]

        if (g + 1) * GROUP % share == 0:
            p = (g + 1) * GROUP // share - 1
            source, target = pl.ds(p * share, share), pl.ds(right_firsts[p], share)
            send(mid_ref.at[source], mid_hbm.at[target])
            send(gate_ref.at[source], gate_hbm.at[target])

    cut = C_TRI // 4
    for part in range(4):

        def turn_step(c, carry):
            sides_ref[c] = rows_ref[pl.ds(c, columns, stride=C_TRI), :].astype(BF16)
            return carry

        lax.fori_loop(part * cut, (part + 1) * cut, turn_step, 0, unroll=8)
        chosen = pl.ds(part * cut, cut)
        send(sides_ref.at[chosen], sides_hbm.at[chosen])
    for copy in copies:
        copy.wait()


def pair_update(left_slots, right_firsts, left, rights, weights, couplings, entry, switch):
    rows, columns, depth = couplings.shape
    whole = jax.ShapeDtypeStruct((columns, rows, depth), F32)
    sides = jax.ShapeDtypeStruct((C_TRI, columns, 2 * rows), BF16)
    smem = pl.BlockSpec(memory_space=pltpu.SMEM)
    vmem = pl.BlockSpec(memory_space=pltpu.VMEM)
    anywhere = pl.BlockSpec(memory_space=pl.ANY)
    return pl.pallas_call(
        pair_kernel,
        in_specs=[smem] * 2 + [vmem] * (5 + len(rights)) + [anywhere],
        out_specs=[anywhere] * 3,
        out_shape=[pltpu.HBM(whole.shape, F32)] * 2 + [pltpu.HBM(sides.shape, BF16)],
        scratch_shapes=[
            pltpu.VMEM((rows * TENSOR_FEATURES, columns * TENSOR_FEATURES), F32),
            pltpu.VMEM((2, 8 * 128, GROUP * depth), BF16),
            pltpu.VMEM((columns // GROUP * rows, GROUP * depth), F32),
            pltpu.VMEM((columns * C_TRI, 2 * rows), F32),
            pltpu.VMEM((rows * columns, depth), F32),
            pltpu.VMEM(whole.shape, F32),
            pltpu.VMEM(whole.shape, F32),
            pltpu.VMEM(sides.shape, BF16),
            pltpu.SemaphoreType.DMA((2 * len(rights) + 5,)),
        ],
        compiler_params=params(28),
        cost_estimate=cost(12),
        name="pair_update",
    )(
        left_slots,
        right_firsts,
        *left,
        *rights,
        weights,
        entry,
        switch,
        couplings.reshape(rows * columns, depth),
    )


def product_kernel(sides_ref, out_ref, *, grid_rows, grid_columns):
    channels, part, lanes = sides_ref.shape[1:]
    half = lanes // 2
    lane = lax.broadcasted_iota(jnp.int32, (grid_columns * part, lanes), 1)
    front = lane < half
    cut = front[: part // 2]
    for channel in range(channels):
        lefts, rights = [], []
        for r in range(0, grid_rows, 2):
            even, odd = [
                jnp.concatenate(
                    [sides_ref[(r + e) * grid_columns + c, channel] for c in range(grid_columns)],
                    axis=0,
                )
                for e in range(2)
            ]
            lefts.append(jnp.where(front, even, pltpu.roll(odd, half, 1)))
            rights.append(jnp.where(front, pltpu.roll(even, half, 1), odd))
        product = matmul_nt(jnp.concatenate(rights, axis=1), jnp.concatenate(lefts, axis=1))
        product = product.astype(BF16)
        for c in range(grid_columns):
            for r in range(0, grid_rows, 2):
                block = product[c * part : (c + 1) * part, r * half : (r + 2) * half]
                top, bottom = block[: part // 2], block[part // 2 :]
                even = jnp.where(cut, top, pltpu.roll(bottom, half, 1))
                out_ref[r * grid_columns + c, channel] = even
                odd = jnp.where(cut, pltpu.roll(top, half, 1), bottom)
                out_ref[(r + 1) * grid_columns + c, channel] = odd


def triangle_product(sides, grid_rows, grid_columns):
    devices, channels, part, lanes = sides.shape
    step = 2 if channels % 2 == 0 else 1
    return pl.pallas_call(
        functools.partial(product_kernel, grid_rows=grid_rows, grid_columns=grid_columns),
        grid=(channels // step,),
        in_specs=[pl.BlockSpec((devices, step, part, lanes), lambda c: (0, c, 0, 0))],
        out_specs=pl.BlockSpec((devices, step, part // 2, lanes), lambda c: (0, c, 0, 0)),
        out_shape=pltpu.HBM((devices, channels, part // 2, lanes), BF16),
        compiler_params=params(8, "arbitrary"),
        cost_estimate=cost(3),
        name="triangle_product",
    )(sides)


def output_kernel(
    product_ref, final_ref, mid_hbm, gate_hbm, out_hbm, wide_ref, mid_ref, gate_ref, out_ref, *copied
):
    channels, part, lanes = product_ref.shape
    columns, rows, depth = mid_ref.shape
    own = 8
    fetched, sent = copied
    fetches, sends = [], []
    for first in range(0, columns, own):
        chosen = pl.ds(first, own)
        for source, target in ((mid_hbm, mid_ref), (gate_hbm, gate_ref)):
            fetches.append(
                pltpu.make_async_copy(
                    source.at[chosen], target.at[chosen], fetched.at[len(fetches)]
                )
            )
            fetches[-1].start()
    wide_ref[...] = product_ref[...].astype(F32).reshape(channels * part, lanes)
    for group in range(part // own):
        updates = []
        for j in range(own):
            product = wide_ref[pl.ds(group * own + j, channels, stride=part), :]
            updates.append(matmul(normalise_rows(product).T, final_ref[...]))
        for half in range(2):
            cut = half * (part // own) + group
            fetches[2 * cut].wait()
            fetches[2 * cut + 1].wait()
            out_rows = out_ref.at[cut].reshape(rows * own, depth)
            for j in range(own):
                b = cut * own + j
                piece = updates[j][half * rows : (half + 1) * rows]
                out_rows[pl.ds(j, rows, stride=own), :] = mid_ref[b] + gate_ref[b] * piece
            sends.append(
                pltpu.make_async_copy(
                    out_ref.at[cut], out_hbm.at[:, pl.ds(cut * own, own)], sent.at[len(sends)]
                )
            )
            sends[-1].start()
    for send in sends:
        send.wait()


def pair_result(product, mid, gate, final_matrix):
    channels, part, lanes = product.shape
    columns, rows, depth = mid.shape
    vmem, hbm = pl.BlockSpec(memory_space=pltpu.VMEM), pl.BlockSpec(memory_space=pltpu.HBM)
    return pl.pallas_call(
        output_kernel,
        in_specs=[vmem, vmem, hbm, hbm],
        out_specs=hbm,
        out_shape=pltpu.HBM((rows, columns, depth), F32),
        scratch_shapes=[
            pltpu.VMEM((channels * part, lanes), F32),
            pltpu.VMEM(mid.shape, F32),
            pltpu.VMEM(mid.shape, F32),
            pltpu.VMEM((columns // 8, rows, 8, depth), F32),
            pltpu.SemaphoreType.DMA((columns // 4,)),
            pltpu.SemaphoreType.DMA((columns // 8,)),
        ],
        compiler_params=params(16),
        cost_estimate=cost(3),
        name="pair_result",
    )(
        product,
        final_matrix,
        pltpu.with_memory_space_constraint(mid, pltpu.HBM),
        pltpu.with_memory_space_constraint(gate, pltpu.HBM),
    )


def swap_cores(block):
    count = lax.axis_size("col")
    return lax.ppermute(block, "col", [(c, c ^ 1) for c in range(count)])


def gather_turned(block, later):
    rows, columns = lax.axis_size("row"), lax.axis_size("col")
    arrived = []
    for shift in range(rows):
        moves = []
        for r in range(rows):
            for q in range(rows):
                for side in range(2):
                    source = r * columns + 2 * q + side
                    moves.append((source, q * columns + 2 * ((r + shift) % rows) + side))
        source = block if shift < 2 else later
        arrived.append(lax.ppermute(source, ("row", "col"), moves))
    return jnp.stack(arrived)


def both_cores(own):
    rows = lax.axis_size("row")
    core = lax.rem(lax.axis_index("col"), 2)
    other = swap_cores(own)
    residues = own.shape[1] // TENSOR_FEATURES
    if residues % 8 == 0:
        return own, other
    order = left_order(rows)
    own, other = jnp.take(own, order, axis=0), jnp.take(other, order, axis=0)
    joined = 8 // residues
    ordered = []
    for side in (jnp.where(core == 0, own, other), jnp.where(core == 0, other, own)):
        side = side.reshape(rows // joined, joined, TENSOR_FEATURES, residues, -1)
        side = jnp.transpose(side, (0, 2, 1, 3, 4))
        ordered.append(side.reshape(rows // joined, joined * own.shape[1], -1))
    return tuple(ordered)


def left_order(rows):
    me = lax.axis_index("col") // 2
    return lax.rem(me - jnp.arange(rows, dtype=jnp.int32) + rows, rows)


def left_groups(rows, residues):
    if residues % 8:
        return jnp.arange(2 * rows * residues // 8, dtype=jnp.int32)
    core = lax.rem(lax.axis_index("col"), 2)
    order = left_order(rows)
    return jnp.concatenate([order + core * rows, order + (1 - core) * rows])


def exchange_rows(pieces):
    arrived = [pieces[0]]
    for shift in range(1, len(pieces)):
        moves = [(r, r ^ shift) for r in range(len(pieces))]
        arrived.append(lax.ppermute(pieces[shift], "row", moves))
    return arrived


def paired_entries(matrices):
    turned = matrices.reshape(C_Z, 2, 2, C_TRI)
    return jnp.transpose(turned, (2, 3, 1, 0)).reshape(2 * C_TRI, 2 * C_Z)


def body(
    homolog_tensor,
    couplings,
    attention_probe_matrix,
    attention_extra_matrices,
    attention_final_matrix,
    tensor_entry_matrices,
    tensor_final_matrix,
    incoming_entry_matrices,
    incoming_switch_matrix,
    incoming_final_matrix,
):
    inner = ATTENTION_UNITS * UNIT_WIDTH
    row_count = lax.axis_size("row")
    seqs, residues, depth = homolog_tensor.shape
    own_residues = residues // row_count
    sources = lax.axis_index("row") ^ jnp.arange(row_count, dtype=jnp.int32)
    high = exchange_rows(standardise_high(sources, homolog_tensor))
    low = standardise_low(sources, homolog_tensor)
    others = jnp.concatenate(
        [attention_probe_matrix.T, attention_extra_matrices[:, inner:].T], axis=0
    )
    early = (
        attention_extra_matrices[:, :inner],
        others,
        attention_final_matrix.T,
        tensor_entry_matrices.T,
        paired_entries(incoming_entry_matrices),
        sources * own_residues,
        left_groups(row_count, own_residues),
    )
    high, low, early = lax.optimization_barrier((high, low, early))
    key_matrix, others, final_turned, tensor_turned, entries, firsts, slots = early
    low = exchange_rows(low)
    turned, *gated = attention(high, key_matrix, others)
    left_piece, right_piece = alignment(
        sources, high, low, turned, final_turned, tensor_turned
    )

    rights = exchange_rows([right_piece] * row_count)
    later, rights[1] = lax.optimization_barrier((left_piece, rights[1]))
    own = gather_turned(left_piece, later)
    own, rights = lax.optimization_barrier((own, rights))
    mid, gate, sides = pair_update(
        slots,
        firsts,
        both_cores(own),
        rights,
        tensor_final_matrix,
        couplings,
        entries,
        incoming_switch_matrix,
    )
    gated, sides = lax.optimization_barrier((gated, sides))
    gated = exchange_rows(gated)

    everywhere = ("row", "col")
    column_count = lax.axis_size("col")
    devices = row_count * column_count
    sides = sides.reshape(devices, C_TRI // devices, *sides.shape[1:])
    sides = lax.all_to_all(sides, everywhere, split_axis=0, concat_axis=0)
    gated, sides = lax.optimization_barrier((gated, sides))
    product = triangle_product(sides, row_count, column_count)
    product = lax.all_to_all(product, everywhere, split_axis=0, concat_axis=0)

    gated = jnp.take(jnp.stack(gated), sources, axis=0)
    gated = jnp.transpose(gated.reshape(residues, seqs, inner), (1, 0, 2))
    change = jnp.dot(
        gated.reshape(-1, inner), attention_final_matrix, preferred_element_type=F32
    )
    refreshed_homologs = homolog_tensor + change.reshape(homolog_tensor.shape)
    product = product.reshape(C_TRI, *product.shape[2:])
    pair_output = pair_result(product, mid, gate, incoming_final_matrix)
    return (refreshed_homologs, pair_output)


def solution(mesh):
    in_specs = (
        P("row", "col", None),
        P("row", "col", None),
        P(),
        P(),
        P(),
        P(),
        P(),
        P(),
        P(),
        P(),
    )
    out_specs = (P("row", "col", None), P("row", "col", None))
    return jax.shard_map(body, mesh=mesh, in_specs=in_specs, out_specs=out_specs, check_vma=False)
```

```python
import functools

import jax
import jax.numpy as jnp
from jax import lax
from jax.experimental import pallas as pl
from jax.experimental.pallas import tpu as pltpu
from jax.sharding import PartitionSpec as P

FEATURE_DEPTH = 256
C_Z = 128
TENSOR_FEATURES = 32
C_TRI = 128
ATTENTION_UNITS = 8
UNIT_WIDTH = 32
EPS = 1e-05
GROUP = 4
F32 = jnp.float32
BF16 = jnp.bfloat16
NT = (((1,), (1,)), ((), ()))


def matmul(left, right):
    return jnp.dot(left, right, preferred_element_type=F32)


def matmul_nt(left, right):
    return lax.dot_general(left, right, NT, preferred_element_type=F32)


def sigmoid(values):
    return 0.5 * jnp.tanh(0.5 * values) + 0.5


def cost(microseconds):
    return pl.CostEstimate(
        flops=int(microseconds * 1e9), bytes_accessed=int(microseconds * 1e6), transcendentals=0
    )


def params(megabytes, *semantics):
    return pltpu.CompilerParams(
        dimension_semantics=semantics or None, vmem_limit_bytes=megabytes * 1024 * 1024
    )


def fold(values, combine):
    while values.shape[0] > 8:
        half = values.shape[0] // 2
        values = combine(values[:half], values[half:])
    return values


def top_rows(values):
    return jnp.max(fold(values, jnp.maximum), axis=0, keepdims=True)


def sum_rows(values):
    return jnp.sum(fold(values, jnp.add), axis=0, keepdims=True)


def normalise_rows(values):
    count = values.shape[0]
    centred = values - sum_rows(values) * (1.0 / count)
    variance = sum_rows(centred * centred) * (1.0 / count)
    return (centred * lax.rsqrt(variance + EPS)).astype(BF16)


def standardised_column(first_rows, second_rows, n, residues):
    seqs = first_rows.shape[0] // residues
    rows = pl.ds(n, seqs, stride=residues)
    column = jnp.concatenate([first_rows[rows, :], second_rows[rows, :]], axis=1)
    centred = column - jnp.mean(column, axis=1, keepdims=True)
    variance = jnp.mean(centred * centred, axis=1, keepdims=True) + EPS
    scale = lax.rsqrt(variance)
    return centred * scale, variance * scale


def high_kernel(sources_ref, block_hbm, *rest):
    *pieces_hbm, first_ref, second_ref, high_ref, fetched, sent = rest
    seqs, residues, lanes = first_ref.shape
    own = residues // len(pieces_hbm)
    step = 16
    fetches, sends = [], []
    for s in range(0, seqs, step):
        chosen = pl.ds(s, step)
        for half, ref in enumerate((first_ref, second_ref)):
            source = block_hbm.at[chosen, :, pl.ds(half * lanes, lanes)]
            fetches.append(
                pltpu.make_async_copy(source, ref.at[chosen], fetched.at[len(fetches)])
            )
            fetches[-1].start()
    for part in range(seqs // step):
        chosen = pl.ds(part * step, step)
        fetches[2 * part].wait()
        fetches[2 * part + 1].wait()
        first_rows = first_ref.at[chosen].reshape(step * residues, lanes)
        second_rows = second_ref.at[chosen].reshape(step * residues, lanes)
        for n in range(residues):
            normed, _ = standardised_column(first_rows, second_rows, n, residues)
            high_ref[part, n] = normed.astype(BF16)
        for p, piece_hbm in enumerate(pieces_hbm):
            source = high_ref.at[part, pl.ds(sources_ref[p] * own, own)]
            sends.append(
                pltpu.make_async_copy(source, piece_hbm.at[:, chosen], sent.at[len(sends)])
            )
            sends[-1].start()
    for send in sends:
        send.wait()


def standardise_high(sources, block):
    seqs, residues, depth = block.shape
    half = depth // 2
    count = sources.shape[0]
    hbm = pl.BlockSpec(memory_space=pltpu.HBM)
    return pl.pallas_call(
        high_kernel,
        in_specs=[pl.BlockSpec(memory_space=pltpu.SMEM), hbm],
        out_specs=[hbm] * count,
        out_shape=[pltpu.HBM((residues // count, seqs, depth), BF16)] * count,
        scratch_shapes=[
            pltpu.VMEM((seqs, residues, half), F32),
            pltpu.VMEM((seqs, residues, half), F32),
            pltpu.VMEM((seqs // 16, residues, 16, depth), BF16),
            pltpu.SemaphoreType.DMA((seqs // 8,)),
            pltpu.SemaphoreType.DMA((seqs // 16 * count,)),
        ],
        compiler_params=params(10),
        cost_estimate=cost(3),
        name="standardise_high",
    )(sources, pltpu.with_memory_space_constraint(block, pltpu.HBM))


def low_kernel(sources_ref, first_ref, second_ref, *rest):
    *pieces_hbm, low_ref, sent = rest
    seqs, residues, lanes = first_ref.shape
    own = residues // len(pieces_hbm)
    first_rows = first_ref.reshape(seqs * residues, lanes)
    second_rows = second_ref.reshape(seqs * residues, lanes)
    lane = lax.broadcasted_iota(jnp.int32, (seqs, 128), 1)
    for p in range(len(pieces_hbm)):
        spreads = jnp.zeros((seqs, 128), F32)
        for n in range(own):
            normed, spread = standardised_column(first_rows, second_rows, p * own + n, residues)
            left = (normed - normed.astype(BF16).astype(F32)).astype(BF16)
            low_ref[p, n * seqs : (n + 1) * seqs, :] = left
            spreads = jnp.where(lane == n, spread, spreads)
        spreads = spreads.T[:8, :]
        coarse = spreads.astype(BF16).astype(F32)
        kept = jnp.concatenate([coarse, spreads - coarse], axis=0)
        kept = jnp.concatenate([kept, jnp.zeros((16, 2 * lanes - seqs), F32)], axis=1)
        low_ref[p, own * seqs :, :] = kept.astype(BF16)
    sends = []
    for p, piece_hbm in enumerate(pieces_hbm):
        source = low_ref.at[sources_ref[p]]
        sends.append(pltpu.make_async_copy(source, piece_hbm, sent.at[p]))
        sends[-1].start()
    for send in sends:
        send.wait()


def standardise_low(sources, block):
    seqs, residues, depth = block.shape
    half = depth // 2
    count = sources.shape[0]
    height = residues // count * seqs + 16
    hbm = pl.BlockSpec(memory_space=pltpu.HBM)
    return pl.pallas_call(
        low_kernel,
        grid=(1,),
        in_specs=[
            pl.BlockSpec(memory_space=pltpu.SMEM),
            pl.BlockSpec((seqs, residues, half), lambda g: (0, 0, 0)),
            pl.BlockSpec((seqs, residues, half), lambda g: (0, 0, 1)),
        ],
        out_specs=[hbm] * count,
        out_shape=[pltpu.HBM((height, depth), BF16)] * count,
        scratch_shapes=[
            pltpu.VMEM((count, height, depth), BF16),
            pltpu.SemaphoreType.DMA((count,)),
        ],
        compiler_params=params(14, "arbitrary"),
        cost_estimate=cost(4),
        name="standardise_low",
    )(sources, block, block)


def attention_kernel(key_ref, others_ref, *rest):
    *refs, scores_ref, weights_ref = rest
    blocks = len(refs) // 2
    normed_refs, turned_ref, gated_refs = refs[:blocks], refs[blocks], refs[blocks + 1 :]
    residues, seqs, _ = normed_refs[0].shape
    total = blocks * seqs
    inner = ATTENTION_UNITS * UNIT_WIDTH
    ring = scores_ref.shape[0]
    columns = []

    def project(n):
        column = jnp.concatenate([ref[n] for ref in normed_refs], axis=0)
        key_rows = matmul(column, key_ref[...]).astype(BF16)
        projected = matmul_nt(others_ref[...], column)
        queries = (projected[:inner] * UNIT_WIDTH ** (-0.5)).astype(BF16)
        value_rows = projected[inner : 2 * inner].astype(BF16)
        gates = sigmoid(projected[2 * inner :])
        columns.append((key_rows, queries, value_rows, gates))
    units = [(n, h) for n in range(residues) for h in range(ATTENTION_UNITS)]

    def score(unit):
        n, h = units[unit]
        key_rows, queries, _, _ = columns[n]
        low, high = h * UNIT_WIDTH, (h + 1) * UNIT_WIDTH
        pieces = [queries[low:high]]
        if low > 0:
            pieces.insert(0, jnp.zeros((low, total), BF16))
        if high < inner:
            pieces.append(jnp.zeros((inner - high, total), BF16))
        scores_ref[unit % ring] = matmul(key_rows, jnp.concatenate(pieces, axis=0))

    def weigh(unit):
        for low in range(0, total, 128):
            scores = scores_ref[unit % ring, :, low : low + 128]
            weights = jnp.exp(scores - top_rows(scores))
            scale = 1.0 / sum_rows(weights)
            weights_ref[unit % ring, :, low : low + 128] = (weights * scale).astype(BF16)

    def attend(unit):
        n, h = units[unit]
        _, _, value_rows, gates = columns[n]
        rows = slice(h * UNIT_WIDTH, (h + 1) * UNIT_WIDTH)
        attended = matmul(value_rows[rows], weights_ref[unit % ring]) * gates[rows]
        turned_ref[n, rows, :] = attended.astype(BF16)

    def turn_back(n):
        back = turned_ref[n].T
        for block, gated_ref in enumerate(gated_refs):
            gated_ref[n] = back[block * seqs : (block + 1) * seqs]

    project(0)
    for step in range(len(units) + 2):
        if step < len(units):
            score(step)
            n, h = units[step]
            if h == ATTENTION_UNITS // 2 and n + 1 < residues:
                project(n + 1)
        if 1 <= step <= len(units):
            weigh(step - 1)
        if step >= 2:
            attend(step - 2)
            n, h = units[step - 2]
            if h == ATTENTION_UNITS - 1:
                turn_back(n)


def attention(normed, key_matrix, other_matrices):
    blocks = len(normed)
    residues, seqs, depth = normed[0].shape
    total = blocks * seqs
    inner = ATTENTION_UNITS * UNIT_WIDTH
    step = 4
    return pl.pallas_call(
        attention_kernel,
        grid=(residues // step,),
        in_specs=[
            pl.BlockSpec((depth, inner), lambda n: (0, 0)),
            pl.BlockSpec((3 * inner, depth), lambda n: (0, 0)),
        ]
        + [pl.BlockSpec((step, seqs, depth), lambda n: (n, 0, 0))] * blocks,
        out_specs=[pl.BlockSpec((step, inner, total), lambda n: (n, 0, 0))]
        + [pl.BlockSpec((step, seqs, inner), lambda n: (n, 0, 0))] * blocks,
        out_shape=[jax.ShapeDtypeStruct((residues, inner, total), BF16)]
        + [pltpu.HBM((residues, seqs, inner), BF16)] * blocks,
        scratch_shapes=[
            pltpu.VMEM((4, total, total), F32),
            pltpu.VMEM((4, total, total), BF16),
        ],
        compiler_params=params(12 + (total // 128) ** 2, "arbitrary"),
        cost_estimate=cost(10),
        name="attention",
    )(key_matrix, other_matrices, *normed)


def alignment_kernel(sources_ref, turned_ref, final_ref, entry_ref, *rest):
    *refs, left_ref, right_ref, rows_ref = rest
    blocks = len(refs) // 3
    high_refs, low_refs, spread_refs = refs[:blocks], refs[blocks : 2 * blocks], refs[2 * blocks :]
    residues, seqs, depth = high_refs[0].shape
    total = blocks * seqs
    features = TENSOR_FEATURES
    step = pl.program_id(0)
    for n in range(residues):
        column = jnp.concatenate([ref[n] for ref in high_refs], axis=0).astype(F32)
        column = column + jnp.concatenate(
            [ref[n * seqs : (n + 1) * seqs, :] for ref in low_refs], axis=0
        ).astype(F32)
        spreads = []
        for ref in spread_refs:
            kept = ref[:, :seqs].astype(F32)
            row = lax.broadcasted_iota(jnp.int32, kept.shape, 0)
            chosen = lax.rem(row, 8) == step * residues + n
            spreads.append(jnp.sum(jnp.where(chosen, kept, 0.0), axis=0, keepdims=True))
        spread = jnp.concatenate(spreads, axis=1)
        updated = column.T * spread + matmul(final_ref[...], turned_ref[n])
        projected = matmul(entry_ref[...], normalise_rows(updated))
        me = sources_ref[0]
        tiles = [projected[:, low : low + 128] for low in range(0, total, 128)]
        odd = lax.rem(me, 2) == 1
        tiles = [jnp.where(odd, pltpu.roll(tile, seqs, 1), tile) for tile in tiles]
        width = 1
        while width < len(tiles):
            crossed = lax.rem(lax.div(me, 2 * width), 2) == 1
            tiles = [
                jnp.where(crossed, tiles[t ^ width], tiles[t]) for t in range(len(tiles))
            ]
            width *= 2
        first = pl.multiple_of((step * residues + n) * features, features)
        for t, tile in enumerate(tiles):
            right_ref[n, :, t * 128 : (t + 1) * 128] = tile[features:].astype(BF16)
            rows_ref[t, pl.ds(first, features), :] = tile[:features]

    @pl.when(step == pl.num_programs(0) - 1)
    def _():
        count = rows_ref.shape[1] // features
        together = max(1, 16 // count)
        for c in range(0, features, together):
            pieces = []
            for e in range(together):
                chosen = pl.ds(c + e, count, stride=features)
                tiles = [rows_ref[tile, chosen, :] for tile in range(total // 128)]
                pieces.append(jnp.concatenate(tiles, axis=1))
            piece = jnp.concatenate(pieces, axis=0).astype(BF16)
            left_ref[c * count : (c + together) * count, :] = piece


def alignment(sources, high, low, turned, final_matrix, entry_matrices):
    blocks = len(high)
    residues, seqs, depth = high[0].shape
    total = blocks * seqs
    features = TENSOR_FEATURES
    step = 4
    height = residues * seqs + 16
    return pl.pallas_call(
        alignment_kernel,
        grid=(residues // step,),
        in_specs=[
            pl.BlockSpec(memory_space=pltpu.SMEM),
            pl.BlockSpec((step, depth, total), lambda n: (n, 0, 0)),
            pl.BlockSpec(final_matrix.shape, lambda n: (0, 0)),
            pl.BlockSpec(entry_matrices.shape, lambda n: (0, 0)),
        ]
        + [pl.BlockSpec((step, seqs, depth), lambda n: (n, 0, 0))] * blocks
        + [pl.BlockSpec((step * seqs, depth), lambda n: (n, 0))] * blocks
        + [pl.BlockSpec((16, depth), lambda n: (height // 16 - 1, 0))] * blocks,
        out_specs=[
            pl.BlockSpec((features * residues, total), lambda n: (0, 0)),
            pl.BlockSpec((step, features, total), lambda n: (n, 0, 0)),
        ],
        out_shape=[
            jax.ShapeDtypeStruct((features * residues, total), BF16),
            jax.ShapeDtypeStruct((residues, features, total), BF16),
        ],
        scratch_shapes=[pltpu.VMEM((total // 128, residues * features, 128), F32)],
        compiler_params=params(16, "arbitrary"),
        cost_estimate=cost(4),
        name="alignment",
    )(sources, turned, final_matrix, entry_matrices, *high, *low, *low)


def pair_kernel(places_ref, *rest, slots, pieces):
    *refs, outer_ref, spread_ref, sum_ref, rows_ref, near_ref, far_ref, mids_ref, gates_ref = rest[:-2]
    sides_ref, copied = rest[-2:]
    left_refs, right_refs = refs[:slots], refs[slots : slots + pieces]
    rights_ref, weights_ref, entry_ref, switch_ref = refs[slots + pieces : slots + pieces + 4]
    near_hbm, far_hbm, mid_hbm, gate_hbm, away_hbm, sides_hbm = refs[slots + pieces + 4 :]
    features = TENSOR_FEATURES
    piece_rows, total = left_refs[0].shape
    residues = piece_rows // features
    rows = slots * residues
    share = right_refs[0].shape[0]
    columns = pieces * share
    groups = 2 * columns // GROUP
    wide = share * features
    together = spread_ref.shape[1] // 64
    core = places_ref[slots + pieces]
    fetches = []
    for source, target in ((near_hbm, near_ref), (far_hbm, far_ref)):
        fetches.append(pltpu.make_async_copy(source, target, copied.at[len(fetches)]))
        fetches[-1].start()
    copies = []

    def send(source, target):
        copies.append(pltpu.make_async_copy(source, target, copied.at[len(copies) + 2]))
        copies[-1].start()

    left = jnp.concatenate([ref[...] for ref in left_refs], axis=0)
    for p in range(2 * pieces):
        right = right_refs[p][...] if p < pieces else rights_ref[p - pieces]
        outer = matmul_nt(left, right.reshape(wide, total)) * (1.0 / total)
        outer_ref[:, p * wide : (p + 1) * wide] = outer

    spread_ref[...] = jnp.zeros_like(spread_ref)
    front = lax.broadcasted_iota(jnp.int32, (rows, 128), 1) < 64

    def channel_step(p, carry):
        slot = lax.rem(p, 2)
        for e in range(together):
            source = pl.multiple_of((p * together + e) * features, features)
            piece = weights_ref[pl.ds(source, features), :]
            for place in range(2):
                low = e * 64 + place * features
                spread_ref[slot, low : low + features, place * C_Z : (place + 1) * C_Z] = piece
        blocks = []
        for g in range(groups):
            parts = []
            for e in range(together):
                channel = []
                for slot_number in range(slots):
                    first = slot_number * piece_rows + (p * together + e) * residues
                    source = pl.ds(pl.multiple_of(first, residues), residues)
                    channel.append(outer_ref[source, g * 128 : (g + 1) * 128])
                parts.append(jnp.concatenate(channel, axis=0).astype(BF16))
            lows, highs = [], []
            for e in range(0, together, 2):
                lows.append(jnp.where(front, parts[e], pltpu.roll(parts[e + 1], 64, 1)))
                highs.append(jnp.where(front, pltpu.roll(parts[e], 64, 1), parts[e + 1]))
            blocks.append(jnp.concatenate(lows, axis=1))
            blocks.append(jnp.concatenate(highs, axis=1))
        update = matmul(jnp.concatenate(blocks, axis=0), spread_ref[slot])

        @pl.when(p == 0)
        def _():
            sum_ref[...] = update

        @pl.when(p > 0)
        def _():
            sum_ref[...] += update

        return carry

    lax.fori_loop(0, features // together, channel_step, 0)

    left_firsts = [places_ref[j] * residues for j in range(slots)]
    right_firsts = [places_ref[slots + p] for p in range(pieces)]
    for fetch in fetches:
        fetch.wait()
    for g in range(groups // 2):
        normed, places = [], []
        for place in range(GROUP):
            p, n = divmod(g * GROUP + place, share)
            b = right_firsts[p] + n
            places.append(b)
            for side in range(2):
                lanes = slice(place % 2 * C_Z, (place % 2 + 1) * C_Z)
                start = ((g + side * groups // 2) * 2 + place // 2) * rows
                parts = []
                for first in left_firsts:
                    source = pl.ds(pl.multiple_of(start + first, residues), residues)
                    parts.append(sum_ref[source, lanes])
                mid = jnp.concatenate(parts, axis=0)
                if side == 0:
                    mid = mid + near_ref[pl.ds(core * rows * columns + b, rows, stride=columns), :]
                else:
                    mid = mid + far_ref[pl.ds(b, rows, stride=columns), :]
                mids_ref[side, g * GROUP + place] = mid
                centred = mid - jnp.mean(mid, axis=1, keepdims=True)
                variance = jnp.mean(centred * centred, axis=1, keepdims=True)
                normed.append((centred * lax.rsqrt(variance + EPS)).astype(BF16))
        gates = sigmoid(matmul(jnp.concatenate(normed, axis=0), switch_ref[...]))
        for place in range(GROUP):
            for side in range(2):
                first = (2 * place + side) * rows
                gates_ref[side, g * GROUP + place] = gates[first : first + rows]
        blank = jnp.zeros_like(normed[0])
        for place in range(0, GROUP, 2):
            twice = []
            for piece in normed[2 * place : 2 * place + 4]:
                twice.append(jnp.concatenate([piece, blank], axis=1))
                twice.append(jnp.concatenate([blank, piece], axis=1))
            sides = matmul_nt(entry_ref[...], jnp.concatenate(twice, axis=0))
            sides = sigmoid(sides[C_TRI:]) * sides[:C_TRI]
            for e in range(2):
                first = pl.multiple_of(places[place + e] * C_TRI, C_TRI)
                rows_ref[pl.ds(first, C_TRI), :] = sides[:, e * 4 * rows : (e + 1) * 4 * rows]

        if (g + 1) * GROUP % share == 0:
            p = (g + 1) * GROUP // share - 1
            source, target = pl.ds(p * share, share), pl.ds(right_firsts[p], share)
            send(mids_ref.at[0, source], mid_hbm.at[target])
            send(gates_ref.at[0, source], gate_hbm.at[target])
            send(mids_ref.at[1, source], away_hbm.at[0, target])
            send(gates_ref.at[1, source], away_hbm.at[1, target])

    cut = C_TRI // 4
    for part in range(4):

        def turn_step(c, carry):
            sides_ref[c] = rows_ref[pl.ds(c, columns, stride=C_TRI), :].astype(BF16)
            return carry

        lax.fori_loop(part * cut, (part + 1) * cut, turn_step, 0, unroll=8)
        chosen = pl.ds(part * cut, cut)
        send(sides_ref.at[chosen], sides_hbm.at[chosen])
    for copy in copies:
        copy.wait()


def pair_update(places, lefts, rights, far_rights, weights, near, far, entry, switch):
    all_rows, columns, depth = near.shape
    rows = all_rows // 2
    whole = (columns, rows, depth)
    sides = (C_TRI, columns, 4 * rows)
    smem = pl.BlockSpec(memory_space=pltpu.SMEM)
    vmem = pl.BlockSpec(memory_space=pltpu.VMEM)
    anywhere = pl.BlockSpec(memory_space=pl.ANY)
    return pl.pallas_call(
        functools.partial(pair_kernel, slots=len(lefts), pieces=len(rights)),
        in_specs=[smem] + [vmem] * (4 + len(lefts) + len(rights)) + [anywhere] * 2,
        out_specs=[anywhere] * 4,
        out_shape=[
            pltpu.HBM(whole, F32),
            pltpu.HBM(whole, F32),
            pltpu.HBM((2,) + whole, F32),
            pltpu.HBM(sides, BF16),
        ],
        scratch_shapes=[
            pltpu.VMEM((rows * TENSOR_FEATURES, 2 * columns * TENSOR_FEATURES), F32),
            pltpu.VMEM((2, 8 * 64, 2 * depth), BF16),
            pltpu.VMEM((columns * rows, 2 * depth), F32),
            pltpu.VMEM((columns * C_TRI, 4 * rows), F32),
            pltpu.VMEM((all_rows * columns, depth), F32),
            pltpu.VMEM((rows * columns, depth), F32),
            pltpu.VMEM((2,) + whole, F32),
            pltpu.VMEM((2,) + whole, F32),
            pltpu.VMEM(sides, BF16),
            pltpu.SemaphoreType.DMA((4 * len(rights) + 6,)),
        ],
        compiler_params=params(32),
        cost_estimate=cost(10),
        name="pair_update",
    )(
        places,
        *lefts,
        *rights,
        far_rights,
        weights,
        entry,
        switch,
        near.reshape(all_rows * columns, depth),
        far.reshape(rows * columns, depth),
    )


def product_kernel(sides_ref, out_ref, *, grid_rows, grid_columns):
    channels, part, lanes = sides_ref.shape[1:]
    half, quarter = lanes // 2, lanes // 4
    places = grid_columns // 2
    lane = lax.broadcasted_iota(jnp.int32, (places * part, lanes), 1)
    front = lane < half
    cut = front[: part // 2]
    quarters = [(lane >= t * quarter) & (lane < (t + 1) * quarter) for t in range(3)]
    for channel in range(channels):
        lefts, rights = [], []
        for r in range(0, grid_rows, 2):
            turned = []
            for target in range(4):
                row, core = r + target // 2, target % 2
                tile = jnp.concatenate(
                    [
                        sides_ref[row * grid_columns + 2 * place + core, channel]
                        for place in range(places)
                    ],
                    axis=0,
                )
                turned.append(
                    [tile] + [pltpu.roll(tile, t * quarter, 1) for t in range(1, 4)]
                )
            for side, made in enumerate((lefts, rights)):
                by_core = []
                for core in range(2):
                    chosen = []
                    for target in range(4):
                        source = 2 * int(target % 2 != core) + side
                        chosen.append(turned[target][(target - source) % 4])
                    tile = chosen[3]
                    for t in range(3):
                        tile = jnp.where(quarters[t], chosen[t], tile)
                    by_core.append(tile)
                blocks = []
                for place in range(places):
                    for core in range(2):
                        blocks.append(by_core[core][place * part : (place + 1) * part])
                made.append(jnp.concatenate(blocks, axis=0))
        product = matmul_nt(jnp.concatenate(rights, axis=1), jnp.concatenate(lefts, axis=1))
        product = product.astype(BF16)
        for c in range(grid_columns):
            for r in range(0, grid_rows, 2):
                block = product[c * part : (c + 1) * part, r * half : (r + 2) * half]
                top, bottom = block[: part // 2], block[part // 2 :]
                even = jnp.where(cut, top, pltpu.roll(bottom, half, 1))
                out_ref[r * grid_columns + c, channel] = even
                odd = jnp.where(cut, pltpu.roll(top, half, 1), bottom)
                out_ref[(r + 1) * grid_columns + c, channel] = odd


def triangle_product(sides, grid_rows, grid_columns):
    devices, channels, part, lanes = sides.shape
    step = 2 if channels % 2 == 0 else 1
    return pl.pallas_call(
        functools.partial(product_kernel, grid_rows=grid_rows, grid_columns=grid_columns),
        grid=(channels // step,),
        in_specs=[pl.BlockSpec((devices, step, part, lanes), lambda c: (0, c, 0, 0))],
        out_specs=pl.BlockSpec((devices, step, part // 2, lanes), lambda c: (0, c, 0, 0)),
        out_shape=pltpu.HBM((devices, channels, part // 2, lanes), BF16),
        compiler_params=params(8, "arbitrary"),
        cost_estimate=cost(3),
        name="triangle_product",
    )(sides)


def output_kernel(
    core_ref, product_ref, final_ref, mid_hbm, gate_hbm, far_hbm, out_hbm, wide_ref, kept_ref, out_ref, *copied
):
    channels, part, lanes = product_ref.shape
    _, _, columns, rows, depth = kept_ref.shape
    own = 8
    core = core_ref[0]
    fetched, sent = copied
    fetches, sends = [], []
    for first in range(0, columns, own):
        chosen = pl.ds(first, own)
        for kind, near_hbm in enumerate((mid_hbm, gate_hbm)):
            for source, half in ((near_hbm, core), (far_hbm.at[kind], 1 - core)):
                fetches.append(
                    pltpu.make_async_copy(
                        source.at[chosen],
                        kept_ref.at[kind, half, chosen],
                        fetched.at[len(fetches)],
                    )
                )
                fetches[-1].start()
    wide_ref[...] = product_ref[...].astype(F32).reshape(channels * part, lanes)
    for group in range(part // own):
        updates = []
        for j in range(own):
            product = wide_ref[pl.ds(group * own + j, channels, stride=part), :]
            updates.append(matmul(normalise_rows(product).T, final_ref[...]))
        for half in range(2):
            cut = half * (part // own) + group
            for fetch in fetches[4 * cut : 4 * cut + 4]:
                fetch.wait()
            out_rows = out_ref.at[cut].reshape(2 * rows * own, depth)
            for j in range(own):
                b = cut * own + j
                for side in range(2):
                    first = (2 * half + side) * rows
                    piece = kept_ref[1, side, b] * updates[j][first : first + rows]
                    target = pl.ds(side * rows * own + j, rows, stride=own)
                    out_rows[target, :] = kept_ref[0, side, b] + piece
            sends.append(
                pltpu.make_async_copy(
                    out_ref.at[cut], out_hbm.at[:, pl.ds(cut * own, own)], sent.at[len(sends)]
                )
            )
            sends[-1].start()
    for send in sends:
        send.wait()


def pair_result(core, product, mid, gate, far, final_matrix):
    channels, part, lanes = product.shape
    columns, rows, depth = mid.shape
    smem = pl.BlockSpec(memory_space=pltpu.SMEM)
    vmem, hbm = pl.BlockSpec(memory_space=pltpu.VMEM), pl.BlockSpec(memory_space=pltpu.HBM)
    return pl.pallas_call(
        output_kernel,
        in_specs=[smem, vmem, vmem, hbm, hbm, hbm],
        out_specs=hbm,
        out_shape=pltpu.HBM((2 * rows, columns, depth), F32),
        scratch_shapes=[
            pltpu.VMEM((channels * part, lanes), F32),
            pltpu.VMEM((2, 2, columns, rows, depth), F32),
            pltpu.VMEM((columns // 8, 2 * rows, 8, depth), F32),
            pltpu.SemaphoreType.DMA((columns // 2,)),
            pltpu.SemaphoreType.DMA((columns // 8,)),
        ],
        compiler_params=params(16),
        cost_estimate=cost(3),
        name="pair_result",
    )(
        core,
        product,
        final_matrix,
        pltpu.with_memory_space_constraint(mid, pltpu.HBM),
        pltpu.with_memory_space_constraint(gate, pltpu.HBM),
        pltpu.with_memory_space_constraint(far, pltpu.HBM),
    )


def swap_cores(block):
    count = lax.axis_size("col")
    return lax.ppermute(block, "col", [(c, c ^ 1) for c in range(count)])


def gather_turned(block, later):
    rows, columns = lax.axis_size("row"), lax.axis_size("col")
    arrived = []
    for shift in range(rows):
        moves = []
        for r in range(rows):
            for q in range(rows):
                for core in range(2):
                    source = r * columns + 2 * q + core
                    moves.append((source, q * columns + 2 * ((r + shift) % rows) + core))
        source = block if shift < 2 else later
        arrived.append(lax.ppermute(source, ("row", "col"), moves))
    residues = block.shape[0] // TENSOR_FEATURES
    if residues % 8 == 0:
        return arrived
    joined = 8 // residues
    own = jnp.take(jnp.stack(arrived), left_order(), axis=0)
    own = own.reshape(rows // joined, joined, TENSOR_FEATURES, residues, -1)
    own = jnp.transpose(own, (0, 2, 1, 3, 4))
    return list(own.reshape(rows // joined, joined * block.shape[0], -1))


def left_order():
    rows = lax.axis_size("row")
    me = lax.axis_index("col") // 2
    return lax.rem(me - jnp.arange(rows, dtype=jnp.int32) + rows, rows)


def pair_places(sources, residues):
    if residues % 8:
        order = jnp.arange(lax.axis_size("row") * residues // 8, dtype=jnp.int32)
    else:
        order = left_order()
    core = lax.rem(lax.axis_index("col"), 2)
    return order, sources * residues, core.astype(jnp.int32).reshape(1)


def exchange_rows(pieces):
    arrived = [pieces[0]]
    for shift in range(1, len(pieces)):
        moves = [(r, r ^ shift) for r in range(len(pieces))]
        arrived.append(lax.ppermute(pieces[shift], "row", moves))
    return arrived


def paired_entries(matrices):
    turned = matrices.reshape(C_Z, 2, 2, C_TRI)
    return jnp.transpose(turned, (2, 3, 1, 0)).reshape(2 * C_TRI, 2 * C_Z)


def body(
    homolog_tensor,
    couplings,
    attention_probe_matrix,
    attention_extra_matrices,
    attention_final_matrix,
    tensor_entry_matrices,
    tensor_final_matrix,
    incoming_entry_matrices,
    incoming_switch_matrix,
    incoming_final_matrix,
):
    inner = ATTENTION_UNITS * UNIT_WIDTH
    row_count = lax.axis_size("row")
    seqs, residues, depth = homolog_tensor.shape
    own_residues = residues // row_count
    sources = lax.axis_index("row") ^ jnp.arange(row_count, dtype=jnp.int32)
    high = exchange_rows(standardise_high(sources, homolog_tensor))
    low = standardise_low(sources, homolog_tensor)
    others = jnp.concatenate(
        [attention_probe_matrix.T, attention_extra_matrices[:, inner:].T], axis=0
    )
    early = (
        attention_extra_matrices[:, :inner],
        others,
        attention_final_matrix.T,
        tensor_entry_matrices.T,
        paired_entries(incoming_entry_matrices),
        *pair_places(sources, own_residues),
    )
    high, low, early = lax.optimization_barrier((high, low, early))
    key_matrix, others, final_turned, tensor_turned, entries, slots, firsts, core = early
    low = exchange_rows(low)
    turned, *gated = attention(high, key_matrix, others)
    left_piece, right_piece = alignment(
        sources, high, low, turned, final_turned, tensor_turned
    )

    rights = exchange_rows([right_piece] * row_count)
    later, rights[1] = lax.optimization_barrier((left_piece, rights[1]))
    lefts = gather_turned(left_piece, later)
    far_rights = swap_cores(jnp.stack(rights))
    half = couplings.shape[0] // 2
    far = lax.dynamic_slice_in_dim(couplings, (1 - core[0]) * half, half)
    far, rights[1] = lax.optimization_barrier((far, rights[1]))
    far = swap_cores(far)
    mid, gate, away, sides = pair_update(
        jnp.concatenate([slots, firsts, core]),
        lefts,
        rights,
        far_rights,
        tensor_final_matrix,
        couplings,
        far,
        entries,
        incoming_switch_matrix,
    )
    gated, away, sides = lax.optimization_barrier((gated, away, sides))
    away = swap_cores(away)
    gated = exchange_rows(gated)

    everywhere = ("row", "col")
    column_count = lax.axis_size("col")
    devices = row_count * column_count
    sides = sides.reshape(devices, C_TRI // devices, *sides.shape[1:])
    sides = lax.all_to_all(sides, everywhere, split_axis=0, concat_axis=0)
    gated, away, sides = lax.optimization_barrier((gated, away, sides))
    product = triangle_product(sides, row_count, column_count)
    product = lax.all_to_all(product, everywhere, split_axis=0, concat_axis=0)

    gated = jnp.take(jnp.stack(gated), sources, axis=0)
    gated = jnp.transpose(gated.reshape(residues, seqs, inner), (1, 0, 2))
    change = jnp.dot(
        gated.reshape(-1, inner), attention_final_matrix, preferred_element_type=F32
    )
    refreshed_homologs = homolog_tensor + change.reshape(homolog_tensor.shape)
    product = product.reshape(C_TRI, *product.shape[2:])
    pair_output = pair_result(core, product, mid, gate, away, incoming_final_matrix)
    return (refreshed_homologs, pair_output)


def solution(mesh):
    in_specs = (
        P("row", "col", None),
        P("row", "col", None),
        P(),
        P(),
        P(),
        P(),
        P(),
        P(),
        P(),
        P(),
    )
    out_specs = (P("row", "col", None), P("row", "col", None))
    return jax.shard_map(body, mesh=mesh, in_specs=in_specs, out_specs=out_specs, check_vma=False)
```

```python
import functools

import jax
import jax.numpy as jnp
from jax import lax
from jax.experimental import pallas as pl
from jax.experimental.pallas import tpu as pltpu
from jax.sharding import PartitionSpec as P

FEATURE_DEPTH = 256
C_Z = 128
TENSOR_FEATURES = 32
C_TRI = 128
ATTENTION_UNITS = 8
UNIT_WIDTH = 32
EPS = 1e-05
GROUP = 4
F32 = jnp.float32
BF16 = jnp.bfloat16
NT = (((1,), (1,)), ((), ()))


def matmul(left, right):
    return jnp.dot(left, right, preferred_element_type=F32)


def matmul_nt(left, right):
    return lax.dot_general(left, right, NT, preferred_element_type=F32)


def sigmoid(values):
    return 0.5 * jnp.tanh(0.5 * values) + 0.5


def cost(microseconds):
    return pl.CostEstimate(
        flops=int(microseconds * 1e9), bytes_accessed=int(microseconds * 1e6), transcendentals=0
    )


def params(megabytes, *semantics):
    return pltpu.CompilerParams(
        dimension_semantics=semantics or None, vmem_limit_bytes=megabytes * 1024 * 1024
    )


def fold(values, combine):
    while values.shape[0] > 8:
        half = values.shape[0] // 2
        values = combine(values[:half], values[half:])
    return values


def top_rows(values):
    return jnp.max(fold(values, jnp.maximum), axis=0, keepdims=True)


def sum_rows(values):
    return jnp.sum(fold(values, jnp.add), axis=0, keepdims=True)


def normalise_rows(values):
    count = values.shape[0]
    centred = values - sum_rows(values) * (1.0 / count)
    variance = sum_rows(centred * centred) * (1.0 / count)
    return (centred * lax.rsqrt(variance + EPS)).astype(BF16)


def standardised_column(first_rows, second_rows, n, residues):
    seqs = first_rows.shape[0] // residues
    rows = pl.ds(n, seqs, stride=residues)
    column = jnp.concatenate([first_rows[rows, :], second_rows[rows, :]], axis=1)
    centred = column - jnp.mean(column, axis=1, keepdims=True)
    variance = jnp.mean(centred * centred, axis=1, keepdims=True) + EPS
    scale = lax.rsqrt(variance)
    return centred * scale, variance * scale


def high_kernel(sources_ref, block_hbm, *rest):
    *pieces_hbm, first_ref, second_ref, high_ref, fetched, sent = rest
    seqs, residues, lanes = first_ref.shape
    own = residues // len(pieces_hbm)
    step = 16
    fetches, sends = [], []
    for s in range(0, seqs, step):
        chosen = pl.ds(s, step)
        for half, ref in enumerate((first_ref, second_ref)):
            source = block_hbm.at[chosen, :, pl.ds(half * lanes, lanes)]
            fetches.append(
                pltpu.make_async_copy(source, ref.at[chosen], fetched.at[len(fetches)])
            )
            fetches[-1].start()
    for part in range(seqs // step):
        chosen = pl.ds(part * step, step)
        fetches[2 * part].wait()
        fetches[2 * part + 1].wait()
        first_rows = first_ref.at[chosen].reshape(step * residues, lanes)
        second_rows = second_ref.at[chosen].reshape(step * residues, lanes)
        for n in range(residues):
            normed, _ = standardised_column(first_rows, second_rows, n, residues)
            high_ref[part, n] = normed.astype(BF16)
        for p, piece_hbm in enumerate(pieces_hbm):
            source = high_ref.at[part, pl.ds(sources_ref[p] * own, own)]
            sends.append(
                pltpu.make_async_copy(source, piece_hbm.at[:, chosen], sent.at[len(sends)])
            )
            sends[-1].start()
    for send in sends:
        send.wait()


def standardise_high(sources, block):
    seqs, residues, depth = block.shape
    half = depth // 2
    count = sources.shape[0]
    hbm = pl.BlockSpec(memory_space=pltpu.HBM)
    return pl.pallas_call(
        high_kernel,
        in_specs=[pl.BlockSpec(memory_space=pltpu.SMEM), hbm],
        out_specs=[hbm] * count,
        out_shape=[pltpu.HBM((residues // count, seqs, depth), BF16)] * count,
        scratch_shapes=[
            pltpu.VMEM((seqs, residues, half), F32),
            pltpu.VMEM((seqs, residues, half), F32),
            pltpu.VMEM((seqs // 16, residues, 16, depth), BF16),
            pltpu.SemaphoreType.DMA((seqs // 8,)),
            pltpu.SemaphoreType.DMA((seqs // 16 * count,)),
        ],
        compiler_params=params(10),
        cost_estimate=cost(3),
        name="standardise_high",
    )(sources, pltpu.with_memory_space_constraint(block, pltpu.HBM))


def low_kernel(sources_ref, first_ref, second_ref, *rest):
    *pieces_hbm, low_ref, sent = rest
    seqs, residues, lanes = first_ref.shape
    own = residues // len(pieces_hbm)
    first_rows = first_ref.reshape(seqs * residues, lanes)
    second_rows = second_ref.reshape(seqs * residues, lanes)
    lane = lax.broadcasted_iota(jnp.int32, (seqs, 128), 1)
    for p in range(len(pieces_hbm)):
        spreads = jnp.zeros((seqs, 128), F32)
        for n in range(own):
            normed, spread = standardised_column(first_rows, second_rows, p * own + n, residues)
            left = (normed - normed.astype(BF16).astype(F32)).astype(BF16)
            low_ref[p, n * seqs : (n + 1) * seqs, :] = left
            spreads = jnp.where(lane == n, spread, spreads)
        spreads = spreads.T[:8, :]
        coarse = spreads.astype(BF16).astype(F32)
        kept = jnp.concatenate([coarse, spreads - coarse], axis=0)
        kept = jnp.concatenate([kept, jnp.zeros((16, 2 * lanes - seqs), F32)], axis=1)
        low_ref[p, own * seqs :, :] = kept.astype(BF16)
    sends = []
    for p, piece_hbm in enumerate(pieces_hbm):
        source = low_ref.at[sources_ref[p]]
        sends.append(pltpu.make_async_copy(source, piece_hbm, sent.at[p]))
        sends[-1].start()
    for send in sends:
        send.wait()


def standardise_low(sources, block):
    seqs, residues, depth = block.shape
    half = depth // 2
    count = sources.shape[0]
    height = residues // count * seqs + 16
    hbm = pl.BlockSpec(memory_space=pltpu.HBM)
    return pl.pallas_call(
        low_kernel,
        grid=(1,),
        in_specs=[
            pl.BlockSpec(memory_space=pltpu.SMEM),
            pl.BlockSpec((seqs, residues, half), lambda g: (0, 0, 0)),
            pl.BlockSpec((seqs, residues, half), lambda g: (0, 0, 1)),
        ],
        out_specs=[hbm] * count,
        out_shape=[pltpu.HBM((height, depth), BF16)] * count,
        scratch_shapes=[
            pltpu.VMEM((count, height, depth), BF16),
            pltpu.SemaphoreType.DMA((count,)),
        ],
        compiler_params=params(14, "arbitrary"),
        cost_estimate=cost(4),
        name="standardise_low",
    )(sources, block, block)


def attention_kernel(key_ref, others_ref, *rest):
    *refs, scores_ref, weights_ref = rest
    blocks = len(refs) // 2
    normed_refs, turned_ref, gated_refs = refs[:blocks], refs[blocks], refs[blocks + 1 :]
    residues, seqs, _ = normed_refs[0].shape
    total = blocks * seqs
    inner = ATTENTION_UNITS * UNIT_WIDTH
    ring = scores_ref.shape[0]
    columns = []

    def project(n):
        column = jnp.concatenate([ref[n] for ref in normed_refs], axis=0)
        key_rows = matmul(column, key_ref[...]).astype(BF16)
        projected = matmul_nt(others_ref[...], column)
        queries = (projected[:inner] * UNIT_WIDTH ** (-0.5)).astype(BF16)
        value_rows = projected[inner : 2 * inner].astype(BF16)
        gates = sigmoid(projected[2 * inner :])
        columns.append((key_rows, queries, value_rows, gates))
    units = [(n, h) for n in range(residues) for h in range(ATTENTION_UNITS)]

    def score(unit):
        n, h = units[unit]
        key_rows, queries, _, _ = columns[n]
        low, high = h * UNIT_WIDTH, (h + 1) * UNIT_WIDTH
        pieces = [queries[low:high]]
        if low > 0:
            pieces.insert(0, jnp.zeros((low, total), BF16))
        if high < inner:
            pieces.append(jnp.zeros((inner - high, total), BF16))
        scores_ref[unit % ring] = matmul(key_rows, jnp.concatenate(pieces, axis=0))

    def weigh(unit):
        for low in range(0, total, 128):
            scores = scores_ref[unit % ring, :, low : low + 128]
            weights = jnp.exp(scores - top_rows(scores))
            scale = 1.0 / sum_rows(weights)
            weights_ref[unit % ring, :, low : low + 128] = (weights * scale).astype(BF16)

    def attend(unit):
        n, h = units[unit]
        _, _, value_rows, gates = columns[n]
        rows = slice(h * UNIT_WIDTH, (h + 1) * UNIT_WIDTH)
        attended = matmul(value_rows[rows], weights_ref[unit % ring]) * gates[rows]
        turned_ref[n, rows, :] = attended.astype(BF16)

    def turn_back(n):
        back = turned_ref[n].T
        for block, gated_ref in enumerate(gated_refs):
            gated_ref[n] = back[block * seqs : (block + 1) * seqs]

    project(0)
    for step in range(len(units) + 2):
        if step < len(units):
            score(step)
            n, h = units[step]
            if h == ATTENTION_UNITS // 2 and n + 1 < residues:
                project(n + 1)
        if 1 <= step <= len(units):
            weigh(step - 1)
        if step >= 2:
            attend(step - 2)
            n, h = units[step - 2]
            if h == ATTENTION_UNITS - 1:
                turn_back(n)


def attention(normed, key_matrix, other_matrices):
    blocks = len(normed)
    residues, seqs, depth = normed[0].shape
    total = blocks * seqs
    inner = ATTENTION_UNITS * UNIT_WIDTH
    step = 4
    return pl.pallas_call(
        attention_kernel,
        grid=(residues // step,),
        in_specs=[
            pl.BlockSpec((depth, inner), lambda n: (0, 0)),
            pl.BlockSpec((3 * inner, depth), lambda n: (0, 0)),
        ]
        + [pl.BlockSpec((step, seqs, depth), lambda n: (n, 0, 0))] * blocks,
        out_specs=[pl.BlockSpec((step, inner, total), lambda n: (n, 0, 0))]
        + [pl.BlockSpec((step, seqs, inner), lambda n: (n, 0, 0))] * blocks,
        out_shape=[jax.ShapeDtypeStruct((residues, inner, total), BF16)]
        + [pltpu.HBM((residues, seqs, inner), BF16)] * blocks,
        scratch_shapes=[
            pltpu.VMEM((4, total, total), F32),
            pltpu.VMEM((4, total, total), BF16),
        ],
        compiler_params=params(12 + (total // 128) ** 2, "arbitrary"),
        cost_estimate=cost(10),
        name="attention",
    )(key_matrix, other_matrices, *normed)


def alignment_kernel(sources_ref, turned_ref, final_ref, entry_ref, *rest):
    *refs, left_ref, right_ref, rows_ref = rest
    blocks = len(refs) // 3
    high_refs, low_refs, spread_refs = refs[:blocks], refs[blocks : 2 * blocks], refs[2 * blocks :]
    residues, seqs, depth = high_refs[0].shape
    total = blocks * seqs
    features = TENSOR_FEATURES
    step = pl.program_id(0)
    for n in range(residues):
        column = jnp.concatenate([ref[n] for ref in high_refs], axis=0).astype(F32)
        column = column + jnp.concatenate(
            [ref[n * seqs : (n + 1) * seqs, :] for ref in low_refs], axis=0
        ).astype(F32)
        spreads = []
        for ref in spread_refs:
            kept = ref[:, :seqs].astype(F32)
            row = lax.broadcasted_iota(jnp.int32, kept.shape, 0)
            chosen = lax.rem(row, 8) == step * residues + n
            spreads.append(jnp.sum(jnp.where(chosen, kept, 0.0), axis=0, keepdims=True))
        spread = jnp.concatenate(spreads, axis=1)
        updated = column.T * spread + matmul(final_ref[...], turned_ref[n])
        projected = matmul(entry_ref[...], normalise_rows(updated))
        me = sources_ref[0]
        tiles = [projected[:, low : low + 128] for low in range(0, total, 128)]
        odd = lax.rem(me, 2) == 1
        tiles = [jnp.where(odd, pltpu.roll(tile, seqs, 1), tile) for tile in tiles]
        width = 1
        while width < len(tiles):
            crossed = lax.rem(lax.div(me, 2 * width), 2) == 1
            tiles = [
                jnp.where(crossed, tiles[t ^ width], tiles[t]) for t in range(len(tiles))
            ]
            width *= 2
        first = pl.multiple_of((step * residues + n) * features, features)
        for t, tile in enumerate(tiles):
            right_ref[n, :, t * 128 : (t + 1) * 128] = tile[features:].astype(BF16)
            rows_ref[t, pl.ds(first, features), :] = tile[:features]

    @pl.when(step == pl.num_programs(0) - 1)
    def _():
        count = rows_ref.shape[1] // features
        together = max(1, 16 // count)
        for c in range(0, features, together):
            pieces = []
            for e in range(together):
                chosen = pl.ds(c + e, count, stride=features)
                tiles = [rows_ref[tile, chosen, :] for tile in range(total // 128)]
                pieces.append(jnp.concatenate(tiles, axis=1))
            piece = jnp.concatenate(pieces, axis=0).astype(BF16)
            left_ref[c * count : (c + together) * count, :] = piece


def alignment(sources, high, low, turned, final_matrix, entry_matrices):
    blocks = len(high)
    residues, seqs, depth = high[0].shape
    total = blocks * seqs
    features = TENSOR_FEATURES
    step = 4
    height = residues * seqs + 16
    return pl.pallas_call(
        alignment_kernel,
        grid=(residues // step,),
        in_specs=[
            pl.BlockSpec(memory_space=pltpu.SMEM),
            pl.BlockSpec((step, depth, total), lambda n: (n, 0, 0)),
            pl.BlockSpec(final_matrix.shape, lambda n: (0, 0)),
            pl.BlockSpec(entry_matrices.shape, lambda n: (0, 0)),
        ]
        + [pl.BlockSpec((step, seqs, depth), lambda n: (n, 0, 0))] * blocks
        + [pl.BlockSpec((step * seqs, depth), lambda n: (n, 0))] * blocks
        + [pl.BlockSpec((16, depth), lambda n: (height // 16 - 1, 0))] * blocks,
        out_specs=[
            pl.BlockSpec((features * residues, total), lambda n: (0, 0)),
            pl.BlockSpec((step, features, total), lambda n: (n, 0, 0)),
        ],
        out_shape=[
            jax.ShapeDtypeStruct((features * residues, total), BF16),
            jax.ShapeDtypeStruct((residues, features, total), BF16),
        ],
        scratch_shapes=[pltpu.VMEM((total // 128, residues * features, 128), F32)],
        compiler_params=params(16, "arbitrary"),
        cost_estimate=cost(4),
        name="alignment",
    )(sources, turned, final_matrix, entry_matrices, *high, *low, *low)


def pair_kernel(
    left_slots_ref,
    right_firsts_ref,
    own_ref,
    other_ref,
    *rest,
):
    weights_ref, entry_ref, switch_ref, couplings_hbm, mid_hbm, gate_hbm, sides_hbm = rest[-16:-9]
    outer_ref, spread_ref, sum_ref, rows_ref, couplings_ref = rest[-9:-4]
    mid_ref, gate_ref, sides_ref, copied = rest[-4:]
    right_refs = rest[:-16]
    fetched = pltpu.make_async_copy(couplings_hbm, couplings_ref, copied.at[0])
    fetched.start()
    copies = []

    def send(source, target):
        copies.append(pltpu.make_async_copy(source, target, copied.at[len(copies) + 1]))
        copies[-1].start()

    features = TENSOR_FEATURES
    slots, piece_rows, total = own_ref.shape
    residues = piece_rows // features
    rows = 2 * slots * residues
    share = right_refs[0].shape[0]
    columns = len(right_refs) * share
    groups = columns // GROUP
    wide = share * features
    together = spread_ref.shape[1] // 64

    for half, left_ref in enumerate((own_ref, other_ref)):
        piece = left_ref[...].reshape(slots * piece_rows, total)
        target = slice(half * slots * piece_rows, (half + 1) * slots * piece_rows)
        for p, right_ref in enumerate(right_refs):
            right = right_ref[...].reshape(wide, total)
            outer_ref[target, p * wide : (p + 1) * wide] = matmul_nt(piece, right) * (1.0 / total)

    spread_ref[...] = jnp.zeros_like(spread_ref)
    front = lax.broadcasted_iota(jnp.int32, (rows, 128), 1) < 64

    def channel_step(p, carry):
        slot = lax.rem(p, 2)
        for e in range(together):
            source = pl.multiple_of((p * together + e) * features, features)
            piece = weights_ref[pl.ds(source, features), :]
            for place in range(2):
                low = e * 64 + place * features
                spread_ref[slot, low : low + features, place * C_Z : (place + 1) * C_Z] = piece
        pieces = []
        for g in range(groups):
            parts = []
            for e in range(together):
                channel = []
                for slot_number in range(2 * slots):
                    first = slot_number * piece_rows + (p * together + e) * residues
                    source = pl.ds(pl.multiple_of(first, residues), residues)
                    channel.append(outer_ref[source, g * 128 : (g + 1) * 128])
                parts.append(jnp.concatenate(channel, axis=0).astype(BF16))
            lows, highs = [], []
            for e in range(0, together, 2):
                lows.append(jnp.where(front, parts[e], pltpu.roll(parts[e + 1], 64, 1)))
                highs.append(jnp.where(front, pltpu.roll(parts[e], 64, 1), parts[e + 1]))
            pieces.append(jnp.concatenate(lows, axis=1))
            pieces.append(jnp.concatenate(highs, axis=1))
        update = matmul(jnp.concatenate(pieces, axis=0), spread_ref[slot])

        @pl.when(p == 0)
        def _():
            sum_ref[...] = update

        @pl.when(p > 0)
        def _():
            sum_ref[...] += update

        return carry

    lax.fori_loop(0, features // together, channel_step, 0)

    left_firsts = [left_slots_ref[j] * residues for j in range(2 * slots)]
    right_firsts = [right_firsts_ref[p] for p in range(len(right_refs))]
    fetched.wait()
    for g in range(groups):
        normed, places = [], []
        for place in range(GROUP):
            p, n = divmod(g * GROUP + place, share)
            b = right_firsts[p] + n
            places.append(b)
            lanes = slice(place % 2 * C_Z, (place % 2 + 1) * C_Z)
            start = (2 * g + place // 2) * rows
            pieces = []
            for first in left_firsts:
                source = pl.ds(pl.multiple_of(start + first, residues), residues)
                pieces.append(sum_ref[source, lanes])
            mid = jnp.concatenate(pieces, axis=0)
            mid = mid + couplings_ref[pl.ds(b, rows, stride=columns), :]
            mid_ref[g * GROUP + place] = mid
            centred = mid - jnp.mean(mid, axis=1, keepdims=True)
            variance = jnp.mean(centred * centred, axis=1, keepdims=True)
            normed.append((centred * lax.rsqrt(variance + EPS)).astype(BF16))
        gates = sigmoid(matmul(jnp.concatenate(normed, axis=0), switch_ref[...]))
        blank = jnp.zeros_like(normed[0])
        for place in range(0, GROUP, 2):
            twice = []
            for e in range(2):
                part = gates[(place + e) * rows : (place + e + 1) * rows]
                gate_ref[g * GROUP + place + e] = part
                twice.append(jnp.concatenate([normed[place + e], blank], axis=1))
                twice.append(jnp.concatenate([blank, normed[place + e]], axis=1))
            sides = matmul_nt(entry_ref[...], jnp.concatenate(twice, axis=0))
            sides = sigmoid(sides[C_TRI:]) * sides[:C_TRI]
            for e in range(2):
                first = pl.multiple_of(places[place + e] * C_TRI, C_TRI)
                rows_ref[pl.ds(first, C_TRI), :] = sides[:, e * 2 * rows : (e + 1) * 2 * rows]

        if (g + 1) * GROUP % share == 0:
            p = (g + 1) * GROUP // share - 1
            source, target = pl.ds(p * share, share), pl.ds(right_firsts[p], share)
            send(mid_ref.at[source], mid_hbm.at[target])
            send(gate_ref.at[source], gate_hbm.at[target])

    cut = C_TRI // 4
    for part in range(4):

        def turn_step(c, carry):
            sides_ref[c] = rows_ref[pl.ds(c, columns, stride=C_TRI), :].astype(BF16)
            return carry

        lax.fori_loop(part * cut, (part + 1) * cut, turn_step, 0, unroll=8)
        chosen = pl.ds(part * cut, cut)
        send(sides_ref.at[chosen], sides_hbm.at[chosen])
    for copy in copies:
        copy.wait()


def pair_update(left_slots, right_firsts, left, rights, weights, couplings, entry, switch):
    rows, columns, depth = couplings.shape
    whole = jax.ShapeDtypeStruct((columns, rows, depth), F32)
    sides = jax.ShapeDtypeStruct((C_TRI, columns, 2 * rows), BF16)
    smem = pl.BlockSpec(memory_space=pltpu.SMEM)
    vmem = pl.BlockSpec(memory_space=pltpu.VMEM)
    anywhere = pl.BlockSpec(memory_space=pl.ANY)
    return pl.pallas_call(
        pair_kernel,
        in_specs=[smem] * 2 + [vmem] * (5 + len(rights)) + [anywhere],
        out_specs=[anywhere] * 3,
        out_shape=[pltpu.HBM(whole.shape, F32)] * 2 + [pltpu.HBM(sides.shape, BF16)],
        scratch_shapes=[
            pltpu.VMEM((rows * TENSOR_FEATURES, columns * TENSOR_FEATURES), F32),
            pltpu.VMEM((2, 8 * 64, 2 * depth), BF16),
            pltpu.VMEM((columns // 2 * rows, 2 * depth), F32),
            pltpu.VMEM((columns * C_TRI, 2 * rows), F32),
            pltpu.VMEM((rows * columns, depth), F32),
            pltpu.VMEM(whole.shape, F32),
            pltpu.VMEM(whole.shape, F32),
            pltpu.VMEM(sides.shape, BF16),
            pltpu.SemaphoreType.DMA((2 * len(rights) + 5,)),
        ],
        compiler_params=params(28),
        cost_estimate=cost(12),
        name="pair_update",
    )(
        left_slots,
        right_firsts,
        *left,
        *rights,
        weights,
        entry,
        switch,
        couplings.reshape(rows * columns, depth),
    )


def product_kernel(sides_ref, out_ref, *, grid_rows, grid_columns):
    channels, part, lanes = sides_ref.shape[1:]
    half = lanes // 2
    lane = lax.broadcasted_iota(jnp.int32, (grid_columns * part, lanes), 1)
    front = lane < half
    cut = front[: part // 2]
    for channel in range(channels):
        lefts, rights = [], []
        for r in range(0, grid_rows, 2):
            even, odd = [
                jnp.concatenate(
                    [sides_ref[(r + e) * grid_columns + c, channel] for c in range(grid_columns)],
                    axis=0,
                )
                for e in range(2)
            ]
            lefts.append(jnp.where(front, even, pltpu.roll(odd, half, 1)))
            rights.append(jnp.where(front, pltpu.roll(even, half, 1), odd))
        product = matmul_nt(jnp.concatenate(rights, axis=1), jnp.concatenate(lefts, axis=1))
        product = product.astype(BF16)
        for c in range(grid_columns):
            for r in range(0, grid_rows, 2):
                block = product[c * part : (c + 1) * part, r * half : (r + 2) * half]
                top, bottom = block[: part // 2], block[part // 2 :]
                even = jnp.where(cut, top, pltpu.roll(bottom, half, 1))
                out_ref[r * grid_columns + c, channel] = even
                odd = jnp.where(cut, pltpu.roll(top, half, 1), bottom)
                out_ref[(r + 1) * grid_columns + c, channel] = odd


def triangle_product(sides, grid_rows, grid_columns):
    devices, channels, part, lanes = sides.shape
    step = 2 if channels % 2 == 0 else 1
    return pl.pallas_call(
        functools.partial(product_kernel, grid_rows=grid_rows, grid_columns=grid_columns),
        grid=(channels // step,),
        in_specs=[pl.BlockSpec((devices, step, part, lanes), lambda c: (0, c, 0, 0))],
        out_specs=pl.BlockSpec((devices, step, part // 2, lanes), lambda c: (0, c, 0, 0)),
        out_shape=pltpu.HBM((devices, channels, part // 2, lanes), BF16),
        compiler_params=params(8, "arbitrary"),
        cost_estimate=cost(3),
        name="triangle_product",
    )(sides)


def output_kernel(
    product_ref, final_ref, mid_hbm, gate_hbm, out_hbm, wide_ref, mid_ref, gate_ref, out_ref, *copied
):
    channels, part, lanes = product_ref.shape
    columns, rows, depth = mid_ref.shape
    own = 8
    fetched, sent = copied
    fetches, sends = [], []
    for first in range(0, columns, own):
        chosen = pl.ds(first, own)
        for source, target in ((mid_hbm, mid_ref), (gate_hbm, gate_ref)):
            fetches.append(
                pltpu.make_async_copy(
                    source.at[chosen], target.at[chosen], fetched.at[len(fetches)]
                )
            )
            fetches[-1].start()
    wide_ref[...] = product_ref[...].astype(F32).reshape(channels * part, lanes)
    for group in range(part // own):
        updates = []
        for j in range(own):
            product = wide_ref[pl.ds(group * own + j, channels, stride=part), :]
            updates.append(matmul(normalise_rows(product).T, final_ref[...]))
        for half in range(2):
            cut = half * (part // own) + group
            fetches[2 * cut].wait()
            fetches[2 * cut + 1].wait()
            out_rows = out_ref.at[cut].reshape(rows * own, depth)
            for j in range(own):
                b = cut * own + j
                piece = updates[j][half * rows : (half + 1) * rows]
                out_rows[pl.ds(j, rows, stride=own), :] = mid_ref[b] + gate_ref[b] * piece
            sends.append(
                pltpu.make_async_copy(
                    out_ref.at[cut], out_hbm.at[:, pl.ds(cut * own, own)], sent.at[len(sends)]
                )
            )
            sends[-1].start()
    for send in sends:
        send.wait()


def pair_result(product, mid, gate, final_matrix):
    channels, part, lanes = product.shape
    columns, rows, depth = mid.shape
    vmem, hbm = pl.BlockSpec(memory_space=pltpu.VMEM), pl.BlockSpec(memory_space=pltpu.HBM)
    return pl.pallas_call(
        output_kernel,
        in_specs=[vmem, vmem, hbm, hbm],
        out_specs=hbm,
        out_shape=pltpu.HBM((rows, columns, depth), F32),
        scratch_shapes=[
            pltpu.VMEM((channels * part, lanes), F32),
            pltpu.VMEM(mid.shape, F32),
            pltpu.VMEM(mid.shape, F32),
            pltpu.VMEM((columns // 8, rows, 8, depth), F32),
            pltpu.SemaphoreType.DMA((columns // 4,)),
            pltpu.SemaphoreType.DMA((columns // 8,)),
        ],
        compiler_params=params(16),
        cost_estimate=cost(3),
        name="pair_result",
    )(
        product,
        final_matrix,
        pltpu.with_memory_space_constraint(mid, pltpu.HBM),
        pltpu.with_memory_space_constraint(gate, pltpu.HBM),
    )


def swap_cores(block):
    count = lax.axis_size("col")
    return lax.ppermute(block, "col", [(c, c ^ 1) for c in range(count)])


def gather_turned(block):
    rows, columns = lax.axis_size("row"), lax.axis_size("col")
    arrived = []
    for shift in range(rows):
        moves = []
        for r in range(rows):
            for q in range(rows):
                for side in range(2):
                    source = r * columns + 2 * q + side
                    moves.append((source, q * columns + 2 * ((r + shift) % rows) + side))
        arrived.append(lax.ppermute(block, ("row", "col"), moves))
    return arrived


def both_cores(own):
    rows = lax.axis_size("row")
    core = lax.rem(lax.axis_index("col"), 2)
    other = swap_cores(own)
    residues = own.shape[1] // TENSOR_FEATURES
    if residues % 8 == 0:
        return own, other
    order = left_order(rows)
    own, other = jnp.take(own, order, axis=0), jnp.take(other, order, axis=0)
    joined = 8 // residues
    ordered = []
    for side in (jnp.where(core == 0, own, other), jnp.where(core == 0, other, own)):
        side = side.reshape(rows // joined, joined, TENSOR_FEATURES, residues, -1)
        side = jnp.transpose(side, (0, 2, 1, 3, 4))
        ordered.append(side.reshape(rows // joined, joined * own.shape[1], -1))
    return tuple(ordered)


def left_order(rows):
    me = lax.axis_index("col") // 2
    return lax.rem(me - jnp.arange(rows, dtype=jnp.int32) + rows, rows)


def left_groups(rows, residues):
    if residues % 8:
        return jnp.arange(2 * rows * residues // 8, dtype=jnp.int32)
    core = lax.rem(lax.axis_index("col"), 2)
    order = left_order(rows)
    return jnp.concatenate([order + core * rows, order + (1 - core) * rows])


def exchange_rows(pieces):
    arrived = [pieces[0]]
    for shift in range(1, len(pieces)):
        moves = [(r, r ^ shift) for r in range(len(pieces))]
        arrived.append(lax.ppermute(pieces[shift], "row", moves))
    return arrived


def paired_entries(matrices):
    turned = matrices.reshape(C_Z, 2, 2, C_TRI)
    return jnp.transpose(turned, (2, 3, 1, 0)).reshape(2 * C_TRI, 2 * C_Z)


def body(
    homolog_tensor,
    couplings,
    attention_probe_matrix,
    attention_extra_matrices,
    attention_final_matrix,
    tensor_entry_matrices,
    tensor_final_matrix,
    incoming_entry_matrices,
    incoming_switch_matrix,
    incoming_final_matrix,
):
    inner = ATTENTION_UNITS * UNIT_WIDTH
    row_count = lax.axis_size("row")
    seqs, residues, depth = homolog_tensor.shape
    own_residues = residues // row_count
    sources = lax.axis_index("row") ^ jnp.arange(row_count, dtype=jnp.int32)
    high = exchange_rows(standardise_high(sources, homolog_tensor))
    low = standardise_low(sources, homolog_tensor)
    others = jnp.concatenate(
        [attention_probe_matrix.T, attention_extra_matrices[:, inner:].T], axis=0
    )
    early = (
        attention_extra_matrices[:, :inner],
        others,
        attention_final_matrix.T,
        tensor_entry_matrices.T,
        paired_entries(incoming_entry_matrices),
        sources * own_residues,
        left_groups(row_count, own_residues),
    )
    high, _, early = lax.optimization_barrier((high, low, early))
    key_matrix, others, final_turned, tensor_turned, entries, firsts, slots = early
    low = exchange_rows(low)
    turned, *gated = attention(high, key_matrix, others)
    left_piece, right_piece = alignment(
        sources, high, low, turned, final_turned, tensor_turned
    )

    lefts = gather_turned(left_piece)
    right_piece, lefts[0] = lax.optimization_barrier((right_piece, lefts[0]))
    rights = exchange_rows([right_piece] * row_count)
    own = jnp.stack(lefts)
    own, rights = lax.optimization_barrier((own, rights))
    mid, gate, sides = pair_update(
        slots,
        firsts,
        both_cores(own),
        rights,
        tensor_final_matrix,
        couplings,
        entries,
        incoming_switch_matrix,
    )
    gated, sides = lax.optimization_barrier((gated, sides))
    gated = exchange_rows(gated)

    everywhere = ("row", "col")
    column_count = lax.axis_size("col")
    devices = row_count * column_count
    sides = sides.reshape(devices, C_TRI // devices, *sides.shape[1:])
    sides = lax.all_to_all(sides, everywhere, split_axis=0, concat_axis=0)
    gated, sides = lax.optimization_barrier((gated, sides))
    product = triangle_product(sides, row_count, column_count)
    product = lax.all_to_all(product, everywhere, split_axis=0, concat_axis=0)

    gated = jnp.take(jnp.stack(gated), sources, axis=0)
    gated = jnp.transpose(gated.reshape(residues, seqs, inner), (1, 0, 2))
    change = jnp.dot(
        gated.reshape(-1, inner), attention_final_matrix, preferred_element_type=F32
    )
    refreshed_homologs = homolog_tensor + change.reshape(homolog_tensor.shape)
    product = product.reshape(C_TRI, *product.shape[2:])
    pair_output = pair_result(product, mid, gate, incoming_final_matrix)
    return (refreshed_homologs, pair_output)


def solution(mesh):
    in_specs = (
        P("row", "col", None),
        P("row", "col", None),
        P(),
        P(),
        P(),
        P(),
        P(),
        P(),
        P(),
        P(),
    )
    out_specs = (P("row", "col", None), P("row", "col", None))
    return jax.shard_map(body, mesh=mesh, in_specs=in_specs, out_specs=out_specs, check_vma=False)
```

```python
import functools

import jax
import jax.numpy as jnp
from jax import lax
from jax.experimental import pallas as pl
from jax.experimental.pallas import tpu as pltpu
from jax.sharding import PartitionSpec as P

FEATURE_DEPTH = 256
C_Z = 128
TENSOR_FEATURES = 32
C_TRI = 128
ATTENTION_UNITS = 8
UNIT_WIDTH = 32
EPS = 1e-05
GROUP = 4
F32 = jnp.float32
BF16 = jnp.bfloat16
NT = (((1,), (1,)), ((), ()))


def matmul(left, right):
    return jnp.dot(left, right, preferred_element_type=F32)


def matmul_nt(left, right):
    return lax.dot_general(left, right, NT, preferred_element_type=F32)


def sigmoid(values):
    return 0.5 * jnp.tanh(0.5 * values) + 0.5


def cost(microseconds):
    return pl.CostEstimate(
        flops=int(microseconds * 1e9), bytes_accessed=int(microseconds * 1e6), transcendentals=0
    )


def params(megabytes, *semantics):
    return pltpu.CompilerParams(
        dimension_semantics=semantics or None, vmem_limit_bytes=megabytes * 1024 * 1024
    )


def fold(values, combine):
    while values.shape[0] > 8:
        half = values.shape[0] // 2
        values = combine(values[:half], values[half:])
    return values


def top_rows(values):
    return jnp.max(fold(values, jnp.maximum), axis=0, keepdims=True)


def sum_rows(values):
    return jnp.sum(fold(values, jnp.add), axis=0, keepdims=True)


def normalise_rows(values):
    count = values.shape[0]
    centred = values - sum_rows(values) * (1.0 / count)
    variance = sum_rows(centred * centred) * (1.0 / count)
    return (centred * lax.rsqrt(variance + EPS)).astype(BF16)


def standardised_column(first_rows, second_rows, n, residues):
    seqs = first_rows.shape[0] // residues
    rows = pl.ds(n, seqs, stride=residues)
    column = jnp.concatenate([first_rows[rows, :], second_rows[rows, :]], axis=1)
    centred = column - jnp.mean(column, axis=1, keepdims=True)
    variance = jnp.mean(centred * centred, axis=1, keepdims=True) + EPS
    scale = lax.rsqrt(variance)
    return centred * scale, variance * scale


def high_kernel(sources_ref, block_hbm, *rest):
    *pieces_hbm, block_ref, first_ref, second_ref, high_ref, fetched, sent = rest
    seqs, residues, lanes = first_ref.shape
    own = residues // len(pieces_hbm)
    step = 16
    fetches, sends = [], []
    for s in range(0, seqs, step):
        chosen = pl.ds(s, step)
        fetches.append(
            pltpu.make_async_copy(
                block_hbm.at[chosen], block_ref.at[chosen], fetched.at[len(fetches)]
            )
        )
        fetches[-1].start()
    for part in range(seqs // step):
        chosen = pl.ds(part * step, step)
        fetches[part].wait()
        first_ref[chosen] = block_ref[chosen, :, :lanes]
        second_ref[chosen] = block_ref[chosen, :, lanes:]
        first_rows = first_ref.at[chosen].reshape(step * residues, lanes)
        second_rows = second_ref.at[chosen].reshape(step * residues, lanes)
        for n in range(residues):
            normed, _ = standardised_column(first_rows, second_rows, n, residues)
            high_ref[part, n] = normed.astype(BF16)
        for p, piece_hbm in enumerate(pieces_hbm):
            source = high_ref.at[part, pl.ds(sources_ref[p] * own, own)]
            sends.append(
                pltpu.make_async_copy(source, piece_hbm.at[:, chosen], sent.at[len(sends)])
            )
            sends[-1].start()
    for send in sends:
        send.wait()


def standardise_high(sources, block):
    seqs, residues, depth = block.shape
    half = depth // 2
    count = sources.shape[0]
    hbm = pl.BlockSpec(memory_space=pltpu.HBM)
    return pl.pallas_call(
        high_kernel,
        in_specs=[pl.BlockSpec(memory_space=pltpu.SMEM), hbm],
        out_specs=[hbm] * count,
        out_shape=[pltpu.HBM((residues // count, seqs, depth), BF16)] * count,
        scratch_shapes=[
            pltpu.VMEM((seqs, residues, depth), F32),
            pltpu.VMEM((seqs, residues, half), F32),
            pltpu.VMEM((seqs, residues, half), F32),
            pltpu.VMEM((seqs // 16, residues, 16, depth), BF16),
            pltpu.SemaphoreType.DMA((seqs // 16,)),
            pltpu.SemaphoreType.DMA((seqs // 16 * count,)),
        ],
        compiler_params=params(10),
        cost_estimate=cost(3),
        name="standardise_high",
    )(sources, pltpu.with_memory_space_constraint(block, pltpu.HBM))


def low_kernel(sources_ref, first_ref, second_ref, *rest):
    *pieces_hbm, low_ref, sent = rest
    seqs, residues, lanes = first_ref.shape
    own = residues // len(pieces_hbm)
    first_rows = first_ref.reshape(seqs * residues, lanes)
    second_rows = second_ref.reshape(seqs * residues, lanes)
    lane = lax.broadcasted_iota(jnp.int32, (seqs, 128), 1)
    for p in range(len(pieces_hbm)):
        spreads = jnp.zeros((seqs, 128), F32)
        for n in range(own):
            normed, spread = standardised_column(first_rows, second_rows, p * own + n, residues)
            left = (normed - normed.astype(BF16).astype(F32)).astype(BF16)
            low_ref[p, n * seqs : (n + 1) * seqs, :] = left
            spreads = jnp.where(lane == n, spread, spreads)
        spreads = spreads.T[:8, :]
        coarse = spreads.astype(BF16).astype(F32)
        kept = jnp.concatenate([coarse, spreads - coarse], axis=0)
        kept = jnp.concatenate([kept, jnp.zeros((16, 2 * lanes - seqs), F32)], axis=1)
        low_ref[p, own * seqs :, :] = kept.astype(BF16)
    sends = []
    for p, piece_hbm in enumerate(pieces_hbm):
        source = low_ref.at[sources_ref[p]]
        sends.append(pltpu.make_async_copy(source, piece_hbm, sent.at[p]))
        sends[-1].start()
    for send in sends:
        send.wait()


def standardise_low(sources, block):
    seqs, residues, depth = block.shape
    half = depth // 2
    count = sources.shape[0]
    height = residues // count * seqs + 16
    hbm = pl.BlockSpec(memory_space=pltpu.HBM)
    return pl.pallas_call(
        low_kernel,
        grid=(1,),
        in_specs=[
            pl.BlockSpec(memory_space=pltpu.SMEM),
            pl.BlockSpec((seqs, residues, half), lambda g: (0, 0, 0)),
            pl.BlockSpec((seqs, residues, half), lambda g: (0, 0, 1)),
        ],
        out_specs=[hbm] * count,
        out_shape=[pltpu.HBM((height, depth), BF16)] * count,
        scratch_shapes=[
            pltpu.VMEM((count, height, depth), BF16),
            pltpu.SemaphoreType.DMA((count,)),
        ],
        compiler_params=params(14, "arbitrary"),
        cost_estimate=cost(4),
        name="standardise_low",
    )(sources, block, block)


def attention_kernel(key_ref, others_ref, *rest):
    *normed_refs, turned_ref, scores_ref, weights_ref = rest
    blocks = len(normed_refs)
    residues, seqs, _ = normed_refs[0].shape
    total = blocks * seqs
    inner = ATTENTION_UNITS * UNIT_WIDTH
    ring = scores_ref.shape[0]
    columns = []

    def project(n):
        column = jnp.concatenate([ref[n] for ref in normed_refs], axis=0)
        key_rows = matmul(column, key_ref[...]).astype(BF16)
        projected = matmul_nt(others_ref[...], column)
        queries = (projected[:inner] * UNIT_WIDTH ** (-0.5)).astype(BF16)
        value_rows = projected[inner : 2 * inner].astype(BF16)
        gates = sigmoid(projected[2 * inner :])
        columns.append((key_rows, queries, value_rows, gates))
    units = [(n, h) for n in range(residues) for h in range(ATTENTION_UNITS)]

    def score(unit):
        n, h = units[unit]
        key_rows, queries, _, _ = columns[n]
        low, high = h * UNIT_WIDTH, (h + 1) * UNIT_WIDTH
        pieces = [queries[low:high]]
        if low > 0:
            pieces.insert(0, jnp.zeros((low, total), BF16))
        if high < inner:
            pieces.append(jnp.zeros((inner - high, total), BF16))
        scores_ref[unit % ring] = matmul(key_rows, jnp.concatenate(pieces, axis=0))

    def weigh(unit):
        for low in range(0, total, 128):
            scores = scores_ref[unit % ring, :, low : low + 128]
            weights = jnp.exp(scores - top_rows(scores))
            scale = 1.0 / sum_rows(weights)
            weights_ref[unit % ring, :, low : low + 128] = (weights * scale).astype(BF16)

    def attend(unit):
        n, h = units[unit]
        _, _, value_rows, gates = columns[n]
        rows = slice(h * UNIT_WIDTH, (h + 1) * UNIT_WIDTH)
        attended = matmul(value_rows[rows], weights_ref[unit % ring]) * gates[rows]
        turned_ref[n, rows, :] = attended.astype(BF16)

    project(0)
    for step in range(len(units) + 2):
        if step < len(units):
            score(step)
            n, h = units[step]
            if h == ATTENTION_UNITS // 2 and n + 1 < residues:
                project(n + 1)
        if 1 <= step <= len(units):
            weigh(step - 1)
        if step >= 2:
            attend(step - 2)


def attention(normed, key_matrix, other_matrices):
    blocks = len(normed)
    residues, seqs, depth = normed[0].shape
    total = blocks * seqs
    inner = ATTENTION_UNITS * UNIT_WIDTH
    step = 4
    return pl.pallas_call(
        attention_kernel,
        grid=(residues // step,),
        in_specs=[
            pl.BlockSpec((depth, inner), lambda n: (0, 0)),
            pl.BlockSpec((3 * inner, depth), lambda n: (0, 0)),
        ]
        + [pl.BlockSpec((step, seqs, depth), lambda n: (n, 0, 0))] * blocks,
        out_specs=pl.BlockSpec((step, inner, total), lambda n: (n, 0, 0)),
        out_shape=jax.ShapeDtypeStruct((residues, inner, total), BF16),
        scratch_shapes=[
            pltpu.VMEM((4, total, total), F32),
            pltpu.VMEM((4, total, total), BF16),
        ],
        compiler_params=params(12 + (total // 128) ** 2, "arbitrary"),
        cost_estimate=cost(10),
        name="attention",
    )(key_matrix, other_matrices, *normed)


def turn_kernel(turned_ref, *gated_refs):
    seqs = gated_refs[0].shape[1]
    for n in range(turned_ref.shape[0]):
        back = turned_ref[n].T
        for block, gated_ref in enumerate(gated_refs):
            gated_ref[n] = back[block * seqs : (block + 1) * seqs]


def turn_back(turned, blocks):
    residues, inner, total = turned.shape
    seqs = total // blocks
    return pl.pallas_call(
        turn_kernel,
        grid=(residues // 2,),
        in_specs=[pl.BlockSpec((2, inner, total), lambda n: (n, 0, 0))],
        out_specs=[pl.BlockSpec((2, seqs, inner), lambda n: (n, 0, 0))] * blocks,
        out_shape=[pltpu.HBM((residues, seqs, inner), BF16)] * blocks,
        compiler_params=params(12, "arbitrary"),
        cost_estimate=cost(2),
        name="turn_back",
    )(turned)


def alignment_kernel(sources_ref, turned_ref, final_ref, entry_ref, *rest):
    *refs, left_ref, right_ref, rows_ref = rest
    blocks = len(refs) // 3
    high_refs, low_refs, spread_refs = refs[:blocks], refs[blocks : 2 * blocks], refs[2 * blocks :]
    residues, seqs, depth = high_refs[0].shape
    total = blocks * seqs
    features = TENSOR_FEATURES
    step = pl.program_id(0)
    for n in range(residues):
        column = jnp.concatenate([ref[n] for ref in high_refs], axis=0).astype(F32)
        column = column + jnp.concatenate(
            [ref[n * seqs : (n + 1) * seqs, :] for ref in low_refs], axis=0
        ).astype(F32)
        spreads = []
        for ref in spread_refs:
            kept = ref[:, :seqs].astype(F32)
            row = lax.broadcasted_iota(jnp.int32, kept.shape, 0)
            chosen = lax.rem(row, 8) == step * residues + n
            spreads.append(jnp.sum(jnp.where(chosen, kept, 0.0), axis=0, keepdims=True))
        spread = jnp.concatenate(spreads, axis=1)
        updated = column.T * spread + matmul(final_ref[...], turned_ref[n])
        projected = matmul(entry_ref[...], normalise_rows(updated))
        me = sources_ref[0]
        tiles = [projected[:, low : low + 128] for low in range(0, total, 128)]
        odd = lax.rem(me, 2) == 1
        tiles = [jnp.where(odd, pltpu.roll(tile, seqs, 1), tile) for tile in tiles]
        width = 1
        while width < len(tiles):
            crossed = lax.rem(lax.div(me, 2 * width), 2) == 1
            tiles = [
                jnp.where(crossed, tiles[t ^ width], tiles[t]) for t in range(len(tiles))
            ]
            width *= 2
        first = pl.multiple_of((step * residues + n) * features, features)
        for t, tile in enumerate(tiles):
            right_ref[n, :, t * 128 : (t + 1) * 128] = tile[features:].astype(BF16)
            rows_ref[t, pl.ds(first, features), :] = tile[:features]

    @pl.when(step == pl.num_programs(0) - 1)
    def _():
        count = rows_ref.shape[1] // features
        together = max(1, 16 // count)
        for c in range(0, features, together):
            pieces = []
            for e in range(together):
                chosen = pl.ds(c + e, count, stride=features)
                tiles = [rows_ref[tile, chosen, :] for tile in range(total // 128)]
                pieces.append(jnp.concatenate(tiles, axis=1))
            piece = jnp.concatenate(pieces, axis=0).astype(BF16)
            left_ref[c * count : (c + together) * count, :] = piece


def alignment(sources, high, low, turned, final_matrix, entry_matrices):
    blocks = len(high)
    residues, seqs, depth = high[0].shape
    total = blocks * seqs
    features = TENSOR_FEATURES
    step = 4
    height = residues * seqs + 16
    return pl.pallas_call(
        alignment_kernel,
        grid=(residues // step,),
        in_specs=[
            pl.BlockSpec(memory_space=pltpu.SMEM),
            pl.BlockSpec((step, depth, total), lambda n: (n, 0, 0)),
            pl.BlockSpec(final_matrix.shape, lambda n: (0, 0)),
            pl.BlockSpec(entry_matrices.shape, lambda n: (0, 0)),
        ]
        + [pl.BlockSpec((step, seqs, depth), lambda n: (n, 0, 0))] * blocks
        + [pl.BlockSpec((step * seqs, depth), lambda n: (n, 0))] * blocks
        + [pl.BlockSpec((16, depth), lambda n: (height // 16 - 1, 0))] * blocks,
        out_specs=[
            pl.BlockSpec((features * residues, total), lambda n: (0, 0)),
            pl.BlockSpec((step, features, total), lambda n: (n, 0, 0)),
        ],
        out_shape=[
            jax.ShapeDtypeStruct((features * residues, total), BF16),
            jax.ShapeDtypeStruct((residues, features, total), BF16),
        ],
        scratch_shapes=[pltpu.VMEM((total // 128, residues * features, 128), F32)],
        compiler_params=params(16, "arbitrary"),
        cost_estimate=cost(4),
        name="alignment",
    )(sources, turned, final_matrix, entry_matrices, *high, *low, *low)


def pair_kernel(
    left_slots_ref,
    right_firsts_ref,
    own_ref,
    other_ref,
    *rest,
):
    weights_ref, entry_ref, switch_ref, couplings_hbm, mid_hbm, gate_hbm, sides_hbm = rest[-16:-9]
    outer_ref, spread_ref, sum_ref, rows_ref, couplings_ref = rest[-9:-4]
    mid_ref, gate_ref, sides_ref, copied = rest[-4:]
    right_refs = rest[:-16]
    fetched = pltpu.make_async_copy(couplings_hbm, couplings_ref, copied.at[0])
    fetched.start()
    copies = []

    def send(source, target):
        copies.append(pltpu.make_async_copy(source, target, copied.at[len(copies) + 1]))
        copies[-1].start()

    features = TENSOR_FEATURES
    slots, piece_rows, total = own_ref.shape
    residues = piece_rows // features
    rows = 2 * slots * residues
    share = right_refs[0].shape[0]
    columns = len(right_refs) * share
    groups = columns // GROUP
    wide = share * features
    together = spread_ref.shape[1] // 64

    for half, left_ref in enumerate((own_ref, other_ref)):
        piece = left_ref[...].reshape(slots * piece_rows, total)
        target = slice(half * slots * piece_rows, (half + 1) * slots * piece_rows)
        for p, right_ref in enumerate(right_refs):
            right = right_ref[...].reshape(wide, total)
            outer_ref[target, p * wide : (p + 1) * wide] = matmul_nt(piece, right) * (1.0 / total)

    spread_ref[...] = jnp.zeros_like(spread_ref)
    front = lax.broadcasted_iota(jnp.int32, (rows, 128), 1) < 64

    def channel_step(p, carry):
        slot = lax.rem(p, 2)
        for e in range(together):
            source = pl.multiple_of((p * together + e) * features, features)
            piece = weights_ref[pl.ds(source, features), :]
            for place in range(2):
                low = e * 64 + place * features
                spread_ref[slot, low : low + features, place * C_Z : (place + 1) * C_Z] = piece
        pieces = []
        for g in range(groups):
            parts = []
            for e in range(together):
                channel = []
                for slot_number in range(2 * slots):
                    first = slot_number * piece_rows + (p * together + e) * residues
                    source = pl.ds(pl.multiple_of(first, residues), residues)
                    channel.append(outer_ref[source, g * 128 : (g + 1) * 128])
                parts.append(jnp.concatenate(channel, axis=0).astype(BF16))
            lows, highs = [], []
            for e in range(0, together, 2):
                lows.append(jnp.where(front, parts[e], pltpu.roll(parts[e + 1], 64, 1)))
                highs.append(jnp.where(front, pltpu.roll(parts[e], 64, 1), parts[e + 1]))
            pieces.append(jnp.concatenate(lows, axis=1))
            pieces.append(jnp.concatenate(highs, axis=1))
        update = matmul(jnp.concatenate(pieces, axis=0), spread_ref[slot])

        @pl.when(p == 0)
        def _():
            sum_ref[...] = update

        @pl.when(p > 0)
        def _():
            sum_ref[...] += update

        return carry

    lax.fori_loop(0, features // together, channel_step, 0)

    left_firsts = [left_slots_ref[j] * residues for j in range(2 * slots)]
    right_firsts = [right_firsts_ref[p] for p in range(len(right_refs))]
    fetched.wait()
    for g in range(groups):
        normed, places = [], []
        for place in range(GROUP):
            p, n = divmod(g * GROUP + place, share)
            b = right_firsts[p] + n
            places.append(b)
            lanes = slice(place % 2 * C_Z, (place % 2 + 1) * C_Z)
            start = (2 * g + place // 2) * rows
            pieces = []
            for first in left_firsts:
                source = pl.ds(pl.multiple_of(start + first, residues), residues)
                pieces.append(sum_ref[source, lanes])
            mid = jnp.concatenate(pieces, axis=0)
            mid = mid + couplings_ref[pl.ds(b, rows, stride=columns), :]
            mid_ref[g * GROUP + place] = mid
            centred = mid - jnp.mean(mid, axis=1, keepdims=True)
            variance = jnp.mean(centred * centred, axis=1, keepdims=True)
            normed.append((centred * lax.rsqrt(variance + EPS)).astype(BF16))
        gates = sigmoid(matmul(jnp.concatenate(normed, axis=0), switch_ref[...]))
        blank = jnp.zeros_like(normed[0])
        for place in range(0, GROUP, 2):
            twice = []
            for e in range(2):
                part = gates[(place + e) * rows : (place + e + 1) * rows]
                gate_ref[g * GROUP + place + e] = part
                twice.append(jnp.concatenate([normed[place + e], blank], axis=1))
                twice.append(jnp.concatenate([blank, normed[place + e]], axis=1))
            sides = matmul_nt(entry_ref[...], jnp.concatenate(twice, axis=0))
            sides = sigmoid(sides[C_TRI:]) * sides[:C_TRI]
            for e in range(2):
                first = pl.multiple_of(places[place + e] * C_TRI, C_TRI)
                rows_ref[pl.ds(first, C_TRI), :] = sides[:, e * 2 * rows : (e + 1) * 2 * rows]

        if (g + 1) * GROUP % share == 0:
            p = (g + 1) * GROUP // share - 1
            source, target = pl.ds(p * share, share), pl.ds(right_firsts[p], share)
            send(mid_ref.at[source], mid_hbm.at[target])
            send(gate_ref.at[source], gate_hbm.at[target])

    cut = C_TRI // 4
    for part in range(4):

        def turn_step(c, carry):
            sides_ref[c] = rows_ref[pl.ds(c, columns, stride=C_TRI), :].astype(BF16)
            return carry

        lax.fori_loop(part * cut, (part + 1) * cut, turn_step, 0, unroll=8)
        chosen = pl.ds(part * cut, cut)
        send(sides_ref.at[chosen], sides_hbm.at[chosen])
    for copy in copies:
        copy.wait()


def pair_update(left_slots, right_firsts, left, rights, weights, couplings, entry, switch):
    rows, columns, depth = couplings.shape
    whole = jax.ShapeDtypeStruct((columns, rows, depth), F32)
    sides = jax.ShapeDtypeStruct((C_TRI, columns, 2 * rows), BF16)
    smem = pl.BlockSpec(memory_space=pltpu.SMEM)
    vmem = pl.BlockSpec(memory_space=pltpu.VMEM)
    anywhere = pl.BlockSpec(memory_space=pl.ANY)
    return pl.pallas_call(
        pair_kernel,
        in_specs=[smem] * 2 + [vmem] * (5 + len(rights)) + [anywhere],
        out_specs=[anywhere] * 3,
        out_shape=[pltpu.HBM(whole.shape, F32)] * 2 + [pltpu.HBM(sides.shape, BF16)],
        scratch_shapes=[
            pltpu.VMEM((rows * TENSOR_FEATURES, columns * TENSOR_FEATURES), F32),
            pltpu.VMEM((2, 8 * 64, 2 * depth), BF16),
            pltpu.VMEM((columns // 2 * rows, 2 * depth), F32),
            pltpu.VMEM((columns * C_TRI, 2 * rows), F32),
            pltpu.VMEM((rows * columns, depth), F32),
            pltpu.VMEM(whole.shape, F32),
            pltpu.VMEM(whole.shape, F32),
            pltpu.VMEM(sides.shape, BF16),
            pltpu.SemaphoreType.DMA((2 * len(rights) + 5,)),
        ],
        compiler_params=params(28),
        cost_estimate=cost(12),
        name="pair_update",
    )(
        left_slots,
        right_firsts,
        *left,
        *rights,
        weights,
        entry,
        switch,
        couplings.reshape(rows * columns, depth),
    )


def product_kernel(sides_ref, out_ref, *, grid_rows, grid_columns):
    channels, part, lanes = sides_ref.shape[1:]
    half = lanes // 2
    lane = lax.broadcasted_iota(jnp.int32, (grid_columns * part, lanes), 1)
    front = lane < half
    cut = front[: part // 2]
    for channel in range(channels):
        lefts, rights = [], []
        for r in range(0, grid_rows, 2):
            even, odd = [
                jnp.concatenate(
                    [sides_ref[(r + e) * grid_columns + c, channel] for c in range(grid_columns)],
                    axis=0,
                )
                for e in range(2)
            ]
            lefts.append(jnp.where(front, even, pltpu.roll(odd, half, 1)))
            rights.append(jnp.where(front, pltpu.roll(even, half, 1), odd))
        product = matmul_nt(jnp.concatenate(rights, axis=1), jnp.concatenate(lefts, axis=1))
        product = product.astype(BF16)
        for c in range(grid_columns):
            for r in range(0, grid_rows, 2):
                block = product[c * part : (c + 1) * part, r * half : (r + 2) * half]
                top, bottom = block[: part // 2], block[part // 2 :]
                even = jnp.where(cut, top, pltpu.roll(bottom, half, 1))
                out_ref[r * grid_columns + c, channel] = even
                odd = jnp.where(cut, pltpu.roll(top, half, 1), bottom)
                out_ref[(r + 1) * grid_columns + c, channel] = odd


def triangle_product(sides, grid_rows, grid_columns):
    devices, channels, part, lanes = sides.shape
    step = 2 if channels % 2 == 0 else 1
    return pl.pallas_call(
        functools.partial(product_kernel, grid_rows=grid_rows, grid_columns=grid_columns),
        grid=(channels // step,),
        in_specs=[pl.BlockSpec((devices, step, part, lanes), lambda c: (0, c, 0, 0))],
        out_specs=pl.BlockSpec((devices, step, part // 2, lanes), lambda c: (0, c, 0, 0)),
        out_shape=pltpu.HBM((devices, channels, part // 2, lanes), BF16),
        compiler_params=params(8, "arbitrary"),
        cost_estimate=cost(3),
        name="triangle_product",
    )(sides)


def output_kernel(
    product_ref, final_ref, mid_hbm, gate_hbm, out_hbm, wide_ref, mid_ref, gate_ref, out_ref, *copied
):
    channels, part, lanes = product_ref.shape
    columns, rows, depth = mid_ref.shape
    own = 8
    fetched, sent = copied
    fetches, sends = [], []
    for first in range(0, columns, own):
        chosen = pl.ds(first, own)
        for source, target in ((mid_hbm, mid_ref), (gate_hbm, gate_ref)):
            fetches.append(
                pltpu.make_async_copy(
                    source.at[chosen], target.at[chosen], fetched.at[len(fetches)]
                )
            )
            fetches[-1].start()
    wide_ref[...] = product_ref[...].astype(F32).reshape(channels * part, lanes)
    for group in range(part // own):
        updates = []
        for j in range(own):
            product = wide_ref[pl.ds(group * own + j, channels, stride=part), :]
            updates.append(matmul(normalise_rows(product).T, final_ref[...]))
        for half in range(2):
            cut = half * (part // own) + group
            fetches[2 * cut].wait()
            fetches[2 * cut + 1].wait()
            out_rows = out_ref.at[cut].reshape(rows * own, depth)
            for j in range(own):
                b = cut * own + j
                piece = updates[j][half * rows : (half + 1) * rows]
                out_rows[pl.ds(j, rows, stride=own), :] = mid_ref[b] + gate_ref[b] * piece
            sends.append(
                pltpu.make_async_copy(
                    out_ref.at[cut], out_hbm.at[:, pl.ds(cut * own, own)], sent.at[len(sends)]
                )
            )
            sends[-1].start()
    for send in sends:
        send.wait()


def pair_result(product, mid, gate, final_matrix):
    channels, part, lanes = product.shape
    columns, rows, depth = mid.shape
    vmem, hbm = pl.BlockSpec(memory_space=pltpu.VMEM), pl.BlockSpec(memory_space=pltpu.HBM)
    return pl.pallas_call(
        output_kernel,
        in_specs=[vmem, vmem, hbm, hbm],
        out_specs=hbm,
        out_shape=pltpu.HBM((rows, columns, depth), F32),
        scratch_shapes=[
            pltpu.VMEM((channels * part, lanes), F32),
            pltpu.VMEM(mid.shape, F32),
            pltpu.VMEM(mid.shape, F32),
            pltpu.VMEM((columns // 8, rows, 8, depth), F32),
            pltpu.SemaphoreType.DMA((columns // 4,)),
            pltpu.SemaphoreType.DMA((columns // 8,)),
        ],
        compiler_params=params(16),
        cost_estimate=cost(3),
        name="pair_result",
    )(
        product,
        final_matrix,
        pltpu.with_memory_space_constraint(mid, pltpu.HBM),
        pltpu.with_memory_space_constraint(gate, pltpu.HBM),
    )


def swap_cores(block):
    count = lax.axis_size("col")
    return lax.ppermute(block, "col", [(c, c ^ 1) for c in range(count)])


def gather_turned(block, later):
    rows, columns = lax.axis_size("row"), lax.axis_size("col")
    arrived = []
    for shift in range(rows):
        moves = []
        for r in range(rows):
            for q in range(rows):
                for side in range(2):
                    source = r * columns + 2 * q + side
                    moves.append((source, q * columns + 2 * ((r + shift) % rows) + side))
        source = block if shift < 2 else later
        arrived.append(lax.ppermute(source, ("row", "col"), moves))
    return jnp.stack(arrived)


def both_cores(own):
    rows = lax.axis_size("row")
    core = lax.rem(lax.axis_index("col"), 2)
    other = swap_cores(own)
    residues = own.shape[1] // TENSOR_FEATURES
    if residues % 8 == 0:
        return own, other
    order = left_order(rows)
    own, other = jnp.take(own, order, axis=0), jnp.take(other, order, axis=0)
    joined = 8 // residues
    ordered = []
    for side in (jnp.where(core == 0, own, other), jnp.where(core == 0, other, own)):
        side = side.reshape(rows // joined, joined, TENSOR_FEATURES, residues, -1)
        side = jnp.transpose(side, (0, 2, 1, 3, 4))
        ordered.append(side.reshape(rows // joined, joined * own.shape[1], -1))
    return tuple(ordered)


def left_order(rows):
    me = lax.axis_index("col") // 2
    return lax.rem(me - jnp.arange(rows, dtype=jnp.int32) + rows, rows)


def left_groups(rows, residues):
    if residues % 8:
        return jnp.arange(2 * rows * residues // 8, dtype=jnp.int32)
    core = lax.rem(lax.axis_index("col"), 2)
    order = left_order(rows)
    return jnp.concatenate([order + core * rows, order + (1 - core) * rows])


def exchange_rows(pieces):
    arrived = [pieces[0]]
    for shift in range(1, len(pieces)):
        moves = [(r, r ^ shift) for r in range(len(pieces))]
        arrived.append(lax.ppermute(pieces[shift], "row", moves))
    return arrived


def paired_entries(matrices):
    turned = matrices.reshape(C_Z, 2, 2, C_TRI)
    return jnp.transpose(turned, (2, 3, 1, 0)).reshape(2 * C_TRI, 2 * C_Z)


def body(
    homolog_tensor,
    couplings,
    attention_probe_matrix,
    attention_extra_matrices,
    attention_final_matrix,
    tensor_entry_matrices,
    tensor_final_matrix,
    incoming_entry_matrices,
    incoming_switch_matrix,
    incoming_final_matrix,
):
    inner = ATTENTION_UNITS * UNIT_WIDTH
    row_count = lax.axis_size("row")
    seqs, residues, depth = homolog_tensor.shape
    own_residues = residues // row_count
    sources = lax.axis_index("row") ^ jnp.arange(row_count, dtype=jnp.int32)
    high = exchange_rows(standardise_high(sources, homolog_tensor))
    low = standardise_low(sources, homolog_tensor)
    others = jnp.concatenate(
        [attention_probe_matrix.T, attention_extra_matrices[:, inner:].T], axis=0
    )
    early = (
        attention_extra_matrices[:, :inner],
        others,
        attention_final_matrix.T,
        tensor_entry_matrices.T,
        paired_entries(incoming_entry_matrices),
        sources * own_residues,
        left_groups(row_count, own_residues),
    )
    high, low, early = lax.optimization_barrier((high, low, early))
    key_matrix, others, final_turned, tensor_turned, entries, firsts, slots = early
    low = exchange_rows(low)
    turned = attention(high, key_matrix, others)
    gated = turn_back(turned, row_count)
    left_piece, right_piece = alignment(
        sources, high, low, turned, final_turned, tensor_turned
    )

    rights = exchange_rows([right_piece] * row_count)
    later, rights[1] = lax.optimization_barrier((left_piece, rights[1]))
    own = gather_turned(left_piece, later)
    own, rights = lax.optimization_barrier((own, rights))
    mid, gate, sides = pair_update(
        slots,
        firsts,
        both_cores(own),
        rights,
        tensor_final_matrix,
        couplings,
        entries,
        incoming_switch_matrix,
    )
    gated, sides = lax.optimization_barrier((gated, sides))
    gated = exchange_rows(gated)

    everywhere = ("row", "col")
    column_count = lax.axis_size("col")
    devices = row_count * column_count
    sides = sides.reshape(devices, C_TRI // devices, *sides.shape[1:])
    sides = lax.all_to_all(sides, everywhere, split_axis=0, concat_axis=0)
    gated, sides = lax.optimization_barrier((gated, sides))
    product = triangle_product(sides, row_count, column_count)
    product = lax.all_to_all(product, everywhere, split_axis=0, concat_axis=0)

    gated = jnp.take(jnp.stack(gated), sources, axis=0)
    gated = jnp.transpose(gated.reshape(residues, seqs, inner), (1, 0, 2))
    change = jnp.dot(
        gated.reshape(-1, inner), attention_final_matrix, preferred_element_type=F32
    )
    refreshed_homologs = homolog_tensor + change.reshape(homolog_tensor.shape)
    product = product.reshape(C_TRI, *product.shape[2:])
    pair_output = pair_result(product, mid, gate, incoming_final_matrix)
    return (refreshed_homologs, pair_output)


def solution(mesh):
    in_specs = (
        P("row", "col", None),
        P("row", "col", None),
        P(),
        P(),
        P(),
        P(),
        P(),
        P(),
        P(),
        P(),
    )
    out_specs = (P("row", "col", None), P("row", "col", None))
    return jax.shard_map(body, mesh=mesh, in_specs=in_specs, out_specs=out_specs, check_vma=False)
```

```python
import functools

import jax
import jax.numpy as jnp
from jax import lax
from jax.experimental import pallas as pl
from jax.experimental.pallas import tpu as pltpu
from jax.sharding import PartitionSpec as P

FEATURE_DEPTH = 256
C_Z = 128
TENSOR_FEATURES = 32
C_TRI = 128
ATTENTION_UNITS = 8
UNIT_WIDTH = 32
EPS = 1e-05
GROUP = 4
F32 = jnp.float32
BF16 = jnp.bfloat16
NT = (((1,), (1,)), ((), ()))


def matmul(left, right):
    return jnp.dot(left, right, preferred_element_type=F32)


def matmul_nt(left, right):
    return lax.dot_general(left, right, NT, preferred_element_type=F32)


def sigmoid(values):
    return 0.5 * jnp.tanh(0.5 * values) + 0.5


def cost(microseconds):
    return pl.CostEstimate(
        flops=int(microseconds * 1e9), bytes_accessed=int(microseconds * 1e6), transcendentals=0
    )


def params(megabytes, *semantics):
    return pltpu.CompilerParams(
        dimension_semantics=semantics or None, vmem_limit_bytes=megabytes * 1024 * 1024
    )


def fold(values, combine):
    while values.shape[0] > 8:
        half = values.shape[0] // 2
        values = combine(values[:half], values[half:])
    return values


def top_rows(values):
    return jnp.max(fold(values, jnp.maximum), axis=0, keepdims=True)


def sum_rows(values):
    return jnp.sum(fold(values, jnp.add), axis=0, keepdims=True)


def normalise_rows(values):
    count = values.shape[0]
    centred = values - sum_rows(values) * (1.0 / count)
    variance = sum_rows(centred * centred) * (1.0 / count)
    return (centred * lax.rsqrt(variance + EPS)).astype(BF16)


def standardised_column(first_rows, second_rows, n, residues):
    seqs = first_rows.shape[0] // residues
    rows = pl.ds(n, seqs, stride=residues)
    column = jnp.concatenate([first_rows[rows, :], second_rows[rows, :]], axis=1)
    centred = column - jnp.mean(column, axis=1, keepdims=True)
    variance = jnp.mean(centred * centred, axis=1, keepdims=True) + EPS
    scale = lax.rsqrt(variance)
    return centred * scale, variance * scale


def high_kernel(sources_ref, block_hbm, *rest):
    *pieces, first_ref, second_ref, fetched = rest
    seqs, residues, lanes = first_ref.shape
    own = residues // len(pieces)
    step = 16
    fetches = []
    for s in range(0, seqs, step):
        chosen = pl.ds(s, step)
        for half, ref in enumerate((first_ref, second_ref)):
            source = block_hbm.at[chosen, :, pl.ds(half * lanes, lanes)]
            fetches.append(
                pltpu.make_async_copy(source, ref.at[chosen], fetched.at[len(fetches)])
            )
            fetches[-1].start()
    firsts = [sources_ref[p] * own for p in range(len(pieces))]
    for part in range(seqs // step):
        chosen = pl.ds(part * step, step)
        fetches[2 * part].wait()
        fetches[2 * part + 1].wait()
        first_rows = first_ref.at[chosen].reshape(step * residues, lanes)
        second_rows = second_ref.at[chosen].reshape(step * residues, lanes)
        for piece_ref, first in zip(pieces, firsts):
            for n in range(own):
                normed, _ = standardised_column(first_rows, second_rows, first + n, residues)
                piece_ref[n, part * step : (part + 1) * step, :] = normed.astype(BF16)


def standardise_high(sources, block):
    seqs, residues, depth = block.shape
    half = depth // 2
    count = sources.shape[0]
    piece = jax.ShapeDtypeStruct((residues // count, seqs, depth), BF16)
    return pl.pallas_call(
        high_kernel,
        in_specs=[
            pl.BlockSpec(memory_space=pltpu.SMEM),
            pl.BlockSpec(memory_space=pltpu.HBM),
        ],
        out_specs=[pl.BlockSpec(memory_space=pltpu.VMEM)] * count,
        out_shape=[piece] * count,
        scratch_shapes=[
            pltpu.VMEM((seqs, residues, half), F32),
            pltpu.VMEM((seqs, residues, half), F32),
            pltpu.SemaphoreType.DMA((seqs // 8,)),
        ],
        compiler_params=params(10),
        cost_estimate=cost(3),
        name="standardise_high",
    )(sources, pltpu.with_memory_space_constraint(block, pltpu.HBM))


def low_kernel(sources_ref, first_ref, second_ref, *pieces):
    seqs, residues, lanes = first_ref.shape
    own = residues // len(pieces)
    first_rows = first_ref.reshape(seqs * residues, lanes)
    second_rows = second_ref.reshape(seqs * residues, lanes)
    lane = lax.broadcasted_iota(jnp.int32, (seqs, 128), 1)
    for p, piece_ref in enumerate(pieces):
        first = sources_ref[p] * own
        spreads = jnp.zeros((seqs, 128), F32)
        for n in range(own):
            normed, spread = standardised_column(first_rows, second_rows, first + n, residues)
            left = (normed - normed.astype(BF16).astype(F32)).astype(BF16)
            piece_ref[n * seqs : (n + 1) * seqs, :] = left
            spreads = jnp.where(lane == n, spread, spreads)
        spreads = spreads.T[:8, :]
        coarse = spreads.astype(BF16).astype(F32)
        kept = jnp.concatenate([coarse, spreads - coarse], axis=0)
        kept = jnp.concatenate([kept, jnp.zeros((16, 2 * lanes - seqs), F32)], axis=1)
        piece_ref[own * seqs :, :] = kept.astype(BF16)


def standardise_low(sources, block):
    seqs, residues, depth = block.shape
    half = depth // 2
    count = sources.shape[0]
    height = residues // count * seqs + 16
    return pl.pallas_call(
        low_kernel,
        grid=(1,),
        in_specs=[
            pl.BlockSpec(memory_space=pltpu.SMEM),
            pl.BlockSpec((seqs, residues, half), lambda g: (0, 0, 0)),
            pl.BlockSpec((seqs, residues, half), lambda g: (0, 0, 1)),
        ],
        out_specs=[pl.BlockSpec((height, depth), lambda g: (0, 0))] * count,
        out_shape=[jax.ShapeDtypeStruct((height, depth), BF16)] * count,
        compiler_params=params(14, "arbitrary"),
        cost_estimate=cost(4),
        name="standardise_low",
    )(sources, block, block)


def attention_kernel(probe_ref, extra_ref, *rest):
    *normed_refs, turned_ref, scores_ref, weights_ref, others_ref = rest
    blocks = len(normed_refs)
    residues, seqs, _ = normed_refs[0].shape
    total = blocks * seqs
    inner = ATTENTION_UNITS * UNIT_WIDTH
    ring = scores_ref.shape[0]
    columns = []

    @pl.when(pl.program_id(0) == 0)
    def _():
        others_ref[:inner, :] = probe_ref[...].T
        others_ref[inner:, :] = extra_ref[:, inner:].T

    def project(n):
        column = jnp.concatenate([ref[n] for ref in normed_refs], axis=0)
        key_rows = matmul(column, extra_ref[:, :inner]).astype(BF16)
        projected = matmul_nt(others_ref[...], column)
        queries = (projected[:inner] * UNIT_WIDTH ** (-0.5)).astype(BF16)
        value_rows = projected[inner : 2 * inner].astype(BF16)
        gates = sigmoid(projected[2 * inner :])
        columns.append((key_rows, queries, value_rows, gates))
    units = [(n, h) for n in range(residues) for h in range(ATTENTION_UNITS)]

    def score(unit):
        n, h = units[unit]
        key_rows, queries, _, _ = columns[n]
        low, high = h * UNIT_WIDTH, (h + 1) * UNIT_WIDTH
        pieces = [queries[low:high]]
        if low > 0:
            pieces.insert(0, jnp.zeros((low, total), BF16))
        if high < inner:
            pieces.append(jnp.zeros((inner - high, total), BF16))
        scores_ref[unit % ring] = matmul(key_rows, jnp.concatenate(pieces, axis=0))

    def weigh(unit):
        for low in range(0, total, 128):
            scores = scores_ref[unit % ring, :, low : low + 128]
            weights = jnp.exp(scores - top_rows(scores))
            scale = 1.0 / sum_rows(weights)
            weights_ref[unit % ring, :, low : low + 128] = (weights * scale).astype(BF16)

    def attend(unit):
        n, h = units[unit]
        _, _, value_rows, gates = columns[n]
        rows = slice(h * UNIT_WIDTH, (h + 1) * UNIT_WIDTH)
        attended = matmul(value_rows[rows], weights_ref[unit % ring]) * gates[rows]
        turned_ref[n, rows, :] = attended.astype(BF16)

    project(0)
    for step in range(len(units) + 2):
        if step < len(units):
            score(step)
            n, h = units[step]
            if h == ATTENTION_UNITS // 2 and n + 1 < residues:
                project(n + 1)
        if 1 <= step <= len(units):
            weigh(step - 1)
        if step >= 2:
            attend(step - 2)


def attention(normed, probe_matrix, extra_matrices):
    blocks = len(normed)
    residues, seqs, depth = normed[0].shape
    total = blocks * seqs
    inner = ATTENTION_UNITS * UNIT_WIDTH
    step = 4
    return pl.pallas_call(
        attention_kernel,
        grid=(residues // step,),
        in_specs=[
            pl.BlockSpec(probe_matrix.shape, lambda n: (0, 0)),
            pl.BlockSpec(extra_matrices.shape, lambda n: (0, 0)),
        ]
        + [pl.BlockSpec((step, seqs, depth), lambda n: (n, 0, 0))] * blocks,
        out_specs=pl.BlockSpec((step, inner, total), lambda n: (n, 0, 0)),
        out_shape=jax.ShapeDtypeStruct((residues, inner, total), BF16),
        scratch_shapes=[
            pltpu.VMEM((4, total, total), F32),
            pltpu.VMEM((4, total, total), BF16),
            pltpu.VMEM((3 * inner, depth), BF16),
        ],
        compiler_params=params(12 + (total // 128) ** 2, "arbitrary"),
        cost_estimate=cost(10),
        name="attention",
    )(probe_matrix, extra_matrices, *normed)


def turn_kernel(turned_ref, *gated_refs):
    seqs = gated_refs[0].shape[1]
    for n in range(turned_ref.shape[0]):
        back = turned_ref[n].T
        for block, gated_ref in enumerate(gated_refs):
            gated_ref[n] = back[block * seqs : (block + 1) * seqs]


def turn_back(turned, blocks):
    residues, inner, total = turned.shape
    seqs = total // blocks
    return pl.pallas_call(
        turn_kernel,
        grid=(residues // 2,),
        in_specs=[pl.BlockSpec((2, inner, total), lambda n: (n, 0, 0))],
        out_specs=[pl.BlockSpec((2, seqs, inner), lambda n: (n, 0, 0))] * blocks,
        out_shape=[pltpu.HBM((residues, seqs, inner), BF16)] * blocks,
        compiler_params=params(12, "arbitrary"),
        cost_estimate=cost(2),
        name="turn_back",
    )(turned)


def alignment_kernel(sources_ref, turned_ref, final_ref, entry_ref, *rest):
    *refs, left_ref, right_ref, rows_ref, turned_final_ref = rest
    blocks = len(refs) // 3
    high_refs, low_refs, spread_refs = refs[:blocks], refs[blocks : 2 * blocks], refs[2 * blocks :]
    residues, seqs, depth = high_refs[0].shape
    total = blocks * seqs
    features = TENSOR_FEATURES
    step = pl.program_id(0)

    @pl.when(step == 0)
    def _():
        turned_final_ref[...] = final_ref[...].T

    for n in range(residues):
        column = jnp.concatenate([ref[n] for ref in high_refs], axis=0).astype(F32)
        column = column + jnp.concatenate(
            [ref[n * seqs : (n + 1) * seqs, :] for ref in low_refs], axis=0
        ).astype(F32)
        spreads = []
        for ref in spread_refs:
            kept = ref[:, :seqs].astype(F32)
            row = lax.broadcasted_iota(jnp.int32, kept.shape, 0)
            chosen = lax.rem(row, 8) == step * residues + n
            spreads.append(jnp.sum(jnp.where(chosen, kept, 0.0), axis=0, keepdims=True))
        spread = jnp.concatenate(spreads, axis=1)
        updated = column.T * spread + matmul(turned_final_ref[...], turned_ref[n])
        projected = matmul(entry_ref[...], normalise_rows(updated))
        me = sources_ref[0]
        tiles = [projected[:, low : low + 128] for low in range(0, total, 128)]
        odd = lax.rem(me, 2) == 1
        tiles = [jnp.where(odd, pltpu.roll(tile, seqs, 1), tile) for tile in tiles]
        width = 1
        while width < len(tiles):
            crossed = lax.rem(lax.div(me, 2 * width), 2) == 1
            tiles = [
                jnp.where(crossed, tiles[t ^ width], tiles[t]) for t in range(len(tiles))
            ]
            width *= 2
        first = pl.multiple_of((step * residues + n) * features, features)
        for t, tile in enumerate(tiles):
            right_ref[n, :, t * 128 : (t + 1) * 128] = tile[features:].astype(BF16)
            rows_ref[t, pl.ds(first, features), :] = tile[:features]

    @pl.when(step == pl.num_programs(0) - 1)
    def _():
        count = rows_ref.shape[1] // features
        together = max(1, 16 // count)
        for c in range(0, features, together):
            pieces = []
            for e in range(together):
                chosen = pl.ds(c + e, count, stride=features)
                tiles = [rows_ref[tile, chosen, :] for tile in range(total // 128)]
                pieces.append(jnp.concatenate(tiles, axis=1))
            piece = jnp.concatenate(pieces, axis=0).astype(BF16)
            left_ref[c * count : (c + together) * count, :] = piece


def alignment(sources, high, low, turned, final_matrix, entry_matrices):
    blocks = len(high)
    residues, seqs, depth = high[0].shape
    total = blocks * seqs
    features = TENSOR_FEATURES
    step = 4
    height = residues * seqs + 16
    return pl.pallas_call(
        alignment_kernel,
        grid=(residues // step,),
        in_specs=[
            pl.BlockSpec(memory_space=pltpu.SMEM),
            pl.BlockSpec((step, depth, total), lambda n: (n, 0, 0)),
            pl.BlockSpec(final_matrix.shape, lambda n: (0, 0)),
            pl.BlockSpec(entry_matrices.shape, lambda n: (0, 0)),
        ]
        + [pl.BlockSpec((step, seqs, depth), lambda n: (n, 0, 0))] * blocks
        + [pl.BlockSpec((step * seqs, depth), lambda n: (n, 0))] * blocks
        + [pl.BlockSpec((16, depth), lambda n: (height // 16 - 1, 0))] * blocks,
        out_specs=[
            pl.BlockSpec((features * residues, total), lambda n: (0, 0)),
            pl.BlockSpec((step, features, total), lambda n: (n, 0, 0)),
        ],
        out_shape=[
            jax.ShapeDtypeStruct((features * residues, total), BF16),
            jax.ShapeDtypeStruct((residues, features, total), BF16),
        ],
        scratch_shapes=[
            pltpu.VMEM((total // 128, residues * features, 128), F32),
            pltpu.VMEM(final_matrix.shape, BF16),
        ],
        compiler_params=params(16, "arbitrary"),
        cost_estimate=cost(4),
        name="alignment",
    )(sources, turned, final_matrix, entry_matrices, *high, *low, *low)


def pair_kernel(
    left_slots_ref,
    right_firsts_ref,
    own_ref,
    other_ref,
    *rest,
):
    weights_ref, entry_ref, switch_ref, couplings_hbm, mid_hbm, gate_hbm, sides_hbm = rest[-16:-9]
    outer_ref, spread_ref, sum_ref, rows_ref, couplings_ref = rest[-9:-4]
    mid_ref, gate_ref, sides_ref, copied = rest[-4:]
    right_refs = rest[:-16]
    fetched = pltpu.make_async_copy(couplings_hbm, couplings_ref, copied.at[0])
    fetched.start()
    copies = []

    def send(source, target):
        copies.append(pltpu.make_async_copy(source, target, copied.at[len(copies) + 1]))
        copies[-1].start()

    features = TENSOR_FEATURES
    slots, piece_rows, total = own_ref.shape
    residues = piece_rows // features
    rows = 2 * slots * residues
    share = right_refs[0].shape[0]
    columns = len(right_refs) * share
    groups = columns // GROUP
    wide = share * features
    together = spread_ref.shape[1] // 64

    for half, left_ref in enumerate((own_ref, other_ref)):
        piece = left_ref[...].reshape(slots * piece_rows, total)
        target = slice(half * slots * piece_rows, (half + 1) * slots * piece_rows)
        for p, right_ref in enumerate(right_refs):
            right = right_ref[...].reshape(wide, total)
            outer_ref[target, p * wide : (p + 1) * wide] = matmul_nt(piece, right) * (1.0 / total)

    spread_ref[...] = jnp.zeros_like(spread_ref)
    front = lax.broadcasted_iota(jnp.int32, (rows, 128), 1) < 64

    def channel_step(p, carry):
        slot = lax.rem(p, 2)
        for e in range(together):
            source = pl.multiple_of((p * together + e) * features, features)
            piece = weights_ref[pl.ds(source, features), :]
            for place in range(2):
                low = e * 64 + place * features
                spread_ref[slot, low : low + features, place * C_Z : (place + 1) * C_Z] = piece
        pieces = []
        for g in range(groups):
            parts = []
            for e in range(together):
                channel = []
                for slot_number in range(2 * slots):
                    first = slot_number * piece_rows + (p * together + e) * residues
                    source = pl.ds(pl.multiple_of(first, residues), residues)
                    channel.append(outer_ref[source, g * 128 : (g + 1) * 128])
                parts.append(jnp.concatenate(channel, axis=0).astype(BF16))
            lows, highs = [], []
            for e in range(0, together, 2):
                lows.append(jnp.where(front, parts[e], pltpu.roll(parts[e + 1], 64, 1)))
                highs.append(jnp.where(front, pltpu.roll(parts[e], 64, 1), parts[e + 1]))
            pieces.append(jnp.concatenate(lows, axis=1))
            pieces.append(jnp.concatenate(highs, axis=1))
        update = matmul(jnp.concatenate(pieces, axis=0), spread_ref[slot])

        @pl.when(p == 0)
        def _():
            sum_ref[...] = update

        @pl.when(p > 0)
        def _():
            sum_ref[...] += update

        return carry

    lax.fori_loop(0, features // together, channel_step, 0)

    left_firsts = [left_slots_ref[j] * residues for j in range(2 * slots)]
    right_firsts = [right_firsts_ref[p] for p in range(len(right_refs))]
    fetched.wait()
    for g in range(groups):
        normed, places = [], []
        for place in range(GROUP):
            p, n = divmod(g * GROUP + place, share)
            b = right_firsts[p] + n
            places.append(b)
            lanes = slice(place % 2 * C_Z, (place % 2 + 1) * C_Z)
            start = (2 * g + place // 2) * rows
            pieces = []
            for first in left_firsts:
                source = pl.ds(pl.multiple_of(start + first, residues), residues)
                pieces.append(sum_ref[source, lanes])
            mid = jnp.concatenate(pieces, axis=0)
            mid = mid + couplings_ref[pl.ds(b, rows, stride=columns), :]
            mid_ref[g * GROUP + place] = mid
            centred = mid - jnp.mean(mid, axis=1, keepdims=True)
            variance = jnp.mean(centred * centred, axis=1, keepdims=True)
            normed.append((centred * lax.rsqrt(variance + EPS)).astype(BF16))
        gates = sigmoid(matmul(jnp.concatenate(normed, axis=0), switch_ref[...]))
        blank = jnp.zeros_like(normed[0])
        for place in range(0, GROUP, 2):
            twice = []
            for e in range(2):
                part = gates[(place + e) * rows : (place + e + 1) * rows]
                gate_ref[g * GROUP + place + e] = part
                twice.append(jnp.concatenate([normed[place + e], blank], axis=1))
                twice.append(jnp.concatenate([blank, normed[place + e]], axis=1))
            sides = matmul_nt(entry_ref[...], jnp.concatenate(twice, axis=0))
            sides = sigmoid(sides[C_TRI:]) * sides[:C_TRI]
            for e in range(2):
                first = pl.multiple_of(places[place + e] * C_TRI, C_TRI)
                rows_ref[pl.ds(first, C_TRI), :] = sides[:, e * 2 * rows : (e + 1) * 2 * rows]

        if (g + 1) * GROUP % share == 0:
            p = (g + 1) * GROUP // share - 1
            source, target = pl.ds(p * share, share), pl.ds(right_firsts[p], share)
            send(mid_ref.at[source], mid_hbm.at[target])
            send(gate_ref.at[source], gate_hbm.at[target])

    cut = C_TRI // 4
    for part in range(4):

        def turn_step(c, carry):
            sides_ref[c] = rows_ref[pl.ds(c, columns, stride=C_TRI), :].astype(BF16)
            return carry

        lax.fori_loop(part * cut, (part + 1) * cut, turn_step, 0, unroll=8)
        chosen = pl.ds(part * cut, cut)
        send(sides_ref.at[chosen], sides_hbm.at[chosen])
    for copy in copies:
        copy.wait()


def pair_update(left_slots, right_firsts, left, rights, weights, couplings, entry, switch):
    rows, columns, depth = couplings.shape
    whole = jax.ShapeDtypeStruct((columns, rows, depth), F32)
    sides = jax.ShapeDtypeStruct((C_TRI, columns, 2 * rows), BF16)
    smem = pl.BlockSpec(memory_space=pltpu.SMEM)
    vmem = pl.BlockSpec(memory_space=pltpu.VMEM)
    anywhere = pl.BlockSpec(memory_space=pl.ANY)
    return pl.pallas_call(
        pair_kernel,
        in_specs=[smem] * 2 + [vmem] * (5 + len(rights)) + [anywhere],
        out_specs=[anywhere] * 3,
        out_shape=[pltpu.HBM(whole.shape, F32)] * 2 + [pltpu.HBM(sides.shape, BF16)],
        scratch_shapes=[
            pltpu.VMEM((rows * TENSOR_FEATURES, columns * TENSOR_FEATURES), F32),
            pltpu.VMEM((2, 8 * 64, 2 * depth), BF16),
            pltpu.VMEM((columns // 2 * rows, 2 * depth), F32),
            pltpu.VMEM((columns * C_TRI, 2 * rows), F32),
            pltpu.VMEM((rows * columns, depth), F32),
            pltpu.VMEM(whole.shape, F32),
            pltpu.VMEM(whole.shape, F32),
            pltpu.VMEM(sides.shape, BF16),
            pltpu.SemaphoreType.DMA((2 * len(rights) + 5,)),
        ],
        compiler_params=params(28),
        cost_estimate=cost(12),
        name="pair_update",
    )(
        left_slots,
        right_firsts,
        *left,
        *rights,
        weights,
        entry,
        switch,
        couplings.reshape(rows * columns, depth),
    )


def product_kernel(sides_ref, out_ref, *, grid_rows, grid_columns):
    channels, part, lanes = sides_ref.shape[1:]
    half = lanes // 2
    lane = lax.broadcasted_iota(jnp.int32, (grid_columns * part, lanes), 1)
    front = lane < half
    cut = front[: part // 2]
    for channel in range(channels):
        lefts, rights = [], []
        for r in range(0, grid_rows, 2):
            even, odd = [
                jnp.concatenate(
                    [sides_ref[(r + e) * grid_columns + c, channel] for c in range(grid_columns)],
                    axis=0,
                )
                for e in range(2)
            ]
            lefts.append(jnp.where(front, even, pltpu.roll(odd, half, 1)))
            rights.append(jnp.where(front, pltpu.roll(even, half, 1), odd))
        product = matmul_nt(jnp.concatenate(rights, axis=1), jnp.concatenate(lefts, axis=1))
        product = product.astype(BF16)
        for c in range(grid_columns):
            for r in range(0, grid_rows, 2):
                block = product[c * part : (c + 1) * part, r * half : (r + 2) * half]
                top, bottom = block[: part // 2], block[part // 2 :]
                even = jnp.where(cut, top, pltpu.roll(bottom, half, 1))
                out_ref[r * grid_columns + c, channel] = even
                odd = jnp.where(cut, pltpu.roll(top, half, 1), bottom)
                out_ref[(r + 1) * grid_columns + c, channel] = odd


def triangle_product(sides, grid_rows, grid_columns):
    devices, channels, part, lanes = sides.shape
    step = 2 if channels % 2 == 0 else 1
    return pl.pallas_call(
        functools.partial(product_kernel, grid_rows=grid_rows, grid_columns=grid_columns),
        grid=(channels // step,),
        in_specs=[pl.BlockSpec((devices, step, part, lanes), lambda c: (0, c, 0, 0))],
        out_specs=pl.BlockSpec((devices, step, part // 2, lanes), lambda c: (0, c, 0, 0)),
        out_shape=pltpu.HBM((devices, channels, part // 2, lanes), BF16),
        compiler_params=params(8, "arbitrary"),
        cost_estimate=cost(3),
        name="triangle_product",
    )(sides)


def output_kernel(
    product_ref, final_ref, mid_hbm, gate_hbm, out_hbm, wide_ref, mid_ref, gate_ref, out_ref, *copied
):
    channels, part, lanes = product_ref.shape
    columns, rows, depth = mid_ref.shape
    own = 8
    fetched, sent = copied
    fetches, sends = [], []
    for first in range(0, columns, own):
        chosen = pl.ds(first, own)
        for source, target in ((mid_hbm, mid_ref), (gate_hbm, gate_ref)):
            fetches.append(
                pltpu.make_async_copy(
                    source.at[chosen], target.at[chosen], fetched.at[len(fetches)]
                )
            )
            fetches[-1].start()
    wide_ref[...] = product_ref[...].astype(F32).reshape(channels * part, lanes)
    for group in range(part // own):
        updates = []
        for j in range(own):
            product = wide_ref[pl.ds(group * own + j, channels, stride=part), :]
            updates.append(matmul(normalise_rows(product).T, final_ref[...]))
        for half in range(2):
            cut = half * (part // own) + group
            fetches[2 * cut].wait()
            fetches[2 * cut + 1].wait()
            out_rows = out_ref.at[cut].reshape(rows * own, depth)
            for j in range(own):
                b = cut * own + j
                piece = updates[j][half * rows : (half + 1) * rows]
                out_rows[pl.ds(j, rows, stride=own), :] = mid_ref[b] + gate_ref[b] * piece
            sends.append(
                pltpu.make_async_copy(
                    out_ref.at[cut], out_hbm.at[:, pl.ds(cut * own, own)], sent.at[len(sends)]
                )
            )
            sends[-1].start()
    for send in sends:
        send.wait()


def pair_result(product, mid, gate, final_matrix):
    channels, part, lanes = product.shape
    columns, rows, depth = mid.shape
    vmem, hbm = pl.BlockSpec(memory_space=pltpu.VMEM), pl.BlockSpec(memory_space=pltpu.HBM)
    return pl.pallas_call(
        output_kernel,
        in_specs=[vmem, vmem, hbm, hbm],
        out_specs=hbm,
        out_shape=pltpu.HBM((rows, columns, depth), F32),
        scratch_shapes=[
            pltpu.VMEM((channels * part, lanes), F32),
            pltpu.VMEM(mid.shape, F32),
            pltpu.VMEM(mid.shape, F32),
            pltpu.VMEM((columns // 8, rows, 8, depth), F32),
            pltpu.SemaphoreType.DMA((columns // 4,)),
            pltpu.SemaphoreType.DMA((columns // 8,)),
        ],
        compiler_params=params(16),
        cost_estimate=cost(3),
        name="pair_result",
    )(
        product,
        final_matrix,
        pltpu.with_memory_space_constraint(mid, pltpu.HBM),
        pltpu.with_memory_space_constraint(gate, pltpu.HBM),
    )


def swap_cores(block):
    count = lax.axis_size("col")
    return lax.ppermute(block, "col", [(c, c ^ 1) for c in range(count)])


def gather_turned(block, later):
    rows, columns = lax.axis_size("row"), lax.axis_size("col")
    arrived = []
    for shift in range(rows):
        moves = []
        for r in range(rows):
            for q in range(rows):
                for side in range(2):
                    source = r * columns + 2 * q + side
                    moves.append((source, q * columns + 2 * ((r + shift) % rows) + side))
        source = block if shift < 2 else later
        arrived.append(lax.ppermute(source, ("row", "col"), moves))
    return jnp.stack(arrived)


def both_cores(own):
    rows = lax.axis_size("row")
    core = lax.rem(lax.axis_index("col"), 2)
    other = swap_cores(own)
    residues = own.shape[1] // TENSOR_FEATURES
    if residues % 8 == 0:
        return own, other
    order = left_order(rows)
    own, other = jnp.take(own, order, axis=0), jnp.take(other, order, axis=0)
    joined = 8 // residues
    ordered = []
    for side in (jnp.where(core == 0, own, other), jnp.where(core == 0, other, own)):
        side = side.reshape(rows // joined, joined, TENSOR_FEATURES, residues, -1)
        side = jnp.transpose(side, (0, 2, 1, 3, 4))
        ordered.append(side.reshape(rows // joined, joined * own.shape[1], -1))
    return tuple(ordered)


def left_order(rows):
    me = lax.axis_index("col") // 2
    return lax.rem(me - jnp.arange(rows, dtype=jnp.int32) + rows, rows)


def left_groups(rows, residues):
    if residues % 8:
        return jnp.arange(2 * rows * residues // 8, dtype=jnp.int32)
    core = lax.rem(lax.axis_index("col"), 2)
    order = left_order(rows)
    return jnp.concatenate([order + core * rows, order + (1 - core) * rows])


def exchange_rows(pieces):
    arrived = [pieces[0]]
    for shift in range(1, len(pieces)):
        moves = [(r, r ^ shift) for r in range(len(pieces))]
        arrived.append(lax.ppermute(pieces[shift], "row", moves))
    return arrived


def paired_entries(matrices):
    turned = matrices.reshape(C_Z, 2, 2, C_TRI)
    return jnp.transpose(turned, (2, 3, 1, 0)).reshape(2 * C_TRI, 2 * C_Z)


def body(
    homolog_tensor,
    couplings,
    attention_probe_matrix,
    attention_extra_matrices,
    attention_final_matrix,
    tensor_entry_matrices,
    tensor_final_matrix,
    incoming_entry_matrices,
    incoming_switch_matrix,
    incoming_final_matrix,
):
    inner = ATTENTION_UNITS * UNIT_WIDTH
    row_count = lax.axis_size("row")
    seqs, residues, depth = homolog_tensor.shape
    own_residues = residues // row_count
    sources = lax.axis_index("row") ^ jnp.arange(row_count, dtype=jnp.int32)
    high = exchange_rows(standardise_high(sources, homolog_tensor))
    low = standardise_low(sources, homolog_tensor)
    early = (
        tensor_entry_matrices.T,
        paired_entries(incoming_entry_matrices),
        sources * own_residues,
        left_groups(row_count, own_residues),
    )
    low, high[1] = lax.optimization_barrier((low, high[1]))
    high, early = lax.optimization_barrier((high, early))
    tensor_turned, entries, firsts, slots = early
    low = exchange_rows(low)
    turned = attention(high, attention_probe_matrix, attention_extra_matrices)
    gated = turn_back(turned, row_count)
    left_piece, right_piece = alignment(
        sources, high, low, turned, attention_final_matrix, tensor_turned
    )

    rights = exchange_rows([right_piece] * row_count)
    later, rights[1] = lax.optimization_barrier((left_piece, rights[1]))
    own = gather_turned(left_piece, later)
    own, rights = lax.optimization_barrier((own, rights))
    mid, gate, sides = pair_update(
        slots,
        firsts,
        both_cores(own),
        rights,
        tensor_final_matrix,
        couplings,
        entries,
        incoming_switch_matrix,
    )
    gated, sides = lax.optimization_barrier((gated, sides))
    gated = exchange_rows(gated)

    everywhere = ("row", "col")
    column_count = lax.axis_size("col")
    devices = row_count * column_count
    sides = sides.reshape(devices, C_TRI // devices, *sides.shape[1:])
    sides = lax.all_to_all(sides, everywhere, split_axis=0, concat_axis=0)
    gated, sides = lax.optimization_barrier((gated, sides))
    product = triangle_product(sides, row_count, column_count)
    product = lax.all_to_all(product, everywhere, split_axis=0, concat_axis=0)

    gated = jnp.take(jnp.stack(gated), sources, axis=0)
    gated = jnp.transpose(gated.reshape(residues, seqs, inner), (1, 0, 2))
    change = jnp.dot(
        gated.reshape(-1, inner), attention_final_matrix, preferred_element_type=F32
    )
    refreshed_homologs = homolog_tensor + change.reshape(homolog_tensor.shape)
    product = product.reshape(C_TRI, *product.shape[2:])
    pair_output = pair_result(product, mid, gate, incoming_final_matrix)
    return (refreshed_homologs, pair_output)


def solution(mesh):
    in_specs = (
        P("row", "col", None),
        P("row", "col", None),
        P(),
        P(),
        P(),
        P(),
        P(),
        P(),
        P(),
        P(),
    )
    out_specs = (P("row", "col", None), P("row", "col", None))
    return jax.shard_map(body, mesh=mesh, in_specs=in_specs, out_specs=out_specs, check_vma=False)
```

```python
import functools

import jax
import jax.numpy as jnp
from jax import lax
from jax.experimental import pallas as pl
from jax.experimental.pallas import tpu as pltpu
from jax.sharding import PartitionSpec as P

FEATURE_DEPTH = 256
C_Z = 128
TENSOR_FEATURES = 32
C_TRI = 128
ATTENTION_UNITS = 8
UNIT_WIDTH = 32
EPS = 1e-05
GROUP = 4
F32 = jnp.float32
BF16 = jnp.bfloat16
NT = (((1,), (1,)), ((), ()))


def matmul(left, right):
    return jnp.dot(left, right, preferred_element_type=F32)


def matmul_nt(left, right):
    return lax.dot_general(left, right, NT, preferred_element_type=F32)


def sigmoid(values):
    return 0.5 * jnp.tanh(0.5 * values) + 0.5


def cost(microseconds):
    return pl.CostEstimate(
        flops=int(microseconds * 1e9), bytes_accessed=int(microseconds * 1e6), transcendentals=0
    )


def params(megabytes, *semantics):
    return pltpu.CompilerParams(
        dimension_semantics=semantics or None, vmem_limit_bytes=megabytes * 1024 * 1024
    )


def fold(values, combine):
    while values.shape[0] > 8:
        half = values.shape[0] // 2
        values = combine(values[:half], values[half:])
    return values


def top_rows(values):
    return jnp.max(fold(values, jnp.maximum), axis=0, keepdims=True)


def sum_rows(values):
    return jnp.sum(fold(values, jnp.add), axis=0, keepdims=True)


def normalise_rows(values):
    count = values.shape[0]
    centred = values - sum_rows(values) * (1.0 / count)
    variance = sum_rows(centred * centred) * (1.0 / count)
    return (centred * lax.rsqrt(variance + EPS)).astype(BF16)


def standardised_columns(first_rows, second_rows, first, count, residues):
    seqs = first_rows.shape[0] // residues
    columns = []
    for n in range(first, first + count):
        rows = pl.ds(n, seqs, stride=residues)
        columns.append(jnp.concatenate([first_rows[rows, :], second_rows[rows, :]], axis=1))
    column = jnp.concatenate(columns, axis=0)
    centred = column - jnp.mean(column, axis=1, keepdims=True)
    variance = jnp.mean(centred * centred, axis=1, keepdims=True) + EPS
    scale = lax.rsqrt(variance)
    return centred * scale, variance * scale


def high_kernel(sources_ref, block_hbm, *rest):
    *pieces_hbm, first_ref, second_ref, high_ref, fetched, sent = rest
    seqs, residues, lanes = first_ref.shape
    own = residues // len(pieces_hbm)
    step = 16
    fetches, sends = [], []
    for s in range(0, seqs, step):
        chosen = pl.ds(s, step)
        for half, ref in enumerate((first_ref, second_ref)):
            source = block_hbm.at[chosen, :, pl.ds(half * lanes, lanes)]
            fetches.append(
                pltpu.make_async_copy(source, ref.at[chosen], fetched.at[len(fetches)])
            )
            fetches[-1].start()
    for part in range(seqs // step):
        chosen = pl.ds(part * step, step)
        fetches[2 * part].wait()
        fetches[2 * part + 1].wait()
        first_rows = first_ref.at[chosen].reshape(step * residues, lanes)
        second_rows = second_ref.at[chosen].reshape(step * residues, lanes)
        for n in range(0, residues, 8):
            normed, _ = standardised_columns(first_rows, second_rows, n, 8, residues)
            high_ref[part, n : n + 8] = normed.astype(BF16).reshape(8, step, 2 * lanes)
        for p, piece_hbm in enumerate(pieces_hbm):
            source = high_ref.at[part, pl.ds(sources_ref[p] * own, own)]
            sends.append(
                pltpu.make_async_copy(source, piece_hbm.at[:, chosen], sent.at[len(sends)])
            )
            sends[-1].start()
    for send in sends:
        send.wait()


def standardise_high(sources, block):
    seqs, residues, depth = block.shape
    half = depth // 2
    count = sources.shape[0]
    hbm = pl.BlockSpec(memory_space=pltpu.HBM)
    return pl.pallas_call(
        high_kernel,
        in_specs=[pl.BlockSpec(memory_space=pltpu.SMEM), hbm],
        out_specs=[hbm] * count,
        out_shape=[pltpu.HBM((residues // count, seqs, depth), BF16)] * count,
        scratch_shapes=[
            pltpu.VMEM((seqs, residues, half), F32),
            pltpu.VMEM((seqs, residues, half), F32),
            pltpu.VMEM((seqs // 16, residues, 16, depth), BF16),
            pltpu.SemaphoreType.DMA((seqs // 8,)),
            pltpu.SemaphoreType.DMA((seqs // 16 * count,)),
        ],
        compiler_params=params(10),
        cost_estimate=cost(3),
        name="standardise_high",
    )(sources, pltpu.with_memory_space_constraint(block, pltpu.HBM))


def low_kernel(sources_ref, first_ref, second_ref, *rest):
    *pieces_hbm, low_ref, sent = rest
    seqs, residues, lanes = first_ref.shape
    own = residues // len(pieces_hbm)
    first_rows = first_ref.reshape(seqs * residues, lanes)
    second_rows = second_ref.reshape(seqs * residues, lanes)
    lane = lax.broadcasted_iota(jnp.int32, (seqs, 128), 1)
    for p in range(len(pieces_hbm)):
        spreads = jnp.zeros((seqs, 128), F32)
        for n in range(own):
            normed, spread = standardised_columns(
                first_rows, second_rows, p * own + n, 1, residues
            )
            left = (normed - normed.astype(BF16).astype(F32)).astype(BF16)
            low_ref[p, n * seqs : (n + 1) * seqs, :] = left
            spreads = jnp.where(lane == n, spread, spreads)
        spreads = spreads.T[:8, :]
        coarse = spreads.astype(BF16).astype(F32)
        kept = jnp.concatenate([coarse, spreads - coarse], axis=0)
        kept = jnp.concatenate([kept, jnp.zeros((16, 2 * lanes - seqs), F32)], axis=1)
        low_ref[p, own * seqs :, :] = kept.astype(BF16)
    sends = []
    for p, piece_hbm in enumerate(pieces_hbm):
        source = low_ref.at[sources_ref[p]]
        sends.append(pltpu.make_async_copy(source, piece_hbm, sent.at[p]))
        sends[-1].start()
    for send in sends:
        send.wait()


def standardise_low(sources, block):
    seqs, residues, depth = block.shape
    half = depth // 2
    count = sources.shape[0]
    height = residues // count * seqs + 16
    hbm = pl.BlockSpec(memory_space=pltpu.HBM)
    return pl.pallas_call(
        low_kernel,
        grid=(1,),
        in_specs=[
            pl.BlockSpec(memory_space=pltpu.SMEM),
            pl.BlockSpec((seqs, residues, half), lambda g: (0, 0, 0)),
            pl.BlockSpec((seqs, residues, half), lambda g: (0, 0, 1)),
        ],
        out_specs=[hbm] * count,
        out_shape=[pltpu.HBM((height, depth), BF16)] * count,
        scratch_shapes=[
            pltpu.VMEM((count, height, depth), BF16),
            pltpu.SemaphoreType.DMA((count,)),
        ],
        compiler_params=params(14, "arbitrary"),
        cost_estimate=cost(4),
        name="standardise_low",
    )(sources, block, block)


def attention_kernel(key_ref, others_ref, *rest):
    *normed_refs, turned_ref, scores_ref, weights_ref = rest
    blocks = len(normed_refs)
    residues, seqs, _ = normed_refs[0].shape
    total = blocks * seqs
    inner = ATTENTION_UNITS * UNIT_WIDTH
    ring = scores_ref.shape[0]
    columns = []

    def project(n):
        column = jnp.concatenate([ref[n] for ref in normed_refs], axis=0)
        key_rows = matmul(column, key_ref[...]).astype(BF16)
        projected = matmul_nt(others_ref[...], column)
        queries = (projected[:inner] * UNIT_WIDTH ** (-0.5)).astype(BF16)
        value_rows = projected[inner : 2 * inner].astype(BF16)
        gates = sigmoid(projected[2 * inner :])
        columns.append((key_rows, queries, value_rows, gates))
    units = [(n, h) for n in range(residues) for h in range(ATTENTION_UNITS)]

    def score(unit):
        n, h = units[unit]
        key_rows, queries, _, _ = columns[n]
        low, high = h * UNIT_WIDTH, (h + 1) * UNIT_WIDTH
        pieces = [queries[low:high]]
        if low > 0:
            pieces.insert(0, jnp.zeros((low, total), BF16))
        if high < inner:
            pieces.append(jnp.zeros((inner - high, total), BF16))
        scores_ref[unit % ring] = matmul(key_rows, jnp.concatenate(pieces, axis=0))

    def weigh(unit):
        for low in range(0, total, 128):
            scores = scores_ref[unit % ring, :, low : low + 128]
            weights = jnp.exp(scores - top_rows(scores))
            scale = 1.0 / sum_rows(weights)
            weights_ref[unit % ring, :, low : low + 128] = (weights * scale).astype(BF16)

    def attend(unit):
        n, h = units[unit]
        _, _, value_rows, gates = columns[n]
        rows = slice(h * UNIT_WIDTH, (h + 1) * UNIT_WIDTH)
        attended = matmul(value_rows[rows], weights_ref[unit % ring]) * gates[rows]
        turned_ref[n, rows, :] = attended.astype(BF16)

    project(0)
    for step in range(len(units) + 2):
        if step < len(units):
            score(step)
            n, h = units[step]
            if h == ATTENTION_UNITS // 2 and n + 1 < residues:
                project(n + 1)
        if 1 <= step <= len(units):
            weigh(step - 1)
        if step >= 2:
            attend(step - 2)


def attention(normed, key_matrix, other_matrices):
    blocks = len(normed)
    residues, seqs, depth = normed[0].shape
    total = blocks * seqs
    inner = ATTENTION_UNITS * UNIT_WIDTH
    step = 4
    return pl.pallas_call(
        attention_kernel,
        grid=(residues // step,),
        in_specs=[
            pl.BlockSpec((depth, inner), lambda n: (0, 0)),
            pl.BlockSpec((3 * inner, depth), lambda n: (0, 0)),
        ]
        + [pl.BlockSpec((step, seqs, depth), lambda n: (n, 0, 0))] * blocks,
        out_specs=pl.BlockSpec((step, inner, total), lambda n: (n, 0, 0)),
        out_shape=jax.ShapeDtypeStruct((residues, inner, total), BF16),
        scratch_shapes=[
            pltpu.VMEM((4, total, total), F32),
            pltpu.VMEM((4, total, total), BF16),
        ],
        compiler_params=params(12 + (total // 128) ** 2, "arbitrary"),
        cost_estimate=cost(10),
        name="attention",
    )(key_matrix, other_matrices, *normed)


def turn_kernel(turned_ref, *gated_refs):
    seqs = gated_refs[0].shape[1]
    for n in range(turned_ref.shape[0]):
        back = turned_ref[n].T
        for block, gated_ref in enumerate(gated_refs):
            gated_ref[n] = back[block * seqs : (block + 1) * seqs]


def turn_back(turned, blocks):
    residues, inner, total = turned.shape
    seqs = total // blocks
    return pl.pallas_call(
        turn_kernel,
        grid=(residues // 2,),
        in_specs=[pl.BlockSpec((2, inner, total), lambda n: (n, 0, 0))],
        out_specs=[pl.BlockSpec((2, seqs, inner), lambda n: (n, 0, 0))] * blocks,
        out_shape=[pltpu.HBM((residues, seqs, inner), BF16)] * blocks,
        compiler_params=params(12, "arbitrary"),
        cost_estimate=cost(2),
        name="turn_back",
    )(turned)


def alignment_kernel(sources_ref, turned_ref, final_ref, entry_ref, *rest):
    *refs, left_ref, right_ref, rows_ref = rest
    blocks = len(refs) // 3
    high_refs, low_refs, spread_refs = refs[:blocks], refs[blocks : 2 * blocks], refs[2 * blocks :]
    residues, seqs, depth = high_refs[0].shape
    total = blocks * seqs
    features = TENSOR_FEATURES
    step = pl.program_id(0)
    for n in range(residues):
        column = jnp.concatenate([ref[n] for ref in high_refs], axis=0).astype(F32)
        column = column + jnp.concatenate(
            [ref[n * seqs : (n + 1) * seqs, :] for ref in low_refs], axis=0
        ).astype(F32)
        spreads = []
        for ref in spread_refs:
            kept = ref[:, :seqs].astype(F32)
            row = lax.broadcasted_iota(jnp.int32, kept.shape, 0)
            chosen = lax.rem(row, 8) == step * residues + n
            spreads.append(jnp.sum(jnp.where(chosen, kept, 0.0), axis=0, keepdims=True))
        spread = jnp.concatenate(spreads, axis=1)
        updated = column.T * spread + matmul(final_ref[...], turned_ref[n])
        projected = matmul(entry_ref[...], normalise_rows(updated))
        me = sources_ref[0]
        tiles = [projected[:, low : low + 128] for low in range(0, total, 128)]
        odd = lax.rem(me, 2) == 1
        tiles = [jnp.where(odd, pltpu.roll(tile, seqs, 1), tile) for tile in tiles]
        width = 1
        while width < len(tiles):
            crossed = lax.rem(lax.div(me, 2 * width), 2) == 1
            tiles = [
                jnp.where(crossed, tiles[t ^ width], tiles[t]) for t in range(len(tiles))
            ]
            width *= 2
        first = pl.multiple_of((step * residues + n) * features, features)
        for t, tile in enumerate(tiles):
            right_ref[n, :, t * 128 : (t + 1) * 128] = tile[features:].astype(BF16)
            rows_ref[t, pl.ds(first, features), :] = tile[:features]

    @pl.when(step == pl.num_programs(0) - 1)
    def _():
        count = rows_ref.shape[1] // features
        together = max(1, 16 // count)
        for c in range(0, features, together):
            pieces = []
            for e in range(together):
                chosen = pl.ds(c + e, count, stride=features)
                tiles = [rows_ref[tile, chosen, :] for tile in range(total // 128)]
                pieces.append(jnp.concatenate(tiles, axis=1))
            piece = jnp.concatenate(pieces, axis=0).astype(BF16)
            left_ref[c * count : (c + together) * count, :] = piece


def alignment(sources, high, low, turned, final_matrix, entry_matrices):
    blocks = len(high)
    residues, seqs, depth = high[0].shape
    total = blocks * seqs
    features = TENSOR_FEATURES
    step = 4
    height = residues * seqs + 16
    return pl.pallas_call(
        alignment_kernel,
        grid=(residues // step,),
        in_specs=[
            pl.BlockSpec(memory_space=pltpu.SMEM),
            pl.BlockSpec((step, depth, total), lambda n: (n, 0, 0)),
            pl.BlockSpec(final_matrix.shape, lambda n: (0, 0)),
            pl.BlockSpec(entry_matrices.shape, lambda n: (0, 0)),
        ]
        + [pl.BlockSpec((step, seqs, depth), lambda n: (n, 0, 0))] * blocks
        + [pl.BlockSpec((step * seqs, depth), lambda n: (n, 0))] * blocks
        + [pl.BlockSpec((16, depth), lambda n: (height // 16 - 1, 0))] * blocks,
        out_specs=[
            pl.BlockSpec((features * residues, total), lambda n: (0, 0)),
            pl.BlockSpec((step, features, total), lambda n: (n, 0, 0)),
        ],
        out_shape=[
            jax.ShapeDtypeStruct((features * residues, total), BF16),
            jax.ShapeDtypeStruct((residues, features, total), BF16),
        ],
        scratch_shapes=[pltpu.VMEM((total // 128, residues * features, 128), F32)],
        compiler_params=params(16, "arbitrary"),
        cost_estimate=cost(4),
        name="alignment",
    )(sources, turned, final_matrix, entry_matrices, *high, *low, *low)


def pair_kernel(
    left_slots_ref,
    right_firsts_ref,
    *rest,
    slots,
):
    weights_ref, entry_ref, switch_ref, couplings_hbm, mid_hbm, gate_hbm, sides_hbm = rest[-16:-9]
    outer_ref, spread_ref, sum_ref, rows_ref, couplings_ref = rest[-9:-4]
    mid_ref, gate_ref, sides_ref, copied = rest[-4:]
    left_refs, right_refs = rest[: 2 * slots], rest[2 * slots : -16]
    fetched = pltpu.make_async_copy(couplings_hbm, couplings_ref, copied.at[0])
    fetched.start()
    copies = []

    def send(source, target):
        copies.append(pltpu.make_async_copy(source, target, copied.at[len(copies) + 1]))
        copies[-1].start()

    features = TENSOR_FEATURES
    piece_rows, total = left_refs[0].shape
    residues = piece_rows // features
    rows = 2 * slots * residues
    share = right_refs[0].shape[0]
    columns = len(right_refs) * share
    groups = columns // GROUP
    wide = share * features
    together = spread_ref.shape[1] // 64

    for half in range(2):
        halves = left_refs[half * slots : (half + 1) * slots]
        piece = jnp.concatenate([ref[...] for ref in halves], axis=0)
        target = slice(half * slots * piece_rows, (half + 1) * slots * piece_rows)
        for p, right_ref in enumerate(right_refs):
            right = right_ref[...].reshape(wide, total)
            outer_ref[target, p * wide : (p + 1) * wide] = matmul_nt(piece, right) * (1.0 / total)

    spread_ref[...] = jnp.zeros_like(spread_ref)
    front = lax.broadcasted_iota(jnp.int32, (rows, 128), 1) < 64

    def channel_step(p, carry):
        slot = lax.rem(p, 2)
        for e in range(together):
            source = pl.multiple_of((p * together + e) * features, features)
            piece = weights_ref[pl.ds(source, features), :]
            for place in range(2):
                low = e * 64 + place * features
                spread_ref[slot, low : low + features, place * C_Z : (place + 1) * C_Z] = piece
        pieces = []
        for g in range(groups):
            parts = []
            for e in range(together):
                channel = []
                for slot_number in range(2 * slots):
                    first = slot_number * piece_rows + (p * together + e) * residues
                    source = pl.ds(pl.multiple_of(first, residues), residues)
                    channel.append(outer_ref[source, g * 128 : (g + 1) * 128])
                parts.append(jnp.concatenate(channel, axis=0).astype(BF16))
            lows, highs = [], []
            for e in range(0, together, 2):
                lows.append(jnp.where(front, parts[e], pltpu.roll(parts[e + 1], 64, 1)))
                highs.append(jnp.where(front, pltpu.roll(parts[e], 64, 1), parts[e + 1]))
            pieces.append(jnp.concatenate(lows, axis=1))
            pieces.append(jnp.concatenate(highs, axis=1))
        update = matmul(jnp.concatenate(pieces, axis=0), spread_ref[slot])

        @pl.when(p == 0)
        def _():
            sum_ref[...] = update

        @pl.when(p > 0)
        def _():
            sum_ref[...] += update

        return carry

    lax.fori_loop(0, features // together, channel_step, 0)

    left_firsts = [left_slots_ref[j] * residues for j in range(2 * slots)]
    right_firsts = [right_firsts_ref[p] for p in range(len(right_refs))]
    fetched.wait()
    for g in range(groups):
        normed, places = [], []
        for place in range(GROUP):
            p, n = divmod(g * GROUP + place, share)
            b = right_firsts[p] + n
            places.append(b)
            lanes = slice(place % 2 * C_Z, (place % 2 + 1) * C_Z)
            start = (2 * g + place // 2) * rows
            pieces = []
            for first in left_firsts:
                source = pl.ds(pl.multiple_of(start + first, residues), residues)
                pieces.append(sum_ref[source, lanes])
            mid = jnp.concatenate(pieces, axis=0)
            mid = mid + couplings_ref[pl.ds(b, rows, stride=columns), :]
            mid_ref[g * GROUP + place] = mid
            centred = mid - jnp.mean(mid, axis=1, keepdims=True)
            variance = jnp.mean(centred * centred, axis=1, keepdims=True)
            normed.append((centred * lax.rsqrt(variance + EPS)).astype(BF16))
        gates = sigmoid(matmul(jnp.concatenate(normed, axis=0), switch_ref[...]))
        blank = jnp.zeros_like(normed[0])
        for place in range(0, GROUP, 2):
            twice = []
            for e in range(2):
                part = gates[(place + e) * rows : (place + e + 1) * rows]
                gate_ref[g * GROUP + place + e] = part
                twice.append(jnp.concatenate([normed[place + e], blank], axis=1))
                twice.append(jnp.concatenate([blank, normed[place + e]], axis=1))
            sides = matmul_nt(entry_ref[...], jnp.concatenate(twice, axis=0))
            sides = sigmoid(sides[C_TRI:]) * sides[:C_TRI]
            for e in range(2):
                first = pl.multiple_of(places[place + e] * C_TRI, C_TRI)
                rows_ref[pl.ds(first, C_TRI), :] = sides[:, e * 2 * rows : (e + 1) * 2 * rows]

        if (g + 1) * GROUP % share == 0:
            p = (g + 1) * GROUP // share - 1
            source, target = pl.ds(p * share, share), pl.ds(right_firsts[p], share)
            send(mid_ref.at[source], mid_hbm.at[target])
            send(gate_ref.at[source], gate_hbm.at[target])

    cut = C_TRI // 4
    for part in range(4):

        def turn_step(c, carry):
            sides_ref[c] = rows_ref[pl.ds(c, columns, stride=C_TRI), :].astype(BF16)
            return carry

        lax.fori_loop(part * cut, (part + 1) * cut, turn_step, 0, unroll=8)
        chosen = pl.ds(part * cut, cut)
        send(sides_ref.at[chosen], sides_hbm.at[chosen])
    for copy in copies:
        copy.wait()


def pair_update(left_slots, right_firsts, left, rights, weights, couplings, entry, switch):
    rows, columns, depth = couplings.shape
    whole = jax.ShapeDtypeStruct((columns, rows, depth), F32)
    sides = jax.ShapeDtypeStruct((C_TRI, columns, 2 * rows), BF16)
    smem = pl.BlockSpec(memory_space=pltpu.SMEM)
    vmem = pl.BlockSpec(memory_space=pltpu.VMEM)
    anywhere = pl.BlockSpec(memory_space=pl.ANY)
    return pl.pallas_call(
        functools.partial(pair_kernel, slots=len(left) // 2),
        in_specs=[smem] * 2 + [vmem] * (3 + len(left) + len(rights)) + [anywhere],
        out_specs=[anywhere] * 3,
        out_shape=[pltpu.HBM(whole.shape, F32)] * 2 + [pltpu.HBM(sides.shape, BF16)],
        scratch_shapes=[
            pltpu.VMEM((rows * TENSOR_FEATURES, columns * TENSOR_FEATURES), F32),
            pltpu.VMEM((2, 8 * 64, 2 * depth), BF16),
            pltpu.VMEM((columns // 2 * rows, 2 * depth), F32),
            pltpu.VMEM((columns * C_TRI, 2 * rows), F32),
            pltpu.VMEM((rows * columns, depth), F32),
            pltpu.VMEM(whole.shape, F32),
            pltpu.VMEM(whole.shape, F32),
            pltpu.VMEM(sides.shape, BF16),
            pltpu.SemaphoreType.DMA((2 * len(rights) + 5,)),
        ],
        compiler_params=params(28),
        cost_estimate=cost(12),
        name="pair_update",
    )(
        left_slots,
        right_firsts,
        *left,
        *rights,
        weights,
        entry,
        switch,
        couplings.reshape(rows * columns, depth),
    )


def product_kernel(sides_ref, out_ref, *, grid_rows, grid_columns):
    channels, part, lanes = sides_ref.shape[1:]
    half = lanes // 2
    lane = lax.broadcasted_iota(jnp.int32, (grid_columns * part, lanes), 1)
    front = lane < half
    cut = front[: part // 2]
    for channel in range(channels):
        lefts, rights = [], []
        for r in range(0, grid_rows, 2):
            even, odd = [
                jnp.concatenate(
                    [sides_ref[(r + e) * grid_columns + c, channel] for c in range(grid_columns)],
                    axis=0,
                )
                for e in range(2)
            ]
            lefts.append(jnp.where(front, even, pltpu.roll(odd, half, 1)))
            rights.append(jnp.where(front, pltpu.roll(even, half, 1), odd))
        product = matmul_nt(jnp.concatenate(rights, axis=1), jnp.concatenate(lefts, axis=1))
        product = product.astype(BF16)
        for c in range(grid_columns):
            for r in range(0, grid_rows, 2):
                block = product[c * part : (c + 1) * part, r * half : (r + 2) * half]
                top, bottom = block[: part // 2], block[part // 2 :]
                even = jnp.where(cut, top, pltpu.roll(bottom, half, 1))
                out_ref[r * grid_columns + c, channel] = even
                odd = jnp.where(cut, pltpu.roll(top, half, 1), bottom)
                out_ref[(r + 1) * grid_columns + c, channel] = odd


def triangle_product(sides, grid_rows, grid_columns):
    devices, channels, part, lanes = sides.shape
    step = 2 if channels % 2 == 0 else 1
    return pl.pallas_call(
        functools.partial(product_kernel, grid_rows=grid_rows, grid_columns=grid_columns),
        grid=(channels // step,),
        in_specs=[pl.BlockSpec((devices, step, part, lanes), lambda c: (0, c, 0, 0))],
        out_specs=pl.BlockSpec((devices, step, part // 2, lanes), lambda c: (0, c, 0, 0)),
        out_shape=pltpu.HBM((devices, channels, part // 2, lanes), BF16),
        compiler_params=params(8, "arbitrary"),
        cost_estimate=cost(3),
        name="triangle_product",
    )(sides)


def output_kernel(
    product_ref, final_ref, mid_hbm, gate_hbm, out_hbm, wide_ref, mid_ref, gate_ref, out_ref, *copied
):
    channels, part, lanes = product_ref.shape
    columns, rows, depth = mid_ref.shape
    own = 8
    fetched, sent = copied
    fetches, sends = [], []
    for first in range(0, columns, own):
        chosen = pl.ds(first, own)
        for source, target in ((mid_hbm, mid_ref), (gate_hbm, gate_ref)):
            fetches.append(
                pltpu.make_async_copy(
                    source.at[chosen], target.at[chosen], fetched.at[len(fetches)]
                )
            )
            fetches[-1].start()
    wide_ref[...] = product_ref[...].astype(F32).reshape(channels * part, lanes)
    for group in range(part // own):
        updates = []
        for j in range(own):
            product = wide_ref[pl.ds(group * own + j, channels, stride=part), :]
            updates.append(matmul(normalise_rows(product).T, final_ref[...]))
        for half in range(2):
            cut = half * (part // own) + group
            fetches[2 * cut].wait()
            fetches[2 * cut + 1].wait()
            out_rows = out_ref.at[cut].reshape(rows * own, depth)
            for j in range(own):
                b = cut * own + j
                piece = updates[j][half * rows : (half + 1) * rows]
                out_rows[pl.ds(j, rows, stride=own), :] = mid_ref[b] + gate_ref[b] * piece
            sends.append(
                pltpu.make_async_copy(
                    out_ref.at[cut], out_hbm.at[:, pl.ds(cut * own, own)], sent.at[len(sends)]
                )
            )
            sends[-1].start()
    for send in sends:
        send.wait()


def pair_result(product, mid, gate, final_matrix):
    channels, part, lanes = product.shape
    columns, rows, depth = mid.shape
    vmem, hbm = pl.BlockSpec(memory_space=pltpu.VMEM), pl.BlockSpec(memory_space=pltpu.HBM)
    return pl.pallas_call(
        output_kernel,
        in_specs=[vmem, vmem, hbm, hbm],
        out_specs=hbm,
        out_shape=pltpu.HBM((rows, columns, depth), F32),
        scratch_shapes=[
            pltpu.VMEM((channels * part, lanes), F32),
            pltpu.VMEM(mid.shape, F32),
            pltpu.VMEM(mid.shape, F32),
            pltpu.VMEM((columns // 8, rows, 8, depth), F32),
            pltpu.SemaphoreType.DMA((columns // 4,)),
            pltpu.SemaphoreType.DMA((columns // 8,)),
        ],
        compiler_params=params(16),
        cost_estimate=cost(3),
        name="pair_result",
    )(
        product,
        final_matrix,
        pltpu.with_memory_space_constraint(mid, pltpu.HBM),
        pltpu.with_memory_space_constraint(gate, pltpu.HBM),
    )


def swap_cores(block):
    count = lax.axis_size("col")
    return lax.ppermute(block, "col", [(c, c ^ 1) for c in range(count)])


def gather_turned(block, later):
    rows, columns = lax.axis_size("row"), lax.axis_size("col")
    arrived = []
    for shift in range(rows):
        moves = []
        for r in range(rows):
            for q in range(rows):
                for side in range(2):
                    source = r * columns + 2 * q + side
                    moves.append((source, q * columns + 2 * ((r + shift) % rows) + side))
        source = block if shift < 2 else later
        arrived.append(lax.ppermute(source, ("row", "col"), moves))
    return arrived


def both_cores(own):
    rows = lax.axis_size("row")
    core = lax.rem(lax.axis_index("col"), 2)
    other = [swap_cores(piece) for piece in own]
    residues = own[0].shape[0] // TENSOR_FEATURES
    if residues % 8 == 0:
        return own + other
    order = left_order(rows)
    own, other = [jnp.take(jnp.stack(side), order, axis=0) for side in (own, other)]
    joined = 8 // residues
    ordered = []
    for side in (jnp.where(core == 0, own, other), jnp.where(core == 0, other, own)):
        side = side.reshape(rows // joined, joined, TENSOR_FEATURES, residues, -1)
        side = jnp.transpose(side, (0, 2, 1, 3, 4))
        ordered.extend(side.reshape(rows // joined, joined * own.shape[1], -1))
    return ordered


def left_order(rows):
    me = lax.axis_index("col") // 2
    return lax.rem(me - jnp.arange(rows, dtype=jnp.int32) + rows, rows)


def left_groups(rows, residues):
    if residues % 8:
        return jnp.arange(2 * rows * residues // 8, dtype=jnp.int32)
    core = lax.rem(lax.axis_index("col"), 2)
    order = left_order(rows)
    return jnp.concatenate([order + core * rows, order + (1 - core) * rows])


def exchange_rows(pieces):
    arrived = [pieces[0]]
    for shift in range(1, len(pieces)):
        moves = [(r, r ^ shift) for r in range(len(pieces))]
        arrived.append(lax.ppermute(pieces[shift], "row", moves))
    return arrived


def paired_entries(matrices):
    turned = matrices.reshape(C_Z, 2, 2, C_TRI)
    return jnp.transpose(turned, (2, 3, 1, 0)).reshape(2 * C_TRI, 2 * C_Z)


def body(
    homolog_tensor,
    couplings,
    attention_probe_matrix,
    attention_extra_matrices,
    attention_final_matrix,
    tensor_entry_matrices,
    tensor_final_matrix,
    incoming_entry_matrices,
    incoming_switch_matrix,
    incoming_final_matrix,
):
    inner = ATTENTION_UNITS * UNIT_WIDTH
    row_count = lax.axis_size("row")
    seqs, residues, depth = homolog_tensor.shape
    own_residues = residues // row_count
    sources = lax.axis_index("row") ^ jnp.arange(row_count, dtype=jnp.int32)
    high = exchange_rows(standardise_high(sources, homolog_tensor))
    low = standardise_low(sources, homolog_tensor)
    others = jnp.concatenate(
        [attention_probe_matrix.T, attention_extra_matrices[:, inner:].T], axis=0
    )
    early = (
        attention_extra_matrices[:, :inner],
        others,
        attention_final_matrix.T,
        tensor_entry_matrices.T,
        paired_entries(incoming_entry_matrices),
        sources * own_residues,
        left_groups(row_count, own_residues),
    )
    high, low, early = lax.optimization_barrier((high, low, early))
    key_matrix, others, final_turned, tensor_turned, entries, firsts, slots = early
    low = exchange_rows(low)
    turned = attention(high, key_matrix, others)
    gated = turn_back(turned, row_count)
    left_piece, right_piece = alignment(
        sources, high, low, turned, final_turned, tensor_turned
    )

    rights = exchange_rows([right_piece] * row_count)
    later, rights[1] = lax.optimization_barrier((left_piece, rights[1]))
    own = gather_turned(left_piece, later)
    own[-1], rights = lax.optimization_barrier((own[-1], rights))
    mid, gate, sides = pair_update(
        slots,
        firsts,
        both_cores(own),
        rights,
        tensor_final_matrix,
        couplings,
        entries,
        incoming_switch_matrix,
    )
    gated, sides = lax.optimization_barrier((gated, sides))
    gated = exchange_rows(gated)

    everywhere = ("row", "col")
    column_count = lax.axis_size("col")
    devices = row_count * column_count
    sides = sides.reshape(devices, C_TRI // devices, *sides.shape[1:])
    sides = lax.all_to_all(sides, everywhere, split_axis=0, concat_axis=0)
    gated, sides = lax.optimization_barrier((gated, sides))
    product = triangle_product(sides, row_count, column_count)
    product = lax.all_to_all(product, everywhere, split_axis=0, concat_axis=0)

    gated = jnp.take(jnp.stack(gated), sources, axis=0)
    gated = jnp.transpose(gated.reshape(residues, seqs, inner), (1, 0, 2))
    change = jnp.dot(
        gated.reshape(-1, inner), attention_final_matrix, preferred_element_type=F32
    )
    refreshed_homologs = homolog_tensor + change.reshape(homolog_tensor.shape)
    product = product.reshape(C_TRI, *product.shape[2:])
    pair_output = pair_result(product, mid, gate, incoming_final_matrix)
    return (refreshed_homologs, pair_output)


def solution(mesh):
    in_specs = (
        P("row", "col", None),
        P("row", "col", None),
        P(),
        P(),
        P(),
        P(),
        P(),
        P(),
        P(),
        P(),
    )
    out_specs = (P("row", "col", None), P("row", "col", None))
    return jax.shard_map(body, mesh=mesh, in_specs=in_specs, out_specs=out_specs, check_vma=False)
```

```python
import functools

import jax
import jax.numpy as jnp
from jax import lax
from jax.experimental import pallas as pl
from jax.experimental.pallas import tpu as pltpu
from jax.sharding import PartitionSpec as P

FEATURE_DEPTH = 256
C_Z = 128
TENSOR_FEATURES = 32
C_TRI = 128
ATTENTION_UNITS = 8
UNIT_WIDTH = 32
EPS = 1e-05
GROUP = 4
F32 = jnp.float32
BF16 = jnp.bfloat16
NT = (((1,), (1,)), ((), ()))


def matmul(left, right):
    return jnp.dot(left, right, preferred_element_type=F32)


def matmul_nt(left, right):
    return lax.dot_general(left, right, NT, preferred_element_type=F32)


def sigmoid(values):
    return 0.5 * jnp.tanh(0.5 * values) + 0.5


def cost(microseconds):
    return pl.CostEstimate(
        flops=int(microseconds * 1e9), bytes_accessed=int(microseconds * 1e6), transcendentals=0
    )


def params(megabytes, *semantics):
    return pltpu.CompilerParams(
        dimension_semantics=semantics or None, vmem_limit_bytes=megabytes * 1024 * 1024
    )


def fold(values, combine):
    while values.shape[0] > 8:
        half = values.shape[0] // 2
        values = combine(values[:half], values[half:])
    return values


def top_rows(values):
    return jnp.max(fold(values, jnp.maximum), axis=0, keepdims=True)


def sum_rows(values):
    return jnp.sum(fold(values, jnp.add), axis=0, keepdims=True)


def normalise_rows(values):
    count = values.shape[0]
    centred = values - sum_rows(values) * (1.0 / count)
    variance = sum_rows(centred * centred) * (1.0 / count)
    return (centred * lax.rsqrt(variance + EPS)).astype(BF16)


def standardised_columns(first_rows, second_rows, first, count, residues):
    seqs = first_rows.shape[0] // residues
    columns = []
    for n in range(count):
        rows = pl.ds(first + n, seqs, stride=residues)
        columns.append(jnp.concatenate([first_rows[rows, :], second_rows[rows, :]], axis=1))
    column = jnp.concatenate(columns, axis=0)
    centred = column - jnp.mean(column, axis=1, keepdims=True)
    variance = jnp.mean(centred * centred, axis=1, keepdims=True) + EPS
    scale = lax.rsqrt(variance)
    return centred * scale, variance * scale


def high_kernel(sources_ref, first_ref, second_ref, *rest):
    *pieces_hbm, high_ref, sent = rest
    seqs, residues, lanes = first_ref.shape
    count = len(pieces_hbm)
    own = high_ref.shape[1]
    step = pl.program_id(0)
    first_rows = first_ref.reshape(seqs * residues, lanes)
    second_rows = second_ref.reshape(seqs * residues, lanes)
    shift = lax.rem(sources_ref[step] * own, residues) if own < residues else 0
    for n in range(own):
        normed, _ = standardised_columns(first_rows, second_rows, shift + n, 1, residues)
        high_ref[step, n] = normed.astype(BF16)
    copies = [
        pltpu.make_async_copy(high_ref.at[p], piece_hbm, sent.at[p])
        for p, piece_hbm in enumerate(pieces_hbm)
    ]
    for p in range(count):

        @pl.when(step == p)
        def _(p=p):
            copies[p].start()

    @pl.when(step == count - 1)
    def _():
        for copy in copies:
            copy.wait()


def standardise_high(sources, block):
    seqs, residues, depth = block.shape
    half = depth // 2
    count = sources.shape[0]
    own = residues // count
    hbm = pl.BlockSpec(memory_space=pltpu.HBM)
    together = 8 // own
    block = pltpu.with_memory_space_constraint(block, pltpu.HBM)
    return pl.pallas_call(
        high_kernel,
        grid_spec=pltpu.PrefetchScalarGridSpec(
            num_scalar_prefetch=1,
            grid=(count,),
            in_specs=[
                pl.BlockSpec((seqs, 8, half), lambda p, sources: (0, sources[p] // together, 0)),
                pl.BlockSpec((seqs, 8, half), lambda p, sources: (0, sources[p] // together, 1)),
            ],
            out_specs=[hbm] * count,
            scratch_shapes=[
                pltpu.VMEM((count, own, seqs, depth), BF16),
                pltpu.SemaphoreType.DMA((count,)),
            ],
        ),
        out_shape=[pltpu.HBM((own, seqs, depth), BF16)] * count,
        compiler_params=params(10, "arbitrary"),
        cost_estimate=cost(3),
        name="standardise_high",
    )(sources, block, block)


def low_kernel(sources_ref, first_ref, second_ref, *rest):
    *pieces_hbm, low_ref, sent = rest
    seqs, residues, lanes = first_ref.shape
    own = residues // len(pieces_hbm)
    first_rows = first_ref.reshape(seqs * residues, lanes)
    second_rows = second_ref.reshape(seqs * residues, lanes)
    lane = lax.broadcasted_iota(jnp.int32, (seqs, 128), 1)
    for p in range(len(pieces_hbm)):
        spreads = jnp.zeros((seqs, 128), F32)
        for n in range(own):
            normed, spread = standardised_columns(
                first_rows, second_rows, p * own + n, 1, residues
            )
            left = (normed - normed.astype(BF16).astype(F32)).astype(BF16)
            low_ref[p, n * seqs : (n + 1) * seqs, :] = left
            spreads = jnp.where(lane == n, spread, spreads)
        spreads = spreads.T[:8, :]
        coarse = spreads.astype(BF16).astype(F32)
        kept = jnp.concatenate([coarse, spreads - coarse], axis=0)
        kept = jnp.concatenate([kept, jnp.zeros((16, 2 * lanes - seqs), F32)], axis=1)
        low_ref[p, own * seqs :, :] = kept.astype(BF16)
    sends = []
    for p, piece_hbm in enumerate(pieces_hbm):
        source = low_ref.at[sources_ref[p]]
        sends.append(pltpu.make_async_copy(source, piece_hbm, sent.at[p]))
        sends[-1].start()
    for send in sends:
        send.wait()


def standardise_low(sources, block):
    seqs, residues, depth = block.shape
    half = depth // 2
    count = sources.shape[0]
    height = residues // count * seqs + 16
    hbm = pl.BlockSpec(memory_space=pltpu.HBM)
    return pl.pallas_call(
        low_kernel,
        grid=(1,),
        in_specs=[
            pl.BlockSpec(memory_space=pltpu.SMEM),
            pl.BlockSpec((seqs, residues, half), lambda g: (0, 0, 0)),
            pl.BlockSpec((seqs, residues, half), lambda g: (0, 0, 1)),
        ],
        out_specs=[hbm] * count,
        out_shape=[pltpu.HBM((height, depth), BF16)] * count,
        scratch_shapes=[
            pltpu.VMEM((count, height, depth), BF16),
            pltpu.SemaphoreType.DMA((count,)),
        ],
        compiler_params=params(14, "arbitrary"),
        cost_estimate=cost(4),
        name="standardise_low",
    )(sources, block, block)


def attention_kernel(key_ref, others_ref, *rest):
    *normed_refs, turned_ref, scores_ref, weights_ref = rest
    blocks = len(normed_refs)
    residues, seqs, _ = normed_refs[0].shape
    total = blocks * seqs
    inner = ATTENTION_UNITS * UNIT_WIDTH
    ring = scores_ref.shape[0]
    columns = []

    def project(n):
        column = jnp.concatenate([ref[n] for ref in normed_refs], axis=0)
        key_rows = matmul(column, key_ref[...]).astype(BF16)
        projected = matmul_nt(others_ref[...], column)
        queries = (projected[:inner] * UNIT_WIDTH ** (-0.5)).astype(BF16)
        value_rows = projected[inner : 2 * inner].astype(BF16)
        gates = sigmoid(projected[2 * inner :])
        columns.append((key_rows, queries, value_rows, gates))
    units = [(n, h) for n in range(residues) for h in range(ATTENTION_UNITS)]

    def score(unit):
        n, h = units[unit]
        key_rows, queries, _, _ = columns[n]
        low, high = h * UNIT_WIDTH, (h + 1) * UNIT_WIDTH
        pieces = [queries[low:high]]
        if low > 0:
            pieces.insert(0, jnp.zeros((low, total), BF16))
        if high < inner:
            pieces.append(jnp.zeros((inner - high, total), BF16))
        scores_ref[unit % ring] = matmul(key_rows, jnp.concatenate(pieces, axis=0))

    def weigh(unit):
        for low in range(0, total, 128):
            scores = scores_ref[unit % ring, :, low : low + 128]
            weights = jnp.exp(scores - top_rows(scores))
            scale = 1.0 / sum_rows(weights)
            weights_ref[unit % ring, :, low : low + 128] = (weights * scale).astype(BF16)

    def attend(unit):
        n, h = units[unit]
        _, _, value_rows, gates = columns[n]
        rows = slice(h * UNIT_WIDTH, (h + 1) * UNIT_WIDTH)
        attended = matmul(value_rows[rows], weights_ref[unit % ring]) * gates[rows]
        turned_ref[n, rows, :] = attended.astype(BF16)

    project(0)
    for step in range(len(units) + 2):
        if step < len(units):
            score(step)
            n, h = units[step]
            if h == ATTENTION_UNITS // 2 and n + 1 < residues:
                project(n + 1)
        if 1 <= step <= len(units):
            weigh(step - 1)
        if step >= 2:
            attend(step - 2)


def attention(normed, key_matrix, other_matrices):
    blocks = len(normed)
    residues, seqs, depth = normed[0].shape
    total = blocks * seqs
    inner = ATTENTION_UNITS * UNIT_WIDTH
    step = 4
    return pl.pallas_call(
        attention_kernel,
        grid=(residues // step,),
        in_specs=[
            pl.BlockSpec((depth, inner), lambda n: (0, 0)),
            pl.BlockSpec((3 * inner, depth), lambda n: (0, 0)),
        ]
        + [pl.BlockSpec((step, seqs, depth), lambda n: (n, 0, 0))] * blocks,
        out_specs=pl.BlockSpec((step, inner, total), lambda n: (n, 0, 0)),
        out_shape=jax.ShapeDtypeStruct((residues, inner, total), BF16),
        scratch_shapes=[
            pltpu.VMEM((4, total, total), F32),
            pltpu.VMEM((4, total, total), BF16),
        ],
        compiler_params=params(12 + (total // 128) ** 2, "arbitrary"),
        cost_estimate=cost(10),
        name="attention",
    )(key_matrix, other_matrices, *normed)


def turn_kernel(turned_ref, *gated_refs):
    seqs = gated_refs[0].shape[1]
    for n in range(turned_ref.shape[0]):
        back = turned_ref[n].T
        for block, gated_ref in enumerate(gated_refs):
            gated_ref[n] = back[block * seqs : (block + 1) * seqs]


def turn_back(turned, blocks):
    residues, inner, total = turned.shape
    seqs = total // blocks
    return pl.pallas_call(
        turn_kernel,
        grid=(residues // 2,),
        in_specs=[pl.BlockSpec((2, inner, total), lambda n: (n, 0, 0))],
        out_specs=[pl.BlockSpec((2, seqs, inner), lambda n: (n, 0, 0))] * blocks,
        out_shape=[pltpu.HBM((residues, seqs, inner), BF16)] * blocks,
        compiler_params=params(12, "arbitrary"),
        cost_estimate=cost(2),
        name="turn_back",
    )(turned)


def alignment_kernel(sources_ref, turned_ref, final_ref, entry_ref, *rest):
    *refs, left_ref, right_ref, rows_ref = rest
    blocks = len(refs) // 3
    high_refs, low_refs, spread_refs = refs[:blocks], refs[blocks : 2 * blocks], refs[2 * blocks :]
    residues, seqs, depth = high_refs[0].shape
    total = blocks * seqs
    features = TENSOR_FEATURES
    step = pl.program_id(0)
    for n in range(residues):
        column = jnp.concatenate([ref[n] for ref in high_refs], axis=0).astype(F32)
        column = column + jnp.concatenate(
            [ref[n * seqs : (n + 1) * seqs, :] for ref in low_refs], axis=0
        ).astype(F32)
        spreads = []
        for ref in spread_refs:
            kept = ref[:, :seqs].astype(F32)
            row = lax.broadcasted_iota(jnp.int32, kept.shape, 0)
            chosen = lax.rem(row, 8) == step * residues + n
            spreads.append(jnp.sum(jnp.where(chosen, kept, 0.0), axis=0, keepdims=True))
        spread = jnp.concatenate(spreads, axis=1)
        updated = column.T * spread + matmul(final_ref[...], turned_ref[n])
        projected = matmul(entry_ref[...], normalise_rows(updated))
        me = sources_ref[0]
        tiles = [projected[:, low : low + 128] for low in range(0, total, 128)]
        odd = lax.rem(me, 2) == 1
        tiles = [jnp.where(odd, pltpu.roll(tile, seqs, 1), tile) for tile in tiles]
        width = 1
        while width < len(tiles):
            crossed = lax.rem(lax.div(me, 2 * width), 2) == 1
            tiles = [
                jnp.where(crossed, tiles[t ^ width], tiles[t]) for t in range(len(tiles))
            ]
            width *= 2
        first = pl.multiple_of((step * residues + n) * features, features)
        for t, tile in enumerate(tiles):
            right_ref[n, :, t * 128 : (t + 1) * 128] = tile[features:].astype(BF16)
            rows_ref[t, pl.ds(first, features), :] = tile[:features]

    @pl.when(step == pl.num_programs(0) - 1)
    def _():
        count = rows_ref.shape[1] // features
        together = max(1, 16 // count)
        for c in range(0, features, together):
            pieces = []
            for e in range(together):
                chosen = pl.ds(c + e, count, stride=features)
                tiles = [rows_ref[tile, chosen, :] for tile in range(total // 128)]
                pieces.append(jnp.concatenate(tiles, axis=1))
            piece = jnp.concatenate(pieces, axis=0).astype(BF16)
            left_ref[c * count : (c + together) * count, :] = piece


def alignment(sources, high, low, turned, final_matrix, entry_matrices):
    blocks = len(high)
    residues, seqs, depth = high[0].shape
    total = blocks * seqs
    features = TENSOR_FEATURES
    step = 4
    height = residues * seqs + 16
    return pl.pallas_call(
        alignment_kernel,
        grid=(residues // step,),
        in_specs=[
            pl.BlockSpec(memory_space=pltpu.SMEM),
            pl.BlockSpec((step, depth, total), lambda n: (n, 0, 0)),
            pl.BlockSpec(final_matrix.shape, lambda n: (0, 0)),
            pl.BlockSpec(entry_matrices.shape, lambda n: (0, 0)),
        ]
        + [pl.BlockSpec((step, seqs, depth), lambda n: (n, 0, 0))] * blocks
        + [pl.BlockSpec((step * seqs, depth), lambda n: (n, 0))] * blocks
        + [pl.BlockSpec((16, depth), lambda n: (height // 16 - 1, 0))] * blocks,
        out_specs=[
            pl.BlockSpec((features * residues, total), lambda n: (0, 0)),
            pl.BlockSpec((step, features, total), lambda n: (n, 0, 0)),
        ],
        out_shape=[
            jax.ShapeDtypeStruct((features * residues, total), BF16),
            jax.ShapeDtypeStruct((residues, features, total), BF16),
        ],
        scratch_shapes=[pltpu.VMEM((total // 128, residues * features, 128), F32)],
        compiler_params=params(16, "arbitrary"),
        cost_estimate=cost(4),
        name="alignment",
    )(sources, turned, final_matrix, entry_matrices, *high, *low, *low)


def pair_kernel(
    left_slots_ref,
    right_firsts_ref,
    *rest,
    slots,
):
    weights_ref, entry_ref, switch_ref, couplings_hbm, mid_hbm, gate_hbm, sides_hbm = rest[-16:-9]
    outer_ref, spread_ref, sum_ref, rows_ref, couplings_ref = rest[-9:-4]
    mid_ref, gate_ref, sides_ref, copied = rest[-4:]
    left_refs, right_refs = rest[: 2 * slots], rest[2 * slots : -16]
    fetched = pltpu.make_async_copy(couplings_hbm, couplings_ref, copied.at[0])
    fetched.start()
    copies = []

    def send(source, target):
        number = 2 * len(right_refs) + 1 + len(copies)
        copies.append(pltpu.make_async_copy(source, target, copied.at[number]))
        copies[-1].start()

    features = TENSOR_FEATURES
    piece_rows, total = left_refs[0].shape
    residues = piece_rows // features
    rows = 2 * slots * residues
    share = right_refs[0].shape[0]
    columns = len(right_refs) * share
    groups = columns // GROUP
    wide = share * features
    together = spread_ref.shape[1] // 64

    for half in range(2):
        halves = left_refs[half * slots : (half + 1) * slots]
        piece = jnp.concatenate([ref[...] for ref in halves], axis=0)
        target = slice(half * slots * piece_rows, (half + 1) * slots * piece_rows)
        for p, right_ref in enumerate(right_refs):
            right = right_ref[...].reshape(wide, total)
            outer_ref[target, p * wide : (p + 1) * wide] = matmul_nt(piece, right) * (1.0 / total)

    spread_ref[...] = jnp.zeros_like(spread_ref)
    front = lax.broadcasted_iota(jnp.int32, (rows, 128), 1) < 64

    def channel_step(p, carry):
        slot = lax.rem(p, 2)
        for e in range(together):
            source = pl.multiple_of((p * together + e) * features, features)
            piece = weights_ref[pl.ds(source, features), :]
            for place in range(2):
                low = e * 64 + place * features
                spread_ref[slot, low : low + features, place * C_Z : (place + 1) * C_Z] = piece
        pieces = []
        for g in range(groups):
            parts = []
            for e in range(together):
                channel = []
                for slot_number in range(2 * slots):
                    first = slot_number * piece_rows + (p * together + e) * residues
                    source = pl.ds(pl.multiple_of(first, residues), residues)
                    channel.append(outer_ref[source, g * 128 : (g + 1) * 128])
                parts.append(jnp.concatenate(channel, axis=0).astype(BF16))
            lows, highs = [], []
            for e in range(0, together, 2):
                lows.append(jnp.where(front, parts[e], pltpu.roll(parts[e + 1], 64, 1)))
                highs.append(jnp.where(front, pltpu.roll(parts[e], 64, 1), parts[e + 1]))
            pieces.append(jnp.concatenate(lows, axis=1))
            pieces.append(jnp.concatenate(highs, axis=1))
        update = matmul(jnp.concatenate(pieces, axis=0), spread_ref[slot])

        @pl.when(p == 0)
        def _():
            sum_ref[...] = update

        @pl.when(p > 0)
        def _():
            sum_ref[...] += update

        return carry

    lax.fori_loop(0, features // together, channel_step, 0)

    left_firsts = [left_slots_ref[j] * residues for j in range(2 * slots)]
    fetched.wait()

    def piece_copies(p):
        source, target = pl.ds(p * share, share), pl.ds(right_firsts_ref[p], share)
        return [
            pltpu.make_async_copy(ref.at[source], hbm.at[target], copied.at[2 * p + kind + 1])
            for kind, (ref, hbm) in enumerate(((mid_ref, mid_hbm), (gate_ref, gate_hbm)))
        ]

    def piece_step(p, carry):
        first_column = right_firsts_ref[p]
        for g in range(share // GROUP):
            normed = []
            for place in range(GROUP):
                n = g * GROUP + place
                lanes = slice(place % 2 * C_Z, (place % 2 + 1) * C_Z)
                start = ((p * (share // GROUP) + g) * 2 + place // 2) * rows
                pieces = []
                for first in left_firsts:
                    source = pl.ds(pl.multiple_of(start + first, residues), residues)
                    pieces.append(sum_ref[source, lanes])
                mid = jnp.concatenate(pieces, axis=0)
                mid = mid + couplings_ref[pl.ds(first_column + n, rows, stride=columns), :]
                mid_ref[p * share + n] = mid
                centred = mid - jnp.mean(mid, axis=1, keepdims=True)
                variance = jnp.mean(centred * centred, axis=1, keepdims=True)
                normed.append((centred * lax.rsqrt(variance + EPS)).astype(BF16))
            gates = sigmoid(matmul(jnp.concatenate(normed, axis=0), switch_ref[...]))
            blank = jnp.zeros_like(normed[0])
            for place in range(0, GROUP, 2):
                twice = []
                for e in range(2):
                    part = gates[(place + e) * rows : (place + e + 1) * rows]
                    gate_ref[p * share + g * GROUP + place + e] = part
                    twice.append(jnp.concatenate([normed[place + e], blank], axis=1))
                    twice.append(jnp.concatenate([blank, normed[place + e]], axis=1))
                sides = matmul_nt(entry_ref[...], jnp.concatenate(twice, axis=0))
                sides = sigmoid(sides[C_TRI:]) * sides[:C_TRI]
                for e in range(2):
                    column = first_column + g * GROUP + place + e
                    first = pl.multiple_of(column * C_TRI, C_TRI)
                    rows_ref[pl.ds(first, C_TRI), :] = sides[:, e * 2 * rows : (e + 1) * 2 * rows]
        for copy in piece_copies(p):
            copy.start()
        return carry

    lax.fori_loop(0, len(right_refs), piece_step, 0)

    cut = C_TRI // 4
    for part in range(4):

        def turn_step(c, carry):
            sides_ref[c] = rows_ref[pl.ds(c, columns, stride=C_TRI), :].astype(BF16)
            return carry

        lax.fori_loop(part * cut, (part + 1) * cut, turn_step, 0, unroll=8)
        chosen = pl.ds(part * cut, cut)
        send(sides_ref.at[chosen], sides_hbm.at[chosen])
    for p in range(len(right_refs)):
        copies.extend(piece_copies(p))
    for copy in copies:
        copy.wait()


def pair_update(left_slots, right_firsts, left, rights, weights, couplings, entry, switch):
    rows, columns, depth = couplings.shape
    whole = jax.ShapeDtypeStruct((columns, rows, depth), F32)
    sides = jax.ShapeDtypeStruct((C_TRI, columns, 2 * rows), BF16)
    smem = pl.BlockSpec(memory_space=pltpu.SMEM)
    vmem = pl.BlockSpec(memory_space=pltpu.VMEM)
    anywhere = pl.BlockSpec(memory_space=pl.ANY)
    return pl.pallas_call(
        functools.partial(pair_kernel, slots=len(left) // 2),
        in_specs=[smem] * 2 + [vmem] * (3 + len(left) + len(rights)) + [anywhere],
        out_specs=[anywhere] * 3,
        out_shape=[pltpu.HBM(whole.shape, F32)] * 2 + [pltpu.HBM(sides.shape, BF16)],
        scratch_shapes=[
            pltpu.VMEM((rows * TENSOR_FEATURES, columns * TENSOR_FEATURES), F32),
            pltpu.VMEM((2, 8 * 64, 2 * depth), BF16),
            pltpu.VMEM((columns // 2 * rows, 2 * depth), F32),
            pltpu.VMEM((columns * C_TRI, 2 * rows), F32),
            pltpu.VMEM((rows * columns, depth), F32),
            pltpu.VMEM(whole.shape, F32),
            pltpu.VMEM(whole.shape, F32),
            pltpu.VMEM(sides.shape, BF16),
            pltpu.SemaphoreType.DMA((2 * len(rights) + 5,)),
        ],
        compiler_params=params(28),
        cost_estimate=cost(12),
        name="pair_update",
    )(
        left_slots,
        right_firsts,
        *left,
        *rights,
        weights,
        entry,
        switch,
        couplings.reshape(rows * columns, depth),
    )


def product_kernel(sides_ref, out_ref, *, grid_rows, grid_columns):
    channels, part, lanes = sides_ref.shape[1:]
    half = lanes // 2
    lane = lax.broadcasted_iota(jnp.int32, (grid_columns * part, lanes), 1)
    front = lane < half
    cut = front[: part // 2]
    for channel in range(channels):
        lefts, rights = [], []
        for r in range(0, grid_rows, 2):
            even, odd = [
                jnp.concatenate(
                    [sides_ref[(r + e) * grid_columns + c, channel] for c in range(grid_columns)],
                    axis=0,
                )
                for e in range(2)
            ]
            lefts.append(jnp.where(front, even, pltpu.roll(odd, half, 1)))
            rights.append(jnp.where(front, pltpu.roll(even, half, 1), odd))
        product = matmul_nt(jnp.concatenate(rights, axis=1), jnp.concatenate(lefts, axis=1))
        product = product.astype(BF16)
        for c in range(grid_columns):
            for r in range(0, grid_rows, 2):
                block = product[c * part : (c + 1) * part, r * half : (r + 2) * half]
                top, bottom = block[: part // 2], block[part // 2 :]
                even = jnp.where(cut, top, pltpu.roll(bottom, half, 1))
                out_ref[r * grid_columns + c, channel] = even
                odd = jnp.where(cut, pltpu.roll(top, half, 1), bottom)
                out_ref[(r + 1) * grid_columns + c, channel] = odd


def triangle_product(sides, grid_rows, grid_columns):
    devices, channels, part, lanes = sides.shape
    step = 2 if channels % 2 == 0 else 1
    return pl.pallas_call(
        functools.partial(product_kernel, grid_rows=grid_rows, grid_columns=grid_columns),
        grid=(channels // step,),
        in_specs=[pl.BlockSpec((devices, step, part, lanes), lambda c: (0, c, 0, 0))],
        out_specs=pl.BlockSpec((devices, step, part // 2, lanes), lambda c: (0, c, 0, 0)),
        out_shape=pltpu.HBM((devices, channels, part // 2, lanes), BF16),
        compiler_params=params(8, "arbitrary"),
        cost_estimate=cost(3),
        name="triangle_product",
    )(sides)


def output_kernel(
    product_ref, final_ref, mid_hbm, gate_hbm, out_hbm, wide_ref, mid_ref, gate_ref, out_ref, *copied
):
    channels, part, lanes = product_ref.shape
    columns, rows, depth = mid_ref.shape
    own = 8
    fetched, sent = copied
    fetches = []
    for first in range(0, columns, own):
        chosen = pl.ds(first, own)
        for source, target in ((mid_hbm, mid_ref), (gate_hbm, gate_ref)):
            fetches.append(
                pltpu.make_async_copy(
                    source.at[chosen], target.at[chosen], fetched.at[len(fetches)]
                )
            )
            fetches[-1].start()
    wide_ref[...] = product_ref[...].astype(F32).reshape(channels * part, lanes)
    turns = part // own

    def send(cut):
        target = pl.ds(pl.multiple_of(cut * own, own), own)
        return pltpu.make_async_copy(out_ref.at[cut], out_hbm.at[:, target], sent.at[cut])

    def group_step(group, carry):
        updates = []
        for j in range(own):
            product = wide_ref[pl.ds(group * own + j, channels, stride=part), :]
            updates.append(matmul(normalise_rows(product).T, final_ref[...]))
        for half in range(2):
            cut = half * turns + group
            chosen = pl.ds(cut * own, own)
            for kind, (source, target) in enumerate(((mid_hbm, mid_ref), (gate_hbm, gate_ref))):
                pltpu.make_async_copy(
                    source.at[chosen], target.at[chosen], fetched.at[2 * cut + kind]
                ).wait()
            out_rows = out_ref.at[cut].reshape(rows * own, depth)
            for j in range(own):
                b = cut * own + j
                piece = updates[j][half * rows : (half + 1) * rows]
                out_rows[pl.ds(j, rows, stride=own), :] = mid_ref[b] + gate_ref[b] * piece
            send(cut).start()
        return carry

    lax.fori_loop(0, turns, group_step, 0)
    for cut in range(2 * turns):
        send(cut).wait()


def pair_result(product, mid, gate, final_matrix):
    channels, part, lanes = product.shape
    columns, rows, depth = mid.shape
    vmem, hbm = pl.BlockSpec(memory_space=pltpu.VMEM), pl.BlockSpec(memory_space=pltpu.HBM)
    return pl.pallas_call(
        output_kernel,
        in_specs=[vmem, vmem, hbm, hbm],
        out_specs=hbm,
        out_shape=pltpu.HBM((rows, columns, depth), F32),
        scratch_shapes=[
            pltpu.VMEM((channels * part, lanes), F32),
            pltpu.VMEM(mid.shape, F32),
            pltpu.VMEM(mid.shape, F32),
            pltpu.VMEM((columns // 8, rows, 8, depth), F32),
            pltpu.SemaphoreType.DMA((columns // 4,)),
            pltpu.SemaphoreType.DMA((columns // 8,)),
        ],
        compiler_params=params(16),
        cost_estimate=cost(3),
        name="pair_result",
    )(
        product,
        final_matrix,
        pltpu.with_memory_space_constraint(mid, pltpu.HBM),
        pltpu.with_memory_space_constraint(gate, pltpu.HBM),
    )


def swap_cores(block):
    count = lax.axis_size("col")
    return lax.ppermute(block, "col", [(c, c ^ 1) for c in range(count)])


def gather_turned(block, later):
    rows, columns = lax.axis_size("row"), lax.axis_size("col")
    arrived = []
    for shift in range(rows):
        moves = []
        for r in range(rows):
            for q in range(rows):
                for side in range(2):
                    source = r * columns + 2 * q + side
                    moves.append((source, q * columns + 2 * ((r + shift) % rows) + side))
        source = block if shift < 2 else later
        arrived.append(lax.ppermute(source, ("row", "col"), moves))
    return arrived


def both_cores(own):
    rows = lax.axis_size("row")
    core = lax.rem(lax.axis_index("col"), 2)
    other = [swap_cores(piece) for piece in own]
    residues = own[0].shape[0] // TENSOR_FEATURES
    if residues % 8 == 0:
        return own + other
    order = left_order(rows)
    own, other = [jnp.take(jnp.stack(side), order, axis=0) for side in (own, other)]
    joined = 8 // residues
    ordered = []
    for side in (jnp.where(core == 0, own, other), jnp.where(core == 0, other, own)):
        side = side.reshape(rows // joined, joined, TENSOR_FEATURES, residues, -1)
        side = jnp.transpose(side, (0, 2, 1, 3, 4))
        ordered.extend(side.reshape(rows // joined, joined * own.shape[1], -1))
    return ordered


def left_order(rows):
    me = lax.axis_index("col") // 2
    return lax.rem(me - jnp.arange(rows, dtype=jnp.int32) + rows, rows)


def left_groups(rows, residues):
    if residues % 8:
        return jnp.arange(2 * rows * residues // 8, dtype=jnp.int32)
    core = lax.rem(lax.axis_index("col"), 2)
    order = left_order(rows)
    return jnp.concatenate([order + core * rows, order + (1 - core) * rows])


def exchange_rows(pieces):
    arrived = [pieces[0]]
    for shift in range(1, len(pieces)):
        moves = [(r, r ^ shift) for r in range(len(pieces))]
        arrived.append(lax.ppermute(pieces[shift], "row", moves))
    return arrived


def paired_entries(matrices):
    turned = matrices.reshape(C_Z, 2, 2, C_TRI)
    return jnp.transpose(turned, (2, 3, 1, 0)).reshape(2 * C_TRI, 2 * C_Z)


def body(
    homolog_tensor,
    couplings,
    attention_probe_matrix,
    attention_extra_matrices,
    attention_final_matrix,
    tensor_entry_matrices,
    tensor_final_matrix,
    incoming_entry_matrices,
    incoming_switch_matrix,
    incoming_final_matrix,
):
    inner = ATTENTION_UNITS * UNIT_WIDTH
    row_count = lax.axis_size("row")
    seqs, residues, depth = homolog_tensor.shape
    own_residues = residues // row_count
    sources = lax.axis_index("row") ^ jnp.arange(row_count, dtype=jnp.int32)
    high = exchange_rows(standardise_high(sources, homolog_tensor))
    low = standardise_low(sources, homolog_tensor)
    others = jnp.concatenate(
        [attention_probe_matrix.T, attention_extra_matrices[:, inner:].T], axis=0
    )
    early = (
        attention_extra_matrices[:, :inner],
        others,
        attention_final_matrix.T,
        tensor_entry_matrices.T,
        paired_entries(incoming_entry_matrices),
        sources * own_residues,
        left_groups(row_count, own_residues),
    )
    high, low, early = lax.optimization_barrier((high, low, early))
    key_matrix, others, final_turned, tensor_turned, entries, firsts, slots = early
    low = exchange_rows(low)
    turned = attention(high, key_matrix, others)
    gated = turn_back(turned, row_count)
    left_piece, right_piece = alignment(
        sources, high, low, turned, final_turned, tensor_turned
    )

    rights = exchange_rows([right_piece] * row_count)
    later, rights[1] = lax.optimization_barrier((left_piece, rights[1]))
    own = gather_turned(left_piece, later)
    own[-1], rights = lax.optimization_barrier((own[-1], rights))
    mid, gate, sides = pair_update(
        slots,
        firsts,
        both_cores(own),
        rights,
        tensor_final_matrix,
        couplings,
        entries,
        incoming_switch_matrix,
    )
    gated, sides = lax.optimization_barrier((gated, sides))
    gated = exchange_rows(gated)

    everywhere = ("row", "col")
    column_count = lax.axis_size("col")
    devices = row_count * column_count
    sides = sides.reshape(devices, C_TRI // devices, *sides.shape[1:])
    sides = lax.all_to_all(sides, everywhere, split_axis=0, concat_axis=0)
    gated, sides = lax.optimization_barrier((gated, sides))
    product = triangle_product(sides, row_count, column_count)
    product = lax.all_to_all(product, everywhere, split_axis=0, concat_axis=0)

    gated = jnp.take(jnp.stack(gated), sources, axis=0)
    gated = jnp.transpose(gated.reshape(residues, seqs, inner), (1, 0, 2))
    change = jnp.dot(
        gated.reshape(-1, inner), attention_final_matrix, preferred_element_type=F32
    )
    refreshed_homologs = homolog_tensor + change.reshape(homolog_tensor.shape)
    product = product.reshape(C_TRI, *product.shape[2:])
    pair_output = pair_result(product, mid, gate, incoming_final_matrix)
    return (refreshed_homologs, pair_output)


def solution(mesh):
    in_specs = (
        P("row", "col", None),
        P("row", "col", None),
        P(),
        P(),
        P(),
        P(),
        P(),
        P(),
        P(),
        P(),
    )
    out_specs = (P("row", "col", None), P("row", "col", None))
    return jax.shard_map(body, mesh=mesh, in_specs=in_specs, out_specs=out_specs, check_vma=False)
```

```python
import functools

import jax
import jax.numpy as jnp
from jax import lax
from jax.experimental import pallas as pl
from jax.experimental.pallas import tpu as pltpu
from jax.sharding import PartitionSpec as P

FEATURE_DEPTH = 256
C_Z = 128
TENSOR_FEATURES = 32
C_TRI = 128
ATTENTION_UNITS = 8
UNIT_WIDTH = 32
EPS = 1e-05
GROUP = 4
F32 = jnp.float32
BF16 = jnp.bfloat16
NT = (((1,), (1,)), ((), ()))


def matmul(left, right):
    return jnp.dot(left, right, preferred_element_type=F32)


def matmul_nt(left, right):
    return lax.dot_general(left, right, NT, preferred_element_type=F32)


def sigmoid(values):
    return 0.5 * jnp.tanh(0.5 * values) + 0.5


def cost(microseconds):
    return pl.CostEstimate(
        flops=int(microseconds * 1e9), bytes_accessed=int(microseconds * 1e6), transcendentals=0
    )


def params(megabytes, *semantics):
    return pltpu.CompilerParams(
        dimension_semantics=semantics or None, vmem_limit_bytes=megabytes * 1024 * 1024
    )


def fold(values, combine):
    while values.shape[0] > 8:
        half = values.shape[0] // 2
        values = combine(values[:half], values[half:])
    return values


def top_rows(values):
    return jnp.max(fold(values, jnp.maximum), axis=0, keepdims=True)


def sum_rows(values):
    return jnp.sum(fold(values, jnp.add), axis=0, keepdims=True)


def normalise_rows(values):
    count = values.shape[0]
    centred = values - sum_rows(values) * (1.0 / count)
    variance = sum_rows(centred * centred) * (1.0 / count)
    return (centred * lax.rsqrt(variance + EPS)).astype(BF16)


def standardised_columns(first_rows, second_rows, first, count, residues):
    seqs = first_rows.shape[0] // residues
    columns = []
    for n in range(count):
        rows = pl.ds(first + n, seqs, stride=residues)
        columns.append(jnp.concatenate([first_rows[rows, :], second_rows[rows, :]], axis=1))
    column = jnp.concatenate(columns, axis=0)
    centred = column - jnp.mean(column, axis=1, keepdims=True)
    variance = jnp.mean(centred * centred, axis=1, keepdims=True) + EPS
    scale = lax.rsqrt(variance)
    return centred * scale, variance * scale


def high_kernel(sources_ref, first_ref, second_ref, *rest):
    *pieces_hbm, high_ref, sent = rest
    seqs, residues, lanes = first_ref.shape
    count = len(pieces_hbm)
    own = high_ref.shape[1]
    step = pl.program_id(0)
    first_rows = first_ref.reshape(seqs * residues, lanes)
    second_rows = second_ref.reshape(seqs * residues, lanes)
    shift = lax.rem(sources_ref[step] * own, residues) if own < residues else 0
    for n in range(own):
        normed, _ = standardised_columns(first_rows, second_rows, shift + n, 1, residues)
        high_ref[step, n] = normed.astype(BF16)
    copies = [
        pltpu.make_async_copy(high_ref.at[p], piece_hbm, sent.at[p])
        for p, piece_hbm in enumerate(pieces_hbm)
    ]
    for p in range(count):

        @pl.when(step == p)
        def _(p=p):
            copies[p].start()

    @pl.when(step == count - 1)
    def _():
        for copy in copies:
            copy.wait()


def standardise_high(sources, block):
    seqs, residues, depth = block.shape
    half = depth // 2
    count = sources.shape[0]
    own = residues // count
    hbm = pl.BlockSpec(memory_space=pltpu.HBM)
    together = 8 // own
    return pl.pallas_call(
        high_kernel,
        grid_spec=pltpu.PrefetchScalarGridSpec(
            num_scalar_prefetch=1,
            grid=(count,),
            in_specs=[
                pl.BlockSpec((seqs, 8, half), lambda p, sources: (0, sources[p] // together, 0)),
                pl.BlockSpec((seqs, 8, half), lambda p, sources: (0, sources[p] // together, 1)),
            ],
            out_specs=[hbm] * count,
            scratch_shapes=[
                pltpu.VMEM((count, own, seqs, depth), BF16),
                pltpu.SemaphoreType.DMA((count,)),
            ],
        ),
        out_shape=[pltpu.HBM((own, seqs, depth), BF16)] * count,
        compiler_params=params(10, "arbitrary"),
        cost_estimate=cost(3),
        name="standardise_high",
    )(sources, block, block)


def low_kernel(sources_ref, first_ref, second_ref, *rest):
    *pieces_hbm, low_ref, sent = rest
    seqs, residues, lanes = first_ref.shape
    own = residues // len(pieces_hbm)
    first_rows = first_ref.reshape(seqs * residues, lanes)
    second_rows = second_ref.reshape(seqs * residues, lanes)
    lane = lax.broadcasted_iota(jnp.int32, (seqs, 128), 1)
    for p in range(len(pieces_hbm)):
        spreads = jnp.zeros((seqs, 128), F32)
        for n in range(own):
            normed, spread = standardised_columns(
                first_rows, second_rows, p * own + n, 1, residues
            )
            left = (normed - normed.astype(BF16).astype(F32)).astype(BF16)
            low_ref[p, n * seqs : (n + 1) * seqs, :] = left
            spreads = jnp.where(lane == n, spread, spreads)
        spreads = spreads.T[:8, :]
        coarse = spreads.astype(BF16).astype(F32)
        kept = jnp.concatenate([coarse, spreads - coarse], axis=0)
        kept = jnp.concatenate([kept, jnp.zeros((16, 2 * lanes - seqs), F32)], axis=1)
        low_ref[p, own * seqs :, :] = kept.astype(BF16)
    sends = []
    for p, piece_hbm in enumerate(pieces_hbm):
        source = low_ref.at[sources_ref[p]]
        sends.append(pltpu.make_async_copy(source, piece_hbm, sent.at[p]))
        sends[-1].start()
    for send in sends:
        send.wait()


def standardise_low(sources, block):
    seqs, residues, depth = block.shape
    half = depth // 2
    count = sources.shape[0]
    height = residues // count * seqs + 16
    hbm = pl.BlockSpec(memory_space=pltpu.HBM)
    return pl.pallas_call(
        low_kernel,
        grid=(1,),
        in_specs=[
            pl.BlockSpec(memory_space=pltpu.SMEM),
            pl.BlockSpec((seqs, residues, half), lambda g: (0, 0, 0)),
            pl.BlockSpec((seqs, residues, half), lambda g: (0, 0, 1)),
        ],
        out_specs=[hbm] * count,
        out_shape=[pltpu.HBM((height, depth), BF16)] * count,
        scratch_shapes=[
            pltpu.VMEM((count, height, depth), BF16),
            pltpu.SemaphoreType.DMA((count,)),
        ],
        compiler_params=params(14, "arbitrary"),
        cost_estimate=cost(4),
        name="standardise_low",
    )(sources, block, block)


def attention_kernel(key_ref, others_ref, *rest):
    *normed_refs, turned_ref, scores_ref, weights_ref = rest
    blocks = len(normed_refs)
    residues, seqs, _ = normed_refs[0].shape
    total = blocks * seqs
    inner = ATTENTION_UNITS * UNIT_WIDTH
    ring = scores_ref.shape[0]
    columns = []

    def project(n):
        column = jnp.concatenate([ref[n] for ref in normed_refs], axis=0)
        key_rows = matmul(column, key_ref[...]).astype(BF16)
        projected = matmul_nt(others_ref[...], column)
        queries = (projected[:inner] * UNIT_WIDTH ** (-0.5)).astype(BF16)
        value_rows = projected[inner : 2 * inner].astype(BF16)
        gates = sigmoid(projected[2 * inner :])
        columns.append((key_rows, queries, value_rows, gates))
    units = [(n, h) for n in range(residues) for h in range(ATTENTION_UNITS)]

    def score(unit):
        n, h = units[unit]
        key_rows, queries, _, _ = columns[n]
        rows = slice(h * UNIT_WIDTH, (h + 1) * UNIT_WIDTH)
        scores_ref[unit % ring] = matmul(key_rows[:, rows], queries[rows])

    def weigh(unit):
        for low in range(0, total, 128):
            scores = scores_ref[unit % ring, :, low : low + 128]
            weights = jnp.exp(scores - top_rows(scores))
            scale = 1.0 / sum_rows(weights)
            weights_ref[unit % ring, :, low : low + 128] = (weights * scale).astype(BF16)

    def attend(unit):
        n, h = units[unit]
        _, _, value_rows, gates = columns[n]
        rows = slice(h * UNIT_WIDTH, (h + 1) * UNIT_WIDTH)
        attended = matmul(value_rows[rows], weights_ref[unit % ring]) * gates[rows]
        turned_ref[n, rows, :] = attended.astype(BF16)

    project(0)
    for step in range(len(units) + 2):
        if step < len(units):
            score(step)
            n, h = units[step]
            if h == ATTENTION_UNITS // 2 and n + 1 < residues:
                project(n + 1)
        if 1 <= step <= len(units):
            weigh(step - 1)
        if step >= 2:
            attend(step - 2)


def attention(normed, key_matrix, other_matrices):
    blocks = len(normed)
    residues, seqs, depth = normed[0].shape
    total = blocks * seqs
    inner = ATTENTION_UNITS * UNIT_WIDTH
    step = 4
    return pl.pallas_call(
        attention_kernel,
        grid=(residues // step,),
        in_specs=[
            pl.BlockSpec((depth, inner), lambda n: (0, 0)),
            pl.BlockSpec((3 * inner, depth), lambda n: (0, 0)),
        ]
        + [pl.BlockSpec((step, seqs, depth), lambda n: (n, 0, 0))] * blocks,
        out_specs=pl.BlockSpec((step, inner, total), lambda n: (n, 0, 0)),
        out_shape=jax.ShapeDtypeStruct((residues, inner, total), BF16),
        scratch_shapes=[
            pltpu.VMEM((4, total, total), F32),
            pltpu.VMEM((4, total, total), BF16),
        ],
        compiler_params=params(12 + (total // 128) ** 2, "arbitrary"),
        cost_estimate=cost(10),
        name="attention",
    )(key_matrix, other_matrices, *normed)


def turn_kernel(turned_ref, *gated_refs):
    seqs = gated_refs[0].shape[1]
    for n in range(turned_ref.shape[0]):
        back = turned_ref[n].T
        for block, gated_ref in enumerate(gated_refs):
            gated_ref[n] = back[block * seqs : (block + 1) * seqs]


def turn_back(turned, blocks):
    residues, inner, total = turned.shape
    seqs = total // blocks
    return pl.pallas_call(
        turn_kernel,
        grid=(residues // 2,),
        in_specs=[pl.BlockSpec((2, inner, total), lambda n: (n, 0, 0))],
        out_specs=[pl.BlockSpec((2, seqs, inner), lambda n: (n, 0, 0))] * blocks,
        out_shape=[pltpu.HBM((residues, seqs, inner), BF16)] * blocks,
        compiler_params=params(12, "arbitrary"),
        cost_estimate=cost(2),
        name="turn_back",
    )(turned)


def alignment_kernel(sources_ref, turned_ref, final_ref, entry_ref, *rest):
    *refs, left_ref, right_ref, rows_ref = rest
    blocks = len(refs) // 3
    high_refs, low_refs, spread_refs = refs[:blocks], refs[blocks : 2 * blocks], refs[2 * blocks :]
    residues, seqs, depth = high_refs[0].shape
    total = blocks * seqs
    features = TENSOR_FEATURES
    step = pl.program_id(0)
    line = lax.broadcasted_iota(jnp.int32, (depth, depth), 0)
    same = line == lax.broadcasted_iota(jnp.int32, (depth, depth), 1)
    same = jnp.where(same, 1.0, 0.0).astype(BF16)
    twice = jnp.concatenate([same, same], axis=1)
    for n in range(residues):
        high = jnp.concatenate([ref[n] for ref in high_refs], axis=0)
        low = jnp.concatenate(
            [ref[n * seqs : (n + 1) * seqs, :] for ref in low_refs], axis=0
        )
        column = matmul_nt(twice, jnp.concatenate([high, low], axis=1))
        spreads = []
        for ref in spread_refs:
            kept = ref[:, :seqs].astype(F32)
            row = lax.broadcasted_iota(jnp.int32, kept.shape, 0)
            chosen = lax.rem(row, 8) == step * residues + n
            spreads.append(jnp.sum(jnp.where(chosen, kept, 0.0), axis=0, keepdims=True))
        spread = jnp.concatenate(spreads, axis=1)
        updated = column * spread + matmul(final_ref[...], turned_ref[n])
        projected = matmul(entry_ref[...], normalise_rows(updated))
        me = sources_ref[0]
        tiles = [projected[:, low : low + 128] for low in range(0, total, 128)]
        odd = lax.rem(me, 2) == 1
        tiles = [jnp.where(odd, pltpu.roll(tile, seqs, 1), tile) for tile in tiles]
        width = 1
        while width < len(tiles):
            crossed = lax.rem(lax.div(me, 2 * width), 2) == 1
            tiles = [
                jnp.where(crossed, tiles[t ^ width], tiles[t]) for t in range(len(tiles))
            ]
            width *= 2
        first = pl.multiple_of((step * residues + n) * features, features)
        for t, tile in enumerate(tiles):
            right_ref[n, :, t * 128 : (t + 1) * 128] = tile[features:].astype(BF16)
            rows_ref[t, pl.ds(first, features), :] = tile[:features]

    @pl.when(step == pl.num_programs(0) - 1)
    def _():
        count = rows_ref.shape[1] // features
        together = max(1, 16 // count)
        for c in range(0, features, together):
            pieces = []
            for e in range(together):
                chosen = pl.ds(c + e, count, stride=features)
                tiles = [rows_ref[tile, chosen, :] for tile in range(total // 128)]
                pieces.append(jnp.concatenate(tiles, axis=1))
            piece = jnp.concatenate(pieces, axis=0).astype(BF16)
            left_ref[c * count : (c + together) * count, :] = piece


def alignment(sources, high, low, turned, final_matrix, entry_matrices):
    blocks = len(high)
    residues, seqs, depth = high[0].shape
    total = blocks * seqs
    features = TENSOR_FEATURES
    step = 4
    height = residues * seqs + 16
    return pl.pallas_call(
        alignment_kernel,
        grid=(residues // step,),
        in_specs=[
            pl.BlockSpec(memory_space=pltpu.SMEM),
            pl.BlockSpec((step, depth, total), lambda n: (n, 0, 0)),
            pl.BlockSpec(final_matrix.shape, lambda n: (0, 0)),
            pl.BlockSpec(entry_matrices.shape, lambda n: (0, 0)),
        ]
        + [pl.BlockSpec((step, seqs, depth), lambda n: (n, 0, 0))] * blocks
        + [pl.BlockSpec((step * seqs, depth), lambda n: (n, 0))] * blocks
        + [pl.BlockSpec((16, depth), lambda n: (height // 16 - 1, 0))] * blocks,
        out_specs=[
            pl.BlockSpec((features * residues, total), lambda n: (0, 0)),
            pl.BlockSpec((step, features, total), lambda n: (n, 0, 0)),
        ],
        out_shape=[
            jax.ShapeDtypeStruct((features * residues, total), BF16),
            jax.ShapeDtypeStruct((residues, features, total), BF16),
        ],
        scratch_shapes=[pltpu.VMEM((total // 128, residues * features, 128), F32)],
        compiler_params=params(16, "arbitrary"),
        cost_estimate=cost(4),
        name="alignment",
    )(sources, turned, final_matrix, entry_matrices, *high, *low, *low)


def pair_kernel(
    left_slots_ref,
    right_firsts_ref,
    *rest,
    slots,
):
    weights_ref, entry_ref, switch_ref, couplings_hbm, mid_hbm, gate_hbm, sides_hbm = rest[-16:-9]
    outer_ref, spread_ref, sum_ref, rows_ref, couplings_ref = rest[-9:-4]
    mid_ref, gate_ref, sides_ref, copied = rest[-4:]
    left_refs, right_refs = rest[: 2 * slots], rest[2 * slots : -16]
    fetched = pltpu.make_async_copy(couplings_hbm, couplings_ref, copied.at[0])
    fetched.start()
    copies = []

    def send(source, target):
        copies.append(pltpu.make_async_copy(source, target, copied.at[len(copies) + 1]))
        copies[-1].start()

    features = TENSOR_FEATURES
    piece_rows, total = left_refs[0].shape
    residues = piece_rows // features
    rows = 2 * slots * residues
    share = right_refs[0].shape[0]
    columns = len(right_refs) * share
    groups = columns // GROUP
    wide = share * features
    together = spread_ref.shape[1] // 64

    for half in range(2):
        halves = left_refs[half * slots : (half + 1) * slots]
        piece = jnp.concatenate([ref[...] for ref in halves], axis=0)
        target = slice(half * slots * piece_rows, (half + 1) * slots * piece_rows)
        for p, right_ref in enumerate(right_refs):
            right = right_ref[...].reshape(wide, total)
            outer_ref[target, p * wide : (p + 1) * wide] = matmul_nt(piece, right) * (1.0 / total)

    spread_ref[...] = jnp.zeros_like(spread_ref)
    front = lax.broadcasted_iota(jnp.int32, (rows, 128), 1) < 64

    def channel_step(p, carry):
        slot = lax.rem(p, 2)
        for e in range(together):
            source = pl.multiple_of((p * together + e) * features, features)
            piece = weights_ref[pl.ds(source, features), :]
            for place in range(2):
                low = e * 64 + place * features
                spread_ref[slot, low : low + features, place * C_Z : (place + 1) * C_Z] = piece
        pieces = []
        for g in range(groups):
            parts = []
            for e in range(together):
                channel = []
                for slot_number in range(2 * slots):
                    first = slot_number * piece_rows + (p * together + e) * residues
                    source = pl.ds(pl.multiple_of(first, residues), residues)
                    channel.append(outer_ref[source, g * 128 : (g + 1) * 128])
                parts.append(jnp.concatenate(channel, axis=0).astype(BF16))
            lows, highs = [], []
            for e in range(0, together, 2):
                lows.append(jnp.where(front, parts[e], pltpu.roll(parts[e + 1], 64, 1)))
                highs.append(jnp.where(front, pltpu.roll(parts[e], 64, 1), parts[e + 1]))
            pieces.append(jnp.concatenate(lows, axis=1))
            pieces.append(jnp.concatenate(highs, axis=1))
        update = matmul(jnp.concatenate(pieces, axis=0), spread_ref[slot])

        @pl.when(p == 0)
        def _():
            sum_ref[...] = update

        @pl.when(p > 0)
        def _():
            sum_ref[...] += update

        return carry

    lax.fori_loop(0, features // together, channel_step, 0)

    left_firsts = [left_slots_ref[j] * residues for j in range(2 * slots)]
    right_firsts = [right_firsts_ref[p] for p in range(len(right_refs))]
    fetched.wait()
    for g in range(groups):
        normed, places = [], []
        for place in range(GROUP):
            p, n = divmod(g * GROUP + place, share)
            b = right_firsts[p] + n
            places.append(b)
            lanes = slice(place % 2 * C_Z, (place % 2 + 1) * C_Z)
            start = (2 * g + place // 2) * rows
            pieces = []
            for first in left_firsts:
                source = pl.ds(pl.multiple_of(start + first, residues), residues)
                pieces.append(sum_ref[source, lanes])
            mid = jnp.concatenate(pieces, axis=0)
            mid = mid + couplings_ref[pl.ds(b, rows, stride=columns), :]
            mid_ref[g * GROUP + place] = mid
            centred = mid - jnp.mean(mid, axis=1, keepdims=True)
            variance = jnp.mean(centred * centred, axis=1, keepdims=True)
            normed.append((centred * lax.rsqrt(variance + EPS)).astype(BF16))
        gates = sigmoid(matmul(jnp.concatenate(normed, axis=0), switch_ref[...]))
        blank = jnp.zeros_like(normed[0])
        for place in range(0, GROUP, 2):
            twice = []
            for e in range(2):
                part = gates[(place + e) * rows : (place + e + 1) * rows]
                gate_ref[g * GROUP + place + e] = part
                twice.append(jnp.concatenate([normed[place + e], blank], axis=1))
                twice.append(jnp.concatenate([blank, normed[place + e]], axis=1))
            sides = matmul_nt(entry_ref[...], jnp.concatenate(twice, axis=0))
            sides = sigmoid(sides[C_TRI:]) * sides[:C_TRI]
            for e in range(2):
                first = pl.multiple_of(places[place + e] * C_TRI, C_TRI)
                rows_ref[pl.ds(first, C_TRI), :] = sides[:, e * 2 * rows : (e + 1) * 2 * rows]

        if (g + 1) * GROUP % share == 0:
            p = (g + 1) * GROUP // share - 1
            source, target = pl.ds(p * share, share), pl.ds(right_firsts[p], share)
            send(mid_ref.at[source], mid_hbm.at[target])
            send(gate_ref.at[source], gate_hbm.at[target])

    cut = C_TRI // 4
    for part in range(4):

        def turn_step(c, carry):
            sides_ref[c] = rows_ref[pl.ds(c, columns, stride=C_TRI), :].astype(BF16)
            return carry

        lax.fori_loop(part * cut, (part + 1) * cut, turn_step, 0, unroll=8)
        chosen = pl.ds(part * cut, cut)
        send(sides_ref.at[chosen], sides_hbm.at[chosen])
    for copy in copies:
        copy.wait()


def pair_update(left_slots, right_firsts, left, rights, weights, couplings, entry, switch):
    rows, columns, depth = couplings.shape
    whole = jax.ShapeDtypeStruct((columns, rows, depth), F32)
    sides = jax.ShapeDtypeStruct((C_TRI, columns, 2 * rows), BF16)
    smem = pl.BlockSpec(memory_space=pltpu.SMEM)
    vmem = pl.BlockSpec(memory_space=pltpu.VMEM)
    anywhere = pl.BlockSpec(memory_space=pl.ANY)
    return pl.pallas_call(
        functools.partial(pair_kernel, slots=len(left) // 2),
        in_specs=[smem] * 2 + [vmem] * (3 + len(left) + len(rights)) + [anywhere],
        out_specs=[anywhere] * 3,
        out_shape=[pltpu.HBM(whole.shape, F32)] * 2 + [pltpu.HBM(sides.shape, BF16)],
        scratch_shapes=[
            pltpu.VMEM((rows * TENSOR_FEATURES, columns * TENSOR_FEATURES), F32),
            pltpu.VMEM((2, 8 * 64, 2 * depth), BF16),
            pltpu.VMEM((columns // 2 * rows, 2 * depth), F32),
            pltpu.VMEM((columns * C_TRI, 2 * rows), F32),
            pltpu.VMEM((rows * columns, depth), F32),
            pltpu.VMEM(whole.shape, F32),
            pltpu.VMEM(whole.shape, F32),
            pltpu.VMEM(sides.shape, BF16),
            pltpu.SemaphoreType.DMA((2 * len(rights) + 5,)),
        ],
        compiler_params=params(28),
        cost_estimate=cost(12),
        name="pair_update",
    )(
        left_slots,
        right_firsts,
        *left,
        *rights,
        weights,
        entry,
        switch,
        couplings.reshape(rows * columns, depth),
    )


def product_kernel(sides_ref, out_ref, *, grid_rows, grid_columns):
    channels, part, lanes = sides_ref.shape[1:]
    half = lanes // 2
    lane = lax.broadcasted_iota(jnp.int32, (grid_columns * part, lanes), 1)
    front = lane < half
    cut = front[: part // 2]
    for channel in range(channels):
        lefts, rights = [], []
        for r in range(0, grid_rows, 2):
            even, odd = [
                jnp.concatenate(
                    [sides_ref[(r + e) * grid_columns + c, channel] for c in range(grid_columns)],
                    axis=0,
                )
                for e in range(2)
            ]
            lefts.append(jnp.where(front, even, pltpu.roll(odd, half, 1)))
            rights.append(jnp.where(front, pltpu.roll(even, half, 1), odd))
        product = matmul_nt(jnp.concatenate(rights, axis=1), jnp.concatenate(lefts, axis=1))
        product = product.astype(BF16)
        for c in range(grid_columns):
            for r in range(0, grid_rows, 2):
                block = product[c * part : (c + 1) * part, r * half : (r + 2) * half]
                top, bottom = block[: part // 2], block[part // 2 :]
                even = jnp.where(cut, top, pltpu.roll(bottom, half, 1))
                out_ref[r * grid_columns + c, channel] = even
                odd = jnp.where(cut, pltpu.roll(top, half, 1), bottom)
                out_ref[(r + 1) * grid_columns + c, channel] = odd


def triangle_product(sides, grid_rows, grid_columns):
    devices, channels, part, lanes = sides.shape
    step = 2 if channels % 2 == 0 else 1
    return pl.pallas_call(
        functools.partial(product_kernel, grid_rows=grid_rows, grid_columns=grid_columns),
        grid=(channels // step,),
        in_specs=[pl.BlockSpec((devices, step, part, lanes), lambda c: (0, c, 0, 0))],
        out_specs=pl.BlockSpec((devices, step, part // 2, lanes), lambda c: (0, c, 0, 0)),
        out_shape=pltpu.HBM((devices, channels, part // 2, lanes), BF16),
        compiler_params=params(8, "arbitrary"),
        cost_estimate=cost(3),
        name="triangle_product",
    )(sides)


def output_kernel(
    product_ref, final_ref, mid_hbm, gate_hbm, out_hbm, wide_ref, mid_ref, gate_ref, out_ref, *copied
):
    channels, part, lanes = product_ref.shape
    columns, rows, depth = mid_ref.shape
    own = 8
    fetched, sent = copied
    fetches, sends = [], []
    for first in range(0, columns, own):
        chosen = pl.ds(first, own)
        for source, target in ((mid_hbm, mid_ref), (gate_hbm, gate_ref)):
            fetches.append(
                pltpu.make_async_copy(
                    source.at[chosen], target.at[chosen], fetched.at[len(fetches)]
                )
            )
            fetches[-1].start()
    wide_ref[...] = product_ref[...].astype(F32).reshape(channels * part, lanes)
    for group in range(part // own):
        updates = []
        for j in range(own):
            product = wide_ref[pl.ds(group * own + j, channels, stride=part), :]
            updates.append(matmul(normalise_rows(product).T, final_ref[...]))
        for half in range(2):
            cut = half * (part // own) + group
            fetches[2 * cut].wait()
            fetches[2 * cut + 1].wait()
            out_rows = out_ref.at[cut].reshape(rows * own, depth)
            for j in range(own):
                b = cut * own + j
                piece = updates[j][half * rows : (half + 1) * rows]
                out_rows[pl.ds(j, rows, stride=own), :] = mid_ref[b] + gate_ref[b] * piece
            sends.append(
                pltpu.make_async_copy(
                    out_ref.at[cut], out_hbm.at[:, pl.ds(cut * own, own)], sent.at[len(sends)]
                )
            )
            sends[-1].start()
    for send in sends:
        send.wait()


def pair_result(product, mid, gate, final_matrix):
    channels, part, lanes = product.shape
    columns, rows, depth = mid.shape
    vmem, hbm = pl.BlockSpec(memory_space=pltpu.VMEM), pl.BlockSpec(memory_space=pltpu.HBM)
    return pl.pallas_call(
        output_kernel,
        in_specs=[vmem, vmem, hbm, hbm],
        out_specs=hbm,
        out_shape=pltpu.HBM((rows, columns, depth), F32),
        scratch_shapes=[
            pltpu.VMEM((channels * part, lanes), F32),
            pltpu.VMEM(mid.shape, F32),
            pltpu.VMEM(mid.shape, F32),
            pltpu.VMEM((columns // 8, rows, 8, depth), F32),
            pltpu.SemaphoreType.DMA((columns // 4,)),
            pltpu.SemaphoreType.DMA((columns // 8,)),
        ],
        compiler_params=params(16),
        cost_estimate=cost(3),
        name="pair_result",
    )(
        product,
        final_matrix,
        pltpu.with_memory_space_constraint(mid, pltpu.HBM),
        pltpu.with_memory_space_constraint(gate, pltpu.HBM),
    )


def swap_cores(block):
    count = lax.axis_size("col")
    return lax.ppermute(block, "col", [(c, c ^ 1) for c in range(count)])


def gather_turned(block, later):
    rows, columns = lax.axis_size("row"), lax.axis_size("col")
    arrived = []
    for shift in range(rows):
        moves = []
        for r in range(rows):
            for q in range(rows):
                for side in range(2):
                    source = r * columns + 2 * q + side
                    moves.append((source, q * columns + 2 * ((r + shift) % rows) + side))
        source = block if shift < 2 else later
        arrived.append(lax.ppermute(source, ("row", "col"), moves))
    return arrived


def both_cores(own):
    rows = lax.axis_size("row")
    core = lax.rem(lax.axis_index("col"), 2)
    other = [swap_cores(piece) for piece in own]
    residues = own[0].shape[0] // TENSOR_FEATURES
    if residues % 8 == 0:
        return own + other
    order = left_order(rows)
    own, other = [jnp.take(jnp.stack(side), order, axis=0) for side in (own, other)]
    joined = 8 // residues
    ordered = []
    for side in (jnp.where(core == 0, own, other), jnp.where(core == 0, other, own)):
        side = side.reshape(rows // joined, joined, TENSOR_FEATURES, residues, -1)
        side = jnp.transpose(side, (0, 2, 1, 3, 4))
        ordered.extend(side.reshape(rows // joined, joined * own.shape[1], -1))
    return ordered


def left_order(rows):
    me = lax.axis_index("col") // 2
    return lax.rem(me - jnp.arange(rows, dtype=jnp.int32) + rows, rows)


def left_groups(rows, residues):
    if residues % 8:
        return jnp.arange(2 * rows * residues // 8, dtype=jnp.int32)
    core = lax.rem(lax.axis_index("col"), 2)
    order = left_order(rows)
    return jnp.concatenate([order + core * rows, order + (1 - core) * rows])


def exchange_rows(pieces):
    arrived = [pieces[0]]
    for shift in range(1, len(pieces)):
        moves = [(r, r ^ shift) for r in range(len(pieces))]
        arrived.append(lax.ppermute(pieces[shift], "row", moves))
    return arrived


def paired_entries(matrices):
    turned = matrices.reshape(C_Z, 2, 2, C_TRI)
    return jnp.transpose(turned, (2, 3, 1, 0)).reshape(2 * C_TRI, 2 * C_Z)


def body(
    homolog_tensor,
    couplings,
    attention_probe_matrix,
    attention_extra_matrices,
    attention_final_matrix,
    tensor_entry_matrices,
    tensor_final_matrix,
    incoming_entry_matrices,
    incoming_switch_matrix,
    incoming_final_matrix,
):
    inner = ATTENTION_UNITS * UNIT_WIDTH
    row_count = lax.axis_size("row")
    seqs, residues, depth = homolog_tensor.shape
    own_residues = residues // row_count
    sources = lax.axis_index("row") ^ jnp.arange(row_count, dtype=jnp.int32)
    high = exchange_rows(standardise_high(sources, homolog_tensor))
    low = standardise_low(sources, homolog_tensor)
    others = jnp.concatenate(
        [attention_probe_matrix.T, attention_extra_matrices[:, inner:].T], axis=0
    )
    early = (
        attention_extra_matrices[:, :inner],
        others,
        attention_final_matrix.T,
        tensor_entry_matrices.T,
        paired_entries(incoming_entry_matrices),
        sources * own_residues,
        left_groups(row_count, own_residues),
    )
    high, low, early = lax.optimization_barrier((high, low, early))
    key_matrix, others, final_turned, tensor_turned, entries, firsts, slots = early
    low = exchange_rows(low)
    turned = attention(high, key_matrix, others)
    gated = turn_back(turned, row_count)
    left_piece, right_piece = alignment(
        sources, high, low, turned, final_turned, tensor_turned
    )

    rights = exchange_rows([right_piece] * row_count)
    later, rights[1] = lax.optimization_barrier((left_piece, rights[1]))
    own = gather_turned(left_piece, later)
    own[-1], rights = lax.optimization_barrier((own[-1], rights))
    mid, gate, sides = pair_update(
        slots,
        firsts,
        both_cores(own),
        rights,
        tensor_final_matrix,
        couplings,
        entries,
        incoming_switch_matrix,
    )
    gated, sides = lax.optimization_barrier((gated, sides))
    gated = exchange_rows(gated)

    everywhere = ("row", "col")
    column_count = lax.axis_size("col")
    devices = row_count * column_count
    sides = sides.reshape(devices, C_TRI // devices, *sides.shape[1:])
    sides = lax.all_to_all(sides, everywhere, split_axis=0, concat_axis=0)
    gated, sides = lax.optimization_barrier((gated, sides))
    product = triangle_product(sides, row_count, column_count)
    product = lax.all_to_all(product, everywhere, split_axis=0, concat_axis=0)

    gated = jnp.take(jnp.stack(gated), sources, axis=0)
    gated = jnp.transpose(gated.reshape(residues, seqs, inner), (1, 0, 2))
    change = jnp.dot(
        gated.reshape(-1, inner), attention_final_matrix, preferred_element_type=F32
    )
    refreshed_homologs = homolog_tensor + change.reshape(homolog_tensor.shape)
    product = product.reshape(C_TRI, *product.shape[2:])
    pair_output = pair_result(product, mid, gate, incoming_final_matrix)
    return (refreshed_homologs, pair_output)


def solution(mesh):
    in_specs = (
        P("row", "col", None),
        P("row", "col", None),
        P(),
        P(),
        P(),
        P(),
        P(),
        P(),
        P(),
        P(),
    )
    out_specs = (P("row", "col", None), P("row", "col", None))
    return jax.shard_map(body, mesh=mesh, in_specs=in_specs, out_specs=out_specs, check_vma=False)
```

```python
import functools

import jax
import jax.numpy as jnp
from jax import lax
from jax.experimental import pallas as pl
from jax.experimental.pallas import tpu as pltpu
from jax.sharding import PartitionSpec as P

FEATURE_DEPTH = 256
C_Z = 128
TENSOR_FEATURES = 32
C_TRI = 128
ATTENTION_UNITS = 8
UNIT_WIDTH = 32
EPS = 1e-05
GROUP = 4
F32 = jnp.float32
BF16 = jnp.bfloat16
NT = (((1,), (1,)), ((), ()))


def matmul(left, right):
    return jnp.dot(left, right, preferred_element_type=F32)


def matmul_nt(left, right):
    return lax.dot_general(left, right, NT, preferred_element_type=F32)


def sigmoid(values):
    return 0.5 * jnp.tanh(0.5 * values) + 0.5


def cost(microseconds):
    return pl.CostEstimate(
        flops=int(microseconds * 1e9), bytes_accessed=int(microseconds * 1e6), transcendentals=0
    )


def params(megabytes, *semantics):
    return pltpu.CompilerParams(
        dimension_semantics=semantics or None, vmem_limit_bytes=megabytes * 1024 * 1024
    )


def fold(values, combine):
    while values.shape[0] > 8:
        half = values.shape[0] // 2
        values = combine(values[:half], values[half:])
    return values


def top_rows(values):
    return jnp.max(fold(values, jnp.maximum), axis=0, keepdims=True)


def sum_rows(values):
    return jnp.sum(fold(values, jnp.add), axis=0, keepdims=True)


def normalise_rows(values):
    count = values.shape[0]
    centred = values - sum_rows(values) * (1.0 / count)
    variance = sum_rows(centred * centred) * (1.0 / count)
    return (centred * lax.rsqrt(variance + EPS)).astype(BF16)


def standardised_columns(first_rows, second_rows, first, count, residues):
    seqs = first_rows.shape[0] // residues
    columns = []
    for n in range(first, first + count):
        rows = pl.ds(n, seqs, stride=residues)
        columns.append(jnp.concatenate([first_rows[rows, :], second_rows[rows, :]], axis=1))
    column = jnp.concatenate(columns, axis=0)
    centred = column - jnp.mean(column, axis=1, keepdims=True)
    variance = jnp.mean(centred * centred, axis=1, keepdims=True) + EPS
    scale = lax.rsqrt(variance)
    return centred * scale, variance * scale


def high_kernel(sources_ref, block_hbm, *rest):
    *pieces_hbm, first_ref, second_ref, high_ref, fetched, sent = rest
    seqs, residues, lanes = first_ref.shape
    own = residues // len(pieces_hbm)
    step = 16
    fetches, sends = [], []
    for s in range(0, seqs, step):
        chosen = pl.ds(s, step)
        for half, ref in enumerate((first_ref, second_ref)):
            source = block_hbm.at[chosen, :, pl.ds(half * lanes, lanes)]
            fetches.append(
                pltpu.make_async_copy(source, ref.at[chosen], fetched.at[len(fetches)])
            )
            fetches[-1].start()
    for part in range(seqs // step):
        chosen = pl.ds(part * step, step)
        fetches[2 * part].wait()
        fetches[2 * part + 1].wait()
        first_rows = first_ref.at[chosen].reshape(step * residues, lanes)
        second_rows = second_ref.at[chosen].reshape(step * residues, lanes)
        for n in range(0, residues, 8):
            normed, _ = standardised_columns(first_rows, second_rows, n, 8, residues)
            high_ref[part, n : n + 8] = normed.astype(BF16).reshape(8, step, 2 * lanes)
        for p, piece_hbm in enumerate(pieces_hbm):
            source = high_ref.at[part, pl.ds(sources_ref[p] * own, own)]
            sends.append(
                pltpu.make_async_copy(source, piece_hbm.at[:, chosen], sent.at[len(sends)])
            )
            sends[-1].start()
    for send in sends:
        send.wait()


def standardise_high(sources, block):
    seqs, residues, depth = block.shape
    half = depth // 2
    count = sources.shape[0]
    hbm = pl.BlockSpec(memory_space=pltpu.HBM)
    return pl.pallas_call(
        high_kernel,
        in_specs=[pl.BlockSpec(memory_space=pltpu.SMEM), hbm],
        out_specs=[hbm] * count,
        out_shape=[pltpu.HBM((residues // count, seqs, depth), BF16)] * count,
        scratch_shapes=[
            pltpu.VMEM((seqs, residues, half), F32),
            pltpu.VMEM((seqs, residues, half), F32),
            pltpu.VMEM((seqs // 16, residues, 16, depth), BF16),
            pltpu.SemaphoreType.DMA((seqs // 8,)),
            pltpu.SemaphoreType.DMA((seqs // 16 * count,)),
        ],
        compiler_params=params(10),
        cost_estimate=cost(3),
        name="standardise_high",
    )(sources, pltpu.with_memory_space_constraint(block, pltpu.HBM))


def low_kernel(sources_ref, first_ref, second_ref, *rest):
    *pieces_hbm, low_ref, sent = rest
    seqs, residues, lanes = first_ref.shape
    own = residues // len(pieces_hbm)
    first_rows = first_ref.reshape(seqs * residues, lanes)
    second_rows = second_ref.reshape(seqs * residues, lanes)
    lane = lax.broadcasted_iota(jnp.int32, (seqs, 128), 1)
    for p in range(len(pieces_hbm)):
        spreads = jnp.zeros((seqs, 128), F32)
        for n in range(own):
            normed, spread = standardised_columns(
                first_rows, second_rows, p * own + n, 1, residues
            )
            left = (normed - normed.astype(BF16).astype(F32)).astype(BF16)
            low_ref[p, n * seqs : (n + 1) * seqs, :] = left
            spreads = jnp.where(lane == n, spread, spreads)
        spreads = spreads.T[:8, :]
        coarse = spreads.astype(BF16).astype(F32)
        kept = jnp.concatenate([coarse, spreads - coarse], axis=0)
        kept = jnp.concatenate([kept, jnp.zeros((16, 2 * lanes - seqs), F32)], axis=1)
        low_ref[p, own * seqs :, :] = kept.astype(BF16)
    sends = []
    for p, piece_hbm in enumerate(pieces_hbm):
        source = low_ref.at[sources_ref[p]]
        sends.append(pltpu.make_async_copy(source, piece_hbm, sent.at[p]))
        sends[-1].start()
    for send in sends:
        send.wait()


def standardise_low(sources, block):
    seqs, residues, depth = block.shape
    half = depth // 2
    count = sources.shape[0]
    height = residues // count * seqs + 16
    hbm = pl.BlockSpec(memory_space=pltpu.HBM)
    return pl.pallas_call(
        low_kernel,
        grid=(1,),
        in_specs=[
            pl.BlockSpec(memory_space=pltpu.SMEM),
            pl.BlockSpec((seqs, residues, half), lambda g: (0, 0, 0)),
            pl.BlockSpec((seqs, residues, half), lambda g: (0, 0, 1)),
        ],
        out_specs=[hbm] * count,
        out_shape=[pltpu.HBM((height, depth), BF16)] * count,
        scratch_shapes=[
            pltpu.VMEM((count, height, depth), BF16),
            pltpu.SemaphoreType.DMA((count,)),
        ],
        compiler_params=params(14, "arbitrary"),
        cost_estimate=cost(4),
        name="standardise_low",
    )(sources, block, block)


def attention_kernel(key_ref, others_ref, *rest):
    *normed_refs, turned_ref, scores_ref, weights_ref = rest
    blocks = len(normed_refs)
    residues, seqs, _ = normed_refs[0].shape
    total = blocks * seqs
    inner = ATTENTION_UNITS * UNIT_WIDTH
    ring = scores_ref.shape[0]
    columns = []

    def project(n):
        column = jnp.concatenate([ref[n] for ref in normed_refs], axis=0)
        key_rows = matmul(column, key_ref[...]).astype(BF16)
        projected = matmul_nt(others_ref[...], column)
        queries = (projected[:inner] * UNIT_WIDTH ** (-0.5)).astype(BF16)
        value_rows = projected[inner : 2 * inner].astype(BF16)
        gates = sigmoid(projected[2 * inner :])
        columns.append((key_rows, queries, value_rows, gates))
    units = [(n, h) for n in range(residues) for h in range(ATTENTION_UNITS)]

    def score(unit):
        n, h = units[unit]
        key_rows, queries, _, _ = columns[n]
        rows = slice(h * UNIT_WIDTH, (h + 1) * UNIT_WIDTH)
        scores_ref[unit % ring] = matmul(key_rows[:, rows], queries[rows])

    def weigh(unit):
        for low in range(0, total, 128):
            scores = scores_ref[unit % ring, :, low : low + 128]
            weights = jnp.exp(scores - top_rows(scores))
            scale = 1.0 / sum_rows(weights)
            weights_ref[unit % ring, :, low : low + 128] = (weights * scale).astype(BF16)

    def attend(unit):
        n, h = units[unit]
        _, _, value_rows, gates = columns[n]
        rows = slice(h * UNIT_WIDTH, (h + 1) * UNIT_WIDTH)
        attended = matmul(value_rows[rows], weights_ref[unit % ring]) * gates[rows]
        turned_ref[n, rows, :] = attended.astype(BF16)

    project(0)
    for step in range(len(units) + 2):
        if step < len(units):
            score(step)
            n, h = units[step]
            if h == ATTENTION_UNITS // 2 and n + 1 < residues:
                project(n + 1)
        if 1 <= step <= len(units):
            weigh(step - 1)
        if step >= 2:
            attend(step - 2)


def attention(normed, key_matrix, other_matrices):
    blocks = len(normed)
    residues, seqs, depth = normed[0].shape
    total = blocks * seqs
    inner = ATTENTION_UNITS * UNIT_WIDTH
    step = 4
    return pl.pallas_call(
        attention_kernel,
        grid=(residues // step,),
        in_specs=[
            pl.BlockSpec((depth, inner), lambda n: (0, 0)),
            pl.BlockSpec((3 * inner, depth), lambda n: (0, 0)),
        ]
        + [pl.BlockSpec((step, seqs, depth), lambda n: (n, 0, 0))] * blocks,
        out_specs=pl.BlockSpec((step, inner, total), lambda n: (n, 0, 0)),
        out_shape=jax.ShapeDtypeStruct((residues, inner, total), BF16),
        scratch_shapes=[
            pltpu.VMEM((4, total, total), F32),
            pltpu.VMEM((4, total, total), BF16),
        ],
        compiler_params=params(12 + (total // 128) ** 2, "arbitrary"),
        cost_estimate=cost(10),
        name="attention",
    )(key_matrix, other_matrices, *normed)


def turn_kernel(turned_ref, *gated_refs):
    seqs = gated_refs[0].shape[1]
    for n in range(turned_ref.shape[0]):
        back = turned_ref[n].T
        for block, gated_ref in enumerate(gated_refs):
            gated_ref[n] = back[block * seqs : (block + 1) * seqs]


def turn_back(turned, blocks):
    residues, inner, total = turned.shape
    seqs = total // blocks
    return pl.pallas_call(
        turn_kernel,
        grid=(residues // 2,),
        in_specs=[pl.BlockSpec((2, inner, total), lambda n: (n, 0, 0))],
        out_specs=[pl.BlockSpec((2, seqs, inner), lambda n: (n, 0, 0))] * blocks,
        out_shape=[pltpu.HBM((residues, seqs, inner), BF16)] * blocks,
        compiler_params=params(12, "arbitrary"),
        cost_estimate=cost(2),
        name="turn_back",
    )(turned)


def alignment_kernel(sources_ref, turned_ref, final_ref, entry_ref, *rest):
    *refs, left_ref, right_ref, rows_ref = rest
    blocks = len(refs) // 3
    high_refs, low_refs, spread_refs = refs[:blocks], refs[blocks : 2 * blocks], refs[2 * blocks :]
    residues, seqs, depth = high_refs[0].shape
    total = blocks * seqs
    features = TENSOR_FEATURES
    step = pl.program_id(0)
    for n in range(residues):
        column = jnp.concatenate([ref[n] for ref in high_refs], axis=0).astype(F32)
        column = column + jnp.concatenate(
            [ref[n * seqs : (n + 1) * seqs, :] for ref in low_refs], axis=0
        ).astype(F32)
        spreads = []
        for ref in spread_refs:
            kept = ref[:, :seqs].astype(F32)
            row = lax.broadcasted_iota(jnp.int32, kept.shape, 0)
            chosen = lax.rem(row, 8) == step * residues + n
            spreads.append(jnp.sum(jnp.where(chosen, kept, 0.0), axis=0, keepdims=True))
        spread = jnp.concatenate(spreads, axis=1)
        updated = column.T * spread + matmul(final_ref[...], turned_ref[n])
        projected = matmul(entry_ref[...], normalise_rows(updated))
        me = sources_ref[0]
        tiles = [projected[:, low : low + 128] for low in range(0, total, 128)]
        odd = lax.rem(me, 2) == 1
        tiles = [jnp.where(odd, pltpu.roll(tile, seqs, 1), tile) for tile in tiles]
        width = 1
        while width < len(tiles):
            crossed = lax.rem(lax.div(me, 2 * width), 2) == 1
            tiles = [
                jnp.where(crossed, tiles[t ^ width], tiles[t]) for t in range(len(tiles))
            ]
            width *= 2
        first = pl.multiple_of((step * residues + n) * features, features)
        for t, tile in enumerate(tiles):
            right_ref[n, :, t * 128 : (t + 1) * 128] = tile[features:].astype(BF16)
            rows_ref[t, pl.ds(first, features), :] = tile[:features]

    @pl.when(step == pl.num_programs(0) - 1)
    def _():
        count = rows_ref.shape[1] // features
        together = max(1, 16 // count)
        for c in range(0, features, together):
            pieces = []
            for e in range(together):
                chosen = pl.ds(c + e, count, stride=features)
                tiles = [rows_ref[tile, chosen, :] for tile in range(total // 128)]
                pieces.append(jnp.concatenate(tiles, axis=1))
            piece = jnp.concatenate(pieces, axis=0).astype(BF16)
            left_ref[c * count : (c + together) * count, :] = piece


def alignment(sources, high, low, turned, final_matrix, entry_matrices):
    blocks = len(high)
    residues, seqs, depth = high[0].shape
    total = blocks * seqs
    features = TENSOR_FEATURES
    step = 4
    height = residues * seqs + 16
    return pl.pallas_call(
        alignment_kernel,
        grid=(residues // step,),
        in_specs=[
            pl.BlockSpec(memory_space=pltpu.SMEM),
            pl.BlockSpec((step, depth, total), lambda n: (n, 0, 0)),
            pl.BlockSpec(final_matrix.shape, lambda n: (0, 0)),
            pl.BlockSpec(entry_matrices.shape, lambda n: (0, 0)),
        ]
        + [pl.BlockSpec((step, seqs, depth), lambda n: (n, 0, 0))] * blocks
        + [pl.BlockSpec((step * seqs, depth), lambda n: (n, 0))] * blocks
        + [pl.BlockSpec((16, depth), lambda n: (height // 16 - 1, 0))] * blocks,
        out_specs=[
            pl.BlockSpec((features * residues, total), lambda n: (0, 0)),
            pl.BlockSpec((step, features, total), lambda n: (n, 0, 0)),
        ],
        out_shape=[
            jax.ShapeDtypeStruct((features * residues, total), BF16),
            jax.ShapeDtypeStruct((residues, features, total), BF16),
        ],
        scratch_shapes=[pltpu.VMEM((total // 128, residues * features, 128), F32)],
        compiler_params=params(16, "arbitrary"),
        cost_estimate=cost(4),
        name="alignment",
    )(sources, turned, final_matrix, entry_matrices, *high, *low, *low)


def pair_kernel(
    left_slots_ref,
    right_firsts_ref,
    *rest,
    slots,
):
    weights_ref, entry_ref, switch_ref, couplings_hbm, mid_hbm, gate_hbm, sides_hbm = rest[-16:-9]
    outer_ref, spread_ref, sum_ref, rows_ref, couplings_ref = rest[-9:-4]
    mid_ref, gate_ref, sides_ref, copied = rest[-4:]
    left_refs, right_refs = rest[: 2 * slots], rest[2 * slots : -16]
    fetched = pltpu.make_async_copy(couplings_hbm, couplings_ref, copied.at[0])
    fetched.start()
    copies = []

    def send(source, target):
        copies.append(pltpu.make_async_copy(source, target, copied.at[len(copies) + 1]))
        copies[-1].start()

    features = TENSOR_FEATURES
    piece_rows, total = left_refs[0].shape
    residues = piece_rows // features
    rows = 2 * slots * residues
    share = right_refs[0].shape[0]
    columns = len(right_refs) * share
    groups = columns // GROUP
    wide = share * features
    together = spread_ref.shape[1] // 64

    for half in range(2):
        halves = left_refs[half * slots : (half + 1) * slots]
        piece = jnp.concatenate([ref[...] for ref in halves], axis=0)
        target = slice(half * slots * piece_rows, (half + 1) * slots * piece_rows)
        for p, right_ref in enumerate(right_refs):
            right = right_ref[...].reshape(wide, total)
            outer_ref[target, p * wide : (p + 1) * wide] = matmul_nt(piece, right) * (1.0 / total)

    spread_ref[...] = jnp.zeros_like(spread_ref)
    front = lax.broadcasted_iota(jnp.int32, (rows, 128), 1) < 64

    def channel_step(p, carry):
        slot = lax.rem(p, 2)
        for e in range(together):
            source = pl.multiple_of((p * together + e) * features, features)
            piece = weights_ref[pl.ds(source, features), :]
            for place in range(2):
                low = e * 64 + place * features
                spread_ref[slot, low : low + features, place * C_Z : (place + 1) * C_Z] = piece
        pieces = []
        for g in range(groups):
            parts = []
            for e in range(together):
                channel = []
                for slot_number in range(2 * slots):
                    first = slot_number * piece_rows + (p * together + e) * residues
                    source = pl.ds(pl.multiple_of(first, residues), residues)
                    channel.append(outer_ref[source, g * 128 : (g + 1) * 128])
                parts.append(jnp.concatenate(channel, axis=0).astype(BF16))
            lows, highs = [], []
            for e in range(0, together, 2):
                lows.append(jnp.where(front, parts[e], pltpu.roll(parts[e + 1], 64, 1)))
                highs.append(jnp.where(front, pltpu.roll(parts[e], 64, 1), parts[e + 1]))
            pieces.append(jnp.concatenate(lows, axis=1))
            pieces.append(jnp.concatenate(highs, axis=1))
        update = matmul(jnp.concatenate(pieces, axis=0), spread_ref[slot])

        @pl.when(p == 0)
        def _():
            sum_ref[...] = update

        @pl.when(p > 0)
        def _():
            sum_ref[...] += update

        return carry

    lax.fori_loop(0, features // together, channel_step, 0)

    left_firsts = [left_slots_ref[j] * residues for j in range(2 * slots)]
    right_firsts = [right_firsts_ref[p] for p in range(len(right_refs))]
    fetched.wait()
    for g in range(groups):
        normed, places = [], []
        for place in range(GROUP):
            p, n = divmod(g * GROUP + place, share)
            b = right_firsts[p] + n
            places.append(b)
            lanes = slice(place % 2 * C_Z, (place % 2 + 1) * C_Z)
            start = (2 * g + place // 2) * rows
            pieces = []
            for first in left_firsts:
                source = pl.ds(pl.multiple_of(start + first, residues), residues)
                pieces.append(sum_ref[source, lanes])
            mid = jnp.concatenate(pieces, axis=0)
            mid = mid + couplings_ref[pl.ds(b, rows, stride=columns), :]
            mid_ref[g * GROUP + place] = mid
            centred = mid - jnp.mean(mid, axis=1, keepdims=True)
            variance = jnp.mean(centred * centred, axis=1, keepdims=True)
            normed.append((centred * lax.rsqrt(variance + EPS)).astype(BF16))
        gates = sigmoid(matmul(jnp.concatenate(normed, axis=0), switch_ref[...]))
        blank = jnp.zeros_like(normed[0])
        for place in range(0, GROUP, 2):
            twice = []
            for e in range(2):
                part = gates[(place + e) * rows : (place + e + 1) * rows]
                gate_ref[g * GROUP + place + e] = part
                twice.append(jnp.concatenate([normed[place + e], blank], axis=1))
                twice.append(jnp.concatenate([blank, normed[place + e]], axis=1))
            sides = matmul_nt(entry_ref[...], jnp.concatenate(twice, axis=0))
            sides = sigmoid(sides[C_TRI:]) * sides[:C_TRI]
            for e in range(2):
                first = pl.multiple_of(places[place + e] * C_TRI, C_TRI)
                rows_ref[pl.ds(first, C_TRI), :] = sides[:, e * 2 * rows : (e + 1) * 2 * rows]

        if (g + 1) * GROUP % share == 0:
            p = (g + 1) * GROUP // share - 1
            source, target = pl.ds(p * share, share), pl.ds(right_firsts[p], share)
            send(mid_ref.at[source], mid_hbm.at[target])
            send(gate_ref.at[source], gate_hbm.at[target])

    cut = C_TRI // 4
    for part in range(4):

        def turn_step(c, carry):
            sides_ref[c] = rows_ref[pl.ds(c, columns, stride=C_TRI), :].astype(BF16)
            return carry

        lax.fori_loop(part * cut, (part + 1) * cut, turn_step, 0, unroll=8)
        chosen = pl.ds(part * cut, cut)
        send(sides_ref.at[chosen], sides_hbm.at[chosen])
    for copy in copies:
        copy.wait()


def pair_update(left_slots, right_firsts, left, rights, weights, couplings, entry, switch):
    rows, columns, depth = couplings.shape
    whole = jax.ShapeDtypeStruct((columns, rows, depth), F32)
    sides = jax.ShapeDtypeStruct((C_TRI, columns, 2 * rows), BF16)
    smem = pl.BlockSpec(memory_space=pltpu.SMEM)
    vmem = pl.BlockSpec(memory_space=pltpu.VMEM)
    anywhere = pl.BlockSpec(memory_space=pl.ANY)
    return pl.pallas_call(
        functools.partial(pair_kernel, slots=len(left) // 2),
        in_specs=[smem] * 2 + [vmem] * (3 + len(left) + len(rights)) + [anywhere],
        out_specs=[anywhere] * 3,
        out_shape=[pltpu.HBM(whole.shape, F32)] * 2 + [pltpu.HBM(sides.shape, BF16)],
        scratch_shapes=[
            pltpu.VMEM((rows * TENSOR_FEATURES, columns * TENSOR_FEATURES), F32),
            pltpu.VMEM((2, 8 * 64, 2 * depth), BF16),
            pltpu.VMEM((columns // 2 * rows, 2 * depth), F32),
            pltpu.VMEM((columns * C_TRI, 2 * rows), F32),
            pltpu.VMEM((rows * columns, depth), F32),
            pltpu.VMEM(whole.shape, F32),
            pltpu.VMEM(whole.shape, F32),
            pltpu.VMEM(sides.shape, BF16),
            pltpu.SemaphoreType.DMA((2 * len(rights) + 5,)),
        ],
        compiler_params=params(28),
        cost_estimate=cost(12),
        name="pair_update",
    )(
        left_slots,
        right_firsts,
        *left,
        *rights,
        weights,
        entry,
        switch,
        couplings.reshape(rows * columns, depth),
    )


def product_kernel(sides_ref, out_ref, *, grid_rows, grid_columns):
    channels, part, lanes = sides_ref.shape[1:]
    half = lanes // 2
    lane = lax.broadcasted_iota(jnp.int32, (grid_columns * part, lanes), 1)
    front = lane < half
    cut = front[: part // 2]
    for channel in range(channels):
        lefts, rights = [], []
        for r in range(0, grid_rows, 2):
            even, odd = [
                jnp.concatenate(
                    [sides_ref[(r + e) * grid_columns + c, channel] for c in range(grid_columns)],
                    axis=0,
                )
                for e in range(2)
            ]
            lefts.append(jnp.where(front, even, pltpu.roll(odd, half, 1)))
            rights.append(jnp.where(front, pltpu.roll(even, half, 1), odd))
        product = matmul_nt(jnp.concatenate(rights, axis=1), jnp.concatenate(lefts, axis=1))
        product = product.astype(BF16)
        for c in range(grid_columns):
            for r in range(0, grid_rows, 2):
                block = product[c * part : (c + 1) * part, r * half : (r + 2) * half]
                top, bottom = block[: part // 2], block[part // 2 :]
                even = jnp.where(cut, top, pltpu.roll(bottom, half, 1))
                out_ref[r * grid_columns + c, channel] = even
                odd = jnp.where(cut, pltpu.roll(top, half, 1), bottom)
                out_ref[(r + 1) * grid_columns + c, channel] = odd


def triangle_product(sides, grid_rows, grid_columns):
    devices, channels, part, lanes = sides.shape
    step = 2 if channels % 2 == 0 else 1
    return pl.pallas_call(
        functools.partial(product_kernel, grid_rows=grid_rows, grid_columns=grid_columns),
        grid=(channels // step,),
        in_specs=[pl.BlockSpec((devices, step, part, lanes), lambda c: (0, c, 0, 0))],
        out_specs=pl.BlockSpec((devices, step, part // 2, lanes), lambda c: (0, c, 0, 0)),
        out_shape=pltpu.HBM((devices, channels, part // 2, lanes), BF16),
        compiler_params=params(8, "arbitrary"),
        cost_estimate=cost(3),
        name="triangle_product",
    )(sides)


def output_kernel(
    product_ref, final_ref, mid_hbm, gate_hbm, out_hbm, wide_ref, mid_ref, gate_ref, out_ref, *copied
):
    channels, part, lanes = product_ref.shape
    columns, rows, depth = mid_ref.shape
    own = 8
    fetched, sent = copied
    fetches, sends = [], []
    for first in range(0, columns, own):
        chosen = pl.ds(first, own)
        for source, target in ((mid_hbm, mid_ref), (gate_hbm, gate_ref)):
            fetches.append(
                pltpu.make_async_copy(
                    source.at[chosen], target.at[chosen], fetched.at[len(fetches)]
                )
            )
            fetches[-1].start()
    wide_ref[...] = product_ref[...].astype(F32).reshape(channels * part, lanes)
    for group in range(part // own):
        updates = []
        for j in range(own):
            product = wide_ref[pl.ds(group * own + j, channels, stride=part), :]
            updates.append(matmul(normalise_rows(product).T, final_ref[...]))
        for half in range(2):
            cut = half * (part // own) + group
            fetches[2 * cut].wait()
            fetches[2 * cut + 1].wait()
            out_rows = out_ref.at[cut].reshape(rows * own, depth)
            for j in range(own):
                b = cut * own + j
                piece = updates[j][half * rows : (half + 1) * rows]
                out_rows[pl.ds(j, rows, stride=own), :] = mid_ref[b] + gate_ref[b] * piece
            sends.append(
                pltpu.make_async_copy(
                    out_ref.at[cut], out_hbm.at[:, pl.ds(cut * own, own)], sent.at[len(sends)]
                )
            )
            sends[-1].start()
    for send in sends:
        send.wait()


def pair_result(product, mid, gate, final_matrix):
    channels, part, lanes = product.shape
    columns, rows, depth = mid.shape
    vmem, hbm = pl.BlockSpec(memory_space=pltpu.VMEM), pl.BlockSpec(memory_space=pltpu.HBM)
    return pl.pallas_call(
        output_kernel,
        in_specs=[vmem, vmem, hbm, hbm],
        out_specs=hbm,
        out_shape=pltpu.HBM((rows, columns, depth), F32),
        scratch_shapes=[
            pltpu.VMEM((channels * part, lanes), F32),
            pltpu.VMEM(mid.shape, F32),
            pltpu.VMEM(mid.shape, F32),
            pltpu.VMEM((columns // 8, rows, 8, depth), F32),
            pltpu.SemaphoreType.DMA((columns // 4,)),
            pltpu.SemaphoreType.DMA((columns // 8,)),
        ],
        compiler_params=params(16),
        cost_estimate=cost(3),
        name="pair_result",
    )(
        product,
        final_matrix,
        pltpu.with_memory_space_constraint(mid, pltpu.HBM),
        pltpu.with_memory_space_constraint(gate, pltpu.HBM),
    )


def swap_cores(block):
    count = lax.axis_size("col")
    return lax.ppermute(block, "col", [(c, c ^ 1) for c in range(count)])


def gather_turned(block, later):
    rows, columns = lax.axis_size("row"), lax.axis_size("col")
    arrived = []
    for shift in range(rows):
        moves = []
        for r in range(rows):
            for q in range(rows):
                for side in range(2):
                    source = r * columns + 2 * q + side
                    moves.append((source, q * columns + 2 * ((r + shift) % rows) + side))
        source = block if shift < 2 else later
        arrived.append(lax.ppermute(source, ("row", "col"), moves))
    return arrived


def both_cores(own):
    rows = lax.axis_size("row")
    core = lax.rem(lax.axis_index("col"), 2)
    other = [swap_cores(piece) for piece in own]
    residues = own[0].shape[0] // TENSOR_FEATURES
    if residues % 8 == 0:
        return own + other
    order = left_order(rows)
    own, other = [jnp.take(jnp.stack(side), order, axis=0) for side in (own, other)]
    joined = 8 // residues
    ordered = []
    for side in (jnp.where(core == 0, own, other), jnp.where(core == 0, other, own)):
        side = side.reshape(rows // joined, joined, TENSOR_FEATURES, residues, -1)
        side = jnp.transpose(side, (0, 2, 1, 3, 4))
        ordered.extend(side.reshape(rows // joined, joined * own.shape[1], -1))
    return ordered


def left_order(rows):
    me = lax.axis_index("col") // 2
    return lax.rem(me - jnp.arange(rows, dtype=jnp.int32) + rows, rows)


def left_groups(rows, residues):
    if residues % 8:
        return jnp.arange(2 * rows * residues // 8, dtype=jnp.int32)
    core = lax.rem(lax.axis_index("col"), 2)
    order = left_order(rows)
    return jnp.concatenate([order + core * rows, order + (1 - core) * rows])


def exchange_rows(pieces):
    arrived = [pieces[0]]
    for shift in range(1, len(pieces)):
        moves = [(r, r ^ shift) for r in range(len(pieces))]
        arrived.append(lax.ppermute(pieces[shift], "row", moves))
    return arrived


def paired_entries(matrices):
    turned = matrices.reshape(C_Z, 2, 2, C_TRI)
    return jnp.transpose(turned, (2, 3, 1, 0)).reshape(2 * C_TRI, 2 * C_Z)


def body(
    homolog_tensor,
    couplings,
    attention_probe_matrix,
    attention_extra_matrices,
    attention_final_matrix,
    tensor_entry_matrices,
    tensor_final_matrix,
    incoming_entry_matrices,
    incoming_switch_matrix,
    incoming_final_matrix,
):
    inner = ATTENTION_UNITS * UNIT_WIDTH
    row_count = lax.axis_size("row")
    seqs, residues, depth = homolog_tensor.shape
    own_residues = residues // row_count
    sources = lax.axis_index("row") ^ jnp.arange(row_count, dtype=jnp.int32)
    high = exchange_rows(standardise_high(sources, homolog_tensor))
    others = jnp.concatenate(
        [attention_probe_matrix.T, attention_extra_matrices[:, inner:].T], axis=0
    )
    early = (
        attention_extra_matrices[:, :inner],
        others,
        attention_final_matrix.T,
        tensor_entry_matrices.T,
        paired_entries(incoming_entry_matrices),
        sources * own_residues,
        left_groups(row_count, own_residues),
    )
    after, early = lax.optimization_barrier((sources, early))
    low = standardise_low(after, homolog_tensor)
    high, _, early = lax.optimization_barrier((high, low, early))
    key_matrix, others, final_turned, tensor_turned, entries, firsts, slots = early
    low = exchange_rows(low)
    turned = attention(high, key_matrix, others)
    gated = turn_back(turned, row_count)
    low, gated = lax.optimization_barrier((low, gated))
    left_piece, right_piece = alignment(
        sources, high, low, turned, final_turned, tensor_turned
    )

    rights = exchange_rows([right_piece] * row_count)
    later, rights[1] = lax.optimization_barrier((left_piece, rights[1]))
    own = gather_turned(left_piece, later)
    own[-1], rights = lax.optimization_barrier((own[-1], rights))
    mid, gate, sides = pair_update(
        slots,
        firsts,
        both_cores(own),
        rights,
        tensor_final_matrix,
        couplings,
        entries,
        incoming_switch_matrix,
    )
    gated, sides = lax.optimization_barrier((gated, sides))
    gated = exchange_rows(gated)

    everywhere = ("row", "col")
    column_count = lax.axis_size("col")
    devices = row_count * column_count
    sides = sides.reshape(devices, C_TRI // devices, *sides.shape[1:])
    sides = lax.all_to_all(sides, everywhere, split_axis=0, concat_axis=0)
    gated, sides = lax.optimization_barrier((gated, sides))
    product = triangle_product(sides, row_count, column_count)
    product = lax.all_to_all(product, everywhere, split_axis=0, concat_axis=0)

    gated = jnp.take(jnp.stack(gated), sources, axis=0)
    gated = jnp.transpose(gated.reshape(residues, seqs, inner), (1, 0, 2))
    change = jnp.dot(
        gated.reshape(-1, inner), attention_final_matrix, preferred_element_type=F32
    )
    refreshed_homologs = homolog_tensor + change.reshape(homolog_tensor.shape)
    product = product.reshape(C_TRI, *product.shape[2:])
    pair_output = pair_result(product, mid, gate, incoming_final_matrix)
    return (refreshed_homologs, pair_output)


def solution(mesh):
    in_specs = (
        P("row", "col", None),
        P("row", "col", None),
        P(),
        P(),
        P(),
        P(),
        P(),
        P(),
        P(),
        P(),
    )
    out_specs = (P("row", "col", None), P("row", "col", None))
    return jax.shard_map(body, mesh=mesh, in_specs=in_specs, out_specs=out_specs, check_vma=False)
```

```python
import functools

import jax
import jax.numpy as jnp
from jax import lax
from jax.experimental import pallas as pl
from jax.experimental.pallas import tpu as pltpu
from jax.sharding import PartitionSpec as P

FEATURE_DEPTH = 256
C_Z = 128
TENSOR_FEATURES = 32
C_TRI = 128
ATTENTION_UNITS = 8
UNIT_WIDTH = 32
EPS = 1e-05
GROUP = 4
F32 = jnp.float32
BF16 = jnp.bfloat16
NT = (((1,), (1,)), ((), ()))


def matmul(left, right):
    return jnp.dot(left, right, preferred_element_type=F32)


def matmul_nt(left, right):
    return lax.dot_general(left, right, NT, preferred_element_type=F32)


def sigmoid(values):
    return 0.5 * jnp.tanh(0.5 * values) + 0.5


def cost(microseconds):
    return pl.CostEstimate(
        flops=int(microseconds * 1e9), bytes_accessed=int(microseconds * 1e6), transcendentals=0
    )


def params(megabytes, *semantics):
    return pltpu.CompilerParams(
        dimension_semantics=semantics or None, vmem_limit_bytes=megabytes * 1024 * 1024
    )


def fold(values, combine):
    while values.shape[0] > 8:
        half = values.shape[0] // 2
        values = combine(values[:half], values[half:])
    return values


def top_rows(values):
    return jnp.max(fold(values, jnp.maximum), axis=0, keepdims=True)


def sum_rows(values):
    return jnp.sum(fold(values, jnp.add), axis=0, keepdims=True)


def normalise_rows(values):
    count = values.shape[0]
    centred = values - sum_rows(values) * (1.0 / count)
    variance = sum_rows(centred * centred) * (1.0 / count)
    return (centred * lax.rsqrt(variance + EPS)).astype(BF16)


def standardised_columns(first_rows, second_rows, first, count, residues):
    seqs = first_rows.shape[0] // residues
    columns = []
    for n in range(count):
        rows = pl.ds(first + n, seqs, stride=residues)
        columns.append(jnp.concatenate([first_rows[rows, :], second_rows[rows, :]], axis=1))
    column = jnp.concatenate(columns, axis=0)
    centred = column - jnp.mean(column, axis=1, keepdims=True)
    variance = jnp.mean(centred * centred, axis=1, keepdims=True) + EPS
    scale = lax.rsqrt(variance)
    return centred * scale, variance * scale


def high_kernel(sources_ref, block_hbm, *rest):
    *pieces_hbm, first_ref, second_ref, high_ref, fetched, sent = rest
    seqs, residues, lanes = first_ref.shape
    own = residues // len(pieces_hbm)
    step = 16
    fetches, sends = [], []
    for s in range(0, seqs, step):
        chosen = pl.ds(s, step)
        for half, ref in enumerate((first_ref, second_ref)):
            source = block_hbm.at[chosen, :, pl.ds(half * lanes, lanes)]
            fetches.append(
                pltpu.make_async_copy(source, ref.at[chosen], fetched.at[len(fetches)])
            )
            fetches[-1].start()
    for part in range(seqs // step):
        chosen = pl.ds(part * step, step)
        fetches[2 * part].wait()
        fetches[2 * part + 1].wait()
        first_rows = first_ref.at[chosen].reshape(step * residues, lanes)
        second_rows = second_ref.at[chosen].reshape(step * residues, lanes)
        for n in range(0, residues, 8):
            normed, _ = standardised_columns(first_rows, second_rows, n, 8, residues)
            high_ref[part, n : n + 8] = normed.astype(BF16).reshape(8, step, 2 * lanes)
        for p, piece_hbm in enumerate(pieces_hbm):
            source = high_ref.at[part, pl.ds(sources_ref[p] * own, own)]
            sends.append(
                pltpu.make_async_copy(source, piece_hbm.at[:, chosen], sent.at[len(sends)])
            )
            sends[-1].start()
    for send in sends:
        send.wait()


def standardise_high(sources, block):
    seqs, residues, depth = block.shape
    half = depth // 2
    count = sources.shape[0]
    hbm = pl.BlockSpec(memory_space=pltpu.HBM)
    return pl.pallas_call(
        high_kernel,
        in_specs=[pl.BlockSpec(memory_space=pltpu.SMEM), hbm],
        out_specs=[hbm] * count,
        out_shape=[pltpu.HBM((residues // count, seqs, depth), BF16)] * count,
        scratch_shapes=[
            pltpu.VMEM((seqs, residues, half), F32),
            pltpu.VMEM((seqs, residues, half), F32),
            pltpu.VMEM((seqs // 16, residues, 16, depth), BF16),
            pltpu.SemaphoreType.DMA((seqs // 8,)),
            pltpu.SemaphoreType.DMA((seqs // 16 * count,)),
        ],
        compiler_params=params(10),
        cost_estimate=cost(3),
        name="standardise_high",
    )(sources, pltpu.with_memory_space_constraint(block, pltpu.HBM))


def low_kernel(sources_ref, first_ref, second_ref, *rest):
    *pieces_hbm, low_ref, sent = rest
    seqs, residues, lanes = first_ref.shape
    count = len(pieces_hbm)
    own = (low_ref.shape[1] - 16) // seqs
    step = pl.program_id(0)
    first_rows = first_ref.reshape(seqs * residues, lanes)
    second_rows = second_ref.reshape(seqs * residues, lanes)
    shift = lax.rem(sources_ref[step] * own, residues) if own < residues else 0
    lane = lax.broadcasted_iota(jnp.int32, (seqs, 128), 1)
    spreads = jnp.zeros((seqs, 128), F32)
    for n in range(own):
        normed, spread = standardised_columns(first_rows, second_rows, shift + n, 1, residues)
        left = (normed - normed.astype(BF16).astype(F32)).astype(BF16)
        low_ref[step, n * seqs : (n + 1) * seqs, :] = left
        spreads = jnp.where(lane == n, spread, spreads)
    spreads = spreads.T[:8, :]
    coarse = spreads.astype(BF16).astype(F32)
    kept = jnp.concatenate([coarse, spreads - coarse], axis=0)
    kept = jnp.concatenate([kept, jnp.zeros((16, 2 * lanes - seqs), F32)], axis=1)
    low_ref[step, own * seqs :, :] = kept.astype(BF16)
    copies = [
        pltpu.make_async_copy(low_ref.at[p], piece_hbm, sent.at[p])
        for p, piece_hbm in enumerate(pieces_hbm)
    ]
    for p in range(count):

        @pl.when(step == p)
        def _(p=p):
            copies[p].start()

    @pl.when(step == count - 1)
    def _():
        for copy in copies:
            copy.wait()


def standardise_low(sources, block):
    seqs, residues, depth = block.shape
    half = depth // 2
    count = sources.shape[0]
    own = residues // count
    height = own * seqs + 16
    together = 8 // own
    hbm = pl.BlockSpec(memory_space=pltpu.HBM)
    return pl.pallas_call(
        low_kernel,
        grid_spec=pltpu.PrefetchScalarGridSpec(
            num_scalar_prefetch=1,
            grid=(count,),
            in_specs=[
                pl.BlockSpec((seqs, 8, half), lambda p, sources: (0, sources[p] // together, 0)),
                pl.BlockSpec((seqs, 8, half), lambda p, sources: (0, sources[p] // together, 1)),
            ],
            out_specs=[hbm] * count,
            scratch_shapes=[
                pltpu.VMEM((count, height, depth), BF16),
                pltpu.SemaphoreType.DMA((count,)),
            ],
        ),
        out_shape=[pltpu.HBM((height, depth), BF16)] * count,
        compiler_params=params(10, "arbitrary"),
        cost_estimate=cost(4),
        name="standardise_low",
    )(sources, block, block)


def attention_kernel(key_ref, others_ref, *rest):
    *normed_refs, turned_ref, scores_ref, weights_ref = rest
    blocks = len(normed_refs)
    residues, seqs, _ = normed_refs[0].shape
    total = blocks * seqs
    inner = ATTENTION_UNITS * UNIT_WIDTH
    ring = scores_ref.shape[0]
    columns = []

    def project(n):
        column = jnp.concatenate([ref[n] for ref in normed_refs], axis=0)
        key_rows = matmul(column, key_ref[...]).astype(BF16)
        projected = matmul_nt(others_ref[...], column)
        queries = (projected[:inner] * UNIT_WIDTH ** (-0.5)).astype(BF16)
        value_rows = projected[inner : 2 * inner].astype(BF16)
        gates = sigmoid(projected[2 * inner :])
        columns.append((key_rows, queries, value_rows, gates))
    units = [(n, h) for n in range(residues) for h in range(ATTENTION_UNITS)]

    def score(unit):
        n, h = units[unit]
        key_rows, queries, _, _ = columns[n]
        rows = slice(h * UNIT_WIDTH, (h + 1) * UNIT_WIDTH)
        scores_ref[unit % ring] = matmul(key_rows[:, rows], queries[rows])

    def weigh(unit):
        for low in range(0, total, 128):
            scores = scores_ref[unit % ring, :, low : low + 128]
            weights = jnp.exp(scores - top_rows(scores))
            scale = 1.0 / sum_rows(weights)
            weights_ref[unit % ring, :, low : low + 128] = (weights * scale).astype(BF16)

    def attend(unit):
        n, h = units[unit]
        _, _, value_rows, gates = columns[n]
        rows = slice(h * UNIT_WIDTH, (h + 1) * UNIT_WIDTH)
        attended = matmul(value_rows[rows], weights_ref[unit % ring]) * gates[rows]
        turned_ref[n, rows, :] = attended.astype(BF16)

    project(0)
    for step in range(len(units) + 2):
        if step < len(units):
            score(step)
            n, h = units[step]
            if h == ATTENTION_UNITS // 2 and n + 1 < residues:
                project(n + 1)
        if 1 <= step <= len(units):
            weigh(step - 1)
        if step >= 2:
            attend(step - 2)


def attention(normed, key_matrix, other_matrices):
    blocks = len(normed)
    residues, seqs, depth = normed[0].shape
    total = blocks * seqs
    inner = ATTENTION_UNITS * UNIT_WIDTH
    step = 4
    return pl.pallas_call(
        attention_kernel,
        grid=(residues // step,),
        in_specs=[
            pl.BlockSpec((depth, inner), lambda n: (0, 0)),
            pl.BlockSpec((3 * inner, depth), lambda n: (0, 0)),
        ]
        + [pl.BlockSpec((step, seqs, depth), lambda n: (n, 0, 0))] * blocks,
        out_specs=pl.BlockSpec((step, inner, total), lambda n: (n, 0, 0)),
        out_shape=jax.ShapeDtypeStruct((residues, inner, total), BF16),
        scratch_shapes=[
            pltpu.VMEM((4, total, total), F32),
            pltpu.VMEM((4, total, total), BF16),
        ],
        compiler_params=params(12 + (total // 128) ** 2, "arbitrary"),
        cost_estimate=cost(10),
        name="attention",
    )(key_matrix, other_matrices, *normed)


def turn_kernel(turned_ref, *gated_refs):
    seqs = gated_refs[0].shape[1]
    for n in range(turned_ref.shape[0]):
        back = turned_ref[n].T
        for block, gated_ref in enumerate(gated_refs):
            gated_ref[n] = back[block * seqs : (block + 1) * seqs]


def turn_back(turned, blocks):
    residues, inner, total = turned.shape
    seqs = total // blocks
    return pl.pallas_call(
        turn_kernel,
        grid=(residues // 2,),
        in_specs=[pl.BlockSpec((2, inner, total), lambda n: (n, 0, 0))],
        out_specs=[pl.BlockSpec((2, seqs, inner), lambda n: (n, 0, 0))] * blocks,
        out_shape=[pltpu.HBM((residues, seqs, inner), BF16)] * blocks,
        compiler_params=params(12, "arbitrary"),
        cost_estimate=cost(2),
        name="turn_back",
    )(turned)


def alignment_kernel(sources_ref, turned_ref, final_ref, entry_ref, *rest):
    *refs, left_ref, right_ref, rows_ref = rest
    blocks = len(refs) // 3
    high_refs, low_refs, spread_refs = refs[:blocks], refs[blocks : 2 * blocks], refs[2 * blocks :]
    residues, seqs, depth = high_refs[0].shape
    total = blocks * seqs
    features = TENSOR_FEATURES
    step = pl.program_id(0)
    for n in range(residues):
        column = jnp.concatenate([ref[n] for ref in high_refs], axis=0).astype(F32)
        column = column + jnp.concatenate(
            [ref[n * seqs : (n + 1) * seqs, :] for ref in low_refs], axis=0
        ).astype(F32)
        spreads = []
        for ref in spread_refs:
            kept = ref[:, :seqs].astype(F32)
            row = lax.broadcasted_iota(jnp.int32, kept.shape, 0)
            chosen = lax.rem(row, 8) == step * residues + n
            spreads.append(jnp.sum(jnp.where(chosen, kept, 0.0), axis=0, keepdims=True))
        spread = jnp.concatenate(spreads, axis=1)
        updated = column.T * spread + matmul(final_ref[...], turned_ref[n])
        projected = matmul(entry_ref[...], normalise_rows(updated))
        me = sources_ref[0]
        tiles = [projected[:, low : low + 128] for low in range(0, total, 128)]
        odd = lax.rem(me, 2) == 1
        tiles = [jnp.where(odd, pltpu.roll(tile, seqs, 1), tile) for tile in tiles]
        width = 1
        while width < len(tiles):
            crossed = lax.rem(lax.div(me, 2 * width), 2) == 1
            tiles = [
                jnp.where(crossed, tiles[t ^ width], tiles[t]) for t in range(len(tiles))
            ]
            width *= 2
        first = pl.multiple_of((step * residues + n) * features, features)
        for t, tile in enumerate(tiles):
            right_ref[n, :, t * 128 : (t + 1) * 128] = tile[features:].astype(BF16)
            rows_ref[t, pl.ds(first, features), :] = tile[:features]

    @pl.when(step == pl.num_programs(0) - 1)
    def _():
        count = rows_ref.shape[1] // features
        together = max(1, 16 // count)
        for c in range(0, features, together):
            pieces = []
            for e in range(together):
                chosen = pl.ds(c + e, count, stride=features)
                tiles = [rows_ref[tile, chosen, :] for tile in range(total // 128)]
                pieces.append(jnp.concatenate(tiles, axis=1))
            piece = jnp.concatenate(pieces, axis=0).astype(BF16)
            left_ref[c * count : (c + together) * count, :] = piece


def alignment(sources, high, low, turned, final_matrix, entry_matrices):
    blocks = len(high)
    residues, seqs, depth = high[0].shape
    total = blocks * seqs
    features = TENSOR_FEATURES
    step = 4
    height = residues * seqs + 16
    return pl.pallas_call(
        alignment_kernel,
        grid=(residues // step,),
        in_specs=[
            pl.BlockSpec(memory_space=pltpu.SMEM),
            pl.BlockSpec((step, depth, total), lambda n: (n, 0, 0)),
            pl.BlockSpec(final_matrix.shape, lambda n: (0, 0)),
            pl.BlockSpec(entry_matrices.shape, lambda n: (0, 0)),
        ]
        + [pl.BlockSpec((step, seqs, depth), lambda n: (n, 0, 0))] * blocks
        + [pl.BlockSpec((step * seqs, depth), lambda n: (n, 0))] * blocks
        + [pl.BlockSpec((16, depth), lambda n: (height // 16 - 1, 0))] * blocks,
        out_specs=[
            pl.BlockSpec((features * residues, total), lambda n: (0, 0)),
            pl.BlockSpec((step, features, total), lambda n: (n, 0, 0)),
        ],
        out_shape=[
            jax.ShapeDtypeStruct((features * residues, total), BF16),
            jax.ShapeDtypeStruct((residues, features, total), BF16),
        ],
        scratch_shapes=[pltpu.VMEM((total // 128, residues * features, 128), F32)],
        compiler_params=params(16, "arbitrary"),
        cost_estimate=cost(4),
        name="alignment",
    )(sources, turned, final_matrix, entry_matrices, *high, *low, *low)


def pair_kernel(
    left_slots_ref,
    right_firsts_ref,
    *rest,
    slots,
):
    weights_ref, entry_ref, switch_ref, couplings_hbm, mid_hbm, gate_hbm, sides_hbm = rest[-16:-9]
    outer_ref, spread_ref, sum_ref, rows_ref, couplings_ref = rest[-9:-4]
    mid_ref, gate_ref, sides_ref, copied = rest[-4:]
    left_refs, right_refs = rest[: 2 * slots], rest[2 * slots : -16]
    fetched = pltpu.make_async_copy(couplings_hbm, couplings_ref, copied.at[0])
    fetched.start()
    copies = []

    def send(source, target):
        copies.append(pltpu.make_async_copy(source, target, copied.at[len(copies) + 1]))
        copies[-1].start()

    features = TENSOR_FEATURES
    piece_rows, total = left_refs[0].shape
    residues = piece_rows // features
    rows = 2 * slots * residues
    share = right_refs[0].shape[0]
    columns = len(right_refs) * share
    groups = columns // GROUP
    wide = share * features
    together = spread_ref.shape[1] // 64

    for half in range(2):
        halves = left_refs[half * slots : (half + 1) * slots]
        piece = jnp.concatenate([ref[...] for ref in halves], axis=0)
        target = slice(half * slots * piece_rows, (half + 1) * slots * piece_rows)
        for p, right_ref in enumerate(right_refs):
            right = right_ref[...].reshape(wide, total)
            outer_ref[target, p * wide : (p + 1) * wide] = matmul_nt(piece, right) * (1.0 / total)

    spread_ref[...] = jnp.zeros_like(spread_ref)
    front = lax.broadcasted_iota(jnp.int32, (rows, 128), 1) < 64

    def channel_step(p, carry):
        slot = lax.rem(p, 2)
        for e in range(together):
            source = pl.multiple_of((p * together + e) * features, features)
            piece = weights_ref[pl.ds(source, features), :]
            for place in range(2):
                low = e * 64 + place * features
                spread_ref[slot, low : low + features, place * C_Z : (place + 1) * C_Z] = piece
        pieces = []
        for g in range(groups):
            parts = []
            for e in range(together):
                channel = []
                for slot_number in range(2 * slots):
                    first = slot_number * piece_rows + (p * together + e) * residues
                    source = pl.ds(pl.multiple_of(first, residues), residues)
                    channel.append(outer_ref[source, g * 128 : (g + 1) * 128])
                parts.append(jnp.concatenate(channel, axis=0).astype(BF16))
            lows, highs = [], []
            for e in range(0, together, 2):
                lows.append(jnp.where(front, parts[e], pltpu.roll(parts[e + 1], 64, 1)))
                highs.append(jnp.where(front, pltpu.roll(parts[e], 64, 1), parts[e + 1]))
            pieces.append(jnp.concatenate(lows, axis=1))
            pieces.append(jnp.concatenate(highs, axis=1))
        update = matmul(jnp.concatenate(pieces, axis=0), spread_ref[slot])

        @pl.when(p == 0)
        def _():
            sum_ref[...] = update

        @pl.when(p > 0)
        def _():
            sum_ref[...] += update

        return carry

    lax.fori_loop(0, features // together, channel_step, 0)

    left_firsts = [left_slots_ref[j] * residues for j in range(2 * slots)]
    right_firsts = [right_firsts_ref[p] for p in range(len(right_refs))]
    fetched.wait()
    for g in range(groups):
        normed, places = [], []
        for place in range(GROUP):
            p, n = divmod(g * GROUP + place, share)
            b = right_firsts[p] + n
            places.append(b)
            lanes = slice(place % 2 * C_Z, (place % 2 + 1) * C_Z)
            start = (2 * g + place // 2) * rows
            pieces = []
            for first in left_firsts:
                source = pl.ds(pl.multiple_of(start + first, residues), residues)
                pieces.append(sum_ref[source, lanes])
            mid = jnp.concatenate(pieces, axis=0)
            mid = mid + couplings_ref[pl.ds(b, rows, stride=columns), :]
            mid_ref[g * GROUP + place] = mid
            centred = mid - jnp.mean(mid, axis=1, keepdims=True)
            variance = jnp.mean(centred * centred, axis=1, keepdims=True)
            normed.append((centred * lax.rsqrt(variance + EPS)).astype(BF16))
        gates = sigmoid(matmul(jnp.concatenate(normed, axis=0), switch_ref[...]))
        blank = jnp.zeros_like(normed[0])
        for place in range(0, GROUP, 2):
            twice = []
            for e in range(2):
                part = gates[(place + e) * rows : (place + e + 1) * rows]
                gate_ref[g * GROUP + place + e] = part
                twice.append(jnp.concatenate([normed[place + e], blank], axis=1))
                twice.append(jnp.concatenate([blank, normed[place + e]], axis=1))
            sides = matmul_nt(entry_ref[...], jnp.concatenate(twice, axis=0))
            sides = sigmoid(sides[C_TRI:]) * sides[:C_TRI]
            for e in range(2):
                first = pl.multiple_of(places[place + e] * C_TRI, C_TRI)
                rows_ref[pl.ds(first, C_TRI), :] = sides[:, e * 2 * rows : (e + 1) * 2 * rows]

        if (g + 1) * GROUP % share == 0:
            p = (g + 1) * GROUP // share - 1
            source, target = pl.ds(p * share, share), pl.ds(right_firsts[p], share)
            send(mid_ref.at[source], mid_hbm.at[target])
            send(gate_ref.at[source], gate_hbm.at[target])

    cut = C_TRI // 4
    for part in range(4):

        def turn_step(c, carry):
            sides_ref[c] = rows_ref[pl.ds(c, columns, stride=C_TRI), :].astype(BF16)
            return carry

        lax.fori_loop(part * cut, (part + 1) * cut, turn_step, 0, unroll=8)
        chosen = pl.ds(part * cut, cut)
        send(sides_ref.at[chosen], sides_hbm.at[chosen])
    for copy in copies:
        copy.wait()


def pair_update(left_slots, right_firsts, left, rights, weights, couplings, entry, switch):
    rows, columns, depth = couplings.shape
    whole = jax.ShapeDtypeStruct((columns, rows, depth), F32)
    sides = jax.ShapeDtypeStruct((C_TRI, columns, 2 * rows), BF16)
    smem = pl.BlockSpec(memory_space=pltpu.SMEM)
    vmem = pl.BlockSpec(memory_space=pltpu.VMEM)
    anywhere = pl.BlockSpec(memory_space=pl.ANY)
    return pl.pallas_call(
        functools.partial(pair_kernel, slots=len(left) // 2),
        in_specs=[smem] * 2 + [vmem] * (3 + len(left) + len(rights)) + [anywhere],
        out_specs=[anywhere] * 3,
        out_shape=[pltpu.HBM(whole.shape, F32)] * 2 + [pltpu.HBM(sides.shape, BF16)],
        scratch_shapes=[
            pltpu.VMEM((rows * TENSOR_FEATURES, columns * TENSOR_FEATURES), F32),
            pltpu.VMEM((2, 8 * 64, 2 * depth), BF16),
            pltpu.VMEM((columns // 2 * rows, 2 * depth), F32),
            pltpu.VMEM((columns * C_TRI, 2 * rows), F32),
            pltpu.VMEM((rows * columns, depth), F32),
            pltpu.VMEM(whole.shape, F32),
            pltpu.VMEM(whole.shape, F32),
            pltpu.VMEM(sides.shape, BF16),
            pltpu.SemaphoreType.DMA((2 * len(rights) + 5,)),
        ],
        compiler_params=params(28),
        cost_estimate=cost(12),
        name="pair_update",
    )(
        left_slots,
        right_firsts,
        *left,
        *rights,
        weights,
        entry,
        switch,
        couplings.reshape(rows * columns, depth),
    )


def product_kernel(sides_ref, out_ref, *, grid_rows, grid_columns):
    channels, part, lanes = sides_ref.shape[1:]
    half = lanes // 2
    lane = lax.broadcasted_iota(jnp.int32, (grid_columns * part, lanes), 1)
    front = lane < half
    cut = front[: part // 2]
    for channel in range(channels):
        lefts, rights = [], []
        for r in range(0, grid_rows, 2):
            even, odd = [
                jnp.concatenate(
                    [sides_ref[(r + e) * grid_columns + c, channel] for c in range(grid_columns)],
                    axis=0,
                )
                for e in range(2)
            ]
            lefts.append(jnp.where(front, even, pltpu.roll(odd, half, 1)))
            rights.append(jnp.where(front, pltpu.roll(even, half, 1), odd))
        product = matmul_nt(jnp.concatenate(rights, axis=1), jnp.concatenate(lefts, axis=1))
        product = product.astype(BF16)
        for c in range(grid_columns):
            for r in range(0, grid_rows, 2):
                block = product[c * part : (c + 1) * part, r * half : (r + 2) * half]
                top, bottom = block[: part // 2], block[part // 2 :]
                even = jnp.where(cut, top, pltpu.roll(bottom, half, 1))
                out_ref[r * grid_columns + c, channel] = even
                odd = jnp.where(cut, pltpu.roll(top, half, 1), bottom)
                out_ref[(r + 1) * grid_columns + c, channel] = odd


def triangle_product(sides, grid_rows, grid_columns):
    devices, channels, part, lanes = sides.shape
    step = 2 if channels % 2 == 0 else 1
    return pl.pallas_call(
        functools.partial(product_kernel, grid_rows=grid_rows, grid_columns=grid_columns),
        grid=(channels // step,),
        in_specs=[pl.BlockSpec((devices, step, part, lanes), lambda c: (0, c, 0, 0))],
        out_specs=pl.BlockSpec((devices, step, part // 2, lanes), lambda c: (0, c, 0, 0)),
        out_shape=pltpu.HBM((devices, channels, part // 2, lanes), BF16),
        compiler_params=params(8, "arbitrary"),
        cost_estimate=cost(3),
        name="triangle_product",
    )(sides)


def output_kernel(
    product_ref, final_ref, mid_hbm, gate_hbm, out_hbm, wide_ref, mid_ref, gate_ref, out_ref, *copied
):
    channels, part, lanes = product_ref.shape
    columns, rows, depth = mid_ref.shape
    own = 8
    fetched, sent = copied
    fetches, sends = [], []
    for first in range(0, columns, own):
        chosen = pl.ds(first, own)
        for source, target in ((mid_hbm, mid_ref), (gate_hbm, gate_ref)):
            fetches.append(
                pltpu.make_async_copy(
                    source.at[chosen], target.at[chosen], fetched.at[len(fetches)]
                )
            )
            fetches[-1].start()
    wide_ref[...] = product_ref[...].astype(F32).reshape(channels * part, lanes)
    for group in range(part // own):
        updates = []
        for j in range(own):
            product = wide_ref[pl.ds(group * own + j, channels, stride=part), :]
            updates.append(matmul(normalise_rows(product).T, final_ref[...]))
        for half in range(2):
            cut = half * (part // own) + group
            fetches[2 * cut].wait()
            fetches[2 * cut + 1].wait()
            out_rows = out_ref.at[cut].reshape(rows * own, depth)
            for j in range(own):
                b = cut * own + j
                piece = updates[j][half * rows : (half + 1) * rows]
                out_rows[pl.ds(j, rows, stride=own), :] = mid_ref[b] + gate_ref[b] * piece
            sends.append(
                pltpu.make_async_copy(
                    out_ref.at[cut], out_hbm.at[:, pl.ds(cut * own, own)], sent.at[len(sends)]
                )
            )
            sends[-1].start()
    for send in sends:
        send.wait()


def pair_result(product, mid, gate, final_matrix):
    channels, part, lanes = product.shape
    columns, rows, depth = mid.shape
    vmem, hbm = pl.BlockSpec(memory_space=pltpu.VMEM), pl.BlockSpec(memory_space=pltpu.HBM)
    return pl.pallas_call(
        output_kernel,
        in_specs=[vmem, vmem, hbm, hbm],
        out_specs=hbm,
        out_shape=pltpu.HBM((rows, columns, depth), F32),
        scratch_shapes=[
            pltpu.VMEM((channels * part, lanes), F32),
            pltpu.VMEM(mid.shape, F32),
            pltpu.VMEM(mid.shape, F32),
            pltpu.VMEM((columns // 8, rows, 8, depth), F32),
            pltpu.SemaphoreType.DMA((columns // 4,)),
            pltpu.SemaphoreType.DMA((columns // 8,)),
        ],
        compiler_params=params(16),
        cost_estimate=cost(3),
        name="pair_result",
    )(
        product,
        final_matrix,
        pltpu.with_memory_space_constraint(mid, pltpu.HBM),
        pltpu.with_memory_space_constraint(gate, pltpu.HBM),
    )


def swap_cores(block):
    count = lax.axis_size("col")
    return lax.ppermute(block, "col", [(c, c ^ 1) for c in range(count)])


def gather_turned(block, later):
    rows, columns = lax.axis_size("row"), lax.axis_size("col")
    arrived = []
    for shift in range(rows):
        moves = []
        for r in range(rows):
            for q in range(rows):
                for side in range(2):
                    source = r * columns + 2 * q + side
                    moves.append((source, q * columns + 2 * ((r + shift) % rows) + side))
        source = block if shift < 2 else later
        arrived.append(lax.ppermute(source, ("row", "col"), moves))
    return arrived


def both_cores(own):
    rows = lax.axis_size("row")
    core = lax.rem(lax.axis_index("col"), 2)
    other = [swap_cores(piece) for piece in own]
    residues = own[0].shape[0] // TENSOR_FEATURES
    if residues % 8 == 0:
        return own + other
    order = left_order(rows)
    own, other = [jnp.take(jnp.stack(side), order, axis=0) for side in (own, other)]
    joined = 8 // residues
    ordered = []
    for side in (jnp.where(core == 0, own, other), jnp.where(core == 0, other, own)):
        side = side.reshape(rows // joined, joined, TENSOR_FEATURES, residues, -1)
        side = jnp.transpose(side, (0, 2, 1, 3, 4))
        ordered.extend(side.reshape(rows // joined, joined * own.shape[1], -1))
    return ordered


def left_order(rows):
    me = lax.axis_index("col") // 2
    return lax.rem(me - jnp.arange(rows, dtype=jnp.int32) + rows, rows)


def left_groups(rows, residues):
    if residues % 8:
        return jnp.arange(2 * rows * residues // 8, dtype=jnp.int32)
    core = lax.rem(lax.axis_index("col"), 2)
    order = left_order(rows)
    return jnp.concatenate([order + core * rows, order + (1 - core) * rows])


def exchange_rows(pieces):
    arrived = [pieces[0]]
    for shift in range(1, len(pieces)):
        moves = [(r, r ^ shift) for r in range(len(pieces))]
        arrived.append(lax.ppermute(pieces[shift], "row", moves))
    return arrived


def paired_entries(matrices):
    turned = matrices.reshape(C_Z, 2, 2, C_TRI)
    return jnp.transpose(turned, (2, 3, 1, 0)).reshape(2 * C_TRI, 2 * C_Z)


def body(
    homolog_tensor,
    couplings,
    attention_probe_matrix,
    attention_extra_matrices,
    attention_final_matrix,
    tensor_entry_matrices,
    tensor_final_matrix,
    incoming_entry_matrices,
    incoming_switch_matrix,
    incoming_final_matrix,
):
    inner = ATTENTION_UNITS * UNIT_WIDTH
    row_count = lax.axis_size("row")
    seqs, residues, depth = homolog_tensor.shape
    own_residues = residues // row_count
    sources = lax.axis_index("row") ^ jnp.arange(row_count, dtype=jnp.int32)
    high = exchange_rows(standardise_high(sources, homolog_tensor))
    others = jnp.concatenate(
        [attention_probe_matrix.T, attention_extra_matrices[:, inner:].T], axis=0
    )
    early = (
        attention_extra_matrices[:, :inner],
        others,
        attention_final_matrix.T,
        tensor_entry_matrices.T,
        paired_entries(incoming_entry_matrices),
        sources * own_residues,
        left_groups(row_count, own_residues),
    )
    after, early = lax.optimization_barrier((sources, early))
    low = standardise_low(after, homolog_tensor)
    high, _, early = lax.optimization_barrier((high, low, early))
    key_matrix, others, final_turned, tensor_turned, entries, firsts, slots = early
    low = exchange_rows(low)
    turned = attention(high, key_matrix, others)
    gated = turn_back(turned, row_count)
    low, gated = lax.optimization_barrier((low, gated))
    left_piece, right_piece = alignment(
        sources, high, low, turned, final_turned, tensor_turned
    )

    rights = exchange_rows([right_piece] * row_count)
    later, rights[1] = lax.optimization_barrier((left_piece, rights[1]))
    own = gather_turned(left_piece, later)
    own[-1], rights = lax.optimization_barrier((own[-1], rights))
    mid, gate, sides = pair_update(
        slots,
        firsts,
        both_cores(own),
        rights,
        tensor_final_matrix,
        couplings,
        entries,
        incoming_switch_matrix,
    )
    gated, sides = lax.optimization_barrier((gated, sides))
    gated = exchange_rows(gated)

    everywhere = ("row", "col")
    column_count = lax.axis_size("col")
    devices = row_count * column_count
    sides = sides.reshape(devices, C_TRI // devices, *sides.shape[1:])
    sides = lax.all_to_all(sides, everywhere, split_axis=0, concat_axis=0)
    gated, sides = lax.optimization_barrier((gated, sides))
    product = triangle_product(sides, row_count, column_count)
    product = lax.all_to_all(product, everywhere, split_axis=0, concat_axis=0)

    gated = jnp.take(jnp.stack(gated), sources, axis=0)
    gated = jnp.transpose(gated.reshape(residues, seqs, inner), (1, 0, 2))
    change = jnp.dot(
        gated.reshape(-1, inner), attention_final_matrix, preferred_element_type=F32
    )
    refreshed_homologs = homolog_tensor + change.reshape(homolog_tensor.shape)
    product = product.reshape(C_TRI, *product.shape[2:])
    pair_output = pair_result(product, mid, gate, incoming_final_matrix)
    return (refreshed_homologs, pair_output)


def solution(mesh):
    in_specs = (
        P("row", "col", None),
        P("row", "col", None),
        P(),
        P(),
        P(),
        P(),
        P(),
        P(),
        P(),
        P(),
    )
    out_specs = (P("row", "col", None), P("row", "col", None))
    return jax.shard_map(body, mesh=mesh, in_specs=in_specs, out_specs=out_specs, check_vma=False)
```

```python
import functools

import jax
import jax.numpy as jnp
from jax import lax
from jax.experimental import pallas as pl
from jax.experimental.pallas import tpu as pltpu
from jax.sharding import PartitionSpec as P

FEATURE_DEPTH = 256
C_Z = 128
TENSOR_FEATURES = 32
C_TRI = 128
ATTENTION_UNITS = 8
UNIT_WIDTH = 32
EPS = 1e-05
GROUP = 4
F32 = jnp.float32
BF16 = jnp.bfloat16
NT = (((1,), (1,)), ((), ()))


def matmul(left, right):
    return jnp.dot(left, right, preferred_element_type=F32)


def matmul_nt(left, right):
    return lax.dot_general(left, right, NT, preferred_element_type=F32)


def sigmoid(values):
    return 0.5 * jnp.tanh(0.5 * values) + 0.5


def cost(microseconds):
    return pl.CostEstimate(
        flops=int(microseconds * 1e9), bytes_accessed=int(microseconds * 1e6), transcendentals=0
    )


def params(megabytes, *semantics):
    return pltpu.CompilerParams(
        dimension_semantics=semantics or None, vmem_limit_bytes=megabytes * 1024 * 1024
    )


def fold(values, combine):
    while values.shape[0] > 8:
        half = values.shape[0] // 2
        values = combine(values[:half], values[half:])
    return values


def top_rows(values):
    return jnp.max(fold(values, jnp.maximum), axis=0, keepdims=True)


def sum_rows(values):
    return jnp.sum(fold(values, jnp.add), axis=0, keepdims=True)


def normalise_rows(values):
    count = values.shape[0]
    centred = values - sum_rows(values) * (1.0 / count)
    variance = sum_rows(centred * centred) * (1.0 / count)
    return (centred * lax.rsqrt(variance + EPS)).astype(BF16)


def standardised_columns(first_rows, second_rows, first, count, residues):
    seqs = first_rows.shape[0] // residues
    columns = []
    for n in range(count):
        rows = pl.ds(first + n, seqs, stride=residues)
        columns.append(jnp.concatenate([first_rows[rows, :], second_rows[rows, :]], axis=1))
    column = jnp.concatenate(columns, axis=0)
    centred = column - jnp.mean(column, axis=1, keepdims=True)
    variance = jnp.mean(centred * centred, axis=1, keepdims=True) + EPS
    scale = lax.rsqrt(variance)
    return centred * scale, variance * scale


def high_kernel(sources_ref, block_hbm, *rest):
    *pieces_hbm, first_ref, second_ref, high_ref, fetched, sent = rest
    seqs, residues, lanes = first_ref.shape
    own = residues // len(pieces_hbm)
    step = 16
    fetches, sends = [], []
    for s in range(0, seqs, step):
        chosen = pl.ds(s, step)
        for half, ref in enumerate((first_ref, second_ref)):
            source = block_hbm.at[chosen, :, pl.ds(half * lanes, lanes)]
            fetches.append(
                pltpu.make_async_copy(source, ref.at[chosen], fetched.at[len(fetches)])
            )
            fetches[-1].start()
    for part in range(seqs // step):
        chosen = pl.ds(part * step, step)
        fetches[2 * part].wait()
        fetches[2 * part + 1].wait()
        first_rows = first_ref.at[chosen].reshape(step * residues, lanes)
        second_rows = second_ref.at[chosen].reshape(step * residues, lanes)
        for n in range(0, residues, 8):
            normed, _ = standardised_columns(first_rows, second_rows, n, 8, residues)
            high_ref[part, n : n + 8] = normed.astype(BF16).reshape(8, step, 2 * lanes)
        for p, piece_hbm in enumerate(pieces_hbm):
            source = high_ref.at[part, pl.ds(sources_ref[p] * own, own)]
            sends.append(
                pltpu.make_async_copy(source, piece_hbm.at[:, chosen], sent.at[len(sends)])
            )
            sends[-1].start()
    for send in sends:
        send.wait()


def standardise_high(sources, block):
    seqs, residues, depth = block.shape
    half = depth // 2
    count = sources.shape[0]
    hbm = pl.BlockSpec(memory_space=pltpu.HBM)
    return pl.pallas_call(
        high_kernel,
        in_specs=[pl.BlockSpec(memory_space=pltpu.SMEM), hbm],
        out_specs=[hbm] * count,
        out_shape=[pltpu.HBM((residues // count, seqs, depth), BF16)] * count,
        scratch_shapes=[
            pltpu.VMEM((seqs, residues, half), F32),
            pltpu.VMEM((seqs, residues, half), F32),
            pltpu.VMEM((seqs // 16, residues, 16, depth), BF16),
            pltpu.SemaphoreType.DMA((seqs // 8,)),
            pltpu.SemaphoreType.DMA((seqs // 16 * count,)),
        ],
        compiler_params=params(10),
        cost_estimate=cost(3),
        name="standardise_high",
    )(sources, pltpu.with_memory_space_constraint(block, pltpu.HBM))


def low_kernel(sources_ref, first_ref, second_ref, *rest):
    *pieces_hbm, low_ref, sent = rest
    seqs, residues, lanes = first_ref.shape
    count = len(pieces_hbm)
    own = (low_ref.shape[1] - 16) // seqs
    step = pl.program_id(0)
    first_rows = first_ref.reshape(seqs * residues, lanes)
    second_rows = second_ref.reshape(seqs * residues, lanes)
    shift = lax.rem(sources_ref[step] * own, residues) if own < residues else 0
    lane = lax.broadcasted_iota(jnp.int32, (seqs, 128), 1)
    spreads = jnp.zeros((seqs, 128), F32)
    for n in range(own):
        normed, spread = standardised_columns(first_rows, second_rows, shift + n, 1, residues)
        left = (normed - normed.astype(BF16).astype(F32)).astype(BF16)
        low_ref[step, n * seqs : (n + 1) * seqs, :] = left
        spreads = jnp.where(lane == n, spread, spreads)
    spreads = spreads.T[:8, :]
    coarse = spreads.astype(BF16).astype(F32)
    kept = jnp.concatenate([coarse, spreads - coarse], axis=0)
    kept = jnp.concatenate([kept, jnp.zeros((16, 2 * lanes - seqs), F32)], axis=1)
    low_ref[step, own * seqs :, :] = kept.astype(BF16)
    copies = [
        pltpu.make_async_copy(low_ref.at[p], piece_hbm, sent.at[p])
        for p, piece_hbm in enumerate(pieces_hbm)
    ]
    for p in range(count):

        @pl.when(step == p)
        def _(p=p):
            copies[p].start()

    @pl.when(step == count - 1)
    def _():
        for copy in copies:
            copy.wait()


def standardise_low(sources, block):
    seqs, residues, depth = block.shape
    half = depth // 2
    count = sources.shape[0]
    own = residues // count
    height = own * seqs + 16
    together = 8 // own
    hbm = pl.BlockSpec(memory_space=pltpu.HBM)
    return pl.pallas_call(
        low_kernel,
        grid_spec=pltpu.PrefetchScalarGridSpec(
            num_scalar_prefetch=1,
            grid=(count,),
            in_specs=[
                pl.BlockSpec((seqs, 8, half), lambda p, sources: (0, sources[p] // together, 0)),
                pl.BlockSpec((seqs, 8, half), lambda p, sources: (0, sources[p] // together, 1)),
            ],
            out_specs=[hbm] * count,
            scratch_shapes=[
                pltpu.VMEM((count, height, depth), BF16),
                pltpu.SemaphoreType.DMA((count,)),
            ],
        ),
        out_shape=[pltpu.HBM((height, depth), BF16)] * count,
        compiler_params=params(10, "arbitrary"),
        cost_estimate=cost(4),
        name="standardise_low",
    )(sources, block, block)


def attention_kernel(key_ref, probe_ref, others_ref, *rest):
    *normed_refs, turned_ref, scores_ref, weights_ref = rest
    blocks = len(normed_refs)
    residues, seqs, _ = normed_refs[0].shape
    total = blocks * seqs
    inner = ATTENTION_UNITS * UNIT_WIDTH
    ring = scores_ref.shape[0]
    columns = []

    def project(n):
        column = jnp.concatenate([ref[n] for ref in normed_refs], axis=0)
        key_rows = matmul(column, key_ref[...]).astype(BF16)
        queries = (matmul_nt(probe_ref[...], column) * UNIT_WIDTH ** (-0.5)).astype(BF16)
        projected = matmul_nt(others_ref[...], column)
        value_rows = projected[:inner].astype(BF16)
        gates = sigmoid(projected[inner:])
        columns.append((key_rows, queries, value_rows, gates))
    units = [(n, h) for n in range(residues) for h in range(ATTENTION_UNITS)]

    def score(unit):
        n, h = units[unit]
        key_rows, queries, _, _ = columns[n]
        rows = slice(h * UNIT_WIDTH, (h + 1) * UNIT_WIDTH)
        scores_ref[unit % ring] = matmul(key_rows[:, rows], queries[rows])

    def weigh(unit):
        for low in range(0, total, 128):
            scores = scores_ref[unit % ring, :, low : low + 128]
            weights = jnp.exp(scores - top_rows(scores))
            scale = 1.0 / sum_rows(weights)
            weights_ref[unit % ring, :, low : low + 128] = (weights * scale).astype(BF16)

    def attend(unit):
        n, h = units[unit]
        _, _, value_rows, gates = columns[n]
        rows = slice(h * UNIT_WIDTH, (h + 1) * UNIT_WIDTH)
        attended = matmul(value_rows[rows], weights_ref[unit % ring]) * gates[rows]
        turned_ref[n, rows, :] = attended.astype(BF16)

    project(0)
    for step in range(len(units) + 2):
        if step < len(units):
            score(step)
            n, h = units[step]
            if h == ATTENTION_UNITS // 2 and n + 1 < residues:
                project(n + 1)
        if 1 <= step <= len(units):
            weigh(step - 1)
        if step >= 2:
            attend(step - 2)


def attention(normed, key_matrix, probe_matrix, other_matrices):
    blocks = len(normed)
    residues, seqs, depth = normed[0].shape
    total = blocks * seqs
    inner = ATTENTION_UNITS * UNIT_WIDTH
    step = 4
    return pl.pallas_call(
        attention_kernel,
        grid=(residues // step,),
        in_specs=[
            pl.BlockSpec((depth, inner), lambda n: (0, 0)),
            pl.BlockSpec((inner, depth), lambda n: (0, 0)),
            pl.BlockSpec((2 * inner, depth), lambda n: (0, 0)),
        ]
        + [pl.BlockSpec((step, seqs, depth), lambda n: (n, 0, 0))] * blocks,
        out_specs=pl.BlockSpec((step, inner, total), lambda n: (n, 0, 0)),
        out_shape=jax.ShapeDtypeStruct((residues, inner, total), BF16),
        scratch_shapes=[
            pltpu.VMEM((4, total, total), F32),
            pltpu.VMEM((4, total, total), BF16),
        ],
        compiler_params=params(12 + (total // 128) ** 2, "arbitrary"),
        cost_estimate=cost(10),
        name="attention",
    )(key_matrix, probe_matrix, other_matrices, *normed)


def turn_kernel(turned_ref, *gated_refs):
    seqs = gated_refs[0].shape[1]
    for n in range(turned_ref.shape[0]):
        back = turned_ref[n].T
        for block, gated_ref in enumerate(gated_refs):
            gated_ref[n] = back[block * seqs : (block + 1) * seqs]


def turn_back(turned, blocks):
    residues, inner, total = turned.shape
    seqs = total // blocks
    return pl.pallas_call(
        turn_kernel,
        grid=(residues // 2,),
        in_specs=[pl.BlockSpec((2, inner, total), lambda n: (n, 0, 0))],
        out_specs=[pl.BlockSpec((2, seqs, inner), lambda n: (n, 0, 0))] * blocks,
        out_shape=[pltpu.HBM((residues, seqs, inner), BF16)] * blocks,
        compiler_params=params(12, "arbitrary"),
        cost_estimate=cost(2),
        name="turn_back",
    )(turned)


def alignment_kernel(sources_ref, turned_ref, final_ref, entry_ref, *rest):
    *refs, left_ref, right_ref, rows_ref = rest
    blocks = len(refs) // 3
    high_refs, low_refs, spread_refs = refs[:blocks], refs[blocks : 2 * blocks], refs[2 * blocks :]
    residues, seqs, depth = high_refs[0].shape
    total = blocks * seqs
    features = TENSOR_FEATURES
    step = pl.program_id(0)
    for n in range(residues):
        column = jnp.concatenate([ref[n] for ref in high_refs], axis=0).astype(F32)
        column = column + jnp.concatenate(
            [ref[n * seqs : (n + 1) * seqs, :] for ref in low_refs], axis=0
        ).astype(F32)
        spreads = []
        for ref in spread_refs:
            kept = ref[:, :seqs].astype(F32)
            row = lax.broadcasted_iota(jnp.int32, kept.shape, 0)
            chosen = lax.rem(row, 8) == step * residues + n
            spreads.append(jnp.sum(jnp.where(chosen, kept, 0.0), axis=0, keepdims=True))
        spread = jnp.concatenate(spreads, axis=1)
        updated = column.T * spread + matmul(final_ref[...], turned_ref[n])
        projected = matmul(entry_ref[...], normalise_rows(updated))
        me = sources_ref[0]
        tiles = [projected[:, low : low + 128] for low in range(0, total, 128)]
        odd = lax.rem(me, 2) == 1
        tiles = [jnp.where(odd, pltpu.roll(tile, seqs, 1), tile) for tile in tiles]
        width = 1
        while width < len(tiles):
            crossed = lax.rem(lax.div(me, 2 * width), 2) == 1
            tiles = [
                jnp.where(crossed, tiles[t ^ width], tiles[t]) for t in range(len(tiles))
            ]
            width *= 2
        first = pl.multiple_of((step * residues + n) * features, features)
        for t, tile in enumerate(tiles):
            right_ref[n, :, t * 128 : (t + 1) * 128] = tile[features:].astype(BF16)
            rows_ref[t, pl.ds(first, features), :] = tile[:features]

    @pl.when(step == pl.num_programs(0) - 1)
    def _():
        count = rows_ref.shape[1] // features
        together = max(1, 16 // count)
        for c in range(0, features, together):
            pieces = []
            for e in range(together):
                chosen = pl.ds(c + e, count, stride=features)
                tiles = [rows_ref[tile, chosen, :] for tile in range(total // 128)]
                pieces.append(jnp.concatenate(tiles, axis=1))
            piece = jnp.concatenate(pieces, axis=0).astype(BF16)
            left_ref[c * count : (c + together) * count, :] = piece


def alignment(sources, high, low, turned, final_matrix, entry_matrices):
    blocks = len(high)
    residues, seqs, depth = high[0].shape
    total = blocks * seqs
    features = TENSOR_FEATURES
    step = 4
    height = residues * seqs + 16
    return pl.pallas_call(
        alignment_kernel,
        grid=(residues // step,),
        in_specs=[
            pl.BlockSpec(memory_space=pltpu.SMEM),
            pl.BlockSpec((step, depth, total), lambda n: (n, 0, 0)),
            pl.BlockSpec(final_matrix.shape, lambda n: (0, 0)),
            pl.BlockSpec(entry_matrices.shape, lambda n: (0, 0)),
        ]
        + [pl.BlockSpec((step, seqs, depth), lambda n: (n, 0, 0))] * blocks
        + [pl.BlockSpec((step * seqs, depth), lambda n: (n, 0))] * blocks
        + [pl.BlockSpec((16, depth), lambda n: (height // 16 - 1, 0))] * blocks,
        out_specs=[
            pl.BlockSpec((features * residues, total), lambda n: (0, 0)),
            pl.BlockSpec((step, features, total), lambda n: (n, 0, 0)),
        ],
        out_shape=[
            jax.ShapeDtypeStruct((features * residues, total), BF16),
            jax.ShapeDtypeStruct((residues, features, total), BF16),
        ],
        scratch_shapes=[pltpu.VMEM((total // 128, residues * features, 128), F32)],
        compiler_params=params(16, "arbitrary"),
        cost_estimate=cost(4),
        name="alignment",
    )(sources, turned, final_matrix, entry_matrices, *high, *low, *low)


def pair_kernel(
    left_slots_ref,
    right_firsts_ref,
    *rest,
    slots,
):
    weights_ref, entry_ref, switch_ref, couplings_hbm, mid_hbm, gate_hbm, sides_hbm = rest[-16:-9]
    outer_ref, spread_ref, sum_ref, rows_ref, couplings_ref = rest[-9:-4]
    mid_ref, gate_ref, sides_ref, copied = rest[-4:]
    left_refs, right_refs = rest[: 2 * slots], rest[2 * slots : -16]
    fetched = pltpu.make_async_copy(couplings_hbm, couplings_ref, copied.at[0])
    fetched.start()
    copies = []

    def send(source, target):
        copies.append(pltpu.make_async_copy(source, target, copied.at[len(copies) + 1]))
        copies[-1].start()

    features = TENSOR_FEATURES
    piece_rows, total = left_refs[0].shape
    residues = piece_rows // features
    rows = 2 * slots * residues
    share = right_refs[0].shape[0]
    columns = len(right_refs) * share
    groups = columns // GROUP
    wide = share * features
    together = spread_ref.shape[1] // 64

    for half in range(2):
        halves = left_refs[half * slots : (half + 1) * slots]
        piece = jnp.concatenate([ref[...] for ref in halves], axis=0)
        target = slice(half * slots * piece_rows, (half + 1) * slots * piece_rows)
        for p, right_ref in enumerate(right_refs):
            right = right_ref[...].reshape(wide, total)
            outer_ref[target, p * wide : (p + 1) * wide] = matmul_nt(piece, right) * (1.0 / total)

    spread_ref[...] = jnp.zeros_like(spread_ref)
    front = lax.broadcasted_iota(jnp.int32, (rows, 128), 1) < 64

    def channel_step(p, carry):
        slot = lax.rem(p, 2)
        for e in range(together):
            source = pl.multiple_of((p * together + e) * features, features)
            piece = weights_ref[pl.ds(source, features), :]
            for place in range(2):
                low = e * 64 + place * features
                spread_ref[slot, low : low + features, place * C_Z : (place + 1) * C_Z] = piece
        pieces = []
        for g in range(groups):
            parts = []
            for e in range(together):
                channel = []
                for slot_number in range(2 * slots):
                    first = slot_number * piece_rows + (p * together + e) * residues
                    source = pl.ds(pl.multiple_of(first, residues), residues)
                    channel.append(outer_ref[source, g * 128 : (g + 1) * 128])
                parts.append(jnp.concatenate(channel, axis=0).astype(BF16))
            lows, highs = [], []
            for e in range(0, together, 2):
                lows.append(jnp.where(front, parts[e], pltpu.roll(parts[e + 1], 64, 1)))
                highs.append(jnp.where(front, pltpu.roll(parts[e], 64, 1), parts[e + 1]))
            pieces.append(jnp.concatenate(lows, axis=1))
            pieces.append(jnp.concatenate(highs, axis=1))
        update = matmul(jnp.concatenate(pieces, axis=0), spread_ref[slot])

        @pl.when(p == 0)
        def _():
            sum_ref[...] = update

        @pl.when(p > 0)
        def _():
            sum_ref[...] += update

        return carry

    lax.fori_loop(0, features // together, channel_step, 0)

    left_firsts = [left_slots_ref[j] * residues for j in range(2 * slots)]
    right_firsts = [right_firsts_ref[p] for p in range(len(right_refs))]
    fetched.wait()
    for g in range(groups):
        normed, places = [], []
        for place in range(GROUP):
            p, n = divmod(g * GROUP + place, share)
            b = right_firsts[p] + n
            places.append(b)
            lanes = slice(place % 2 * C_Z, (place % 2 + 1) * C_Z)
            start = (2 * g + place // 2) * rows
            pieces = []
            for first in left_firsts:
                source = pl.ds(pl.multiple_of(start + first, residues), residues)
                pieces.append(sum_ref[source, lanes])
            mid = jnp.concatenate(pieces, axis=0)
            mid = mid + couplings_ref[pl.ds(b, rows, stride=columns), :]
            mid_ref[g * GROUP + place] = mid
            centred = mid - jnp.mean(mid, axis=1, keepdims=True)
            variance = jnp.mean(centred * centred, axis=1, keepdims=True)
            normed.append((centred * lax.rsqrt(variance + EPS)).astype(BF16))
        gates = sigmoid(matmul(jnp.concatenate(normed, axis=0), switch_ref[...]))
        blank = jnp.zeros_like(normed[0])
        for place in range(0, GROUP, 2):
            twice = []
            for e in range(2):
                part = gates[(place + e) * rows : (place + e + 1) * rows]
                gate_ref[g * GROUP + place + e] = part
                twice.append(jnp.concatenate([normed[place + e], blank], axis=1))
                twice.append(jnp.concatenate([blank, normed[place + e]], axis=1))
            sides = matmul_nt(entry_ref[...], jnp.concatenate(twice, axis=0))
            sides = sigmoid(sides[C_TRI:]) * sides[:C_TRI]
            for e in range(2):
                first = pl.multiple_of(places[place + e] * C_TRI, C_TRI)
                rows_ref[pl.ds(first, C_TRI), :] = sides[:, e * 2 * rows : (e + 1) * 2 * rows]

        if (g + 1) * GROUP % share == 0:
            p = (g + 1) * GROUP // share - 1
            source, target = pl.ds(p * share, share), pl.ds(right_firsts[p], share)
            send(mid_ref.at[source], mid_hbm.at[target])
            send(gate_ref.at[source], gate_hbm.at[target])

    cut = C_TRI // 8
    for part in range(8):

        def turn_step(c, carry):
            sides_ref[c] = rows_ref[pl.ds(c, columns, stride=C_TRI), :].astype(BF16)
            return carry

        lax.fori_loop(part * cut, (part + 1) * cut, turn_step, 0, unroll=8)
        chosen = pl.ds(part * cut, cut)
        send(sides_ref.at[chosen], sides_hbm.at[chosen])
    for copy in copies:
        copy.wait()


def pair_update(left_slots, right_firsts, left, rights, weights, couplings, entry, switch):
    rows, columns, depth = couplings.shape
    whole = jax.ShapeDtypeStruct((columns, rows, depth), F32)
    sides = jax.ShapeDtypeStruct((C_TRI, columns, 2 * rows), BF16)
    smem = pl.BlockSpec(memory_space=pltpu.SMEM)
    vmem = pl.BlockSpec(memory_space=pltpu.VMEM)
    anywhere = pl.BlockSpec(memory_space=pl.ANY)
    return pl.pallas_call(
        functools.partial(pair_kernel, slots=len(left) // 2),
        in_specs=[smem] * 2 + [vmem] * (3 + len(left) + len(rights)) + [anywhere],
        out_specs=[anywhere] * 3,
        out_shape=[pltpu.HBM(whole.shape, F32)] * 2 + [pltpu.HBM(sides.shape, BF16)],
        scratch_shapes=[
            pltpu.VMEM((rows * TENSOR_FEATURES, columns * TENSOR_FEATURES), F32),
            pltpu.VMEM((2, 8 * 64, 2 * depth), BF16),
            pltpu.VMEM((columns // 2 * rows, 2 * depth), F32),
            pltpu.VMEM((columns * C_TRI, 2 * rows), F32),
            pltpu.VMEM((rows * columns, depth), F32),
            pltpu.VMEM(whole.shape, F32),
            pltpu.VMEM(whole.shape, F32),
            pltpu.VMEM(sides.shape, BF16),
            pltpu.SemaphoreType.DMA((2 * len(rights) + 9,)),
        ],
        compiler_params=params(28),
        cost_estimate=cost(12),
        name="pair_update",
    )(
        left_slots,
        right_firsts,
        *left,
        *rights,
        weights,
        entry,
        switch,
        couplings.reshape(rows * columns, depth),
    )


def product_kernel(sides_ref, out_ref, *, grid_rows, grid_columns):
    channels, part, lanes = sides_ref.shape[1:]
    half = lanes // 2
    lane = lax.broadcasted_iota(jnp.int32, (grid_columns * part, lanes), 1)
    front = lane < half
    cut = front[: part // 2]
    for channel in range(channels):
        lefts, rights = [], []
        for r in range(0, grid_rows, 2):
            even, odd = [
                jnp.concatenate(
                    [sides_ref[(r + e) * grid_columns + c, channel] for c in range(grid_columns)],
                    axis=0,
                )
                for e in range(2)
            ]
            lefts.append(jnp.where(front, even, pltpu.roll(odd, half, 1)))
            rights.append(jnp.where(front, pltpu.roll(even, half, 1), odd))
        product = matmul_nt(jnp.concatenate(rights, axis=1), jnp.concatenate(lefts, axis=1))
        product = product.astype(BF16)
        for c in range(grid_columns):
            for r in range(0, grid_rows, 2):
                block = product[c * part : (c + 1) * part, r * half : (r + 2) * half]
                top, bottom = block[: part // 2], block[part // 2 :]
                even = jnp.where(cut, top, pltpu.roll(bottom, half, 1))
                out_ref[r * grid_columns + c, channel] = even
                odd = jnp.where(cut, pltpu.roll(top, half, 1), bottom)
                out_ref[(r + 1) * grid_columns + c, channel] = odd


def triangle_product(sides, grid_rows, grid_columns):
    devices, channels, part, lanes = sides.shape
    step = 2 if channels % 2 == 0 else 1
    return pl.pallas_call(
        functools.partial(product_kernel, grid_rows=grid_rows, grid_columns=grid_columns),
        grid=(channels // step,),
        in_specs=[pl.BlockSpec((devices, step, part, lanes), lambda c: (0, c, 0, 0))],
        out_specs=pl.BlockSpec((devices, step, part // 2, lanes), lambda c: (0, c, 0, 0)),
        out_shape=pltpu.HBM((devices, channels, part // 2, lanes), BF16),
        compiler_params=params(8, "arbitrary"),
        cost_estimate=cost(3),
        name="triangle_product",
    )(sides)


def output_kernel(
    product_ref, final_ref, mid_hbm, gate_hbm, out_hbm, wide_ref, mid_ref, gate_ref, out_ref, *copied
):
    channels, part, lanes = product_ref.shape
    columns, rows, depth = mid_ref.shape
    own = 8
    fetched, sent = copied
    fetches, sends = [], []
    for first in range(0, columns, own):
        chosen = pl.ds(first, own)
        for source, target in ((mid_hbm, mid_ref), (gate_hbm, gate_ref)):
            fetches.append(
                pltpu.make_async_copy(
                    source.at[chosen], target.at[chosen], fetched.at[len(fetches)]
                )
            )
            fetches[-1].start()
    wide_ref[...] = product_ref[...].astype(F32).reshape(channels * part, lanes)
    for group in range(part // own):
        updates = []
        for j in range(own):
            product = wide_ref[pl.ds(group * own + j, channels, stride=part), :]
            updates.append(matmul(normalise_rows(product).T, final_ref[...]))
        for half in range(2):
            cut = half * (part // own) + group
            fetches[2 * cut].wait()
            fetches[2 * cut + 1].wait()
            out_rows = out_ref.at[cut].reshape(rows * own, depth)
            for j in range(own):
                b = cut * own + j
                piece = updates[j][half * rows : (half + 1) * rows]
                out_rows[pl.ds(j, rows, stride=own), :] = mid_ref[b] + gate_ref[b] * piece
            sends.append(
                pltpu.make_async_copy(
                    out_ref.at[cut], out_hbm.at[:, pl.ds(cut * own, own)], sent.at[len(sends)]
                )
            )
            sends[-1].start()
    for send in sends:
        send.wait()


def pair_result(product, mid, gate, final_matrix):
    channels, part, lanes = product.shape
    columns, rows, depth = mid.shape
    vmem, hbm = pl.BlockSpec(memory_space=pltpu.VMEM), pl.BlockSpec(memory_space=pltpu.HBM)
    return pl.pallas_call(
        output_kernel,
        in_specs=[vmem, vmem, hbm, hbm],
        out_specs=hbm,
        out_shape=pltpu.HBM((rows, columns, depth), F32),
        scratch_shapes=[
            pltpu.VMEM((channels * part, lanes), F32),
            pltpu.VMEM(mid.shape, F32),
            pltpu.VMEM(mid.shape, F32),
            pltpu.VMEM((columns // 8, rows, 8, depth), F32),
            pltpu.SemaphoreType.DMA((columns // 4,)),
            pltpu.SemaphoreType.DMA((columns // 8,)),
        ],
        compiler_params=params(16),
        cost_estimate=cost(3),
        name="pair_result",
    )(
        product,
        final_matrix,
        pltpu.with_memory_space_constraint(mid, pltpu.HBM),
        pltpu.with_memory_space_constraint(gate, pltpu.HBM),
    )


def swap_cores(block):
    count = lax.axis_size("col")
    return lax.ppermute(block, "col", [(c, c ^ 1) for c in range(count)])


def gather_turned(block, later):
    rows, columns = lax.axis_size("row"), lax.axis_size("col")
    arrived = []
    for shift in range(rows):
        moves = []
        for r in range(rows):
            for q in range(rows):
                for side in range(2):
                    source = r * columns + 2 * q + side
                    moves.append((source, q * columns + 2 * ((r + shift) % rows) + side))
        source = block if shift < 2 else later
        arrived.append(lax.ppermute(source, ("row", "col"), moves))
    return arrived


def both_cores(own):
    rows = lax.axis_size("row")
    core = lax.rem(lax.axis_index("col"), 2)
    other = [swap_cores(piece) for piece in own]
    residues = own[0].shape[0] // TENSOR_FEATURES
    if residues % 8 == 0:
        return own + other
    order = left_order(rows)
    own, other = [jnp.take(jnp.stack(side), order, axis=0) for side in (own, other)]
    joined = 8 // residues
    ordered = []
    for side in (jnp.where(core == 0, own, other), jnp.where(core == 0, other, own)):
        side = side.reshape(rows // joined, joined, TENSOR_FEATURES, residues, -1)
        side = jnp.transpose(side, (0, 2, 1, 3, 4))
        ordered.extend(side.reshape(rows // joined, joined * own.shape[1], -1))
    return ordered


def left_order(rows):
    me = lax.axis_index("col") // 2
    return lax.rem(me - jnp.arange(rows, dtype=jnp.int32) + rows, rows)


def left_groups(rows, residues):
    if residues % 8:
        return jnp.arange(2 * rows * residues // 8, dtype=jnp.int32)
    core = lax.rem(lax.axis_index("col"), 2)
    order = left_order(rows)
    return jnp.concatenate([order + core * rows, order + (1 - core) * rows])


def exchange_rows(pieces):
    arrived = [pieces[0]]
    for shift in range(1, len(pieces)):
        moves = [(r, r ^ shift) for r in range(len(pieces))]
        arrived.append(lax.ppermute(pieces[shift], "row", moves))
    return arrived


def paired_entries(matrices):
    turned = matrices.reshape(C_Z, 2, 2, C_TRI)
    return jnp.transpose(turned, (2, 3, 1, 0)).reshape(2 * C_TRI, 2 * C_Z)


def body(
    homolog_tensor,
    couplings,
    attention_probe_matrix,
    attention_extra_matrices,
    attention_final_matrix,
    tensor_entry_matrices,
    tensor_final_matrix,
    incoming_entry_matrices,
    incoming_switch_matrix,
    incoming_final_matrix,
):
    inner = ATTENTION_UNITS * UNIT_WIDTH
    row_count = lax.axis_size("row")
    seqs, residues, depth = homolog_tensor.shape
    own_residues = residues // row_count
    sources = lax.axis_index("row") ^ jnp.arange(row_count, dtype=jnp.int32)
    high = exchange_rows(standardise_high(sources, homolog_tensor))
    early = (
        attention_extra_matrices[:, :inner],
        attention_probe_matrix.T,
        attention_extra_matrices[:, inner:].T,
        attention_final_matrix.T,
        tensor_entry_matrices.T,
        paired_entries(incoming_entry_matrices),
        sources * own_residues,
        left_groups(row_count, own_residues),
    )
    after, early = lax.optimization_barrier((sources, early))
    low = standardise_low(after, homolog_tensor)
    high, _, early = lax.optimization_barrier((high, low, early))
    key_matrix, probe_turned, others, final_turned, tensor_turned, entries, firsts, slots = early
    low = exchange_rows(low)
    turned = attention(high, key_matrix, probe_turned, others)
    gated = turn_back(turned, row_count)
    low, gated = lax.optimization_barrier((low, gated))
    left_piece, right_piece = alignment(
        sources, high, low, turned, final_turned, tensor_turned
    )

    rights = exchange_rows([right_piece] * row_count)
    later, rights[1] = lax.optimization_barrier((left_piece, rights[1]))
    own = gather_turned(left_piece, later)
    own[-1], rights = lax.optimization_barrier((own[-1], rights))
    mid, gate, sides = pair_update(
        slots,
        firsts,
        both_cores(own),
        rights,
        tensor_final_matrix,
        couplings,
        entries,
        incoming_switch_matrix,
    )
    gated, sides = lax.optimization_barrier((gated, sides))
    gated = exchange_rows(gated)

    everywhere = ("row", "col")
    column_count = lax.axis_size("col")
    devices = row_count * column_count
    sides = sides.reshape(devices, C_TRI // devices, *sides.shape[1:])
    sides = lax.all_to_all(sides, everywhere, split_axis=0, concat_axis=0)
    gated, sides = lax.optimization_barrier((gated, sides))
    product = triangle_product(sides, row_count, column_count)
    product = lax.all_to_all(product, everywhere, split_axis=0, concat_axis=0)

    gated = jnp.take(jnp.stack(gated), sources, axis=0)
    gated = jnp.transpose(gated.reshape(residues, seqs, inner), (1, 0, 2))
    change = jnp.dot(
        gated.reshape(-1, inner), attention_final_matrix, preferred_element_type=F32
    )
    refreshed_homologs = homolog_tensor + change.reshape(homolog_tensor.shape)
    product = product.reshape(C_TRI, *product.shape[2:])
    pair_output = pair_result(product, mid, gate, incoming_final_matrix)
    return (refreshed_homologs, pair_output)


def solution(mesh):
    in_specs = (
        P("row", "col", None),
        P("row", "col", None),
        P(),
        P(),
        P(),
        P(),
        P(),
        P(),
        P(),
        P(),
    )
    out_specs = (P("row", "col", None), P("row", "col", None))
    return jax.shard_map(body, mesh=mesh, in_specs=in_specs, out_specs=out_specs, check_vma=False)
```
